32 devices in a mesh: ctx: 4 (over y, core), exp: 8 (over z, x).
Axes of the slice: x: 2, y: 2, z: 4, core: 2. Of those that a mesh axis runs over, the one named last changes fastest.
Arguments:
- tokens: bfloat16 [8, 1024, 1024], P('exp', 'ctx'), may hold values from -6 to 6
- segments: int32 [8, 1024], P('exp'), may hold values from 0 to 2, as said below
- routes: int32 [8, 1024, 8], P('exp', 'ctx'), may hold values from 0 to 31, all different within a row
- gain_attn: bfloat16 [1024], P(('ctx', 'exp')), may hold values from 0.5 to 1.5
- gain_moe: bfloat16 [1024], P(('ctx', 'exp')), may hold values from 0.5 to 1.5
- query_weight: bfloat16 [1024, 1024], P(('ctx', 'exp')), may hold values from -0.375 to 0.375
- key_weight: bfloat16 [1024, 512], P(('ctx', 'exp')), may hold values from -0.1875 to 0.1875
- value_weight: bfloat16 [1024, 512], P(('ctx', 'exp')), may hold values from -0.1875 to 0.1875
- w_output: bfloat16 [1024, 1024], P(('ctx', 'exp')), may hold values from -0.75 to 0.75
- w_router: bfloat16 [1024, 32], P(('ctx', 'exp')), may hold values from -0.09375 to 0.09375
- w_expert_in: bfloat16 [32, 1024, 1024], P('exp', 'ctx'), may hold values from -0.1875 to 0.1875
- w_expert_out: bfloat16 [32, 512, 1024], P('exp', 'ctx'), may hold values from -0.5 to 0.5
- cotangent: bfloat16 [8, 1024, 1024], P('exp', 'ctx'), may hold values from -6 to 6
Outputs:
- mixed_out: bfloat16 [8, 1024, 1024], P('exp', 'ctx')
- grad_tokens: float32 [8, 1024, 1024], P('exp', 'ctx')
- grad_gain_attn: float32 [1024], P(('ctx', 'exp'))
- grad_gain_moe: float32 [1024], P(('ctx', 'exp'))
- grad_w_query: float32 [1024, 1024], P(('ctx', 'exp'))
- grad_w_key: float32 [1024, 512], P(('ctx', 'exp'))
- grad_w_value: float32 [1024, 512], P(('ctx', 'exp'))
- grad_w_output: float32 [1024, 1024], P(('ctx', 'exp'))
- grad_w_router: float32 [1024, 32], P(('ctx', 'exp'))
- grad_w_expert_in: float32 [32, 1024, 1024], P('exp', 'ctx')
- grad_w_expert_out: float32 [32, 512, 1024], P('exp', 'ctx')
The draws below stay inside these ranges and needn't reach their ends.
Inputs may be any that keep to these rules, and one draw needn't show every extreme that they name: `routes`: each position names 8 different experts, and every expert is named somewhere. `segments`: in every pack the numbers never fall; document 0 ends within the first 256 positions, document 2 begins within the last 256 positions, document 1 lies between.
All inputs are finite; a program needn't handle non-finite values.
Results may differ from the reference program's by a relative error of at most 0.022.
Values may be sent and summed in bfloat16 or wider, within the bound.
A program may use at most 256 MiB of HBM per device.

```python
import math
import jax
import jax.numpy as jnp
from jax import lax

MODEL_WIDTH = 1024
QUERY_HEADS = 16
KEY_VALUE_HEADS = 8
HEAD_SIZE = 64
EXPERTS = 32
TOPK = 8
FF = 512
BLK = 256
LEN = 1024
SEQS = 8
CAP = 72


def draw_segments(key, part):
    key = jax.random.fold_in(key, 11)
    first_key, last_key = jax.random.split(key)
    first_end = jax.random.randint(first_key, (SEQS, 1), 1, BLK, dtype=jnp.int32)
    last_start = jax.random.randint(last_key, (SEQS, 1), LEN - BLK + 1, LEN, dtype=jnp.int32)
    positions = jnp.arange(LEN, dtype=jnp.int32)[None, :]
    return (positions >= first_end).astype(jnp.int32) + (positions >= last_start).astype(jnp.int32)


def block_scale(own_key, dims, cuts, least, largest):
    gain = 1.0
    for axis_at, parts in cuts:
        draws = jax.random.uniform(jax.random.fold_in(jax.random.fold_in(own_key, 6), axis_at), (parts,), jnp.float32, least / len(cuts), largest / len(cuts))
        gain = gain * jnp.repeat(jnp.exp(draws), dims[axis_at] // parts).reshape((-1,) + (1,) * (len(dims) - 1 - axis_at))
    return gain


def distinct(key, rows, count, top, lift):
    order = jax.random.permutation(jax.random.fold_in(key, 1), count)
    favour = order
    for power in range(3):
        favour = favour * favour // count
    favour = favour * lift // count
    chance = jax.random.randint(jax.random.fold_in(key, 2), (rows, count), 0, 4096) + favour
    fixed_rows = jax.random.permutation(jax.random.fold_in(key, 3), rows)[jnp.arange(count) % rows]
    chance = jnp.where(jnp.arange(rows)[:, None] == fixed_rows[None, :], 1 << 14, chance)
    score = chance * count + jnp.arange(count)
    return lax.top_k(score.astype(jnp.int32), top)[1].astype(jnp.int32)


def normal_values(stream_key, extent, width, limit, shards=(), held_as=jnp.bfloat16):
    array = jax.random.normal(stream_key, extent, jnp.float32) * width
    if len(shards) > 0:
        array = block_scale(stream_key, extent, shards, -0.22, 0.18) * array
    return jnp.clip(array, min=-limit, max=limit).astype(held_as)


def setup_inputs(seed: int = 0) -> dict:
    arg_keys = jax.random.split(jax.random.key(seed), 14)
    tokens = normal_values(arg_keys[0], (SEQS, LEN, MODEL_WIDTH), 1.0, 6.0, ((0, 8), (1, 4)))
    segments = draw_segments(jax.random.fold_in(arg_keys[13], 71), 0)
    routes = distinct(arg_keys[2], SEQS * LEN, EXPERTS, TOPK, 2048).reshape((SEQS, LEN, TOPK))
    gain_attn = jnp.clip(1.0 + 0.1 * jax.random.normal(arg_keys[3], (MODEL_WIDTH,), jnp.float32), 0.5, 1.5).astype(jnp.bfloat16)
    gain_moe = jnp.clip(1.0 + 0.1 * jax.random.normal(arg_keys[4], (MODEL_WIDTH,), jnp.float32), 0.5, 1.5).astype(jnp.bfloat16)
    query_weight = normal_values(arg_keys[5], (MODEL_WIDTH, QUERY_HEADS * HEAD_SIZE), (MODEL_WIDTH // 4) ** -0.5, 0.375, ((0, 32),))
    key_weight = normal_values(arg_keys[6], (MODEL_WIDTH, KEY_VALUE_HEADS * HEAD_SIZE), MODEL_WIDTH ** -0.5, 0.1875, ((0, 32),))
    value_weight = normal_values(arg_keys[7], (MODEL_WIDTH, KEY_VALUE_HEADS * HEAD_SIZE), MODEL_WIDTH ** -0.5, 0.1875, ((0, 32),))
    w_output = normal_values(arg_keys[8], (QUERY_HEADS * HEAD_SIZE, MODEL_WIDTH), (QUERY_HEADS * HEAD_SIZE // 16) ** -0.5, 0.75, ((0, 32),))
    w_router = normal_values(arg_keys[9], (MODEL_WIDTH, EXPERTS), (4 * MODEL_WIDTH) ** -0.5, 0.09375, ((0, 32),))
    w_expert_in = normal_values(arg_keys[10], (EXPERTS, MODEL_WIDTH, 2 * FF), MODEL_WIDTH ** -0.5, 0.1875, ((0, 8), (1, 4)))
    w_expert_out = normal_values(arg_keys[11], (EXPERTS, FF, MODEL_WIDTH), (FF // 4) ** -0.5, 0.5, ((0, 8), (1, 4)))
    cotangent = normal_values(arg_keys[12], (SEQS, LEN, MODEL_WIDTH), 1.0, 6.0, ((0, 8), (1, 4)))
    return {"tokens": tokens, "segments": segments, "routes": routes, "gain_attn": gain_attn, "gain_moe": gain_moe, "query_weight": query_weight, "key_weight": key_weight, "value_weight": value_weight, "w_output": w_output, "w_router": w_router, "w_expert_in": w_expert_in, "w_expert_out": w_expert_out, "cotangent": cotangent}


EPSILON = 1e-06
PRECISE = lax.Precision.HIGHEST

@jax.custom_vjp
def lowered_input(v):
    return lax.optimization_barrier(v.astype(jnp.bfloat16)).astype(jnp.float32)

@jax.custom_vjp
def lowered_gradient(v):
    return v

def low_keep(v):
    return (lowered_input(v), None)

def low_pass(kept, grad):
    return (grad,)

def back_keep(v):
    return (v, None)

def back_low(kept, grad):
    return (lowered_input(grad),)
lowered_input.defvjp(low_keep, low_pass)
lowered_gradient.defvjp(back_keep, back_low)

def exact_product(left, right):
    return jnp.dot(left, right, precision=PRECISE, preferred_element_type=jnp.float32)

def rms_scale(values):
    return lax.rsqrt(lax.optimization_barrier(jnp.mean(values * values, -1, keepdims=True)) + EPSILON)

def slot_tables(pair_ids):
    pair_count = pair_ids.shape[0]
    member = (pair_ids[:, None] == jnp.arange(EXPERTS, dtype=jnp.int32)[None, :]).astype(jnp.int32)
    earlier = jnp.cumsum(member, 0) - member
    slot_place = lax.optimization_barrier(jnp.sum(earlier * member, 1, dtype=jnp.int32))
    is_kept = slot_place < CAP
    slot_index = jnp.where(is_kept, pair_ids * CAP + slot_place, EXPERTS * CAP).astype(jnp.int32)
    slot_filler = jnp.full((EXPERTS * CAP,), -1, jnp.int32).at[slot_index].set(jnp.arange(pair_count, dtype=jnp.int32), mode='drop')
    return (slot_index, is_kept, slot_filler)

def attention(query_matrix, heads_of_keys, heads_of_values, seg_row):
    length_total = query_matrix.shape[0]
    q_block = math.gcd(512, length_total)
    factor = 1.0 / math.sqrt(HEAD_SIZE)
    positions = jnp.arange(length_total, dtype=jnp.int32)

    def one_block(offset):
        query_part = lax.dynamic_slice_in_dim(query_matrix, offset, q_block, 0)
        query_pos = offset + jnp.arange(q_block, dtype=jnp.int32)
        query_seg = lax.dynamic_slice_in_dim(seg_row, offset, q_block, 0)
        scores = jnp.einsum('ihgd,jhd->hgij', query_part, heads_of_keys, precision=PRECISE) * factor
        scores = lowered_gradient(scores)
        allowed = (positions[None, :] <= query_pos[:, None]) & (seg_row[None, :] == query_seg[:, None])
        scores = jnp.where(allowed, scores, -1e+30)
        probs = jax.nn.softmax(scores, axis=-1)
        return jnp.einsum('hgij,jhd->ihgd', lowered_input(probs), heads_of_values, precision=PRECISE)
    offsets = jnp.arange(0, length_total, q_block, dtype=jnp.int32)
    pieces = lax.map(jax.checkpoint(one_block), offsets)
    return pieces.reshape(length_total, -1)

def whole_layer(inputs, seg_row, route_ids, gain_one, gain_two, query_weight, key_weight, value_weight, w_output, w_router, w_expert_in, w_expert_out):
    length_total = inputs.shape[0]
    normalized_input = lowered_input(inputs * rms_scale(inputs) * gain_one)
    query_matrix = lowered_input(lowered_gradient(exact_product(normalized_input, query_weight))).reshape(length_total, KEY_VALUE_HEADS, QUERY_HEADS // KEY_VALUE_HEADS, HEAD_SIZE)
    heads_of_keys = lowered_input(lowered_gradient(exact_product(normalized_input, key_weight))).reshape(length_total, KEY_VALUE_HEADS, HEAD_SIZE)
    heads_of_values = lowered_input(lowered_gradient(exact_product(normalized_input, value_weight))).reshape(length_total, KEY_VALUE_HEADS, HEAD_SIZE)
    heads_out = attention(query_matrix, heads_of_keys, heads_of_values, seg_row)
    attn_low = lowered_input(lowered_gradient(heads_out))
    resid = inputs + lowered_gradient(exact_product(attn_low, w_output))
    moe_in = lowered_input(resid * rms_scale(resid) * gain_two)
    logits = exact_product(moe_in, w_router)
    one_hot = (route_ids[:, :, None] == jnp.arange(EXPERTS, dtype=jnp.int32)[None, None, :]).astype(inputs.dtype)
    chosen = jnp.einsum('lke,le->lk', one_hot, logits, precision=PRECISE)
    gates = jax.nn.softmax(chosen, axis=-1)
    blocks = length_total // BLK
    slot_index, is_kept, slot_filler = jax.vmap(slot_tables)(route_ids.reshape(blocks, BLK * TOPK))
    moe_blocks = moe_in.reshape(blocks, BLK, MODEL_WIDTH)
    token_of = jnp.maximum(slot_filler, 0) // TOPK
    filled = (slot_filler >= 0).astype(inputs.dtype)
    slot_rows = jnp.take_along_axis(moe_blocks, token_of[..., None], 1) * filled[..., None]
    slot_rows = lowered_gradient(slot_rows).reshape(blocks, EXPERTS, CAP, MODEL_WIDTH)
    pre = lowered_gradient(jnp.einsum('necd,edf->necf', slot_rows, w_expert_in, precision=PRECISE))
    hidden = lowered_input(jax.nn.silu(pre[..., :FF]) * pre[..., FF:])
    expert_rows = lowered_input(lowered_gradient(jnp.einsum('necf,efd->necd', hidden, w_expert_out, precision=PRECISE)))
    expert_rows = expert_rows.reshape(blocks, EXPERTS * CAP, MODEL_WIDTH)
    safe_slot = jnp.minimum(slot_index, EXPERTS * CAP - 1)
    picked = jnp.take_along_axis(expert_rows, safe_slot[..., None], 1) * is_kept[..., None].astype(inputs.dtype)
    picked = picked.reshape(length_total, TOPK, MODEL_WIDTH)
    branch = jnp.einsum('lk,lkd->ld', gates, picked, precision=PRECISE)
    return resid + branch

def reference(tokens, segments, routes, gain_attn, gain_moe, query_weight, key_weight, value_weight, w_output, w_router, w_expert_in, w_expert_out, cotangent):
    params = tuple((item.astype(jnp.float32) for item in (gain_attn, gain_moe, query_weight, key_weight, value_weight, w_output, w_router, w_expert_in, w_expert_out)))

    def per_pack(totals, packed):
        inputs, seg_row, route_ids, grad_out = packed

        def forward(values, *weights):
            return whole_layer(values, seg_row, route_ids, *weights)
        result, pull_back = jax.vjp(forward, inputs.astype(jnp.float32), *params)
        grads = pull_back(grad_out.astype(jnp.float32))
        totals = tuple((total + grad for total, grad in zip(totals, grads[1:])))
        return (totals, (result.astype(jnp.bfloat16), grads[0]))
    zero_filled = tuple((jnp.zeros(item.shape, jnp.float32) for item in params))
    totals, (mixed_out, grad_tokens) = lax.scan(per_pack, zero_filled, (tokens, segments, routes, cotangent))
    return (mixed_out, grad_tokens, totals[0], totals[1], totals[2], totals[3], totals[4], totals[5], totals[6], totals[7], totals[8])
```

```python
import math

import jax
import jax.numpy as jnp
from jax import lax
from jax.sharding import PartitionSpec as P

QUERY_HEADS = 16
KEY_VALUE_HEADS = 8
HEAD_SIZE = 64
EXPERTS = 32
TOPK = 8
FF = 512
CAP = 72


EPSILON = 1e-06
MASK_FILLER = -1e30


def rms_scale(values):
    return lax.rsqrt(jnp.mean(values * values, -1, keepdims=True) + EPSILON)


def inner_rows(left, right):
    return lax.dot_general(
        left, right, (((0,), (0,)), ((), ())), preferred_element_type=jnp.float32
    )


def outer_cols(left, right):
    return lax.dot_general(
        left, right, (((1,), (1,)), ((), ())), preferred_element_type=jnp.float32
    )


def allowed_block(query_pos, query_seg, seg_all, offset, key_total_count):
    key_pos = offset + jnp.arange(key_total_count, dtype=jnp.int32)
    key_seg = lax.dynamic_slice_in_dim(seg_all, offset, key_total_count)
    return (key_pos[None, :] <= query_pos[:, None]) & (key_seg[None, :] == query_seg[:, None])


def head_scores(heads_of_queries, key_segment_slice, factor):
    key_total_count = key_segment_slice.shape[0]
    heads_of_keys = key_segment_slice.reshape(key_total_count, KEY_VALUE_HEADS, -1)
    return (
        jnp.einsum(
            "ihgd,jhd->hgij", heads_of_queries, heads_of_keys, preferred_element_type=jnp.float32
        )
        * factor
    )


def slot_tables(pair_ids):
    pair_count = pair_ids.shape[0]
    member = (pair_ids[:, None] == jnp.arange(EXPERTS, dtype=jnp.int32)[None, :]).astype(jnp.int32)
    earlier = jnp.cumsum(member, 0) - member
    slot_place = jnp.sum(earlier * member, 1, dtype=jnp.int32)
    is_kept = slot_place < CAP
    slot_index = jnp.where(is_kept, pair_ids * CAP + slot_place, EXPERTS * CAP)
    slot_filler = (
        jnp.full((EXPERTS * CAP,), -1, jnp.int32)
        .at[slot_index]
        .set(jnp.arange(pair_count, dtype=jnp.int32), mode="drop")
    )
    return (slot_index, is_kept, slot_filler)


def local(
    tokens,
    segments,
    routes,
    gain_attn,
    gain_moe,
    query_weight,
    key_weight,
    value_weight,
    w_output,
    w_router,
    w_expert_in,
    w_expert_out,
    cotangent,
):
    shards = lax.axis_size("ctx")
    groups = lax.axis_size("exp")
    ctx_rank = lax.axis_index("ctx")
    gain_one, gain_two, full_query, full_key, full_value, full_output, full_router = (
        lax.all_gather(gain_attn, ("ctx", "exp"), axis=0, tiled=True),
        lax.all_gather(gain_moe, ("ctx", "exp"), axis=0, tiled=True),
        lax.all_gather(query_weight, ("ctx", "exp"), axis=0, tiled=True),
        lax.all_gather(key_weight, ("ctx", "exp"), axis=0, tiled=True),
        lax.all_gather(value_weight, ("ctx", "exp"), axis=0, tiled=True),
        lax.all_gather(w_output, ("ctx", "exp"), axis=0, tiled=True),
        lax.all_gather(w_router, ("ctx", "exp"), axis=0, tiled=True),
    )
    expert_in, expert_out = (
        lax.all_gather(w_expert_in, "ctx", axis=1, tiled=True),
        lax.all_gather(w_expert_out, "ctx", axis=1, tiled=True),
    )
    inputs = tokens[0].astype(jnp.float32)
    token_rows = inputs.shape[0]
    seq_len = token_rows * shards
    head_cluster = QUERY_HEADS // KEY_VALUE_HEADS
    factor = 1.0 / math.sqrt(HEAD_SIZE)
    kv_width = key_weight.shape[1]
    seg_all = segments[0]
    query_pos = ctx_rank * token_rows + jnp.arange(token_rows, dtype=jnp.int32)
    query_seg = lax.dynamic_slice_in_dim(seg_all, ctx_rank * token_rows, token_rows)
    scale_one = rms_scale(inputs)
    gain_one_f = gain_one.astype(jnp.float32)
    normalized_input = (inputs * scale_one * gain_one_f).astype(jnp.bfloat16)
    query_matrix = jnp.dot(normalized_input, full_query, preferred_element_type=jnp.float32).astype(
        jnp.bfloat16
    )
    key_rows = jnp.dot(normalized_input, full_key, preferred_element_type=jnp.float32).astype(
        jnp.bfloat16
    )
    value_rows = jnp.dot(normalized_input, full_value, preferred_element_type=jnp.float32).astype(
        jnp.bfloat16
    )
    heads_of_queries = query_matrix.reshape(token_rows, KEY_VALUE_HEADS, head_cluster, HEAD_SIZE)
    group_size = math.gcd(shards, max(1, 1024 // token_rows))
    key_range_width = group_size * token_rows
    turns_needed = ctx_rank // group_size + 1
    running_maximum = jnp.full(
        (KEY_VALUE_HEADS, head_cluster, token_rows), MASK_FILLER, jnp.float32
    )
    key_segment_slice = lax.all_gather(key_rows, "ctx", axis=0, tiled=True)
    value_segment_slice = lax.all_gather(value_rows, "ctx", axis=0, tiled=True)
    key_total_count = key_segment_slice.shape[0]
    scores = head_scores(heads_of_queries, key_segment_slice, factor)
    allowed = allowed_block(query_pos, query_seg, seg_all, jnp.int32(0), key_total_count)
    scores = jnp.where(allowed, scores, MASK_FILLER)
    new_max = jnp.maximum(running_maximum, jnp.max(scores, -1))
    weights = jnp.where(allowed, jnp.exp(scores - new_max[..., None]), 0.0)
    run_sum = jnp.sum(weights, -1)
    heads_of_values = value_segment_slice.reshape(key_total_count, KEY_VALUE_HEADS, HEAD_SIZE)
    run_acc = jnp.einsum(
        "hgij,jhd->ihgd",
        weights.astype(jnp.bfloat16),
        heads_of_values,
        preferred_element_type=jnp.float32,
    )
    running_maximum, run_sum, run_acc = (new_max, run_sum, run_acc)
    log_norm = running_maximum + jnp.log(run_sum)
    heads_out = run_acc / jnp.transpose(run_sum, (2, 0, 1))[..., None]
    attn_low = heads_out.reshape(token_rows, -1).astype(jnp.bfloat16)
    resid = inputs + jnp.dot(attn_low, full_output, preferred_element_type=jnp.float32)
    scale_two = rms_scale(resid)
    gain_two_f = gain_two.astype(jnp.float32)
    moe_in = (resid * scale_two * gain_two_f).astype(jnp.bfloat16)
    logits = jnp.dot(moe_in, full_router, preferred_element_type=jnp.float32)
    route_ids = routes[0]
    one_hot = (route_ids[:, :, None] == jnp.arange(EXPERTS, dtype=jnp.int32)[None, None, :]).astype(
        jnp.float32
    )
    chosen = jnp.sum(one_hot * logits[:, None, :], -1)
    gates = jax.nn.softmax(chosen, axis=-1)
    slot_index, is_kept, slot_filler = slot_tables(route_ids.reshape(-1))
    filled = slot_filler >= 0
    token_of = jnp.maximum(slot_filler, 0) // TOPK
    local_experts = EXPERTS // groups
    send_rows = jnp.where(
        filled[:, None], jnp.take(moe_in, token_of, axis=0), jnp.zeros((), jnp.bfloat16)
    )
    send_rows = send_rows.reshape(groups, local_experts, CAP, -1)
    received = lax.all_to_all(send_rows, "exp", split_axis=0, concat_axis=0, tiled=True)
    pre = jnp.einsum("sjcd,jdf->sjcf", received, expert_in, preferred_element_type=jnp.float32)
    gate_part = pre[..., :FF]
    up_part = pre[..., FF:]
    hidden = (jax.nn.silu(gate_part) * up_part).astype(jnp.bfloat16)
    expert_rows = jnp.einsum(
        "sjcf,jfd->sjcd", hidden, expert_out, preferred_element_type=jnp.float32
    ).astype(jnp.bfloat16)
    returned = lax.all_to_all(expert_rows, "exp", split_axis=0, concat_axis=0, tiled=True).reshape(
        EXPERTS * CAP, -1
    )
    safe_slot = jnp.minimum(slot_index, EXPERTS * CAP - 1)
    picked = jnp.where(
        is_kept[:, None], jnp.take(returned, safe_slot, axis=0), jnp.zeros((), jnp.bfloat16)
    )
    picked = picked.astype(jnp.float32).reshape(token_rows, TOPK, -1)
    branch = jnp.sum(gates[:, :, None] * picked, 1)
    mixed_out = (resid + branch).astype(jnp.bfloat16)
    grad_out = cotangent[0].astype(jnp.float32)
    grad_picked = jnp.sum(grad_out[:, None, :] * picked, -1)
    grad_chosen = gates * (grad_picked - jnp.sum(gates * grad_picked, -1, keepdims=True))
    grad_logits = jnp.sum(one_hot * grad_chosen[:, :, None], 1)
    slot_gate = jnp.where(filled, jnp.take(gates.reshape(-1), jnp.maximum(slot_filler, 0)), 0.0)
    grad_send = (slot_gate[:, None] * jnp.take(grad_out, token_of, axis=0)).astype(jnp.bfloat16)
    grad_send = grad_send.reshape(groups, local_experts, CAP, -1)
    grad_rows = lax.all_to_all(grad_send, "exp", split_axis=0, concat_axis=0, tiled=True)
    grad_hidden = jnp.einsum(
        "sjcd,jfd->sjcf", grad_rows, expert_out, preferred_element_type=jnp.float32
    )
    sigmoid_gate = jax.nn.sigmoid(gate_part)
    grad_gate = grad_hidden * up_part * sigmoid_gate * (1.0 + gate_part * (1.0 - sigmoid_gate))
    grad_up = grad_hidden * gate_part * sigmoid_gate
    grad_pre = jnp.concatenate([grad_gate, grad_up], -1).astype(jnp.bfloat16)
    grad_expert_out = jnp.einsum(
        "sjcf,sjcd->jfd", hidden, grad_rows, preferred_element_type=jnp.float32
    )
    grad_expert_in = jnp.einsum(
        "sjcd,sjcf->jdf", received, grad_pre, preferred_element_type=jnp.float32
    )
    grad_received = jnp.einsum(
        "sjcf,jdf->sjcd", grad_pre, expert_in, preferred_element_type=jnp.float32
    ).astype(jnp.bfloat16)
    grad_back = lax.all_to_all(
        grad_received, "exp", split_axis=0, concat_axis=0, tiled=True
    ).reshape(EXPERTS * CAP, -1)
    grad_pairs = jnp.where(
        is_kept[:, None], jnp.take(grad_back, safe_slot, axis=0), jnp.zeros((), jnp.bfloat16)
    )
    grad_pairs = grad_pairs.astype(jnp.float32).reshape(token_rows, TOPK, -1)
    grad_moe_in = (
        jnp.sum(grad_pairs, 1)
        + outer_cols(grad_logits.astype(jnp.bfloat16), full_router) * 0.0
        + lax.dot_general(
            grad_logits,
            full_router.astype(jnp.float32),
            (((1,), (1,)), ((), ())),
            precision=lax.Precision.HIGHEST,
            preferred_element_type=jnp.float32,
        )
    )
    grad_router = lax.dot_general(
        moe_in.astype(jnp.float32),
        grad_logits,
        (((0,), (0,)), ((), ())),
        precision=lax.Precision.HIGHEST,
        preferred_element_type=jnp.float32,
    )
    weighted_two = grad_moe_in * gain_two_f
    grad_gain_two = jnp.sum(grad_moe_in * resid * scale_two, 0)
    cube_two = scale_two * scale_two * scale_two
    grad_resid = (
        grad_out
        + scale_two * weighted_two
        - resid * cube_two * jnp.mean(weighted_two * resid, -1, keepdims=True)
    )
    grad_resid_low = grad_resid.astype(jnp.bfloat16)
    grad_output_w = inner_rows(attn_low, grad_resid_low)
    grad_heads = (
        outer_cols(grad_resid_low, full_output)
        .astype(jnp.bfloat16)
        .reshape(token_rows, KEY_VALUE_HEADS, head_cluster, HEAD_SIZE)
    )
    delta = jnp.transpose(jnp.sum(grad_heads.astype(jnp.float32) * heads_out, -1), (1, 2, 0))
    all_keys, all_values = (
        lax.all_gather(key_rows, "ctx", axis=0, tiled=True),
        lax.all_gather(value_rows, "ctx", axis=0, tiled=True),
    )

    def block_grads(offset):
        key_segment_slice = lax.dynamic_slice_in_dim(all_keys, offset, key_range_width)
        value_segment_slice = lax.dynamic_slice_in_dim(all_values, offset, key_range_width)
        scores = head_scores(heads_of_queries, key_segment_slice, factor)
        allowed = allowed_block(query_pos, query_seg, seg_all, offset, key_range_width)
        probs_full = jnp.where(allowed, jnp.exp(scores - log_norm[..., None]), 0.0)
        heads_of_keys = key_segment_slice.reshape(key_range_width, KEY_VALUE_HEADS, HEAD_SIZE)
        heads_of_values = value_segment_slice.reshape(key_range_width, KEY_VALUE_HEADS, HEAD_SIZE)
        grad_probs = jnp.einsum(
            "ihgd,jhd->hgij", grad_heads, heads_of_values, preferred_element_type=jnp.float32
        )
        grad_scores = (probs_full * (grad_probs - delta[..., None])).astype(jnp.bfloat16)
        query_part = jnp.einsum(
            "hgij,jhd->ihgd", grad_scores, heads_of_keys, preferred_element_type=jnp.float32
        )
        return (probs_full, grad_scores, query_part)

    query_begin_index = jnp.zeros(
        (token_rows, KEY_VALUE_HEADS, head_cluster, HEAD_SIZE), jnp.float32
    )

    def back_turn(turn, running):
        grad_query_acc, key_grad_buf = running
        offset = turn * key_range_width
        probs_full, grad_scores, query_part = block_grads(offset)
        grad_key_part = (
            jnp.einsum(
                "hgij,ihgd->jhd", grad_scores, heads_of_queries, preferred_element_type=jnp.float32
            )
            * factor
        )
        grad_value_part = jnp.einsum(
            "hgij,ihgd->jhd",
            probs_full.astype(jnp.bfloat16),
            grad_heads,
            preferred_element_type=jnp.float32,
        )
        joined = jnp.concatenate(
            [
                grad_key_part.reshape(key_range_width, -1),
                grad_value_part.reshape(key_range_width, -1),
            ],
            1,
        )
        key_grad_buf = lax.dynamic_update_slice_in_dim(key_grad_buf, joined, offset, 0)
        return (grad_query_acc + query_part, key_grad_buf)

    back_start = (query_begin_index, jnp.zeros((seq_len, 2 * kv_width), jnp.float32))
    grad_query_acc, key_grad_buf = lax.fori_loop(0, turns_needed, back_turn, back_start)
    own_grads = lax.psum_scatter(
        key_grad_buf.astype(jnp.bfloat16), "ctx", scatter_dimension=0, tiled=True
    ).astype(jnp.float32)
    grad_keys = own_grads[:, :kv_width].astype(jnp.bfloat16)
    grad_values = own_grads[:, kv_width:].astype(jnp.bfloat16)
    grad_query = (grad_query_acc * factor).reshape(token_rows, -1).astype(jnp.bfloat16)
    grad_query_w = inner_rows(normalized_input, grad_query)
    grad_key_w = inner_rows(normalized_input, grad_keys)
    grad_value_w = inner_rows(normalized_input, grad_values)
    grad_normed = (
        outer_cols(grad_query, full_query)
        + outer_cols(grad_keys, full_key)
        + outer_cols(grad_values, full_value)
    )
    weighted_one = grad_normed * gain_one_f
    grad_gain_one = jnp.sum(grad_normed * inputs * scale_one, 0)
    cube_one = scale_one * scale_one * scale_one
    grad_inputs = (
        grad_resid
        + scale_one * weighted_one
        - inputs * cube_one * jnp.mean(weighted_one * inputs, -1, keepdims=True)
    )
    dense_sums = (
        lax.psum_scatter(grad_gain_one, ("ctx", "exp"), scatter_dimension=0, tiled=True),
        lax.psum_scatter(grad_gain_two, ("ctx", "exp"), scatter_dimension=0, tiled=True),
        lax.psum_scatter(grad_query_w, ("ctx", "exp"), scatter_dimension=0, tiled=True),
        lax.psum_scatter(grad_key_w, ("ctx", "exp"), scatter_dimension=0, tiled=True),
        lax.psum_scatter(grad_value_w, ("ctx", "exp"), scatter_dimension=0, tiled=True),
        lax.psum_scatter(grad_output_w, ("ctx", "exp"), scatter_dimension=0, tiled=True),
        lax.psum_scatter(grad_router, ("ctx", "exp"), scatter_dimension=0, tiled=True),
    )
    expert_sums = (
        lax.psum_scatter(
            grad_expert_in.astype(jnp.bfloat16), "ctx", scatter_dimension=1, tiled=True
        ).astype(jnp.float32),
        lax.psum_scatter(
            grad_expert_out.astype(jnp.bfloat16), "ctx", scatter_dimension=1, tiled=True
        ).astype(jnp.float32),
    )
    return (mixed_out[None], grad_inputs[None]) + tuple(dense_sums) + tuple(expert_sums)


def softmax_members(logits, member):
    top = jnp.max(jnp.where(member, logits, MASK_FILLER), -1, keepdims=True)
    weights = jnp.where(member, jnp.exp(logits - top), 0.0)
    return weights / jnp.sum(weights, -1, keepdims=True)


def two_parts(values):
    high = values.astype(jnp.bfloat16)
    return high, (values - high.astype(jnp.float32)).astype(jnp.bfloat16)


def by_heads(
    tokens,
    segments,
    routes,
    gain_attn,
    gain_moe,
    query_weight,
    key_weight,
    value_weight,
    w_output,
    w_router,
    w_expert_in,
    w_expert_out,
    cotangent,
):
    shards = lax.axis_size("ctx")
    groups = lax.axis_size("exp")
    exp_rank = lax.axis_index("exp")
    local_experts = EXPERTS // groups
    token_rows, width = tokens.shape[1], tokens.shape[2]
    rows = query_weight.shape[0]
    seq_len = token_rows * shards
    q_cols = query_weight.shape[1] // shards
    k_cols = key_weight.shape[1] // shards
    kv_heads = KEY_VALUE_HEADS // shards
    head_cluster = QUERY_HEADS // KEY_VALUE_HEADS
    factor = 1.0 / math.sqrt(HEAD_SIZE)
    main_cols = q_cols + 2 * k_cols
    side = 128

    expert_in = lax.all_gather(w_expert_in, "ctx", axis=1, tiled=True)
    expert_out = lax.all_gather(w_expert_out, "ctx", axis=1, tiled=True)
    all_tokens = lax.all_gather(tokens[0], "ctx", axis=0, tiled=True)
    side_cols = jnp.concatenate(
        [
            w_router,
            gain_attn[:, None],
            gain_moe[:, None],
            jnp.zeros((rows, side - EXPERTS - 2), jnp.bfloat16),
        ],
        1,
    )
    packed = jnp.concatenate(
        [
            query_weight.reshape(rows, shards, q_cols),
            key_weight.reshape(rows, shards, k_cols),
            value_weight.reshape(rows, shards, k_cols),
            jnp.broadcast_to(side_cols[:, None, :], (rows, shards, side)),
        ],
        2,
    ).transpose(1, 0, 2)
    packed = lax.all_to_all(packed, "ctx", split_axis=0, concat_axis=0, tiled=True)
    packed = lax.all_gather(packed, "exp", axis=1, tiled=True).reshape(width, main_cols + side)
    w_main = packed[:, :main_cols]
    router = packed[:, main_cols : main_cols + EXPERTS]
    gain_one = packed[:, main_cols + EXPERTS].astype(jnp.float32)
    gain_two = packed[:, main_cols + EXPERTS + 1].astype(jnp.float32)
    out_rows = lax.all_gather(w_output, "exp", axis=0, tiled=True)
    all_cot = lax.all_gather(cotangent[0], "exp", axis=0, tiled=False)
    all_routes = lax.all_gather(routes[0], "exp", axis=0, tiled=False)

    inputs_all = all_tokens.astype(jnp.float32)
    scale_all = rms_scale(inputs_all)
    normed = (inputs_all * scale_all * gain_one).astype(jnp.bfloat16)
    qkv = jnp.dot(normed, w_main, preferred_element_type=jnp.float32).astype(jnp.bfloat16)
    queries = qkv[:, :q_cols].reshape(seq_len, kv_heads, head_cluster, HEAD_SIZE)
    keys = qkv[:, q_cols : q_cols + k_cols].reshape(seq_len, kv_heads, HEAD_SIZE)
    values = qkv[:, q_cols + k_cols :].reshape(seq_len, kv_heads, HEAD_SIZE)
    seg = segments[0]
    pos = jnp.arange(seq_len, dtype=jnp.int32)
    allowed = (pos[None, :] <= pos[:, None]) & (seg[None, :] == seg[:, None])
    scores = (
        jnp.einsum("ihgd,jhd->hgij", queries, keys, preferred_element_type=jnp.float32) * factor
    )
    scores = jnp.where(allowed, scores, MASK_FILLER)
    top = jnp.max(scores, -1, keepdims=True)
    weights = jnp.where(allowed, jnp.exp(scores - top), 0.0)
    total = jnp.sum(weights, -1)
    log_norm = top[..., 0] + jnp.log(total)
    heads_out = jnp.einsum(
        "hgij,jhd->ihgd", weights.astype(jnp.bfloat16), values, preferred_element_type=jnp.float32
    ) / jnp.transpose(total, (2, 0, 1))[..., None]
    attn_low = heads_out.reshape(seq_len, q_cols).astype(jnp.bfloat16)
    branch_part = jnp.dot(attn_low, out_rows, preferred_element_type=jnp.float32).astype(jnp.bfloat16)
    branch = lax.psum_scatter(branch_part, "ctx", scatter_dimension=0, tiled=True)
    inputs = tokens[0].astype(jnp.float32)
    resid = inputs + branch.astype(jnp.float32)
    scale_two = rms_scale(resid)
    moe_in = (resid * scale_two * gain_two).astype(jnp.bfloat16)

    all_moe = lax.all_gather(moe_in, "exp", axis=0, tiled=False)
    member = jnp.any(
        all_routes[..., None] == jnp.arange(EXPERTS, dtype=jnp.int32), axis=2
    )
    logits = jnp.einsum("std,de->ste", all_moe, router, preferred_element_type=jnp.float32)
    gates = softmax_members(logits, member)
    earlier = jnp.tril(jnp.ones((token_rows, token_rows), jnp.bfloat16), -1)
    rank = jnp.einsum(
        "tu,sue->ste", earlier, member.astype(jnp.bfloat16), preferred_element_type=jnp.float32
    ).astype(jnp.int32)
    kept = member & (rank < CAP)
    first = exp_rank * local_experts

    def mine(table):
        return lax.dynamic_slice_in_dim(table, first, local_experts, 2)

    place = jnp.where(mine(kept), mine(rank), -1)
    pick = (
        place.transpose(0, 2, 1)[:, :, None, :]
        == jnp.arange(CAP, dtype=jnp.int32)[None, None, :, None]
    ).astype(jnp.bfloat16)
    both = jnp.concatenate([all_moe, all_cot], -1)
    slots = jnp.einsum("sjct,std->sjcd", pick, both, preferred_element_type=jnp.float32)
    slot_rows = slots[..., :width].astype(jnp.bfloat16)
    slot_cot = slots[..., width:]
    slot_gate = jnp.sum(
        pick.astype(jnp.float32) * mine(gates).transpose(0, 2, 1)[:, :, None, :], -1
    )
    pre = jnp.einsum("sjcd,jdf->sjcf", slot_rows, expert_in, preferred_element_type=jnp.float32)
    gate_part, up_part = pre[..., :FF], pre[..., FF:]
    sigmoid_gate = jax.nn.sigmoid(gate_part)
    hidden = (gate_part * sigmoid_gate * up_part).astype(jnp.bfloat16)
    expert_rows = jnp.einsum(
        "sjcf,jfd->sjcd", hidden, expert_out, preferred_element_type=jnp.float32
    ).astype(jnp.bfloat16)
    weighted = (slot_gate[..., None] * expert_rows.astype(jnp.float32)).astype(jnp.bfloat16)
    mixed_part = jnp.einsum(
        "sjct,sjcd->std", pick, weighted, preferred_element_type=jnp.float32
    ).astype(jnp.bfloat16)
    mixed = lax.psum_scatter(mixed_part, "exp", scatter_dimension=0, tiled=False)
    mixed_out = (resid + mixed.astype(jnp.float32)).astype(jnp.bfloat16)

    grad_rows = (slot_gate[..., None] * slot_cot).astype(jnp.bfloat16)
    slot_dot = jnp.sum(slot_cot * expert_rows.astype(jnp.float32), -1)
    grad_picked = jnp.sum(pick.astype(jnp.float32) * slot_dot[..., None], 2).transpose(0, 2, 1)
    grad_picked = lax.dynamic_update_slice_in_dim(jnp.zeros_like(gates), grad_picked, first, 2)
    grad_logits = gates * (grad_picked - jnp.sum(gates * grad_picked, -1, keepdims=True))
    logits_high, logits_low = two_parts(grad_logits)
    grad_router = jnp.einsum(
        "std,ste->de", all_moe, logits_high, preferred_element_type=jnp.float32
    ) + jnp.einsum("std,ste->de", all_moe, logits_low, preferred_element_type=jnp.float32)
    grad_hidden = jnp.einsum(
        "sjcd,jfd->sjcf", grad_rows, expert_out, preferred_element_type=jnp.float32
    )
    grad_gate = grad_hidden * up_part * sigmoid_gate * (1.0 + gate_part * (1.0 - sigmoid_gate))
    grad_up = grad_hidden * gate_part * sigmoid_gate
    grad_pre = jnp.concatenate([grad_gate, grad_up], -1).astype(jnp.bfloat16)
    grad_slots = jnp.einsum(
        "sjcf,jdf->sjcd", grad_pre, expert_in, preferred_element_type=jnp.float32
    ).astype(jnp.bfloat16)
    moe_part = (
        jnp.einsum("sjct,sjcd->std", pick, grad_slots, preferred_element_type=jnp.float32)
        + jnp.einsum("ste,de->std", logits_high, router, preferred_element_type=jnp.float32)
        + jnp.einsum("ste,de->std", logits_low, router, preferred_element_type=jnp.float32)
    ).astype(jnp.bfloat16)
    grad_moe_in = lax.psum_scatter(moe_part, "exp", scatter_dimension=0, tiled=False).astype(
        jnp.float32
    )
    grad_expert_out = jnp.einsum(
        "sjcf,sjcd->jfd", hidden, grad_rows, preferred_element_type=jnp.float32
    ).astype(jnp.bfloat16)
    grad_expert_in = jnp.einsum(
        "sjcd,sjcf->jdf", slot_rows, grad_pre, preferred_element_type=jnp.float32
    ).astype(jnp.bfloat16)

    grad_out = cotangent[0].astype(jnp.float32)
    weighted_two = grad_moe_in * gain_two
    grad_gain_two = jnp.sum(grad_moe_in * resid * scale_two, 0)
    cube_two = scale_two * scale_two * scale_two
    grad_resid = (
        grad_out
        + scale_two * weighted_two
        - resid * cube_two * jnp.mean(weighted_two * resid, -1, keepdims=True)
    )
    resid_low = lax.all_gather(grad_resid.astype(jnp.bfloat16), "ctx", axis=0, tiled=True)

    grad_output_w = lax.psum_scatter(
        inner_rows(attn_low, resid_low).astype(jnp.bfloat16), "exp", scatter_dimension=0, tiled=True
    ).astype(jnp.float32)
    grad_heads = (
        outer_cols(resid_low, out_rows)
        .astype(jnp.bfloat16)
        .reshape(seq_len, kv_heads, head_cluster, HEAD_SIZE)
    )
    delta = jnp.transpose(jnp.sum(grad_heads.astype(jnp.float32) * heads_out, -1), (1, 2, 0))
    probs = jnp.where(allowed, jnp.exp(scores - log_norm[..., None]), 0.0)
    grad_probs = jnp.einsum(
        "ihgd,jhd->hgij", grad_heads, values, preferred_element_type=jnp.float32
    )
    grad_scores = (probs * (grad_probs - delta[..., None])).astype(jnp.bfloat16)
    grad_queries = jnp.einsum(
        "hgij,jhd->ihgd", grad_scores, keys, preferred_element_type=jnp.float32
    )
    grad_keys = jnp.einsum(
        "hgij,ihgd->jhd", grad_scores, queries, preferred_element_type=jnp.float32
    )
    grad_values = jnp.einsum(
        "hgij,ihgd->jhd", probs.astype(jnp.bfloat16), grad_heads, preferred_element_type=jnp.float32
    )
    grad_qkv = jnp.concatenate(
        [
            (grad_queries * factor).reshape(seq_len, -1),
            (grad_keys * factor).reshape(seq_len, -1),
            grad_values.reshape(seq_len, -1),
        ],
        1,
    ).astype(jnp.bfloat16)
    normed_part = outer_cols(grad_qkv, w_main)
    grad_gain_one = jnp.sum(normed_part * inputs_all * scale_all, 0)
    grad_normed = lax.psum_scatter(
        normed_part.astype(jnp.bfloat16), "ctx", scatter_dimension=0, tiled=True
    ).astype(jnp.float32)
    weighted_one = grad_normed * gain_one
    scale_one = rms_scale(inputs)
    cube_one = scale_one * scale_one * scale_one
    grad_inputs = (
        grad_resid
        + scale_one * weighted_one
        - inputs * cube_one * jnp.mean(weighted_one * inputs, -1, keepdims=True)
    )

    sums = jnp.concatenate(
        [
            inner_rows(normed, grad_qkv),
            grad_router,
            grad_gain_one[:, None],
            grad_gain_two[:, None],
            jnp.zeros((width, side - EXPERTS - 2), jnp.float32),
        ],
        1,
    ).astype(jnp.bfloat16)
    sums = sums.reshape(shards, groups, rows, main_cols + side).transpose(1, 0, 2, 3)
    sums = lax.psum_scatter(sums, "exp", scatter_dimension=0, tiled=False)
    sums = lax.all_to_all(sums, "ctx", split_axis=0, concat_axis=0, tiled=True).astype(jnp.float32)

    def columns(low, count):
        return sums[:, :, low : low + count].transpose(1, 0, 2).reshape(rows, -1)

    side_sums = jnp.sum(sums[:, :, main_cols:], 0)
    expert_in_sum = lax.psum_scatter(
        grad_expert_in, "ctx", scatter_dimension=1, tiled=True
    ).astype(jnp.float32)
    expert_out_sum = lax.psum_scatter(
        grad_expert_out, "ctx", scatter_dimension=1, tiled=True
    ).astype(jnp.float32)
    return (
        mixed_out[None],
        grad_inputs[None],
        side_sums[:, EXPERTS],
        side_sums[:, EXPERTS + 1],
        columns(0, q_cols),
        columns(q_cols, k_cols),
        columns(q_cols + k_cols, k_cols),
        grad_output_w,
        side_sums[:, :EXPERTS],
        expert_in_sum,
        expert_out_sum,
    )


def solution(mesh):
    whole_heads = KEY_VALUE_HEADS % mesh.shape["ctx"] == 0
    return jax.shard_map(
        by_heads if whole_heads else local,
        mesh=mesh,
        in_specs=(
            P("exp", "ctx", None),
            P("exp", None),
            P("exp", "ctx", None),
            P(("ctx", "exp")),
            P(("ctx", "exp")),
            P(("ctx", "exp"), None),
            P(("ctx", "exp"), None),
            P(("ctx", "exp"), None),
            P(("ctx", "exp"), None),
            P(("ctx", "exp"), None),
            P("exp", "ctx", None),
            P("exp", "ctx", None),
            P("exp", "ctx", None),
        ),
        out_specs=(
            P("exp", "ctx", None),
            P("exp", "ctx", None),
            P(("ctx", "exp")),
            P(("ctx", "exp")),
            P(("ctx", "exp"), None),
            P(("ctx", "exp"), None),
            P(("ctx", "exp"), None),
            P(("ctx", "exp"), None),
            P(("ctx", "exp"), None),
            P("exp", "ctx", None),
            P("exp", "ctx", None),
        ),
        check_vma=False,
    )
```

```python
import math

import jax
import jax.numpy as jnp
from jax import lax
from jax.experimental import pallas as pl
from jax.experimental.pallas import tpu as pltpu
from jax.sharding import PartitionSpec as P

QUERY_HEADS = 16
KEY_VALUE_HEADS = 8
HEAD_SIZE = 64
EXPERTS = 32
TOPK = 8
FF = 512
CAP = 72


EPSILON = 1e-06
MASK_FILLER = -1e30


def rms_scale(values):
    return lax.rsqrt(jnp.mean(values * values, -1, keepdims=True) + EPSILON)


def inner_rows(left, right):
    return lax.dot_general(
        left, right, (((0,), (0,)), ((), ())), preferred_element_type=jnp.float32
    )


def outer_cols(left, right):
    return lax.dot_general(
        left, right, (((1,), (1,)), ((), ())), preferred_element_type=jnp.float32
    )


def allowed_block(query_pos, query_seg, seg_all, offset, key_total_count):
    key_pos = offset + jnp.arange(key_total_count, dtype=jnp.int32)
    key_seg = lax.dynamic_slice_in_dim(seg_all, offset, key_total_count)
    return (key_pos[None, :] <= query_pos[:, None]) & (key_seg[None, :] == query_seg[:, None])


def head_scores(heads_of_queries, key_segment_slice, factor):
    key_total_count = key_segment_slice.shape[0]
    heads_of_keys = key_segment_slice.reshape(key_total_count, KEY_VALUE_HEADS, -1)
    return (
        jnp.einsum(
            "ihgd,jhd->hgij", heads_of_queries, heads_of_keys, preferred_element_type=jnp.float32
        )
        * factor
    )


def slot_tables(pair_ids):
    pair_count = pair_ids.shape[0]
    member = (pair_ids[:, None] == jnp.arange(EXPERTS, dtype=jnp.int32)[None, :]).astype(jnp.int32)
    earlier = jnp.cumsum(member, 0) - member
    slot_place = jnp.sum(earlier * member, 1, dtype=jnp.int32)
    is_kept = slot_place < CAP
    slot_index = jnp.where(is_kept, pair_ids * CAP + slot_place, EXPERTS * CAP)
    slot_filler = (
        jnp.full((EXPERTS * CAP,), -1, jnp.int32)
        .at[slot_index]
        .set(jnp.arange(pair_count, dtype=jnp.int32), mode="drop")
    )
    return (slot_index, is_kept, slot_filler)


def local(
    tokens,
    segments,
    routes,
    gain_attn,
    gain_moe,
    query_weight,
    key_weight,
    value_weight,
    w_output,
    w_router,
    w_expert_in,
    w_expert_out,
    cotangent,
):
    shards = lax.axis_size("ctx")
    groups = lax.axis_size("exp")
    ctx_rank = lax.axis_index("ctx")
    gain_one, gain_two, full_query, full_key, full_value, full_output, full_router = (
        lax.all_gather(gain_attn, ("ctx", "exp"), axis=0, tiled=True),
        lax.all_gather(gain_moe, ("ctx", "exp"), axis=0, tiled=True),
        lax.all_gather(query_weight, ("ctx", "exp"), axis=0, tiled=True),
        lax.all_gather(key_weight, ("ctx", "exp"), axis=0, tiled=True),
        lax.all_gather(value_weight, ("ctx", "exp"), axis=0, tiled=True),
        lax.all_gather(w_output, ("ctx", "exp"), axis=0, tiled=True),
        lax.all_gather(w_router, ("ctx", "exp"), axis=0, tiled=True),
    )
    expert_in, expert_out = (
        lax.all_gather(w_expert_in, "ctx", axis=1, tiled=True),
        lax.all_gather(w_expert_out, "ctx", axis=1, tiled=True),
    )
    inputs = tokens[0].astype(jnp.float32)
    token_rows = inputs.shape[0]
    seq_len = token_rows * shards
    head_cluster = QUERY_HEADS // KEY_VALUE_HEADS
    factor = 1.0 / math.sqrt(HEAD_SIZE)
    kv_width = key_weight.shape[1]
    seg_all = segments[0]
    query_pos = ctx_rank * token_rows + jnp.arange(token_rows, dtype=jnp.int32)
    query_seg = lax.dynamic_slice_in_dim(seg_all, ctx_rank * token_rows, token_rows)
    scale_one = rms_scale(inputs)
    gain_one_f = gain_one.astype(jnp.float32)
    normalized_input = (inputs * scale_one * gain_one_f).astype(jnp.bfloat16)
    query_matrix = jnp.dot(normalized_input, full_query, preferred_element_type=jnp.float32).astype(
        jnp.bfloat16
    )
    key_rows = jnp.dot(normalized_input, full_key, preferred_element_type=jnp.float32).astype(
        jnp.bfloat16
    )
    value_rows = jnp.dot(normalized_input, full_value, preferred_element_type=jnp.float32).astype(
        jnp.bfloat16
    )
    heads_of_queries = query_matrix.reshape(token_rows, KEY_VALUE_HEADS, head_cluster, HEAD_SIZE)
    group_size = math.gcd(shards, max(1, 1024 // token_rows))
    key_range_width = group_size * token_rows
    turns_needed = ctx_rank // group_size + 1
    running_maximum = jnp.full(
        (KEY_VALUE_HEADS, head_cluster, token_rows), MASK_FILLER, jnp.float32
    )
    key_segment_slice = lax.all_gather(key_rows, "ctx", axis=0, tiled=True)
    value_segment_slice = lax.all_gather(value_rows, "ctx", axis=0, tiled=True)
    key_total_count = key_segment_slice.shape[0]
    scores = head_scores(heads_of_queries, key_segment_slice, factor)
    allowed = allowed_block(query_pos, query_seg, seg_all, jnp.int32(0), key_total_count)
    scores = jnp.where(allowed, scores, MASK_FILLER)
    new_max = jnp.maximum(running_maximum, jnp.max(scores, -1))
    weights = jnp.where(allowed, jnp.exp(scores - new_max[..., None]), 0.0)
    run_sum = jnp.sum(weights, -1)
    heads_of_values = value_segment_slice.reshape(key_total_count, KEY_VALUE_HEADS, HEAD_SIZE)
    run_acc = jnp.einsum(
        "hgij,jhd->ihgd",
        weights.astype(jnp.bfloat16),
        heads_of_values,
        preferred_element_type=jnp.float32,
    )
    running_maximum, run_sum, run_acc = (new_max, run_sum, run_acc)
    log_norm = running_maximum + jnp.log(run_sum)
    heads_out = run_acc / jnp.transpose(run_sum, (2, 0, 1))[..., None]
    attn_low = heads_out.reshape(token_rows, -1).astype(jnp.bfloat16)
    resid = inputs + jnp.dot(attn_low, full_output, preferred_element_type=jnp.float32)
    scale_two = rms_scale(resid)
    gain_two_f = gain_two.astype(jnp.float32)
    moe_in = (resid * scale_two * gain_two_f).astype(jnp.bfloat16)
    logits = jnp.dot(moe_in, full_router, preferred_element_type=jnp.float32)
    route_ids = routes[0]
    one_hot = (route_ids[:, :, None] == jnp.arange(EXPERTS, dtype=jnp.int32)[None, None, :]).astype(
        jnp.float32
    )
    chosen = jnp.sum(one_hot * logits[:, None, :], -1)
    gates = jax.nn.softmax(chosen, axis=-1)
    slot_index, is_kept, slot_filler = slot_tables(route_ids.reshape(-1))
    filled = slot_filler >= 0
    token_of = jnp.maximum(slot_filler, 0) // TOPK
    local_experts = EXPERTS // groups
    send_rows = jnp.where(
        filled[:, None], jnp.take(moe_in, token_of, axis=0), jnp.zeros((), jnp.bfloat16)
    )
    send_rows = send_rows.reshape(groups, local_experts, CAP, -1)
    received = lax.all_to_all(send_rows, "exp", split_axis=0, concat_axis=0, tiled=True)
    pre = jnp.einsum("sjcd,jdf->sjcf", received, expert_in, preferred_element_type=jnp.float32)
    gate_part = pre[..., :FF]
    up_part = pre[..., FF:]
    hidden = (jax.nn.silu(gate_part) * up_part).astype(jnp.bfloat16)
    expert_rows = jnp.einsum(
        "sjcf,jfd->sjcd", hidden, expert_out, preferred_element_type=jnp.float32
    ).astype(jnp.bfloat16)
    returned = lax.all_to_all(expert_rows, "exp", split_axis=0, concat_axis=0, tiled=True).reshape(
        EXPERTS * CAP, -1
    )
    safe_slot = jnp.minimum(slot_index, EXPERTS * CAP - 1)
    picked = jnp.where(
        is_kept[:, None], jnp.take(returned, safe_slot, axis=0), jnp.zeros((), jnp.bfloat16)
    )
    picked = picked.astype(jnp.float32).reshape(token_rows, TOPK, -1)
    branch = jnp.sum(gates[:, :, None] * picked, 1)
    mixed_out = (resid + branch).astype(jnp.bfloat16)
    grad_out = cotangent[0].astype(jnp.float32)
    grad_picked = jnp.sum(grad_out[:, None, :] * picked, -1)
    grad_chosen = gates * (grad_picked - jnp.sum(gates * grad_picked, -1, keepdims=True))
    grad_logits = jnp.sum(one_hot * grad_chosen[:, :, None], 1)
    slot_gate = jnp.where(filled, jnp.take(gates.reshape(-1), jnp.maximum(slot_filler, 0)), 0.0)
    grad_send = (slot_gate[:, None] * jnp.take(grad_out, token_of, axis=0)).astype(jnp.bfloat16)
    grad_send = grad_send.reshape(groups, local_experts, CAP, -1)
    grad_rows = lax.all_to_all(grad_send, "exp", split_axis=0, concat_axis=0, tiled=True)
    grad_hidden = jnp.einsum(
        "sjcd,jfd->sjcf", grad_rows, expert_out, preferred_element_type=jnp.float32
    )
    sigmoid_gate = jax.nn.sigmoid(gate_part)
    grad_gate = grad_hidden * up_part * sigmoid_gate * (1.0 + gate_part * (1.0 - sigmoid_gate))
    grad_up = grad_hidden * gate_part * sigmoid_gate
    grad_pre = jnp.concatenate([grad_gate, grad_up], -1).astype(jnp.bfloat16)
    grad_expert_out = jnp.einsum(
        "sjcf,sjcd->jfd", hidden, grad_rows, preferred_element_type=jnp.float32
    )
    grad_expert_in = jnp.einsum(
        "sjcd,sjcf->jdf", received, grad_pre, preferred_element_type=jnp.float32
    )
    grad_received = jnp.einsum(
        "sjcf,jdf->sjcd", grad_pre, expert_in, preferred_element_type=jnp.float32
    ).astype(jnp.bfloat16)
    grad_back = lax.all_to_all(
        grad_received, "exp", split_axis=0, concat_axis=0, tiled=True
    ).reshape(EXPERTS * CAP, -1)
    grad_pairs = jnp.where(
        is_kept[:, None], jnp.take(grad_back, safe_slot, axis=0), jnp.zeros((), jnp.bfloat16)
    )
    grad_pairs = grad_pairs.astype(jnp.float32).reshape(token_rows, TOPK, -1)
    grad_moe_in = (
        jnp.sum(grad_pairs, 1)
        + outer_cols(grad_logits.astype(jnp.bfloat16), full_router) * 0.0
        + lax.dot_general(
            grad_logits,
            full_router.astype(jnp.float32),
            (((1,), (1,)), ((), ())),
            precision=lax.Precision.HIGHEST,
            preferred_element_type=jnp.float32,
        )
    )
    grad_router = lax.dot_general(
        moe_in.astype(jnp.float32),
        grad_logits,
        (((0,), (0,)), ((), ())),
        precision=lax.Precision.HIGHEST,
        preferred_element_type=jnp.float32,
    )
    weighted_two = grad_moe_in * gain_two_f
    grad_gain_two = jnp.sum(grad_moe_in * resid * scale_two, 0)
    cube_two = scale_two * scale_two * scale_two
    grad_resid = (
        grad_out
        + scale_two * weighted_two
        - resid * cube_two * jnp.mean(weighted_two * resid, -1, keepdims=True)
    )
    grad_resid_low = grad_resid.astype(jnp.bfloat16)
    grad_output_w = inner_rows(attn_low, grad_resid_low)
    grad_heads = (
        outer_cols(grad_resid_low, full_output)
        .astype(jnp.bfloat16)
        .reshape(token_rows, KEY_VALUE_HEADS, head_cluster, HEAD_SIZE)
    )
    delta = jnp.transpose(jnp.sum(grad_heads.astype(jnp.float32) * heads_out, -1), (1, 2, 0))
    all_keys, all_values = (
        lax.all_gather(key_rows, "ctx", axis=0, tiled=True),
        lax.all_gather(value_rows, "ctx", axis=0, tiled=True),
    )

    def block_grads(offset):
        key_segment_slice = lax.dynamic_slice_in_dim(all_keys, offset, key_range_width)
        value_segment_slice = lax.dynamic_slice_in_dim(all_values, offset, key_range_width)
        scores = head_scores(heads_of_queries, key_segment_slice, factor)
        allowed = allowed_block(query_pos, query_seg, seg_all, offset, key_range_width)
        probs_full = jnp.where(allowed, jnp.exp(scores - log_norm[..., None]), 0.0)
        heads_of_keys = key_segment_slice.reshape(key_range_width, KEY_VALUE_HEADS, HEAD_SIZE)
        heads_of_values = value_segment_slice.reshape(key_range_width, KEY_VALUE_HEADS, HEAD_SIZE)
        grad_probs = jnp.einsum(
            "ihgd,jhd->hgij", grad_heads, heads_of_values, preferred_element_type=jnp.float32
        )
        grad_scores = (probs_full * (grad_probs - delta[..., None])).astype(jnp.bfloat16)
        query_part = jnp.einsum(
            "hgij,jhd->ihgd", grad_scores, heads_of_keys, preferred_element_type=jnp.float32
        )
        return (probs_full, grad_scores, query_part)

    query_begin_index = jnp.zeros(
        (token_rows, KEY_VALUE_HEADS, head_cluster, HEAD_SIZE), jnp.float32
    )

    def back_turn(turn, running):
        grad_query_acc, key_grad_buf = running
        offset = turn * key_range_width
        probs_full, grad_scores, query_part = block_grads(offset)
        grad_key_part = (
            jnp.einsum(
                "hgij,ihgd->jhd", grad_scores, heads_of_queries, preferred_element_type=jnp.float32
            )
            * factor
        )
        grad_value_part = jnp.einsum(
            "hgij,ihgd->jhd",
            probs_full.astype(jnp.bfloat16),
            grad_heads,
            preferred_element_type=jnp.float32,
        )
        joined = jnp.concatenate(
            [
                grad_key_part.reshape(key_range_width, -1),
                grad_value_part.reshape(key_range_width, -1),
            ],
            1,
        )
        key_grad_buf = lax.dynamic_update_slice_in_dim(key_grad_buf, joined, offset, 0)
        return (grad_query_acc + query_part, key_grad_buf)

    back_start = (query_begin_index, jnp.zeros((seq_len, 2 * kv_width), jnp.float32))
    grad_query_acc, key_grad_buf = lax.fori_loop(0, turns_needed, back_turn, back_start)
    own_grads = lax.psum_scatter(
        key_grad_buf.astype(jnp.bfloat16), "ctx", scatter_dimension=0, tiled=True
    ).astype(jnp.float32)
    grad_keys = own_grads[:, :kv_width].astype(jnp.bfloat16)
    grad_values = own_grads[:, kv_width:].astype(jnp.bfloat16)
    grad_query = (grad_query_acc * factor).reshape(token_rows, -1).astype(jnp.bfloat16)
    grad_query_w = inner_rows(normalized_input, grad_query)
    grad_key_w = inner_rows(normalized_input, grad_keys)
    grad_value_w = inner_rows(normalized_input, grad_values)
    grad_normed = (
        outer_cols(grad_query, full_query)
        + outer_cols(grad_keys, full_key)
        + outer_cols(grad_values, full_value)
    )
    weighted_one = grad_normed * gain_one_f
    grad_gain_one = jnp.sum(grad_normed * inputs * scale_one, 0)
    cube_one = scale_one * scale_one * scale_one
    grad_inputs = (
        grad_resid
        + scale_one * weighted_one
        - inputs * cube_one * jnp.mean(weighted_one * inputs, -1, keepdims=True)
    )
    dense_sums = (
        lax.psum_scatter(grad_gain_one, ("ctx", "exp"), scatter_dimension=0, tiled=True),
        lax.psum_scatter(grad_gain_two, ("ctx", "exp"), scatter_dimension=0, tiled=True),
        lax.psum_scatter(grad_query_w, ("ctx", "exp"), scatter_dimension=0, tiled=True),
        lax.psum_scatter(grad_key_w, ("ctx", "exp"), scatter_dimension=0, tiled=True),
        lax.psum_scatter(grad_value_w, ("ctx", "exp"), scatter_dimension=0, tiled=True),
        lax.psum_scatter(grad_output_w, ("ctx", "exp"), scatter_dimension=0, tiled=True),
        lax.psum_scatter(grad_router, ("ctx", "exp"), scatter_dimension=0, tiled=True),
    )
    expert_sums = (
        lax.psum_scatter(
            grad_expert_in.astype(jnp.bfloat16), "ctx", scatter_dimension=1, tiled=True
        ).astype(jnp.float32),
        lax.psum_scatter(
            grad_expert_out.astype(jnp.bfloat16), "ctx", scatter_dimension=1, tiled=True
        ).astype(jnp.float32),
    )
    return (mixed_out[None], grad_inputs[None]) + tuple(dense_sums) + tuple(expert_sums)


MESH = pl.DeviceIdType.MESH
VMEM = pltpu.VMEM
DMA = pltpu.SemaphoreType.DMA
LINES = 4
GRANT = 56 * 2**20


def to_f32(value):
    return value.astype(jnp.float32)


def dot_rows(left, right):
    return jnp.dot(left, right, preferred_element_type=jnp.float32)


def remote(source, target, send, recv, to):
    return pltpu.make_async_remote_copy(
        src_ref=source,
        dst_ref=target,
        send_sem=send,
        recv_sem=recv,
        device_id=to,
        device_id_type=MESH,
    )


class Place:
    def __init__(self):
        ctx, exp = lax.axis_index("ctx"), lax.axis_index("exp")
        self.ctx, self.exp = ctx, exp
        self.y, self.half = ctx // 2, ctx % 2
        self.z, self.x = exp // 2, exp % 2
        other_half = ctx + 1 - 2 * (ctx % 2)
        self.up, self.down = (ctx, exp + 2), (ctx, exp - 2)
        self.across = (ctx, exp + 1 - 2 * (exp % 2))
        self.core = (other_half, exp)
        self.side = (lax.rem(ctx + 2, 4), exp)
        self.far = (lax.rem(other_half + 2, 4), exp)

    def greet(self, lines=True, square=True):
        barrier = pltpu.get_barrier_semaphore()
        count = jnp.int32(0)
        if square:
            for to in (self.core, self.side, self.far):
                pl.semaphore_signal(barrier, inc=1, device_id=to, device_id_type=MESH)
            count = count + 3
        if lines:
            pl.semaphore_signal(barrier, inc=1, device_id=self.across, device_id_type=MESH)

            @pl.when(self.z < LINES - 1)
            def _():
                pl.semaphore_signal(barrier, inc=1, device_id=self.up, device_id_type=MESH)

            @pl.when(self.z > 0)
            def _():
                pl.semaphore_signal(barrier, inc=1, device_id=self.down, device_id_type=MESH)

            count = count + 1 + jnp.where(self.z < LINES - 1, 1, 0) + jnp.where(self.z > 0, 1, 0)
        pl.semaphore_wait(barrier, count)


class ExpGather:
    def __init__(self, place, view, parts, send, recv):
        self.place, self.view, self.parts = place, view, parts
        self.send, self.recv = send, recv

    def copy(self, lane, line, part, to):
        index = line * 2 + self.place.x
        ref = self.view(index, part)
        return remote(ref, ref, self.send.at[lane, line, part], self.recv.at[index, part], to)

    def pass_on(self, line, part, up, down):
        place = self.place
        if up:

            @pl.when(place.z < LINES - 1)
            def _():
                self.copy(1, line, part, place.up).start()

        if down:

            @pl.when(place.z > 0)
            def _():
                self.copy(2, line, part, place.down).start()

        self.copy(0, line, part, place.across).start()

    def begin(self, part):
        self.pass_on(self.place.z, part, True, True)

    def arrived(self, index, part):
        ref = self.view(index, part)
        remote(
            ref, ref, self.send.at[0, 0, part], self.recv.at[index, part], self.place.across
        ).wait_recv()

    def relay(self, step, part):
        place = self.place

        @pl.when(place.z >= step)
        def _():
            line = place.z - step
            self.arrived(line * 2 + place.x, part)
            self.pass_on(line, part, True, False)

        @pl.when(place.z + step < LINES)
        def _():
            line = place.z + step
            self.arrived(line * 2 + place.x, part)
            self.pass_on(line, part, False, True)

    def relays(self):
        for step in range(1, LINES):
            for part in range(self.parts):
                self.relay(step, part)

    def across_arrived(self, line, part):
        self.arrived(line * 2 + 1 - self.place.x, part)

    def finish(self):
        place = self.place
        for part in range(self.parts):
            for line in range(LINES):
                self.across_arrived(line, part)
        for part in range(self.parts):
            for line in range(LINES):
                self.copy(0, line, part, place.across).wait_send()

                @pl.when((place.z >= line) & (place.z < LINES - 1))
                def _():
                    self.copy(1, line, part, place.up).wait_send()

                @pl.when((place.z <= line) & (place.z > 0))
                def _():
                    self.copy(2, line, part, place.down).wait_send()


def gather_sems(parts):
    return [DMA((3, LINES, parts)), DMA((2 * LINES, parts))]


def raised_slot(line):
    return max(line - 1, 0) if isinstance(line, int) else jnp.maximum(line - 1, 0)


def lowered_slot(line):
    return min(line, LINES - 2) if isinstance(line, int) else jnp.minimum(line, LINES - 2)


class ExpScatter:
    def __init__(self, place, outgoing, mine, crossed, raised, lowered, parts, sems):
        self.place, self.parts = place, parts
        self.outgoing, self.mine = outgoing, mine
        self.crossed, self.raised, self.lowered = crossed, raised, lowered
        self.cross_send, self.cross_recv, self.line_send, self.line_recv = sems

    def cross(self, line, part):
        place = self.place
        return remote(
            self.outgoing(line, part),
            self.crossed(line, part),
            self.cross_send.at[line, part],
            self.cross_recv.at[line, part],
            place.across,
        )

    def along(self, up, line, part):
        place = self.place
        side = 0 if up else 1
        return remote(
            self.mine(line, part),
            (self.raised if up else self.lowered)(line, part),
            self.line_send.at[side, line, part],
            self.line_recv.at[side, line, part],
            place.up if up else place.down,
        )

    def begin(self, line, part):
        self.cross(line, part).start()

    def fold(self, line, part):
        place = self.place

        @pl.when(place.z != line)
        def _():
            self.cross(line, part).wait_recv()
            ref = self.mine(line, part)
            ref[...] = (to_f32(ref[...]) + to_f32(self.crossed(line, part)[...])).astype(ref.dtype)

        for up in (True, False):
            towards = place.z < line if up else place.z > line
            inner = place.z > 0 if up else place.z < LINES - 1

            @pl.when(towards)
            def _():
                ref = self.mine(line, part)

                @pl.when(inner)
                def _():
                    self.along(up, line, part).wait_recv()
                    came = (self.raised if up else self.lowered)(line, part)
                    ref[...] = (to_f32(ref[...]) + to_f32(came[...])).astype(ref.dtype)

                self.along(up, line, part).start()

    def total(self, part):
        place = self.place
        line = place.z
        self.cross(line, part).wait_recv()
        value = to_f32(self.mine(line, part)[...]) + to_f32(self.crossed(line, part)[...])
        for up in (True, False):
            came = (self.raised if up else self.lowered)(line, part)
            some = line > 0 if up else line < LINES - 1

            @pl.when(some)
            def _():
                self.along(up, line, part).wait_recv()

            value = value + jnp.where(some, to_f32(came[...]), 0.0)
        return value

    def finish(self):
        place = self.place
        for part in range(self.parts):
            for line in range(LINES):
                self.cross(line, part).wait_send()
                for up in (True, False):

                    @pl.when(place.z < line if up else place.z > line)
                    def _():
                        self.along(up, line, part).wait_send()


def scatter_sems(parts):
    return [DMA((LINES, parts)), DMA((LINES, parts)), DMA((2, LINES, parts)), DMA((2, LINES, parts))]


class CtxGather:
    def __init__(self, place, view, parts, send, recv):
        self.place, self.view, self.parts = place, view, parts
        self.send, self.recv = send, recv

    def copy(self, lane, part):
        place = self.place
        index = lax.rem(place.ctx + 2, 4) if lane == 2 else place.ctx
        ref = self.view(index, part)
        to = place.side if lane == 1 else place.core
        return remote(ref, ref, self.send.at[lane, part], self.recv.at[lane, part], to)

    def landed(self, lane, part):
        place = self.place
        index = (place.core, place.side, place.far)[lane][0]
        ref = self.view(index, part)
        return remote(ref, ref, self.send.at[lane, part], self.recv.at[lane, part], place.core)

    def begin(self, part):
        self.copy(1, part).start()
        self.copy(0, part).start()

    def relay(self, part):
        self.landed(1, part).wait_recv()
        self.copy(2, part).start()

    def arrived(self, part):
        self.landed(0, part).wait_recv()
        self.landed(2, part).wait_recv()

    def sent(self, part):
        for lane in range(3):
            self.copy(lane, part).wait_send()


def square_sems(parts):
    return [DMA((3, parts)), DMA((3, parts))]


class CtxScatter:
    def __init__(self, place, outgoing, mine, swapped, crossed, parts, send, recv):
        self.place, self.parts = place, parts
        self.outgoing, self.mine = outgoing, mine
        self.swapped, self.crossed = swapped, crossed
        self.send, self.recv = send, recv

    def swap(self, near, part):
        place = self.place
        y = place.y if near else 1 - place.y
        lane = 0 if near else 1
        return remote(
            self.outgoing(y, part),
            self.swapped(lane, part),
            self.send.at[lane, part],
            self.recv.at[lane, part],
            place.core,
        )

    def over(self, part):
        place = self.place
        return remote(
            self.mine(1 - place.y, part),
            self.crossed(part),
            self.send.at[2, part],
            self.recv.at[2, part],
            place.side,
        )

    def fold(self, part):
        self.swap(False, part).wait_recv()
        ref = self.mine(1 - self.place.y, part)
        ref[...] = (to_f32(ref[...]) + to_f32(self.swapped(1, part)[...])).astype(ref.dtype)
        self.over(part).start()

    def total(self, part):
        self.swap(True, part).wait_recv()
        self.over(part).wait_recv()
        return (
            to_f32(self.mine(self.place.y, part)[...])
            + to_f32(self.swapped(0, part)[...])
            + to_f32(self.crossed(part)[...])
        )

    def finish(self):
        for part in range(self.parts):
            self.swap(False, part).wait_send()
            self.swap(True, part).wait_send()
            self.over(part).wait_send()


def front_kernel(
    tokens,
    side_cols,
    wq,
    wk,
    wv,
    wo,
    routes,
    seg_col,
    seg_row,
    cot,
    exp_in,
    exp_out,
    all_moe,
    all_cot,
    all_routes,
    all_in,
    all_out,
    all_tokens,
    weights,
    out_rows,
    qkv,
    heads_out,
    log_norm,
    resid_out,
    packed,
    partial,
    swapped,
    crossed,
    stage,
    local_sem,
    tok_send,
    tok_recv,
    mix_send,
    mix_recv,
    w_send,
    w_recv,
    o_send,
    o_recv,
    r_send,
    r_recv,
    c_send,
    c_recv,
    m_send,
    m_recv,
    i_send,
    i_recv,
    u_send,
    u_recv,
    s_send,
    s_recv,
):
    place = Place()
    ctx, exp = place.ctx, place.exp
    shards, rows = packed.shape[0], packed.shape[1]
    token_rows, width = tokens.shape
    q_cols = wq.shape[1] // shards
    k_cols = wk.shape[1] // shards
    main_cols = q_cols + 2 * k_cols
    factor = 1.0 / math.sqrt(HEAD_SIZE)
    keep = [
        pltpu.make_async_copy(cot, all_cot.at[exp], local_sem.at[0]),
        pltpu.make_async_copy(exp_in, all_in.at[:, ctx], local_sem.at[1]),
        pltpu.make_async_copy(exp_out, all_out.at[:, ctx], local_sem.at[2]),
    ]
    for copy in keep:
        copy.start()
    all_tokens[ctx] = tokens[...]
    for shard in range(shards):
        packed[shard, :, :q_cols] = wq[:, shard * q_cols : (shard + 1) * q_cols]
        packed[shard, :, q_cols : q_cols + k_cols] = wk[:, shard * k_cols : (shard + 1) * k_cols]
        packed[shard, :, q_cols + k_cols : main_cols] = wv[:, shard * k_cols : (shard + 1) * k_cols]
        packed[shard, :, main_cols:] = side_cols[...]
    weights[ctx, exp] = packed[ctx]
    out_rows[exp] = wo[...]
    all_routes[exp] = routes[...]
    place.greet()

    mixes = []
    for lane, to in enumerate((place.core, place.side, place.far)):
        copy = remote(
            packed.at[to[0]],
            weights.at[ctx, exp],
            mix_send.at[lane],
            mix_recv.at[lane],
            to,
        )
        copy.start()
        mixes.append(copy)
    token_gather = CtxGather(
        place,
        lambda index, part: all_tokens.at[index, pl.ds(part * (token_rows // 2), token_rows // 2)],
        2,
        tok_send,
        tok_recv,
    )
    for part in range(2):
        token_gather.begin(part)
    route_gather = ExpGather(place, lambda index, part: all_routes.at[index], 1, r_send, r_recv)
    weight_gather = ExpGather(place, lambda index, part: weights.at[:, index], 1, w_send, w_recv)
    out_gather = ExpGather(place, lambda index, part: out_rows.at[index], 1, o_send, o_recv)
    for lane, copy in enumerate(mixes):
        source = (place.core, place.side, place.far)[lane][0]
        remote(
            packed.at[0], weights.at[source, exp], mix_send.at[lane], mix_recv.at[lane], place.core
        ).wait_recv()
    weight_gather.begin(0)
    route_gather.begin(0)
    out_gather.begin(0)
    for part in range(2):
        token_gather.relay(part)
    for step in range(1, LINES):
        weight_gather.relay(step, 0)
        route_gather.relay(step, 0)
        out_gather.relay(step, 0)

    for copy in keep:
        copy.wait()
    local_experts = exp_in.shape[0]
    in_gather = CtxGather(
        place, lambda index, part: all_in.at[part, index], local_experts, i_send, i_recv
    )
    down_gather = CtxGather(
        place, lambda index, part: all_out.at[part, index], local_experts, u_send, u_recv
    )
    cot_parts = 2
    cot_rows = token_rows // cot_parts
    cot_gather = ExpGather(
        place,
        lambda index, part: all_cot.at[index, pl.ds(part * cot_rows, cot_rows)],
        cot_parts,
        c_send,
        c_recv,
    )
    for part in range(2):
        token_gather.arrived(part)
    weight_gather.finish()
    for part in range(cot_parts):
        cot_gather.begin(part)
    for part in range(local_experts):
        in_gather.begin(part)

    gain_pick = (
        lax.broadcasted_iota(jnp.int32, (8, weights.shape[3] - main_cols), 1)
        == EXPERTS + lax.broadcasted_iota(jnp.int32, (8, weights.shape[3] - main_cols), 0)
    ).astype(jnp.bfloat16)
    full = weights[...].reshape(width, weights.shape[3])
    gains = outer_cols(gain_pick, full[:, main_cols:])
    gain_one, gain_two = gains[0:1], gains[1:2]
    for block in range(shards):
        values = to_f32(all_tokens[block])
        normed = (values * rms_scale(values) * gain_one).astype(jnp.bfloat16)
        qkv[pl.ds(block * token_rows, token_rows), :] = dot_rows(normed, full[:, :main_cols]).astype(
            jnp.bfloat16
        )
    out_gather.finish()
    route_gather.finish()

    low = lax.broadcasted_iota(jnp.int32, (1, 2 * HEAD_SIZE), 1) < HEAD_SIZE

    def spread(first):
        plain = to_f32(qkv[:, first : first + k_cols])
        turned = pltpu.roll(plain, HEAD_SIZE, 1)
        zero = jnp.zeros((), jnp.float32)
        return [
            [
                jnp.where(low, plain, zero).astype(jnp.bfloat16),
                jnp.where(low, zero, turned).astype(jnp.bfloat16),
            ],
            [
                jnp.where(low, turned, zero).astype(jnp.bfloat16),
                jnp.where(low, zero, plain).astype(jnp.bfloat16),
            ],
        ]

    keys, values = spread(q_cols), spread(q_cols + k_cols)
    full_out = out_rows[...].reshape(q_cols, width)
    for block in range(shards - 1, -1, -1):
        here = pl.ds(block * token_rows, token_rows)
        count = (block + 1) * token_rows
        at_row = block * token_rows + lax.broadcasted_iota(jnp.int32, (token_rows, 1), 0)
        at_col = lax.broadcasted_iota(jnp.int32, (1, count), 1)
        bias = jnp.where(
            (at_col <= at_row) & (seg_col[here, :] == seg_row[:, :count]), 0.0, MASK_FILLER
        )
        lows = []
        norms = jnp.zeros((token_rows, 128), jnp.float32)
        at_lane = lax.broadcasted_iota(jnp.int32, (1, 128), 1)
        for pair in range(2):
            queries = qkv[here, pair * 128 : pair * 128 + 128]
            heads = jnp.zeros((token_rows, 128), jnp.float32)
            for head in range(2):
                scores = outer_cols(queries, keys[pair][head][:count]) * factor + bias
                top = jnp.max(scores, -1, keepdims=True)
                shares = jnp.exp(scores - top)
                total = jnp.sum(shares, -1, keepdims=True)
                norms = jnp.where(at_lane == 2 * pair + head, top + jnp.log(total), norms)
                heads = heads + dot_rows(
                    shares.astype(jnp.bfloat16), values[pair][head][:count]
                ) / total
            heads_out[here, pair * 128 : pair * 128 + 128] = heads
            lows.append(heads.astype(jnp.bfloat16))
        log_norm[here, :] = norms
        partial[block] = dot_rows(jnp.concatenate(lows, 1), full_out).astype(jnp.bfloat16)
        if block == 3:
            for part in range(cot_parts):
                cot_gather.relay(1, part)
        if block == 2:
            for part in range(local_experts // 2):
                in_gather.relay(part)
        if block == 1:
            for part in range(cot_parts):
                cot_gather.relay(2, part)

    half_rows = token_rows // 2
    branch = CtxScatter(
        place,
        lambda y, part: partial.at[2 * y + 1 - place.half, pl.ds(part * half_rows, half_rows)],
        lambda y, part: partial.at[2 * y + place.half, pl.ds(part * half_rows, half_rows)],
        lambda lane, part: swapped.at[lane, pl.ds(part * half_rows, half_rows)],
        lambda part: crossed.at[pl.ds(part * half_rows, half_rows)],
        2,
        s_send,
        s_recv,
    )
    for part in range(2):
        branch.swap(False, part).start()
    for part in range(2):
        branch.swap(True, part).start()
    for part in range(2):
        branch.fold(part)
    moe_parts = 4
    moe_rows = token_rows // moe_parts
    moe_gather = ExpGather(
        place,
        lambda index, part: all_moe.at[index, pl.ds(part * moe_rows, moe_rows)],
        moe_parts,
        m_send,
        m_recv,
    )
    for part in range(2):
        here = pl.ds(part * half_rows, half_rows)
        resid = to_f32(tokens[here, :]) + branch.total(part)
        resid_out[here, :] = resid
        stage[here, :] = (resid * rms_scale(resid) * gain_two).astype(jnp.bfloat16)
        copy = pltpu.make_async_copy(
            stage.at[here], all_moe.at[exp, here], local_sem.at[3 + part]
        )
        copy.start()
        copy.wait()
        for piece in range(2):
            moe_gather.begin(2 * part + piece)
    for part in range(local_experts):
        down_gather.begin(part)
    for part in range(cot_parts):
        cot_gather.relay(3, part)
    for part in range(local_experts // 2, local_experts):
        in_gather.relay(part)
    moe_gather.relays()
    for part in range(local_experts):
        down_gather.relay(part)
    moe_gather.finish()
    cot_gather.finish()
    branch.finish()
    for part in range(2):
        token_gather.sent(part)
    for copy in mixes:
        copy.wait_send()
    for part in range(local_experts):
        in_gather.arrived(part)
        in_gather.sent(part)
        down_gather.arrived(part)
        down_gather.sent(part)


def front(tokens, side_cols, wq, wk, wv, wo, routes, seg_col, seg_row, cot, exp_in, exp_out):
    shards, groups = lax.axis_size("ctx"), lax.axis_size("exp")
    token_rows, width = tokens.shape
    rows = wq.shape[0]
    q_cols, k_cols = wq.shape[1] // shards, wk.shape[1] // shards
    pack_cols = q_cols + 2 * k_cols + side_cols.shape[1]
    seq_len = token_rows * shards
    low, f32 = jnp.bfloat16, jnp.float32
    experts, in_rows, in_cols = exp_in.shape
    out_count = exp_out.shape[1]

    def shape(dims, dtype):
        return jax.ShapeDtypeStruct(dims, dtype)

    whole, anywhere = pl.BlockSpec(memory_space=VMEM), pl.BlockSpec(memory_space=pl.ANY)
    return pl.pallas_call(
        front_kernel,
        name="front",
        out_shape=[
            shape((groups, token_rows, width), low),
            shape((groups, token_rows, width), low),
            shape((groups,) + routes.shape, jnp.int32),
            shape((experts, shards, in_rows, in_cols), low),
            shape((experts, shards, out_count, width), low),
            shape((shards, token_rows, width), low),
            shape((shards, groups, rows, pack_cols), low),
            shape((groups, rows, width), low),
            shape((seq_len, q_cols + 2 * k_cols), low),
            shape((seq_len, q_cols), f32),
            shape((seq_len, 128), f32),
            shape((token_rows, width), f32),
        ],
        in_specs=[whole] * 9 + [anywhere] * 3,
        out_specs=[anywhere] * 2 + [whole] + [anywhere] * 2 + [whole] * 7,
        scratch_shapes=[
            VMEM((shards, rows, pack_cols), low),
            VMEM((shards, token_rows, width), low),
            VMEM((2, token_rows, width), low),
            VMEM((token_rows, width), low),
            VMEM((token_rows, width), low),
            DMA((5,)),
            *square_sems(2),
            DMA((3,)),
            DMA((3,)),
            *gather_sems(1),
            *gather_sems(1),
            *gather_sems(1),
            *gather_sems(2),
            *gather_sems(4),
            *square_sems(experts),
            *square_sems(experts),
            *square_sems(2),
        ],
        compiler_params=pltpu.CompilerParams(
            collective_id=0, has_side_effects=True, vmem_limit_bytes=GRANT
        ),
    )(tokens, side_cols, wq, wk, wv, wo, routes, seg_col, seg_row, cot, exp_in, exp_out)


def back_kernel(
    moe_part,
    mixed_part,
    grad_in,
    grad_down,
    tokens,
    cot,
    resid,
    gain_two,
    gain_one,
    router_sum,
    all_tokens,
    weights,
    out_rows,
    qkv,
    heads_out,
    log_norm,
    seg_col,
    seg_row,
    mixed_out,
    grad_tokens,
    query_sum,
    key_sum,
    value_sum,
    side_sum,
    output_sum,
    in_sum,
    down_sum,
    moe_mine,
    moe_crossed,
    moe_raised,
    moe_lowered,
    mix_mine,
    mix_crossed,
    mix_raised,
    mix_lowered,
    in_mine,
    in_swapped,
    in_crossed,
    down_mine,
    down_swapped,
    down_crossed,
    grad_resid,
    all_resid,
    head_grads,
    turned,
    key_grads,
    value_grads,
    qkv_grads,
    sums,
    sums_crossed,
    sums_raised,
    sums_lowered,
    sums_own,
    sums_all,
    out_grads,
    out_crossed,
    out_raised,
    out_lowered,
    in_stage,
    down_stage,
    store_sem,
    local_sem,
    token_sem,
    moe_xs,
    moe_xr,
    moe_ls,
    moe_lr,
    mix_xs,
    mix_xr,
    mix_ls,
    mix_lr,
    sum_xs,
    sum_xr,
    sum_ls,
    sum_lr,
    out_xs,
    out_xr,
    out_ls,
    out_lr,
    in_send,
    in_recv,
    down_send,
    down_recv,
    normed_send,
    normed_recv,
    resid_send,
    resid_recv,
    last_send,
    last_recv,
):
    place = Place()
    ctx, exp = place.ctx, place.exp
    token_rows, width = tokens.shape
    shards, groups, rows, pack_cols = weights.shape
    local_experts = grad_in.shape[0]
    q_cols = heads_out.shape[1]
    main_cols = qkv.shape[1]
    k_cols = (main_cols - q_cols) // 2
    factor = 1.0 / math.sqrt(HEAD_SIZE)
    order = (3, 0, 2, 1)

    loads = []

    def load(source, target):
        copy = pltpu.make_async_copy(source, target, local_sem.at[len(loads)])
        copy.start()
        loads.append(copy)

    for line in order:
        load(moe_part.at[line * 2 + place.x], moe_mine.at[line])
    for y in range(2):
        load(grad_in.at[:, 2 * y + place.half], in_mine.at[y])
        load(grad_down.at[:, 2 * y + place.half], down_mine.at[y])
    for line in order:
        load(mixed_part.at[line * 2 + place.x], mix_mine.at[line])
    place.greet()

    def piece(ref, count, part):
        size = ref.shape[0] // count
        return ref.at[pl.ds(part * size, size)]

    moe_parts, mix_parts = 4, 2
    moe = ExpScatter(
        place,
        lambda line, part: piece(moe_part.at[line * 2 + 1 - place.x], moe_parts, part),
        lambda line, part: piece(moe_mine.at[line], moe_parts, part),
        lambda line, part: piece(moe_crossed.at[line], moe_parts, part),
        lambda line, part: piece(moe_raised.at[raised_slot(line)], moe_parts, part),
        lambda line, part: piece(moe_lowered.at[lowered_slot(line)], moe_parts, part),
        moe_parts,
        (moe_xs, moe_xr, moe_ls, moe_lr),
    )
    mix = ExpScatter(
        place,
        lambda line, part: piece(mixed_part.at[line * 2 + 1 - place.x], mix_parts, part),
        lambda line, part: piece(mix_mine.at[line], mix_parts, part),
        lambda line, part: piece(mix_crossed.at[line], mix_parts, part),
        lambda line, part: piece(mix_raised.at[raised_slot(line)], mix_parts, part),
        lambda line, part: piece(mix_lowered.at[lowered_slot(line)], mix_parts, part),
        mix_parts,
        (mix_xs, mix_xr, mix_ls, mix_lr),
    )
    into = CtxScatter(
        place,
        lambda y, part: grad_in.at[part, 2 * y + 1 - place.half],
        lambda y, part: in_mine.at[y, part],
        lambda lane, part: in_swapped.at[lane, part],
        lambda part: in_crossed.at[part],
        local_experts,
        in_send,
        in_recv,
    )
    downs = CtxScatter(
        place,
        lambda y, part: grad_down.at[part, 2 * y + 1 - place.half],
        lambda y, part: down_mine.at[y, part],
        lambda lane, part: down_swapped.at[lane, part],
        lambda part: down_crossed.at[part],
        local_experts,
        down_send,
        down_recv,
    )
    for first, second in ((3, 0), (2, 1)):
        for part in range(moe_parts):
            moe.begin(first, part)
            moe.begin(second, part)
    for near in (False, True):
        for part in range(local_experts):
            into.swap(near, part).start()
        for part in range(local_experts):
            downs.swap(near, part).start()
    for copy in loads:
        copy.wait()

    expert = 0
    for first, second in ((3, 0), (2, 1)):
        for part in range(moe_parts):
            moe.fold(first, part)
            moe.fold(second, part)
            if part % 2 == 1:
                into.fold(expert)
                expert += 1
    gain_one_row, gain_two_row = gain_one[...], gain_two[...]
    moe_rows = token_rows // moe_parts
    gain_two_sum = jnp.zeros((1, width), jnp.float32)
    resid_gather = CtxGather(
        place,
        lambda index, part: all_resid.at[index, pl.ds(part * moe_rows, moe_rows)],
        moe_parts,
        resid_send,
        resid_recv,
    )
    for part in range(moe_parts):
        here = pl.ds(part * moe_rows, moe_rows)
        grad_moe_in = moe.total(part)
        values = resid[here, :]
        scale = rms_scale(values)
        weighted = grad_moe_in * gain_two_row
        gain_two_sum = gain_two_sum + jnp.sum(grad_moe_in * values * scale, 0, keepdims=True)
        grads = (
            to_f32(cot[here, :])
            + scale * weighted
            - values * (scale * scale * scale) * jnp.mean(weighted * values, -1, keepdims=True)
        )
        grad_resid[here, :] = grads
        all_resid[ctx, here, :] = grads.astype(jnp.bfloat16)
        resid_gather.begin(part)
    for first, second in ((3, 0), (2, 1)):
        for part in range(mix_parts):
            mix.begin(first, part)
            mix.begin(second, part)
    moe.finish()
    token_blocks, normed_part = moe_crossed, moe_mine
    token_load = pltpu.make_async_copy(all_tokens, token_blocks, token_sem)
    token_load.start()

    full = weights[...].reshape(width, pack_cols)
    full_out = out_rows[...].reshape(q_cols, width)
    low = lax.broadcasted_iota(jnp.int32, (1, 2 * HEAD_SIZE), 1) < HEAD_SIZE

    def spread(first):
        plain = to_f32(qkv[:, first : first + k_cols])
        other = pltpu.roll(plain, HEAD_SIZE, 1)
        zero = jnp.zeros((), jnp.float32)
        return [
            [
                jnp.where(low, plain, zero).astype(jnp.bfloat16),
                jnp.where(low, zero, other).astype(jnp.bfloat16),
            ],
            [
                jnp.where(low, other, zero).astype(jnp.bfloat16),
                jnp.where(low, zero, plain).astype(jnp.bfloat16),
            ],
        ]

    keys, values = spread(q_cols), spread(q_cols + k_cols)
    norm_rows = log_norm[...].T
    for part in range(moe_parts):
        resid_gather.relay(part)
    for part in range(moe_parts):
        resid_gather.arrived(part)
    for part in range(local_experts):
        downs.fold(part)
    at_lane = lax.broadcasted_iota(jnp.int32, (1, 128), 1)
    for block in range(shards):
        here = pl.ds(block * token_rows, token_rows)
        grads = outer_cols(all_resid[block], full_out).astype(jnp.bfloat16)
        head_grads[here, :] = grads
        products = to_f32(grads) * heads_out[here, :]
        deltas = jnp.zeros((token_rows, 128), jnp.float32)
        for pair in range(2):
            both = products[:, pair * 128 : pair * 128 + 128]
            first = jnp.sum(jnp.where(low, both, 0.0), -1, keepdims=True)
            second = jnp.sum(jnp.where(low, 0.0, both), -1, keepdims=True)
            deltas = jnp.where(at_lane == 2 * pair, first, deltas)
            deltas = jnp.where(at_lane == 2 * pair + 1, second, deltas)
        turned[:, here] = deltas.T
    attn_low = heads_out[...].astype(jnp.bfloat16)
    flat_resid = all_resid[...].reshape(shards * token_rows, width)
    out_grads[...] = (
        inner_rows(attn_low, flat_resid).astype(jnp.bfloat16).reshape(groups, rows, width)
    )
    out_scatter = ExpScatter(
        place,
        lambda line, part: out_grads.at[line * 2 + 1 - place.x],
        lambda line, part: out_grads.at[line * 2 + place.x],
        lambda line, part: out_crossed.at[line],
        lambda line, part: out_raised.at[raised_slot(line)],
        lambda line, part: out_lowered.at[lowered_slot(line)],
        1,
        (out_xs, out_xr, out_ls, out_lr),
    )
    for line in order:
        out_scatter.begin(line, 0)
    key_grads[...] = jnp.zeros_like(key_grads)
    value_grads[...] = jnp.zeros_like(value_grads)
    for block in range(shards):
        here = pl.ds(block * token_rows, token_rows)
        count = (block + 1) * token_rows
        at_col = block * token_rows + lax.broadcasted_iota(jnp.int32, (1, token_rows), 1)
        at_row = lax.broadcasted_iota(jnp.int32, (count, 1), 0)
        bias = jnp.where(
            (at_row <= at_col) & (seg_col[:count, :] == seg_row[:, here]), 0.0, MASK_FILLER
        )
        for pair in range(2):
            lanes = slice(pair * 128, pair * 128 + 128)
            queries = qkv[here, lanes]
            grads = head_grads[here, lanes]
            query_grad = jnp.zeros((token_rows, 128), jnp.float32)
            for head in range(2):
                row = 2 * pair + head
                mine = low if head == 0 else jnp.logical_not(low)
                own_queries = jnp.where(mine, queries, jnp.zeros((), jnp.bfloat16))
                own_grads = jnp.where(mine, grads, jnp.zeros((), jnp.bfloat16))
                key, value = keys[pair][head][:count], values[pair][head][:count]
                scores = outer_cols(key, queries) * factor + bias
                probs = jnp.exp(scores - norm_rows[row : row + 1, block * token_rows : count])
                grad_probs = outer_cols(value, grads)
                grad_scores = (probs * (grad_probs - turned[row : row + 1, here])).astype(
                    jnp.bfloat16
                )
                value_grads[pair, :count, :] += dot_rows(probs.astype(jnp.bfloat16), own_grads)
                key_grads[pair, :count, :] += dot_rows(grad_scores, own_queries)
                query_grad = query_grad + inner_rows(grad_scores, key)
            qkv_grads[here, lanes] = (query_grad * factor).astype(jnp.bfloat16)
        if block == 0:
            for line in order:
                out_scatter.fold(line, 0)
        if block == 1:
            for part in range(mix_parts):
                mix.fold(3, part)
                mix.fold(0, part)
        if block == 2:
            for part in range(mix_parts):
                mix.fold(2, part)
                mix.fold(1, part)

    def fold_heads(first, second):
        return jnp.where(
            low,
            first + pltpu.roll(first, HEAD_SIZE, 1),
            second + pltpu.roll(second, HEAD_SIZE, 1),
        )

    qkv_grads[:, q_cols : q_cols + k_cols] = (
        fold_heads(key_grads[0], key_grads[1]) * factor
    ).astype(jnp.bfloat16)
    qkv_grads[:, q_cols + k_cols :] = fold_heads(value_grads[0], value_grads[1]).astype(
        jnp.bfloat16
    )

    token_load.wait()
    normed_scatter = CtxScatter(
        place,
        lambda y, part: normed_part.at[2 * y + 1 - place.half],
        lambda y, part: normed_part.at[2 * y + place.half],
        lambda lane, part: moe_raised.at[lane],
        lambda part: moe_raised.at[2],
        1,
        normed_send,
        normed_recv,
    )
    gain_one_sum = jnp.zeros((1, width), jnp.float32)
    main_sum = jnp.zeros((width, main_cols), jnp.float32)
    for block in range(shards):
        here = pl.ds(block * token_rows, token_rows)
        grads = outer_cols(qkv_grads[here, :], full[:, :main_cols])
        normed_part[block] = grads.astype(jnp.bfloat16)
        own = to_f32(token_blocks[block])
        scaled = own * rms_scale(own)
        gain_one_sum = gain_one_sum + jnp.sum(grads * scaled, 0, keepdims=True)
        normed = (scaled * gain_one_row).astype(jnp.bfloat16)
        main_sum = main_sum + inner_rows(normed, qkv_grads[here, :])
    normed_scatter.swap(False, 0).start()
    normed_scatter.swap(True, 0).start()
    at_sub = lax.broadcasted_iota(jnp.int32, (128, 1), 0)
    gain_rows = jnp.where(
        at_sub == EXPERTS, gain_one_sum, jnp.where(at_sub == EXPERTS + 1, gain_two_sum, 0.0)
    )
    side = router_sum[...] + gain_rows.T
    sums[:, :, :, :main_cols] = main_sum.astype(jnp.bfloat16).reshape(
        shards, groups, rows, main_cols
    )
    sums[:, :, :, main_cols:] = side.astype(jnp.bfloat16).reshape(
        shards, groups, rows, pack_cols - main_cols
    )
    sum_scatter = ExpScatter(
        place,
        lambda line, part: sums.at[:, line * 2 + 1 - place.x],
        lambda line, part: sums.at[:, line * 2 + place.x],
        lambda line, part: sums_crossed.at[line],
        lambda line, part: sums_raised.at[raised_slot(line)],
        lambda line, part: sums_lowered.at[lowered_slot(line)],
        1,
        (sum_xs, sum_xr, sum_ls, sum_lr),
    )
    for line in order:
        sum_scatter.begin(line, 0)
    normed_scatter.fold(0)
    for part in range(mix_parts):
        size = token_rows // mix_parts
        here = pl.ds(part * size, size)
        mixed_out[here, :] = (resid[here, :] + mix.total(part)).astype(jnp.bfloat16)
    output_sum[...] = out_scatter.total(0)
    for line in order:
        sum_scatter.fold(line, 0)
    stores = []
    for part in range(local_experts):
        slot = part % 2
        if part >= 2:
            for copy in stores[2 * (part - 2) : 2 * (part - 1)]:
                copy.wait()
        in_stage[slot] = into.total(part)
        down_stage[slot] = downs.total(part)
        for kind, (source, target) in enumerate(
            ((in_stage.at[slot], in_sum.at[part]), (down_stage.at[slot], down_sum.at[part]))
        ):
            copy = pltpu.make_async_copy(source, target, store_sem.at[kind, part])
            copy.start()
            stores.append(copy)
    sums_own[...] = sum_scatter.total(0).astype(jnp.bfloat16)
    sums_all[ctx] = sums_own[ctx]
    copies = []
    for lane, to in enumerate((place.core, place.side, place.far)):
        copy = remote(
            sums_own.at[to[0]], sums_all.at[ctx], last_send.at[lane], last_recv.at[lane], to
        )
        copy.start()
        copies.append(copy)
    grad_normed = normed_scatter.total(0)
    own = to_f32(tokens[...])
    scale = rms_scale(own)
    weighted = grad_normed * gain_one_row
    grad_tokens[...] = (
        grad_resid[...]
        + scale * weighted
        - own * (scale * scale * scale) * jnp.mean(weighted * own, -1, keepdims=True)
    )
    for lane, to in enumerate((place.core, place.side, place.far)):
        remote(
            sums_own.at[0], sums_all.at[to[0]], last_send.at[lane], last_recv.at[lane], to
        ).wait_recv()
    side = jnp.zeros((rows, pack_cols - main_cols), jnp.float32)
    for shard in range(shards):
        came = to_f32(sums_all[shard])
        query_sum[:, shard * q_cols : (shard + 1) * q_cols] = came[:, :q_cols]
        key_sum[:, shard * k_cols : (shard + 1) * k_cols] = came[:, q_cols : q_cols + k_cols]
        value_sum[:, shard * k_cols : (shard + 1) * k_cols] = came[:, q_cols + k_cols : main_cols]
        side = side + came[:, main_cols:]
    side_sum[...] = side
    for copy in stores[-4:]:
        copy.wait()
    for copy in copies:
        copy.wait_send()
    for scatter in (mix, into, downs, out_scatter, normed_scatter, sum_scatter):
        scatter.finish()
    for part in range(moe_parts):
        resid_gather.sent(part)


def back(
    moe_part, mixed_part, grad_in, grad_down, tokens, cot, resid, gain_two, gain_one, router_sum,
    all_tokens, weights, out_rows, qkv, heads_out, log_norm, seg_col, seg_row,
):
    token_rows, width = tokens.shape
    shards, groups, rows, pack_cols = weights.shape
    seq_len = shards * token_rows
    q_cols, main_cols = heads_out.shape[1], qkv.shape[1]
    k_cols = (main_cols - q_cols) // 2
    experts, _, in_rows, in_cols = grad_in.shape
    down_rows = grad_down.shape[2]
    low, f32 = jnp.bfloat16, jnp.float32

    def shape(dims, dtype):
        return jax.ShapeDtypeStruct(dims, dtype)

    whole, anywhere = pl.BlockSpec(memory_space=VMEM), pl.BlockSpec(memory_space=pl.ANY)
    block, steps = (LINES, token_rows, width), (LINES - 1, token_rows, width)
    pack = (shards, rows, pack_cols)
    return pl.pallas_call(
        back_kernel,
        name="back",
        out_shape=[
            shape((token_rows, width), low),
            shape((token_rows, width), f32),
            shape((rows, shards * q_cols), f32),
            shape((rows, shards * k_cols), f32),
            shape((rows, shards * k_cols), f32),
            shape((rows, pack_cols - main_cols), f32),
            shape((rows, width), f32),
            shape((experts, in_rows, in_cols), f32),
            shape((experts, down_rows, width), f32),
        ],
        in_specs=[anywhere] * 4 + [whole] * 6 + [anywhere] + [whole] * 7,
        out_specs=[whole] * 7 + [anywhere] * 2,
        scratch_shapes=[
            *[VMEM(block, low), VMEM(block, low), VMEM(steps, low), VMEM(steps, low)] * 2,
            VMEM((2, experts, in_rows, in_cols), low),
            VMEM((2, experts, in_rows, in_cols), low),
            VMEM((experts, in_rows, in_cols), low),
            VMEM((2, experts, down_rows, width), low),
            VMEM((2, experts, down_rows, width), low),
            VMEM((experts, down_rows, width), low),
            VMEM((token_rows, width), f32),
            VMEM((shards, token_rows, width), low),
            VMEM((seq_len, q_cols), low),
            VMEM((128, seq_len), f32),
            VMEM((2, seq_len, 128), f32),
            VMEM((2, seq_len, 128), f32),
            VMEM((seq_len, main_cols), low),
            VMEM((shards, groups, rows, pack_cols), low),
            VMEM((LINES,) + pack, low),
            *[VMEM((LINES - 1,) + pack, low)] * 2,
            VMEM((shards, rows, pack_cols), low),
            VMEM((shards, rows, pack_cols), low),
            VMEM((groups, rows, width), low),
            VMEM((LINES, rows, width), low),
            *[VMEM((LINES - 1, rows, width), low)] * 2,
            VMEM((2, in_rows, in_cols), f32),
            VMEM((2, down_rows, width), f32),
            DMA((2, experts)),
            DMA((12,)),
            DMA,
            *scatter_sems(4),
            *scatter_sems(2),
            *scatter_sems(1),
            *scatter_sems(1),
            *square_sems(experts),
            *square_sems(experts),
            *square_sems(1),
            *square_sems(4),
            DMA((3,)),
            DMA((3,)),
        ],
        compiler_params=pltpu.CompilerParams(
            collective_id=1, has_side_effects=True, vmem_limit_bytes=62 * 2**20
        ),
    )(
        moe_part, mixed_part, grad_in, grad_down, tokens, cot, resid, gain_two, gain_one, router_sum,
        all_tokens, weights, out_rows, qkv, heads_out, log_norm, seg_col, seg_row,
    )


def softmax_members(logits, member):
    top = jnp.max(jnp.where(member, logits, MASK_FILLER), -1, keepdims=True)
    weights = jnp.where(member, jnp.exp(logits - top), 0.0)
    return weights / jnp.sum(weights, -1, keepdims=True)


def two_parts(values):
    high = values.astype(jnp.bfloat16)
    return high, (values - high.astype(jnp.float32)).astype(jnp.bfloat16)


def by_heads(
    tokens,
    segments,
    routes,
    gain_attn,
    gain_moe,
    query_weight,
    key_weight,
    value_weight,
    w_output,
    w_router,
    w_expert_in,
    w_expert_out,
    cotangent,
):
    shards = lax.axis_size("ctx")
    groups = lax.axis_size("exp")
    exp_rank = lax.axis_index("exp")
    local_experts = EXPERTS // groups
    token_rows, width = tokens.shape[1], tokens.shape[2]
    rows = query_weight.shape[0]
    q_cols = query_weight.shape[1] // shards
    k_cols = key_weight.shape[1] // shards
    main_cols = q_cols + 2 * k_cols
    side = 128

    side_cols = jnp.concatenate(
        [
            w_router,
            gain_attn[:, None],
            gain_moe[:, None],
            jnp.zeros((rows, side - EXPERTS - 2), jnp.bfloat16),
        ],
        1,
    )
    seg_col, seg_row = segments[0][:, None], segments
    (
        all_moe,
        all_cot,
        all_routes,
        all_in,
        all_out,
        all_tokens,
        all_weights,
        out_rows,
        qkv,
        heads_out,
        log_norm,
        resid,
    ) = front(
        tokens[0],
        side_cols,
        query_weight,
        key_weight,
        value_weight,
        w_output,
        routes[0].T,
        seg_col,
        seg_row,
        cotangent[0],
        w_expert_in,
        w_expert_out,
    )
    expert_in = all_in.reshape(local_experts, width, -1)
    expert_out = all_out.reshape(local_experts, FF, -1)
    side_rows = all_weights[..., main_cols:].reshape(width, side)
    router = side_rows[:, :EXPERTS]
    gains = side_rows[:, EXPERTS : EXPERTS + 2].astype(jnp.float32).T

    member = jnp.any(
        all_routes[..., None] == jnp.arange(EXPERTS, dtype=jnp.int32), axis=1
    )
    logits = jnp.einsum("std,de->ste", all_moe, router, preferred_element_type=jnp.float32)
    gates = softmax_members(logits, member)
    earlier = jnp.tril(jnp.ones((token_rows, token_rows), jnp.bfloat16), -1)
    rank = jnp.einsum(
        "tu,sue->ste", earlier, member.astype(jnp.bfloat16), preferred_element_type=jnp.float32
    ).astype(jnp.int32)
    kept = member & (rank < CAP)
    first = exp_rank * local_experts

    def mine(table):
        return lax.dynamic_slice_in_dim(table, first, local_experts, 2)

    place = jnp.where(mine(kept), mine(rank), -1)
    pick = (
        place.transpose(0, 2, 1)[:, :, None, :]
        == jnp.arange(CAP, dtype=jnp.int32)[None, None, :, None]
    ).astype(jnp.bfloat16)
    both = jnp.concatenate([all_moe, all_cot], -1)
    slots = jnp.einsum("sjct,std->sjcd", pick, both, preferred_element_type=jnp.float32)
    slot_rows = slots[..., :width].astype(jnp.bfloat16)
    slot_cot = slots[..., width:]
    slot_gate = jnp.sum(
        pick.astype(jnp.float32) * mine(gates).transpose(0, 2, 1)[:, :, None, :], -1
    )
    pre = jnp.einsum("sjcd,jdf->sjcf", slot_rows, expert_in, preferred_element_type=jnp.float32)
    gate_part, up_part = pre[..., :FF], pre[..., FF:]
    sigmoid_gate = jax.nn.sigmoid(gate_part)
    hidden = (gate_part * sigmoid_gate * up_part).astype(jnp.bfloat16)
    expert_rows = jnp.einsum(
        "sjcf,jfd->sjcd", hidden, expert_out, preferred_element_type=jnp.float32
    ).astype(jnp.bfloat16)
    weighted = (slot_gate[..., None] * expert_rows.astype(jnp.float32)).astype(jnp.bfloat16)
    mixed_part = jnp.einsum(
        "sjct,sjcd->std", pick, weighted, preferred_element_type=jnp.float32
    ).astype(jnp.bfloat16)
    grad_rows = (slot_gate[..., None] * slot_cot).astype(jnp.bfloat16)
    slot_dot = jnp.sum(slot_cot * expert_rows.astype(jnp.float32), -1)
    grad_picked = jnp.sum(pick.astype(jnp.float32) * slot_dot[..., None], 2).transpose(0, 2, 1)
    grad_picked = lax.dynamic_update_slice_in_dim(jnp.zeros_like(gates), grad_picked, first, 2)
    grad_logits = gates * (grad_picked - jnp.sum(gates * grad_picked, -1, keepdims=True))
    logits_high, logits_low = two_parts(grad_logits)
    grad_router = jnp.einsum(
        "std,ste->de", all_moe, logits_high, preferred_element_type=jnp.float32
    ) + jnp.einsum("std,ste->de", all_moe, logits_low, preferred_element_type=jnp.float32)
    grad_hidden = jnp.einsum(
        "sjcd,jfd->sjcf", grad_rows, expert_out, preferred_element_type=jnp.float32
    )
    grad_gate = grad_hidden * up_part * sigmoid_gate * (1.0 + gate_part * (1.0 - sigmoid_gate))
    grad_up = grad_hidden * gate_part * sigmoid_gate
    grad_pre = jnp.concatenate([grad_gate, grad_up], -1).astype(jnp.bfloat16)
    grad_slots = jnp.einsum(
        "sjcf,jdf->sjcd", grad_pre, expert_in, preferred_element_type=jnp.float32
    ).astype(jnp.bfloat16)
    moe_part = (
        jnp.einsum("sjct,sjcd->std", pick, grad_slots, preferred_element_type=jnp.float32)
        + jnp.einsum("ste,de->std", logits_high, router, preferred_element_type=jnp.float32)
        + jnp.einsum("ste,de->std", logits_low, router, preferred_element_type=jnp.float32)
    ).astype(jnp.bfloat16)
    grad_expert_out = jnp.einsum(
        "sjcf,sjcd->jfd", hidden, grad_rows, preferred_element_type=jnp.float32
    ).astype(jnp.bfloat16)
    grad_expert_in = jnp.einsum(
        "sjcd,sjcf->jdf", slot_rows, grad_pre, preferred_element_type=jnp.float32
    ).astype(jnp.bfloat16)

    router_sum = jnp.pad(grad_router, ((0, 0), (0, side - EXPERTS)))
    (
        mixed_out,
        grad_tokens,
        query_sum,
        key_sum,
        value_sum,
        side_sum,
        output_sum,
        in_sum,
        down_sum,
    ) = back(
        moe_part,
        mixed_part,
        grad_expert_in.reshape(all_in.shape),
        grad_expert_out.reshape(all_out.shape),
        tokens[0],
        cotangent[0],
        resid,
        gains[1:2],
        gains[0:1],
        router_sum,
        all_tokens,
        all_weights,
        out_rows,
        qkv,
        heads_out,
        log_norm,
        seg_col,
        seg_row,
    )
    return (
        mixed_out[None],
        grad_tokens[None],
        side_sum[:, EXPERTS],
        side_sum[:, EXPERTS + 1],
        query_sum,
        key_sum,
        value_sum,
        output_sum,
        side_sum[:, :EXPERTS],
        in_sum,
        down_sum,
    )


def solution(mesh):
    sizes = (mesh.shape["ctx"], mesh.shape["exp"])
    return jax.shard_map(
        by_heads if sizes == (4, 8) else local,
        mesh=mesh,
        in_specs=(
            P("exp", "ctx", None),
            P("exp", None),
            P("exp", "ctx", None),
            P(("ctx", "exp")),
            P(("ctx", "exp")),
            P(("ctx", "exp"), None),
            P(("ctx", "exp"), None),
            P(("ctx", "exp"), None),
            P(("ctx", "exp"), None),
            P(("ctx", "exp"), None),
            P("exp", "ctx", None),
            P("exp", "ctx", None),
            P("exp", "ctx", None),
        ),
        out_specs=(
            P("exp", "ctx", None),
            P("exp", "ctx", None),
            P(("ctx", "exp")),
            P(("ctx", "exp")),
            P(("ctx", "exp"), None),
            P(("ctx", "exp"), None),
            P(("ctx", "exp"), None),
            P(("ctx", "exp"), None),
            P(("ctx", "exp"), None),
            P("exp", "ctx", None),
            P("exp", "ctx", None),
        ),
        check_vma=False,
    )
```

```python
import math

import jax
import jax.numpy as jnp
from jax import lax
from jax.experimental import pallas as pl
from jax.experimental.pallas import tpu as pltpu
from jax.sharding import PartitionSpec as P

QUERY_HEADS = 16
KEY_VALUE_HEADS = 8
HEAD_SIZE = 64
EXPERTS = 32
TOPK = 8
FF = 512
CAP = 72


EPSILON = 1e-06
MASK_FILLER = -1e30


def rms_scale(values):
    return lax.rsqrt(jnp.mean(values * values, -1, keepdims=True) + EPSILON)


def inner_rows(left, right):
    return lax.dot_general(
        left, right, (((0,), (0,)), ((), ())), preferred_element_type=jnp.float32
    )


def outer_cols(left, right):
    return lax.dot_general(
        left, right, (((1,), (1,)), ((), ())), preferred_element_type=jnp.float32
    )


def allowed_block(query_pos, query_seg, seg_all, offset, key_total_count):
    key_pos = offset + jnp.arange(key_total_count, dtype=jnp.int32)
    key_seg = lax.dynamic_slice_in_dim(seg_all, offset, key_total_count)
    return (key_pos[None, :] <= query_pos[:, None]) & (key_seg[None, :] == query_seg[:, None])


def head_scores(heads_of_queries, key_segment_slice, factor):
    key_total_count = key_segment_slice.shape[0]
    heads_of_keys = key_segment_slice.reshape(key_total_count, KEY_VALUE_HEADS, -1)
    return (
        jnp.einsum(
            "ihgd,jhd->hgij", heads_of_queries, heads_of_keys, preferred_element_type=jnp.float32
        )
        * factor
    )


def slot_tables(pair_ids):
    pair_count = pair_ids.shape[0]
    member = (pair_ids[:, None] == jnp.arange(EXPERTS, dtype=jnp.int32)[None, :]).astype(jnp.int32)
    earlier = jnp.cumsum(member, 0) - member
    slot_place = jnp.sum(earlier * member, 1, dtype=jnp.int32)
    is_kept = slot_place < CAP
    slot_index = jnp.where(is_kept, pair_ids * CAP + slot_place, EXPERTS * CAP)
    slot_filler = (
        jnp.full((EXPERTS * CAP,), -1, jnp.int32)
        .at[slot_index]
        .set(jnp.arange(pair_count, dtype=jnp.int32), mode="drop")
    )
    return (slot_index, is_kept, slot_filler)


def local(
    tokens,
    segments,
    routes,
    gain_attn,
    gain_moe,
    query_weight,
    key_weight,
    value_weight,
    w_output,
    w_router,
    w_expert_in,
    w_expert_out,
    cotangent,
):
    shards = lax.axis_size("ctx")
    groups = lax.axis_size("exp")
    ctx_rank = lax.axis_index("ctx")
    gain_one, gain_two, full_query, full_key, full_value, full_output, full_router = (
        lax.all_gather(gain_attn, ("ctx", "exp"), axis=0, tiled=True),
        lax.all_gather(gain_moe, ("ctx", "exp"), axis=0, tiled=True),
        lax.all_gather(query_weight, ("ctx", "exp"), axis=0, tiled=True),
        lax.all_gather(key_weight, ("ctx", "exp"), axis=0, tiled=True),
        lax.all_gather(value_weight, ("ctx", "exp"), axis=0, tiled=True),
        lax.all_gather(w_output, ("ctx", "exp"), axis=0, tiled=True),
        lax.all_gather(w_router, ("ctx", "exp"), axis=0, tiled=True),
    )
    expert_in, expert_out = (
        lax.all_gather(w_expert_in, "ctx", axis=1, tiled=True),
        lax.all_gather(w_expert_out, "ctx", axis=1, tiled=True),
    )
    inputs = tokens[0].astype(jnp.float32)
    token_rows = inputs.shape[0]
    seq_len = token_rows * shards
    head_cluster = QUERY_HEADS // KEY_VALUE_HEADS
    factor = 1.0 / math.sqrt(HEAD_SIZE)
    kv_width = key_weight.shape[1]
    seg_all = segments[0]
    query_pos = ctx_rank * token_rows + jnp.arange(token_rows, dtype=jnp.int32)
    query_seg = lax.dynamic_slice_in_dim(seg_all, ctx_rank * token_rows, token_rows)
    scale_one = rms_scale(inputs)
    gain_one_f = gain_one.astype(jnp.float32)
    normalized_input = (inputs * scale_one * gain_one_f).astype(jnp.bfloat16)
    query_matrix = jnp.dot(normalized_input, full_query, preferred_element_type=jnp.float32).astype(
        jnp.bfloat16
    )
    key_rows = jnp.dot(normalized_input, full_key, preferred_element_type=jnp.float32).astype(
        jnp.bfloat16
    )
    value_rows = jnp.dot(normalized_input, full_value, preferred_element_type=jnp.float32).astype(
        jnp.bfloat16
    )
    heads_of_queries = query_matrix.reshape(token_rows, KEY_VALUE_HEADS, head_cluster, HEAD_SIZE)
    group_size = math.gcd(shards, max(1, 1024 // token_rows))
    key_range_width = group_size * token_rows
    turns_needed = ctx_rank // group_size + 1
    running_maximum = jnp.full(
        (KEY_VALUE_HEADS, head_cluster, token_rows), MASK_FILLER, jnp.float32
    )
    key_segment_slice = lax.all_gather(key_rows, "ctx", axis=0, tiled=True)
    value_segment_slice = lax.all_gather(value_rows, "ctx", axis=0, tiled=True)
    key_total_count = key_segment_slice.shape[0]
    scores = head_scores(heads_of_queries, key_segment_slice, factor)
    allowed = allowed_block(query_pos, query_seg, seg_all, jnp.int32(0), key_total_count)
    scores = jnp.where(allowed, scores, MASK_FILLER)
    new_max = jnp.maximum(running_maximum, jnp.max(scores, -1))
    weights = jnp.where(allowed, jnp.exp(scores - new_max[..., None]), 0.0)
    run_sum = jnp.sum(weights, -1)
    heads_of_values = value_segment_slice.reshape(key_total_count, KEY_VALUE_HEADS, HEAD_SIZE)
    run_acc = jnp.einsum(
        "hgij,jhd->ihgd",
        weights.astype(jnp.bfloat16),
        heads_of_values,
        preferred_element_type=jnp.float32,
    )
    running_maximum, run_sum, run_acc = (new_max, run_sum, run_acc)
    log_norm = running_maximum + jnp.log(run_sum)
    heads_out = run_acc / jnp.transpose(run_sum, (2, 0, 1))[..., None]
    attn_low = heads_out.reshape(token_rows, -1).astype(jnp.bfloat16)
    resid = inputs + jnp.dot(attn_low, full_output, preferred_element_type=jnp.float32)
    scale_two = rms_scale(resid)
    gain_two_f = gain_two.astype(jnp.float32)
    moe_in = (resid * scale_two * gain_two_f).astype(jnp.bfloat16)
    logits = jnp.dot(moe_in, full_router, preferred_element_type=jnp.float32)
    route_ids = routes[0]
    one_hot = (route_ids[:, :, None] == jnp.arange(EXPERTS, dtype=jnp.int32)[None, None, :]).astype(
        jnp.float32
    )
    chosen = jnp.sum(one_hot * logits[:, None, :], -1)
    gates = jax.nn.softmax(chosen, axis=-1)
    slot_index, is_kept, slot_filler = slot_tables(route_ids.reshape(-1))
    filled = slot_filler >= 0
    token_of = jnp.maximum(slot_filler, 0) // TOPK
    local_experts = EXPERTS // groups
    send_rows = jnp.where(
        filled[:, None], jnp.take(moe_in, token_of, axis=0), jnp.zeros((), jnp.bfloat16)
    )
    send_rows = send_rows.reshape(groups, local_experts, CAP, -1)
    received = lax.all_to_all(send_rows, "exp", split_axis=0, concat_axis=0, tiled=True)
    pre = jnp.einsum("sjcd,jdf->sjcf", received, expert_in, preferred_element_type=jnp.float32)
    gate_part = pre[..., :FF]
    up_part = pre[..., FF:]
    hidden = (jax.nn.silu(gate_part) * up_part).astype(jnp.bfloat16)
    expert_rows = jnp.einsum(
        "sjcf,jfd->sjcd", hidden, expert_out, preferred_element_type=jnp.float32
    ).astype(jnp.bfloat16)
    returned = lax.all_to_all(expert_rows, "exp", split_axis=0, concat_axis=0, tiled=True).reshape(
        EXPERTS * CAP, -1
    )
    safe_slot = jnp.minimum(slot_index, EXPERTS * CAP - 1)
    picked = jnp.where(
        is_kept[:, None], jnp.take(returned, safe_slot, axis=0), jnp.zeros((), jnp.bfloat16)
    )
    picked = picked.astype(jnp.float32).reshape(token_rows, TOPK, -1)
    branch = jnp.sum(gates[:, :, None] * picked, 1)
    mixed_out = (resid + branch).astype(jnp.bfloat16)
    grad_out = cotangent[0].astype(jnp.float32)
    grad_picked = jnp.sum(grad_out[:, None, :] * picked, -1)
    grad_chosen = gates * (grad_picked - jnp.sum(gates * grad_picked, -1, keepdims=True))
    grad_logits = jnp.sum(one_hot * grad_chosen[:, :, None], 1)
    slot_gate = jnp.where(filled, jnp.take(gates.reshape(-1), jnp.maximum(slot_filler, 0)), 0.0)
    grad_send = (slot_gate[:, None] * jnp.take(grad_out, token_of, axis=0)).astype(jnp.bfloat16)
    grad_send = grad_send.reshape(groups, local_experts, CAP, -1)
    grad_rows = lax.all_to_all(grad_send, "exp", split_axis=0, concat_axis=0, tiled=True)
    grad_hidden = jnp.einsum(
        "sjcd,jfd->sjcf", grad_rows, expert_out, preferred_element_type=jnp.float32
    )
    sigmoid_gate = jax.nn.sigmoid(gate_part)
    grad_gate = grad_hidden * up_part * sigmoid_gate * (1.0 + gate_part * (1.0 - sigmoid_gate))
    grad_up = grad_hidden * gate_part * sigmoid_gate
    grad_pre = jnp.concatenate([grad_gate, grad_up], -1).astype(jnp.bfloat16)
    grad_expert_out = jnp.einsum(
        "sjcf,sjcd->jfd", hidden, grad_rows, preferred_element_type=jnp.float32
    )
    grad_expert_in = jnp.einsum(
        "sjcd,sjcf->jdf", received, grad_pre, preferred_element_type=jnp.float32
    )
    grad_received = jnp.einsum(
        "sjcf,jdf->sjcd", grad_pre, expert_in, preferred_element_type=jnp.float32
    ).astype(jnp.bfloat16)
    grad_back = lax.all_to_all(
        grad_received, "exp", split_axis=0, concat_axis=0, tiled=True
    ).reshape(EXPERTS * CAP, -1)
    grad_pairs = jnp.where(
        is_kept[:, None], jnp.take(grad_back, safe_slot, axis=0), jnp.zeros((), jnp.bfloat16)
    )
    grad_pairs = grad_pairs.astype(jnp.float32).reshape(token_rows, TOPK, -1)
    grad_moe_in = (
        jnp.sum(grad_pairs, 1)
        + outer_cols(grad_logits.astype(jnp.bfloat16), full_router) * 0.0
        + lax.dot_general(
            grad_logits,
            full_router.astype(jnp.float32),
            (((1,), (1,)), ((), ())),
            precision=lax.Precision.HIGHEST,
            preferred_element_type=jnp.float32,
        )
    )
    grad_router = lax.dot_general(
        moe_in.astype(jnp.float32),
        grad_logits,
        (((0,), (0,)), ((), ())),
        precision=lax.Precision.HIGHEST,
        preferred_element_type=jnp.float32,
    )
    weighted_two = grad_moe_in * gain_two_f
    grad_gain_two = jnp.sum(grad_moe_in * resid * scale_two, 0)
    cube_two = scale_two * scale_two * scale_two
    grad_resid = (
        grad_out
        + scale_two * weighted_two
        - resid * cube_two * jnp.mean(weighted_two * resid, -1, keepdims=True)
    )
    grad_resid_low = grad_resid.astype(jnp.bfloat16)
    grad_output_w = inner_rows(attn_low, grad_resid_low)
    grad_heads = (
        outer_cols(grad_resid_low, full_output)
        .astype(jnp.bfloat16)
        .reshape(token_rows, KEY_VALUE_HEADS, head_cluster, HEAD_SIZE)
    )
    delta = jnp.transpose(jnp.sum(grad_heads.astype(jnp.float32) * heads_out, -1), (1, 2, 0))
    all_keys, all_values = (
        lax.all_gather(key_rows, "ctx", axis=0, tiled=True),
        lax.all_gather(value_rows, "ctx", axis=0, tiled=True),
    )

    def block_grads(offset):
        key_segment_slice = lax.dynamic_slice_in_dim(all_keys, offset, key_range_width)
        value_segment_slice = lax.dynamic_slice_in_dim(all_values, offset, key_range_width)
        scores = head_scores(heads_of_queries, key_segment_slice, factor)
        allowed = allowed_block(query_pos, query_seg, seg_all, offset, key_range_width)
        probs_full = jnp.where(allowed, jnp.exp(scores - log_norm[..., None]), 0.0)
        heads_of_keys = key_segment_slice.reshape(key_range_width, KEY_VALUE_HEADS, HEAD_SIZE)
        heads_of_values = value_segment_slice.reshape(key_range_width, KEY_VALUE_HEADS, HEAD_SIZE)
        grad_probs = jnp.einsum(
            "ihgd,jhd->hgij", grad_heads, heads_of_values, preferred_element_type=jnp.float32
        )
        grad_scores = (probs_full * (grad_probs - delta[..., None])).astype(jnp.bfloat16)
        query_part = jnp.einsum(
            "hgij,jhd->ihgd", grad_scores, heads_of_keys, preferred_element_type=jnp.float32
        )
        return (probs_full, grad_scores, query_part)

    query_begin_index = jnp.zeros(
        (token_rows, KEY_VALUE_HEADS, head_cluster, HEAD_SIZE), jnp.float32
    )

    def back_turn(turn, running):
        grad_query_acc, key_grad_buf = running
        offset = turn * key_range_width
        probs_full, grad_scores, query_part = block_grads(offset)
        grad_key_part = (
            jnp.einsum(
                "hgij,ihgd->jhd", grad_scores, heads_of_queries, preferred_element_type=jnp.float32
            )
            * factor
        )
        grad_value_part = jnp.einsum(
            "hgij,ihgd->jhd",
            probs_full.astype(jnp.bfloat16),
            grad_heads,
            preferred_element_type=jnp.float32,
        )
        joined = jnp.concatenate(
            [
                grad_key_part.reshape(key_range_width, -1),
                grad_value_part.reshape(key_range_width, -1),
            ],
            1,
        )
        key_grad_buf = lax.dynamic_update_slice_in_dim(key_grad_buf, joined, offset, 0)
        return (grad_query_acc + query_part, key_grad_buf)

    back_start = (query_begin_index, jnp.zeros((seq_len, 2 * kv_width), jnp.float32))
    grad_query_acc, key_grad_buf = lax.fori_loop(0, turns_needed, back_turn, back_start)
    own_grads = lax.psum_scatter(
        key_grad_buf.astype(jnp.bfloat16), "ctx", scatter_dimension=0, tiled=True
    ).astype(jnp.float32)
    grad_keys = own_grads[:, :kv_width].astype(jnp.bfloat16)
    grad_values = own_grads[:, kv_width:].astype(jnp.bfloat16)
    grad_query = (grad_query_acc * factor).reshape(token_rows, -1).astype(jnp.bfloat16)
    grad_query_w = inner_rows(normalized_input, grad_query)
    grad_key_w = inner_rows(normalized_input, grad_keys)
    grad_value_w = inner_rows(normalized_input, grad_values)
    grad_normed = (
        outer_cols(grad_query, full_query)
        + outer_cols(grad_keys, full_key)
        + outer_cols(grad_values, full_value)
    )
    weighted_one = grad_normed * gain_one_f
    grad_gain_one = jnp.sum(grad_normed * inputs * scale_one, 0)
    cube_one = scale_one * scale_one * scale_one
    grad_inputs = (
        grad_resid
        + scale_one * weighted_one
        - inputs * cube_one * jnp.mean(weighted_one * inputs, -1, keepdims=True)
    )
    dense_sums = (
        lax.psum_scatter(grad_gain_one, ("ctx", "exp"), scatter_dimension=0, tiled=True),
        lax.psum_scatter(grad_gain_two, ("ctx", "exp"), scatter_dimension=0, tiled=True),
        lax.psum_scatter(grad_query_w, ("ctx", "exp"), scatter_dimension=0, tiled=True),
        lax.psum_scatter(grad_key_w, ("ctx", "exp"), scatter_dimension=0, tiled=True),
        lax.psum_scatter(grad_value_w, ("ctx", "exp"), scatter_dimension=0, tiled=True),
        lax.psum_scatter(grad_output_w, ("ctx", "exp"), scatter_dimension=0, tiled=True),
        lax.psum_scatter(grad_router, ("ctx", "exp"), scatter_dimension=0, tiled=True),
    )
    expert_sums = (
        lax.psum_scatter(
            grad_expert_in.astype(jnp.bfloat16), "ctx", scatter_dimension=1, tiled=True
        ).astype(jnp.float32),
        lax.psum_scatter(
            grad_expert_out.astype(jnp.bfloat16), "ctx", scatter_dimension=1, tiled=True
        ).astype(jnp.float32),
    )
    return (mixed_out[None], grad_inputs[None]) + tuple(dense_sums) + tuple(expert_sums)


MESH = pl.DeviceIdType.MESH
VMEM = pltpu.VMEM
DMA = pltpu.SemaphoreType.DMA
LINES = 4
GRANT = 56 * 2**20


def to_f32(value):
    return value.astype(jnp.float32)


def dot_rows(left, right):
    return jnp.dot(left, right, preferred_element_type=jnp.float32)


def remote(source, target, send, recv, to):
    return pltpu.make_async_remote_copy(
        src_ref=source,
        dst_ref=target,
        send_sem=send,
        recv_sem=recv,
        device_id=to,
        device_id_type=MESH,
    )


class Place:
    def __init__(self):
        ctx, exp = lax.axis_index("ctx"), lax.axis_index("exp")
        self.ctx, self.exp = ctx, exp
        self.y, self.half = ctx // 2, ctx % 2
        self.z, self.x = exp // 2, exp % 2
        other_half = ctx + 1 - 2 * (ctx % 2)
        self.up, self.down = (ctx, exp + 2), (ctx, exp - 2)
        self.across = (ctx, exp + 1 - 2 * (exp % 2))
        self.core = (other_half, exp)
        self.side = (lax.rem(ctx + 2, 4), exp)
        self.far = (lax.rem(other_half + 2, 4), exp)

    def greet(self, lines=True, square=True):
        barrier = pltpu.get_barrier_semaphore()
        count = jnp.int32(0)
        if square:
            for to in (self.core, self.side, self.far):
                pl.semaphore_signal(barrier, inc=1, device_id=to, device_id_type=MESH)
            count = count + 3
        if lines:
            pl.semaphore_signal(barrier, inc=1, device_id=self.across, device_id_type=MESH)

            @pl.when(self.z < LINES - 1)
            def _():
                pl.semaphore_signal(barrier, inc=1, device_id=self.up, device_id_type=MESH)

            @pl.when(self.z > 0)
            def _():
                pl.semaphore_signal(barrier, inc=1, device_id=self.down, device_id_type=MESH)

            count = count + 1 + jnp.where(self.z < LINES - 1, 1, 0) + jnp.where(self.z > 0, 1, 0)
        pl.semaphore_wait(barrier, count)


class ExpGather:
    def __init__(self, place, view, parts, send, recv):
        self.place, self.view, self.parts = place, view, parts
        self.send, self.recv = send, recv

    def copy(self, lane, line, part, to):
        index = line * 2 + self.place.x
        ref = self.view(index, part)
        return remote(ref, ref, self.send.at[lane, line, part], self.recv.at[index, part], to)

    def pass_on(self, line, part, up, down):
        place = self.place
        if up:

            @pl.when(place.z < LINES - 1)
            def _():
                self.copy(1, line, part, place.up).start()

        if down:

            @pl.when(place.z > 0)
            def _():
                self.copy(2, line, part, place.down).start()

        self.copy(0, line, part, place.across).start()

    def begin(self, part):
        self.pass_on(self.place.z, part, True, True)

    def arrived(self, index, part):
        ref = self.view(index, part)
        remote(
            ref, ref, self.send.at[0, 0, part], self.recv.at[index, part], self.place.across
        ).wait_recv()

    def relay(self, step, part):
        place = self.place

        @pl.when(place.z >= step)
        def _():
            line = place.z - step
            self.arrived(line * 2 + place.x, part)
            self.pass_on(line, part, True, False)

        @pl.when(place.z + step < LINES)
        def _():
            line = place.z + step
            self.arrived(line * 2 + place.x, part)
            self.pass_on(line, part, False, True)

    def relays(self):
        for step in range(1, LINES):
            for part in range(self.parts):
                self.relay(step, part)

    def across_arrived(self, line, part):
        self.arrived(line * 2 + 1 - self.place.x, part)

    def finish(self):
        place = self.place
        for part in range(self.parts):
            for line in range(LINES):
                self.across_arrived(line, part)
        for part in range(self.parts):
            for line in range(LINES):
                self.copy(0, line, part, place.across).wait_send()

                @pl.when((place.z >= line) & (place.z < LINES - 1))
                def _():
                    self.copy(1, line, part, place.up).wait_send()

                @pl.when((place.z <= line) & (place.z > 0))
                def _():
                    self.copy(2, line, part, place.down).wait_send()


def gather_sems(parts):
    return [DMA((3, LINES, parts)), DMA((2 * LINES, parts))]


def raised_slot(line):
    return max(line - 1, 0) if isinstance(line, int) else jnp.maximum(line - 1, 0)


def lowered_slot(line):
    return min(line, LINES - 2) if isinstance(line, int) else jnp.minimum(line, LINES - 2)


class ExpScatter:
    def __init__(self, place, outgoing, mine, crossed, raised, lowered, parts, sems):
        self.place, self.parts = place, parts
        self.outgoing, self.mine = outgoing, mine
        self.crossed, self.raised, self.lowered = crossed, raised, lowered
        self.cross_send, self.cross_recv, self.line_send, self.line_recv = sems

    def cross(self, line, part):
        place = self.place
        return remote(
            self.outgoing(line, part),
            self.crossed(line, part),
            self.cross_send.at[line, part],
            self.cross_recv.at[line, part],
            place.across,
        )

    def along(self, up, line, part):
        place = self.place
        side = 0 if up else 1
        return remote(
            self.mine(line, part),
            (self.raised if up else self.lowered)(line, part),
            self.line_send.at[side, line, part],
            self.line_recv.at[side, line, part],
            place.up if up else place.down,
        )

    def begin(self, line, part):
        self.cross(line, part).start()

    def fold(self, line, part):
        place = self.place

        @pl.when(place.z != line)
        def _():
            self.cross(line, part).wait_recv()
            ref = self.mine(line, part)
            ref[...] = (to_f32(ref[...]) + to_f32(self.crossed(line, part)[...])).astype(ref.dtype)

        for up in (True, False):
            towards = place.z < line if up else place.z > line
            inner = place.z > 0 if up else place.z < LINES - 1

            @pl.when(towards)
            def _():
                ref = self.mine(line, part)

                @pl.when(inner)
                def _():
                    self.along(up, line, part).wait_recv()
                    came = (self.raised if up else self.lowered)(line, part)
                    ref[...] = (to_f32(ref[...]) + to_f32(came[...])).astype(ref.dtype)

                self.along(up, line, part).start()

    def total(self, part):
        place = self.place
        line = place.z
        self.cross(line, part).wait_recv()
        value = to_f32(self.mine(line, part)[...]) + to_f32(self.crossed(line, part)[...])
        for up in (True, False):
            came = (self.raised if up else self.lowered)(line, part)
            some = line > 0 if up else line < LINES - 1

            @pl.when(some)
            def _():
                self.along(up, line, part).wait_recv()

            value = value + jnp.where(some, to_f32(came[...]), 0.0)
        return value

    def finish(self):
        place = self.place
        for part in range(self.parts):
            for line in range(LINES):
                self.cross(line, part).wait_send()
                for up in (True, False):

                    @pl.when(place.z < line if up else place.z > line)
                    def _():
                        self.along(up, line, part).wait_send()


def scatter_sems(parts):
    return [DMA((LINES, parts)), DMA((LINES, parts)), DMA((2, LINES, parts)), DMA((2, LINES, parts))]


class CtxGather:
    def __init__(self, place, view, parts, send, recv, own=None):
        self.place, self.view, self.parts = place, view, parts
        self.send, self.recv, self.own = send, recv, own

    def copy(self, lane, part):
        place = self.place
        index = lax.rem(place.ctx + 2, 4) if lane == 2 else place.ctx
        ref = self.view(index, part)
        source = ref if lane == 2 or self.own is None else self.own(part)
        to = place.side if lane == 1 else place.core
        return remote(source, ref, self.send.at[lane, part], self.recv.at[lane, part], to)

    def landed(self, lane, part):
        place = self.place
        index = (place.core, place.side, place.far)[lane][0]
        ref = self.view(index, part)
        return remote(ref, ref, self.send.at[lane, part], self.recv.at[lane, part], place.core)

    def begin(self, part):
        self.copy(1, part).start()
        self.copy(0, part).start()

    def relay(self, part):
        self.landed(1, part).wait_recv()
        self.copy(2, part).start()

    def arrived(self, part):
        self.landed(0, part).wait_recv()
        self.landed(2, part).wait_recv()

    def sent(self, part):
        for lane in range(3):
            self.copy(lane, part).wait_send()


def square_sems(parts):
    return [DMA((3, parts)), DMA((3, parts))]


class CtxScatter:
    def __init__(self, place, outgoing, mine, swapped, crossed, parts, send, recv):
        self.place, self.parts = place, parts
        self.outgoing, self.mine = outgoing, mine
        self.swapped, self.crossed = swapped, crossed
        self.send, self.recv = send, recv

    def swap(self, near, part):
        place = self.place
        y = place.y if near else 1 - place.y
        lane = 0 if near else 1
        return remote(
            self.outgoing(y, part),
            self.swapped(lane, part),
            self.send.at[lane, part],
            self.recv.at[lane, part],
            place.core,
        )

    def over(self, part):
        place = self.place
        return remote(
            self.mine(1 - place.y, part),
            self.crossed(part),
            self.send.at[2, part],
            self.recv.at[2, part],
            place.side,
        )

    def fold(self, part):
        self.swap(False, part).wait_recv()
        ref = self.mine(1 - self.place.y, part)
        ref[...] = (to_f32(ref[...]) + to_f32(self.swapped(1, part)[...])).astype(ref.dtype)
        self.over(part).start()

    def total(self, part):
        self.swap(True, part).wait_recv()
        self.over(part).wait_recv()
        return (
            to_f32(self.mine(self.place.y, part)[...])
            + to_f32(self.swapped(0, part)[...])
            + to_f32(self.crossed(part)[...])
        )

    def finish(self):
        for part in range(self.parts):
            self.swap(False, part).wait_send()
            self.swap(True, part).wait_send()
            self.over(part).wait_send()


def front_kernel(
    tokens,
    side_cols,
    wq,
    wk,
    wv,
    wo,
    routes,
    seg_col,
    seg_row,
    cot,
    exp_in,
    exp_out,
    all_moe,
    all_cot,
    all_routes,
    all_in,
    all_out,
    all_tokens,
    weights,
    out_rows,
    qkv,
    heads_out,
    log_norm,
    resid_out,
    side_rows,
    packed,
    partial,
    swapped,
    crossed,
    stage,
    in_stage,
    out_stage,
    local_sem,
    tok_send,
    tok_recv,
    mix_send,
    mix_recv,
    w_send,
    w_recv,
    o_send,
    o_recv,
    r_send,
    r_recv,
    c_send,
    c_recv,
    m_send,
    m_recv,
    i_send,
    i_recv,
    u_send,
    u_recv,
    s_send,
    s_recv,
):
    place = Place()
    ctx, exp = place.ctx, place.exp
    shards, rows = packed.shape[0], packed.shape[1]
    token_rows, width = tokens.shape
    q_cols = wq.shape[1] // shards
    k_cols = wk.shape[1] // shards
    main_cols = q_cols + 2 * k_cols
    factor = 1.0 / math.sqrt(HEAD_SIZE)
    keep = [
        pltpu.make_async_copy(cot, all_cot.at[exp], local_sem.at[0]),
        pltpu.make_async_copy(exp_in, in_stage, local_sem.at[1]),
        pltpu.make_async_copy(exp_out, out_stage, local_sem.at[2]),
    ]
    for copy in keep:
        copy.start()
    all_tokens[ctx] = tokens[...]
    for shard in range(shards):
        packed[shard, :, :q_cols] = wq[:, shard * q_cols : (shard + 1) * q_cols]
        packed[shard, :, q_cols : q_cols + k_cols] = wk[:, shard * k_cols : (shard + 1) * k_cols]
        packed[shard, :, q_cols + k_cols : main_cols] = wv[:, shard * k_cols : (shard + 1) * k_cols]
        packed[shard, :, main_cols:] = side_cols[...]
    weights[ctx, exp] = packed[ctx]
    out_rows[exp] = wo[...]
    all_routes[exp] = routes[...]
    place.greet()

    mixes = []
    for lane, to in enumerate((place.core, place.side, place.far)):
        copy = remote(
            packed.at[to[0]],
            weights.at[ctx, exp],
            mix_send.at[lane],
            mix_recv.at[lane],
            to,
        )
        copy.start()
        mixes.append(copy)
    token_gather = CtxGather(
        place,
        lambda index, part: all_tokens.at[index, pl.ds(part * (token_rows // 2), token_rows // 2)],
        2,
        tok_send,
        tok_recv,
    )
    for part in range(2):
        token_gather.begin(part)
    route_gather = ExpGather(place, lambda index, part: all_routes.at[index], 1, r_send, r_recv)
    weight_gather = ExpGather(place, lambda index, part: weights.at[:, index], 1, w_send, w_recv)
    out_gather = ExpGather(place, lambda index, part: out_rows.at[index], 1, o_send, o_recv)
    for lane, copy in enumerate(mixes):
        source = (place.core, place.side, place.far)[lane][0]
        remote(
            packed.at[0], weights.at[source, exp], mix_send.at[lane], mix_recv.at[lane], place.core
        ).wait_recv()
    weight_gather.begin(0)
    route_gather.begin(0)
    out_gather.begin(0)
    for part in range(2):
        token_gather.relay(part)
    for step in range(1, LINES):
        weight_gather.relay(step, 0)
        route_gather.relay(step, 0)
        out_gather.relay(step, 0)

    for copy in keep:
        copy.wait()
    keep = [
        pltpu.make_async_copy(in_stage, all_in.at[:, ctx], local_sem.at[1]),
        pltpu.make_async_copy(out_stage, all_out.at[:, ctx], local_sem.at[2]),
    ]
    for copy in keep:
        copy.start()
    local_experts = exp_in.shape[0]
    in_gather = CtxGather(
        place,
        lambda index, part: all_in.at[part, index],
        local_experts,
        i_send,
        i_recv,
        lambda part: in_stage.at[part],
    )
    down_gather = CtxGather(
        place,
        lambda index, part: all_out.at[part, index],
        local_experts,
        u_send,
        u_recv,
        lambda part: out_stage.at[part],
    )
    cot_parts = 2
    cot_rows = token_rows // cot_parts
    cot_gather = ExpGather(
        place,
        lambda index, part: all_cot.at[index, pl.ds(part * cot_rows, cot_rows)],
        cot_parts,
        c_send,
        c_recv,
    )
    for part in range(2):
        token_gather.arrived(part)
    weight_gather.finish()
    for part in range(cot_parts):
        cot_gather.begin(part)
    for part in range(local_experts):
        in_gather.begin(part)

    side = weights.shape[3] - main_cols
    same = (
        lax.broadcasted_iota(jnp.int32, (side, side), 0)
        == lax.broadcasted_iota(jnp.int32, (side, side), 1)
    ).astype(jnp.bfloat16)
    full = weights[...].reshape(width, weights.shape[3])
    side_t = outer_cols(same, full[:, main_cols:])
    side_rows[...] = side_t.astype(jnp.bfloat16)
    gain_one, gain_two = side_t[EXPERTS : EXPERTS + 1], side_t[EXPERTS + 1 : EXPERTS + 2]
    for block in range(shards):
        values = to_f32(all_tokens[block])
        normed = (values * rms_scale(values) * gain_one).astype(jnp.bfloat16)
        qkv[pl.ds(block * token_rows, token_rows), :] = dot_rows(normed, full[:, :main_cols]).astype(
            jnp.bfloat16
        )
    out_gather.finish()
    route_gather.finish()

    low = lax.broadcasted_iota(jnp.int32, (1, 2 * HEAD_SIZE), 1) < HEAD_SIZE

    def spread(first):
        plain = to_f32(qkv[:, first : first + k_cols])
        turned = pltpu.roll(plain, HEAD_SIZE, 1)
        zero = jnp.zeros((), jnp.float32)
        return [
            [
                jnp.where(low, plain, zero).astype(jnp.bfloat16),
                jnp.where(low, zero, turned).astype(jnp.bfloat16),
            ],
            [
                jnp.where(low, turned, zero).astype(jnp.bfloat16),
                jnp.where(low, zero, plain).astype(jnp.bfloat16),
            ],
        ]

    keys, values = spread(q_cols), spread(q_cols + k_cols)
    full_out = out_rows[...].reshape(q_cols, width)
    for block in range(shards - 1, -1, -1):
        here = pl.ds(block * token_rows, token_rows)
        count = (block + 1) * token_rows
        at_row = block * token_rows + lax.broadcasted_iota(jnp.int32, (token_rows, 1), 0)
        at_col = lax.broadcasted_iota(jnp.int32, (1, count), 1)
        bias = jnp.where(
            (at_col <= at_row) & (seg_col[here, :] == seg_row[:, :count]), 0.0, MASK_FILLER
        )
        lows = []
        norms = jnp.zeros((token_rows, 128), jnp.float32)
        at_lane = lax.broadcasted_iota(jnp.int32, (1, 128), 1)
        for pair in range(2):
            queries = qkv[here, pair * 128 : pair * 128 + 128]
            heads = jnp.zeros((token_rows, 128), jnp.float32)
            for head in range(2):
                scores = outer_cols(queries, keys[pair][head][:count]) * factor + bias
                top = jnp.max(scores, -1, keepdims=True)
                shares = jnp.exp(scores - top)
                total = jnp.sum(shares, -1, keepdims=True)
                norms = jnp.where(at_lane == 2 * pair + head, top + jnp.log(total), norms)
                heads = heads + dot_rows(
                    shares.astype(jnp.bfloat16), values[pair][head][:count]
                ) / total
            heads_out[here, pair * 128 : pair * 128 + 128] = heads
            lows.append(heads.astype(jnp.bfloat16))
        log_norm[here, :] = norms
        partial[block] = dot_rows(jnp.concatenate(lows, 1), full_out).astype(jnp.bfloat16)
        if block == 3:
            for part in range(cot_parts):
                cot_gather.relay(1, part)
        if block == 2:
            for part in range(local_experts // 2):
                in_gather.relay(part)
        if block == 1:
            for part in range(cot_parts):
                cot_gather.relay(2, part)

    half_rows = token_rows // 2
    branch = CtxScatter(
        place,
        lambda y, part: partial.at[2 * y + 1 - place.half, pl.ds(part * half_rows, half_rows)],
        lambda y, part: partial.at[2 * y + place.half, pl.ds(part * half_rows, half_rows)],
        lambda lane, part: swapped.at[lane, pl.ds(part * half_rows, half_rows)],
        lambda part: crossed.at[pl.ds(part * half_rows, half_rows)],
        2,
        s_send,
        s_recv,
    )
    for part in range(2):
        branch.swap(False, part).start()
    for part in range(2):
        branch.swap(True, part).start()
    for part in range(2):
        branch.fold(part)
    moe_parts = 4
    moe_rows = token_rows // moe_parts
    moe_gather = ExpGather(
        place,
        lambda index, part: all_moe.at[index, pl.ds(part * moe_rows, moe_rows)],
        moe_parts,
        m_send,
        m_recv,
    )
    for part in range(2):
        here = pl.ds(part * half_rows, half_rows)
        resid = to_f32(tokens[here, :]) + branch.total(part)
        resid_out[here, :] = resid
        stage[here, :] = (resid * rms_scale(resid) * gain_two).astype(jnp.bfloat16)
        copy = pltpu.make_async_copy(
            stage.at[here], all_moe.at[exp, here], local_sem.at[3 + part]
        )
        copy.start()
        copy.wait()
        for piece in range(2):
            moe_gather.begin(2 * part + piece)
    for part in range(local_experts):
        down_gather.begin(part)
    for part in range(cot_parts):
        cot_gather.relay(3, part)
    for part in range(local_experts // 2, local_experts):
        in_gather.relay(part)
    moe_gather.relays()
    for part in range(local_experts):
        down_gather.relay(part)
    moe_gather.finish()
    cot_gather.finish()
    for copy in keep:
        copy.wait()
    branch.finish()
    for part in range(2):
        token_gather.sent(part)
    for copy in mixes:
        copy.wait_send()
    for part in range(local_experts):
        in_gather.arrived(part)
        in_gather.sent(part)
        down_gather.arrived(part)
        down_gather.sent(part)


def front(tokens, side_cols, wq, wk, wv, wo, routes, seg_col, seg_row, cot, exp_in, exp_out):
    shards, groups = lax.axis_size("ctx"), lax.axis_size("exp")
    token_rows, width = tokens.shape
    rows = wq.shape[0]
    q_cols, k_cols = wq.shape[1] // shards, wk.shape[1] // shards
    pack_cols = q_cols + 2 * k_cols + side_cols.shape[1]
    seq_len = token_rows * shards
    low, f32 = jnp.bfloat16, jnp.float32
    experts, in_rows, in_cols = exp_in.shape
    out_count = exp_out.shape[1]

    def shape(dims, dtype):
        return jax.ShapeDtypeStruct(dims, dtype)

    whole, anywhere = pl.BlockSpec(memory_space=VMEM), pl.BlockSpec(memory_space=pl.ANY)
    return pl.pallas_call(
        front_kernel,
        name="front",
        out_shape=[
            shape((groups, token_rows, width), low),
            shape((groups, token_rows, width), low),
            shape((groups,) + routes.shape, jnp.int32),
            shape((experts, shards, in_rows, in_cols), low),
            shape((experts, shards, out_count, width), low),
            shape((shards, token_rows, width), low),
            shape((shards, groups, rows, pack_cols), low),
            shape((groups, rows, width), low),
            shape((seq_len, q_cols + 2 * k_cols), low),
            shape((seq_len, q_cols), f32),
            shape((seq_len, 128), f32),
            shape((token_rows, width), f32),
            shape((side_cols.shape[1], width), low),
        ],
        in_specs=[whole] * 10 + [anywhere] * 2,
        out_specs=[anywhere] * 2 + [whole] + [anywhere] * 2 + [whole] * 8,
        scratch_shapes=[
            VMEM((shards, rows, pack_cols), low),
            VMEM((shards, token_rows, width), low),
            VMEM((2, token_rows, width), low),
            VMEM((token_rows, width), low),
            VMEM((token_rows, width), low),
            VMEM(exp_in.shape, low),
            VMEM(exp_out.shape, low),
            DMA((5,)),
            *square_sems(2),
            DMA((3,)),
            DMA((3,)),
            *gather_sems(1),
            *gather_sems(1),
            *gather_sems(1),
            *gather_sems(2),
            *gather_sems(4),
            *square_sems(experts),
            *square_sems(experts),
            *square_sems(2),
        ],
        compiler_params=pltpu.CompilerParams(
            collective_id=0, has_side_effects=True, vmem_limit_bytes=GRANT
        ),
    )(tokens, side_cols, wq, wk, wv, wo, routes, seg_col, seg_row, cot, exp_in, exp_out)


def experts_kernel(
    all_moe,
    all_cot,
    all_routes,
    all_in,
    all_out,
    side_rows,
    resid,
    grad_moe_in,
    mixed_first,
    mixed_rest,
    router_sum,
    in_first,
    down_first,
    in_rest,
    down_rest,
    moe,
    cot,
    w_in,
    w_out,
    slot_rows,
    slot_cot,
    hidden,
    slopes,
    slot_out,
    pick,
    slot_gate,
    slot_dot,
    gates,
    logit_grads,
    router_grads,
    moe_crossed,
    moe_raised,
    moe_lowered,
    mix_crossed,
    mix_raised,
    mix_lowered,
    in_stage,
    down_stage,
    resid_rows,
    load_sem,
    store_sem,
    free_sem,
    moe_xs,
    moe_xr,
    moe_ls,
    moe_lr,
    mix_xs,
    mix_xr,
    mix_ls,
    mix_lr,
    in_send,
    in_recv,
    down_send,
    down_recv,
):
    place = Place()
    groups, token_rows, width = moe.shape
    local_experts = w_in.shape[0]
    slots = pick.shape[1] // local_experts
    first = place.exp * local_experts
    loads = [
        pltpu.make_async_copy(all_moe, moe, load_sem.at[0]),
        pltpu.make_async_copy(all_cot, cot, load_sem.at[1]),
    ]
    for expert in range(local_experts):
        loads.append(
            pltpu.make_async_copy(all_in.at[expert], w_in.at[expert], load_sem.at[2 + 2 * expert])
        )
        loads.append(
            pltpu.make_async_copy(all_out.at[expert], w_out.at[expert], load_sem.at[3 + 2 * expert])
        )
    loads.append(
        pltpu.make_async_copy(
            resid.at[pl.ds(0, mixed_first.shape[0])], resid_rows, load_sem.at[2 + 2 * local_experts]
        )
    )
    for copy in loads:
        copy.start()
    place.greet()

    at_expert = lax.broadcasted_iota(jnp.int32, (EXPERTS, 1), 0)
    at_lane = lax.broadcasted_iota(jnp.int32, (1, 128), 1)
    at_slot = lax.broadcasted_iota(jnp.int32, (slots, 1), 0)
    before = (
        lax.broadcasted_iota(jnp.int32, (token_rows, token_rows), 0)
        < lax.broadcasted_iota(jnp.int32, (token_rows, token_rows), 1)
    ).astype(jnp.bfloat16)
    router = side_rows[:EXPERTS, :]
    loads[0].wait()
    loads[1].wait()

    def dispatch(block, carry):
        routes = all_routes[block]
        member = routes[0:1, :] == at_expert
        for rank in range(1, TOPK):
            member = member | (routes[rank : rank + 1, :] == at_expert)
        tokens = moe[block]
        logits = outer_cols(router, tokens)
        top = jnp.max(jnp.where(member, logits, MASK_FILLER), 0, keepdims=True)
        weights = jnp.where(member, jnp.exp(logits - top), 0.0)
        shares = weights / jnp.sum(weights, 0, keepdims=True)
        gates[block] = shares
        ranks = dot_rows(jnp.where(member, 1.0, 0.0).astype(jnp.bfloat16), before)
        filled = jnp.where(member & (ranks < CAP), ranks, -1.0)
        columns = jnp.zeros((slots, 128), jnp.float32)
        for expert in range(local_experts):
            mine = at_expert == first + expert
            spot = jnp.sum(jnp.where(mine, filled, 0.0), 0, keepdims=True)
            share = jnp.sum(jnp.where(mine, shares, 0.0), 0, keepdims=True)
            chosen = spot == at_slot.astype(jnp.float32)
            here = pl.ds(expert * slots, slots)
            pick[block, here, :] = jnp.where(chosen, 1.0, 0.0).astype(jnp.bfloat16)
            column = jnp.sum(jnp.where(chosen, share, 0.0), 1, keepdims=True)
            columns = jnp.where(at_lane == expert, column, columns)
        slot_gate[block] = columns
        chosen = pick[block]
        rows = dot_rows(chosen, tokens).astype(jnp.bfloat16)
        cots = dot_rows(chosen, cot[block]).astype(jnp.bfloat16)
        for expert in range(local_experts):
            slot_rows[expert, block] = rows[expert * slots : (expert + 1) * slots]
            slot_cot[expert, block] = cots[expert * slots : (expert + 1) * slots]
        return carry

    lax.fori_loop(0, groups, dispatch, 0)
    for copy in loads[2:]:
        copy.wait()
    all_slots = groups * slots

    def flat(ref, expert):
        return ref[expert].reshape(all_slots, ref.shape[-1])

    def shaped(value):
        return value.reshape(groups, slots, value.shape[-1])

    def forward(expert, carry):
        rows = flat(slot_rows, expert)
        gate_part = dot_rows(rows, w_in[expert, :, :FF])
        up_part = dot_rows(rows, w_in[expert, :, FF:])
        sigmoid_gate = jax.nn.sigmoid(gate_part)
        silu = gate_part * sigmoid_gate
        low_hidden = (silu * up_part).astype(jnp.bfloat16)
        hidden[expert] = low_hidden
        slopes[expert, :, :FF] = (
            up_part * sigmoid_gate * (1.0 + gate_part * (1.0 - sigmoid_gate))
        ).astype(jnp.bfloat16)
        slopes[expert, :, FF:] = silu.astype(jnp.bfloat16)
        out = dot_rows(low_hidden, w_out[expert]).astype(jnp.bfloat16).astype(jnp.float32)
        cots = to_f32(flat(slot_cot, expert))
        lane = at_lane == expert
        table = slot_gate[...].reshape(all_slots, 128)
        share = jnp.sum(jnp.where(lane, table, 0.0), 1, keepdims=True)
        dots = jnp.sum(cots * out, 1, keepdims=True)
        slot_dot[...] = shaped(jnp.where(lane, dots, slot_dot[...].reshape(all_slots, 128)))
        slot_out[expert] = (share * out).astype(jnp.bfloat16)
        slot_cot[expert] = shaped((share * cots).astype(jnp.bfloat16))
        return carry

    slot_dot[...] = jnp.zeros_like(slot_dot)
    lax.fori_loop(0, local_experts, forward, 0)
    router_grads[...] = jnp.zeros_like(router_grads)

    def block_rows(ref, block):
        here = pl.ds(pl.multiple_of(block * slots, slots), slots)
        return jnp.concatenate([ref[expert, here, :] for expert in range(local_experts)], 0)

    def combine(block, carry):
        shares = gates[block]
        chosen = pick[block]
        picked_grads = jnp.zeros_like(shares)
        for expert in range(local_experts):
            part = to_f32(chosen[expert * slots : (expert + 1) * slots])
            row = jnp.sum(part * slot_dot[block, :, expert : expert + 1], 0, keepdims=True)
            picked_grads = jnp.where(at_expert == first + expert, row, picked_grads)
        grads = shares * (picked_grads - jnp.sum(shares * picked_grads, 0, keepdims=True))
        high, low = two_parts(grads)
        both = jnp.concatenate([high, low], 0)
        logit_grads[block] = both
        router_grads[...] += dot_rows(both, moe[block])
        moe[block] = inner_rows(chosen, block_rows(slot_out, block)).astype(jnp.bfloat16)
        return carry

    lax.fori_loop(0, groups, combine, 0)
    router_sum[...] = router_grads[:EXPERTS, :] + router_grads[EXPERTS:, :]

    mix_rows = mixed_first.shape[0]
    rest_store = pltpu.make_async_copy(
        moe.at[:, pl.ds(mix_rows, token_rows - mix_rows)], mixed_rest, load_sem.at[0]
    )
    rest_store.start()
    own_rows = pl.ds(0, mix_rows)
    mix = ExpScatter(
        place,
        lambda line, part: moe.at[line * 2 + 1 - place.x, own_rows],
        lambda line, part: moe.at[line * 2 + place.x, own_rows],
        lambda line, part: mix_crossed.at[line],
        lambda line, part: mix_raised.at[raised_slot(line)],
        lambda line, part: mix_lowered.at[lowered_slot(line)],
        1,
        (mix_xs, mix_xr, mix_ls, mix_lr),
    )
    order = (3, 0, 2, 1)
    for line in order:
        mix.begin(line, 0)

    def backward(expert, carry):
        grads = outer_cols(flat(slot_cot, expert), w_out[expert])
        slopes[expert, :, :FF] = (grads * to_f32(slopes[expert, :, :FF])).astype(jnp.bfloat16)
        slopes[expert, :, FF:] = (grads * to_f32(slopes[expert, :, FF:])).astype(jnp.bfloat16)
        slot_out[expert] = outer_cols(slopes[expert], w_in[expert]).astype(jnp.bfloat16)
        return carry

    lax.fori_loop(0, local_experts, backward, 0)

    def combine_back(block, carry):
        left = jnp.concatenate([pick[block], logit_grads[block]], 0)
        right = jnp.concatenate([block_rows(slot_out, block), router, router], 0)
        cot[block] = inner_rows(left, right).astype(jnp.bfloat16)
        return carry

    lax.fori_loop(0, groups, combine_back, 0)
    moe_parts = moe_xs.shape[1]
    part_rows = token_rows // moe_parts

    def piece(ref, part):
        return ref.at[pl.ds(part * part_rows, part_rows)]

    back_sum = ExpScatter(
        place,
        lambda line, part: piece(cot.at[line * 2 + 1 - place.x], part),
        lambda line, part: piece(cot.at[line * 2 + place.x], part),
        lambda line, part: piece(moe_crossed.at[line], part),
        lambda line, part: piece(moe_raised.at[raised_slot(line)], part),
        lambda line, part: piece(moe_lowered.at[lowered_slot(line)], part),
        moe_parts,
        (moe_xs, moe_xr, moe_ls, moe_lr),
    )
    for pair in ((3, 0), (2, 1)):
        for part in range(moe_parts):
            for line in pair:
                back_sum.begin(line, part)

    for to in (place.core, place.side):
        pl.semaphore_signal(free_sem, inc=1, device_id=to, device_id_type=MESH)

    early = in_first.shape[0]
    in_rows, down_rows = in_first.shape[1], down_first.shape[1]
    into = CtxScatter(
        place,
        lambda y, part: w_in.at[part, pl.ds((2 * y + 1 - place.half) * in_rows, in_rows)],
        lambda y, part: w_in.at[part, pl.ds((2 * y + place.half) * in_rows, in_rows)],
        lambda lane, part: slot_out.at[part, pl.ds(lane * in_rows, in_rows)],
        lambda part: slot_out.at[early + part, pl.ds(2 * down_rows, in_rows)],
        early,
        in_send,
        in_recv,
    )
    downs = CtxScatter(
        place,
        lambda y, part: w_out.at[part, pl.ds((2 * y + 1 - place.half) * down_rows, down_rows)],
        lambda y, part: w_out.at[part, pl.ds((2 * y + place.half) * down_rows, down_rows)],
        lambda lane, part: slot_out.at[early + part, pl.ds(lane * down_rows, down_rows)],
        lambda part: slot_out.at[early + part, pl.ds(2 * down_rows + in_rows, down_rows)],
        early,
        down_send,
        down_recv,
    )
    rest_store.wait()
    pl.semaphore_wait(free_sem, 2)
    stores = []

    def store(source, target, sem):
        copy = pltpu.make_async_copy(source, target, sem)
        copy.start()
        stores.append(copy)

    folds = [(pair, part) for pair in ((3, 0), (2, 1)) for part in range(moe_parts)]

    def fold_next():
        if folds:
            pair, part = folds.pop(0)
            for line in pair:
                back_sum.fold(line, part)

    for expert in range(local_experts):
        w_out[expert] = inner_rows(hidden[expert], flat(slot_cot, expert)).astype(jnp.bfloat16)
        if expert < early:
            downs.swap(False, expert).start()
            downs.swap(True, expert).start()
        else:
            store(w_out.at[expert], down_rest.at[expert - early], store_sem.at[0, expert])
        fold_next()
        w_in[expert] = inner_rows(flat(slot_rows, expert), slopes[expert]).astype(jnp.bfloat16)
        if expert < early:
            into.swap(False, expert).start()
            into.swap(True, expert).start()
        else:
            store(w_in.at[expert], in_rest.at[expert - early], store_sem.at[1, expert])
        if expert == 0:
            for line in order:
                mix.fold(line, 0)
        if expert > 0 and expert <= early:
            downs.fold(expert - 1)
            into.fold(expert - 1)
        fold_next()
    while folds:
        fold_next()
    for part in range(moe_parts):
        grad_moe_in[pl.ds(part * part_rows, part_rows), :] = back_sum.total(part)
    mixed_first[...] = (resid_rows[...] + mix.total(0)).astype(jnp.bfloat16)
    for part in range(early):
        for copy in stores:
            copy.wait()
        stores.clear()
        in_stage[...] = into.total(part)
        store(in_stage, in_first.at[part], store_sem.at[1, part])
        down_stage[...] = downs.total(part)
        store(down_stage, down_first.at[part], store_sem.at[0, part])
    for copy in stores:
        copy.wait()
    for scatter in (mix, back_sum, into, downs):
        scatter.finish()


MIX_FIRST = 64
EARLY = 2
MOE_PARTS = 4


def experts(all_moe, all_cot, all_routes, all_in, all_out, side_rows, resid):
    groups, token_rows, width = all_moe.shape
    local_experts, in_cols = all_in.shape[0], all_in.shape[2]
    shards = lax.axis_size("ctx")
    in_rows, down_rows = width // shards, FF // shards
    slots = -(-CAP // 16) * 16
    low, f32 = jnp.bfloat16, jnp.float32

    def shape(dims, dtype):
        return jax.ShapeDtypeStruct(dims, dtype)

    whole, anywhere = pl.BlockSpec(memory_space=VMEM), pl.BlockSpec(memory_space=pl.ANY)
    rest, rest_rows = local_experts - EARLY, token_rows - MIX_FIRST
    slot_block = (local_experts, groups, slots)
    block, steps = (LINES, token_rows, width), (LINES - 1, token_rows, width)
    short, short_steps = (LINES, MIX_FIRST, width), (LINES - 1, MIX_FIRST, width)
    return pl.pallas_call(
        experts_kernel,
        name="experts",
        out_shape=[
            shape((token_rows, width), f32),
            shape((MIX_FIRST, width), low),
            shape((groups, rest_rows, width), low),
            shape((EXPERTS, width), f32),
            shape((EARLY, in_rows, in_cols), f32),
            shape((EARLY, down_rows, width), f32),
            shape((rest, width, in_cols), low),
            shape((rest, FF, width), low),
        ],
        in_specs=[anywhere] * 2
        + [whole]
        + [anywhere] * 2
        + [whole, anywhere],
        out_specs=[whole] * 2 + [anywhere] + [whole] + [anywhere] * 4,
        scratch_shapes=[
            VMEM(all_moe.shape, low),
            VMEM(all_moe.shape, low),
            VMEM(all_in.shape, low),
            VMEM(all_out.shape, low),
            VMEM(slot_block + (width,), low),
            VMEM(slot_block + (width,), low),
            VMEM((local_experts, groups * slots, FF), low),
            VMEM((local_experts, groups * slots, 2 * FF), low),
            VMEM((local_experts, groups * slots, width), low),
            VMEM((groups, local_experts * slots, token_rows), low),
            VMEM((groups, slots, 128), f32),
            VMEM((groups, slots, 128), f32),
            VMEM((groups, EXPERTS, token_rows), f32),
            VMEM((groups, 2 * EXPERTS, token_rows), low),
            VMEM((2 * EXPERTS, width), f32),
            VMEM(block, low),
            VMEM(steps, low),
            VMEM(steps, low),
            VMEM(short, low),
            VMEM(short_steps, low),
            VMEM(short_steps, low),
            VMEM((in_rows, in_cols), f32),
            VMEM((down_rows, width), f32),
            VMEM((MIX_FIRST, width), f32),
            DMA((3 + 2 * local_experts,)),
            DMA((2, local_experts)),
            pltpu.SemaphoreType.REGULAR,
            *scatter_sems(MOE_PARTS),
            *scatter_sems(1),
            *square_sems(EARLY),
            *square_sems(EARLY),
        ],
        compiler_params=pltpu.CompilerParams(
            collective_id=1, has_side_effects=True, vmem_limit_bytes=62 * 2**20
        ),
    )(all_moe, all_cot, all_routes, all_in, all_out, side_rows, resid)


def back_kernel(
    moe_in_grads,
    mixed_part,
    grad_in,
    grad_down,
    tokens,
    cot,
    resid,
    gain_two,
    gain_one,
    router_sum,
    all_tokens,
    weights,
    out_rows,
    qkv,
    heads_out,
    log_norm,
    seg_col,
    seg_row,
    mixed_out,
    grad_tokens,
    query_sum,
    key_sum,
    value_sum,
    side_sum,
    output_sum,
    in_sum,
    down_sum,
    mix_mine,
    mix_crossed,
    mix_raised,
    mix_lowered,
    in_mine,
    in_swapped,
    in_crossed,
    down_mine,
    down_swapped,
    down_crossed,
    grad_resid,
    all_resid,
    head_grads,
    turned,
    key_grads,
    value_grads,
    qkv_grads,
    normed_part,
    normed_swapped,
    normed_crossed,
    sums,
    sums_crossed,
    sums_raised,
    sums_lowered,
    sums_own,
    sums_all,
    out_grads,
    out_crossed,
    out_raised,
    out_lowered,
    in_stage,
    down_stage,
    store_sem,
    local_sem,
    mix_xs,
    mix_xr,
    mix_ls,
    mix_lr,
    sum_xs,
    sum_xr,
    sum_ls,
    sum_lr,
    out_xs,
    out_xr,
    out_ls,
    out_lr,
    in_send,
    in_recv,
    down_send,
    down_recv,
    normed_send,
    normed_recv,
    resid_send,
    resid_recv,
    last_send,
    last_recv,
):
    place = Place()
    ctx, exp = place.ctx, place.exp
    token_rows, width = tokens.shape
    shards, groups, rows, pack_cols = weights.shape
    local_experts = grad_in.shape[0]
    q_cols = heads_out.shape[1]
    main_cols = qkv.shape[1]
    k_cols = (main_cols - q_cols) // 2
    factor = 1.0 / math.sqrt(HEAD_SIZE)
    order = (3, 0, 2, 1)

    loads = []

    def load(source, target):
        copy = pltpu.make_async_copy(source, target, local_sem.at[len(loads)])
        copy.start()
        loads.append(copy)

    for y in range(2):
        load(grad_in.at[:, 2 * y + place.half], in_mine.at[y])
        load(grad_down.at[:, 2 * y + place.half], down_mine.at[y])
    for line in order:
        load(mixed_part.at[line * 2 + place.x], mix_mine.at[line])
    place.greet()

    def piece(ref, count, part):
        size = ref.shape[0] // count
        return ref.at[pl.ds(part * size, size)]

    moe_parts, mix_parts = 4, mix_xs.shape[1]
    mix = ExpScatter(
        place,
        lambda line, part: piece(mixed_part.at[line * 2 + 1 - place.x], mix_parts, part),
        lambda line, part: piece(mix_mine.at[line], mix_parts, part),
        lambda line, part: piece(mix_crossed.at[line], mix_parts, part),
        lambda line, part: piece(mix_raised.at[raised_slot(line)], mix_parts, part),
        lambda line, part: piece(mix_lowered.at[lowered_slot(line)], mix_parts, part),
        mix_parts,
        (mix_xs, mix_xr, mix_ls, mix_lr),
    )
    into = CtxScatter(
        place,
        lambda y, part: grad_in.at[part, 2 * y + 1 - place.half],
        lambda y, part: in_mine.at[y, part],
        lambda lane, part: in_swapped.at[lane, part],
        lambda part: in_crossed.at[part],
        local_experts,
        in_send,
        in_recv,
    )
    downs = CtxScatter(
        place,
        lambda y, part: grad_down.at[part, 2 * y + 1 - place.half],
        lambda y, part: down_mine.at[y, part],
        lambda lane, part: down_swapped.at[lane, part],
        lambda part: down_crossed.at[part],
        local_experts,
        down_send,
        down_recv,
    )
    for near in (False, True):
        for part in range(local_experts):
            into.swap(near, part).start()
        for part in range(local_experts):
            downs.swap(near, part).start()
    gain_one_row, gain_two_row = gain_one[...], gain_two[...]
    moe_rows = token_rows // moe_parts
    gain_two_sum = jnp.zeros((1, width), jnp.float32)
    resid_gather = CtxGather(
        place,
        lambda index, part: all_resid.at[index, pl.ds(part * moe_rows, moe_rows)],
        moe_parts,
        resid_send,
        resid_recv,
    )
    for part in range(moe_parts):
        here = pl.ds(part * moe_rows, moe_rows)
        grad_moe_in = moe_in_grads[here, :]
        values = resid[here, :]
        scale = rms_scale(values)
        weighted = grad_moe_in * gain_two_row
        gain_two_sum = gain_two_sum + jnp.sum(grad_moe_in * values * scale, 0, keepdims=True)
        grads = (
            to_f32(cot[here, :])
            + scale * weighted
            - values * (scale * scale * scale) * jnp.mean(weighted * values, -1, keepdims=True)
        )
        grad_resid[here, :] = grads
        all_resid[ctx, here, :] = grads.astype(jnp.bfloat16)
        resid_gather.begin(part)
    for first, second in ((3, 0), (2, 1)):
        for part in range(mix_parts):
            mix.begin(first, part)
            mix.begin(second, part)
    for copy in loads:
        copy.wait()

    full = weights[...].reshape(width, pack_cols)
    full_out = out_rows[...].reshape(q_cols, width)
    low = lax.broadcasted_iota(jnp.int32, (1, 2 * HEAD_SIZE), 1) < HEAD_SIZE

    def spread(first):
        plain = to_f32(qkv[:, first : first + k_cols])
        other = pltpu.roll(plain, HEAD_SIZE, 1)
        zero = jnp.zeros((), jnp.float32)
        return [
            [
                jnp.where(low, plain, zero).astype(jnp.bfloat16),
                jnp.where(low, zero, other).astype(jnp.bfloat16),
            ],
            [
                jnp.where(low, other, zero).astype(jnp.bfloat16),
                jnp.where(low, zero, plain).astype(jnp.bfloat16),
            ],
        ]

    keys, values = spread(q_cols), spread(q_cols + k_cols)
    norm_rows = log_norm[...].T
    for part in range(moe_parts):
        resid_gather.relay(part)
    for part in range(moe_parts):
        resid_gather.arrived(part)
    for part in range(local_experts):
        into.fold(part)
        downs.fold(part)
    at_lane = lax.broadcasted_iota(jnp.int32, (1, 128), 1)
    for block in range(shards):
        here = pl.ds(block * token_rows, token_rows)
        grads = outer_cols(all_resid[block], full_out).astype(jnp.bfloat16)
        head_grads[here, :] = grads
        products = to_f32(grads) * heads_out[here, :]
        deltas = jnp.zeros((token_rows, 128), jnp.float32)
        for pair in range(2):
            both = products[:, pair * 128 : pair * 128 + 128]
            first = jnp.sum(jnp.where(low, both, 0.0), -1, keepdims=True)
            second = jnp.sum(jnp.where(low, 0.0, both), -1, keepdims=True)
            deltas = jnp.where(at_lane == 2 * pair, first, deltas)
            deltas = jnp.where(at_lane == 2 * pair + 1, second, deltas)
        turned[:, here] = deltas.T
    attn_low = heads_out[...].astype(jnp.bfloat16)
    flat_resid = all_resid[...].reshape(shards * token_rows, width)
    out_grads[...] = (
        inner_rows(attn_low, flat_resid).astype(jnp.bfloat16).reshape(groups, rows, width)
    )
    out_scatter = ExpScatter(
        place,
        lambda line, part: out_grads.at[line * 2 + 1 - place.x],
        lambda line, part: out_grads.at[line * 2 + place.x],
        lambda line, part: out_crossed.at[line],
        lambda line, part: out_raised.at[raised_slot(line)],
        lambda line, part: out_lowered.at[lowered_slot(line)],
        1,
        (out_xs, out_xr, out_ls, out_lr),
    )
    for line in order:
        out_scatter.begin(line, 0)
    key_grads[...] = jnp.zeros_like(key_grads)
    value_grads[...] = jnp.zeros_like(value_grads)
    for block in range(shards):
        here = pl.ds(block * token_rows, token_rows)
        count = (block + 1) * token_rows
        at_col = block * token_rows + lax.broadcasted_iota(jnp.int32, (1, token_rows), 1)
        at_row = lax.broadcasted_iota(jnp.int32, (count, 1), 0)
        bias = jnp.where(
            (at_row <= at_col) & (seg_col[:count, :] == seg_row[:, here]), 0.0, MASK_FILLER
        )
        for pair in range(2):
            lanes = slice(pair * 128, pair * 128 + 128)
            queries = qkv[here, lanes]
            grads = head_grads[here, lanes]
            query_grad = jnp.zeros((token_rows, 128), jnp.float32)
            for head in range(2):
                row = 2 * pair + head
                mine = low if head == 0 else jnp.logical_not(low)
                own_queries = jnp.where(mine, queries, jnp.zeros((), jnp.bfloat16))
                own_grads = jnp.where(mine, grads, jnp.zeros((), jnp.bfloat16))
                key, value = keys[pair][head][:count], values[pair][head][:count]
                scores = outer_cols(key, queries) * factor + bias
                probs = jnp.exp(scores - norm_rows[row : row + 1, block * token_rows : count])
                grad_probs = outer_cols(value, grads)
                grad_scores = (probs * (grad_probs - turned[row : row + 1, here])).astype(
                    jnp.bfloat16
                )
                value_grads[pair, :count, :] += dot_rows(probs.astype(jnp.bfloat16), own_grads)
                key_grads[pair, :count, :] += dot_rows(grad_scores, own_queries)
                query_grad = query_grad + inner_rows(grad_scores, key)
            qkv_grads[here, lanes] = (query_grad * factor).astype(jnp.bfloat16)
        if block == 0:
            for line in order:
                out_scatter.fold(line, 0)
        if block == 1:
            for part in range(mix_parts):
                mix.fold(3, part)
                mix.fold(0, part)
        if block == 2:
            for part in range(mix_parts):
                mix.fold(2, part)
                mix.fold(1, part)

    def fold_heads(first, second):
        return jnp.where(
            low,
            first + pltpu.roll(first, HEAD_SIZE, 1),
            second + pltpu.roll(second, HEAD_SIZE, 1),
        )

    qkv_grads[:, q_cols : q_cols + k_cols] = (
        fold_heads(key_grads[0], key_grads[1]) * factor
    ).astype(jnp.bfloat16)
    qkv_grads[:, q_cols + k_cols :] = fold_heads(value_grads[0], value_grads[1]).astype(
        jnp.bfloat16
    )

    normed_scatter = CtxScatter(
        place,
        lambda y, part: normed_part.at[2 * y + 1 - place.half],
        lambda y, part: normed_part.at[2 * y + place.half],
        lambda lane, part: normed_swapped.at[lane],
        lambda part: normed_crossed,
        1,
        normed_send,
        normed_recv,
    )
    gain_one_sum = jnp.zeros((1, width), jnp.float32)
    main_sum = jnp.zeros((width, main_cols), jnp.float32)
    for block in range(shards):
        here = pl.ds(block * token_rows, token_rows)
        grads = outer_cols(qkv_grads[here, :], full[:, :main_cols])
        normed_part[block] = grads.astype(jnp.bfloat16)
        own = to_f32(all_tokens[block])
        scaled = own * rms_scale(own)
        gain_one_sum = gain_one_sum + jnp.sum(grads * scaled, 0, keepdims=True)
        normed = (scaled * gain_one_row).astype(jnp.bfloat16)
        main_sum = main_sum + inner_rows(normed, qkv_grads[here, :])
    normed_scatter.swap(False, 0).start()
    normed_scatter.swap(True, 0).start()
    at_sub = lax.broadcasted_iota(jnp.int32, (128, 1), 0)
    gain_rows = jnp.where(
        at_sub == EXPERTS, gain_one_sum, jnp.where(at_sub == EXPERTS + 1, gain_two_sum, 0.0)
    )
    side = jnp.concatenate([router_sum[...], gain_rows[EXPERTS:, :]], 0).T
    sums[:, :, :, :main_cols] = main_sum.astype(jnp.bfloat16).reshape(
        shards, groups, rows, main_cols
    )
    sums[:, :, :, main_cols:] = side.astype(jnp.bfloat16).reshape(
        shards, groups, rows, pack_cols - main_cols
    )
    sum_scatter = ExpScatter(
        place,
        lambda line, part: sums.at[:, line * 2 + 1 - place.x],
        lambda line, part: sums.at[:, line * 2 + place.x],
        lambda line, part: sums_crossed.at[line],
        lambda line, part: sums_raised.at[raised_slot(line)],
        lambda line, part: sums_lowered.at[lowered_slot(line)],
        1,
        (sum_xs, sum_xr, sum_ls, sum_lr),
    )
    for line in order:
        sum_scatter.begin(line, 0)
    normed_scatter.fold(0)
    size = mixed_out.shape[0] // mix_parts
    for part in range(mix_parts):
        mixed_out[pl.ds(part * size, size), :] = (
            resid[pl.ds(token_rows - (mix_parts - part) * size, size), :] + mix.total(part)
        ).astype(jnp.bfloat16)
    output_sum[...] = out_scatter.total(0)
    for line in order:
        sum_scatter.fold(line, 0)
    stores = []
    for part in range(local_experts):
        slot = part % 2
        if part >= 2:
            for copy in stores[2 * (part - 2) : 2 * (part - 1)]:
                copy.wait()
        in_stage[slot] = into.total(part)
        down_stage[slot] = downs.total(part)
        for kind, (source, target) in enumerate(
            ((in_stage.at[slot], in_sum.at[part]), (down_stage.at[slot], down_sum.at[part]))
        ):
            copy = pltpu.make_async_copy(source, target, store_sem.at[kind, part])
            copy.start()
            stores.append(copy)
    sums_own[...] = sum_scatter.total(0).astype(jnp.bfloat16)
    sums_all[ctx] = sums_own[ctx]
    copies = []
    for lane, to in enumerate((place.core, place.side, place.far)):
        copy = remote(
            sums_own.at[to[0]], sums_all.at[ctx], last_send.at[lane], last_recv.at[lane], to
        )
        copy.start()
        copies.append(copy)
    grad_normed = normed_scatter.total(0)
    own = to_f32(tokens[...])
    scale = rms_scale(own)
    weighted = grad_normed * gain_one_row
    grad_tokens[...] = (
        grad_resid[...]
        + scale * weighted
        - own * (scale * scale * scale) * jnp.mean(weighted * own, -1, keepdims=True)
    )
    for lane, to in enumerate((place.core, place.side, place.far)):
        remote(
            sums_own.at[0], sums_all.at[to[0]], last_send.at[lane], last_recv.at[lane], to
        ).wait_recv()
    side = jnp.zeros((rows, pack_cols - main_cols), jnp.float32)
    for shard in range(shards):
        came = to_f32(sums_all[shard])
        query_sum[:, shard * q_cols : (shard + 1) * q_cols] = came[:, :q_cols]
        key_sum[:, shard * k_cols : (shard + 1) * k_cols] = came[:, q_cols : q_cols + k_cols]
        value_sum[:, shard * k_cols : (shard + 1) * k_cols] = came[:, q_cols + k_cols : main_cols]
        side = side + came[:, main_cols:]
    side_sum[...] = side
    for copy in stores[-4:]:
        copy.wait()
    for copy in copies:
        copy.wait_send()
    for scatter in (mix, into, downs, out_scatter, normed_scatter, sum_scatter):
        scatter.finish()
    for part in range(moe_parts):
        resid_gather.sent(part)


def back(
    moe_in_grads, mixed_part, grad_in, grad_down, tokens, cot, resid, gain_two, gain_one, router_sum,
    all_tokens, weights, out_rows, qkv, heads_out, log_norm, seg_col, seg_row,
):
    token_rows, width = tokens.shape
    shards, groups, rows, pack_cols = weights.shape
    seq_len = shards * token_rows
    q_cols, main_cols = heads_out.shape[1], qkv.shape[1]
    k_cols = (main_cols - q_cols) // 2
    experts, _, in_rows, in_cols = grad_in.shape
    down_rows = grad_down.shape[2]
    low, f32 = jnp.bfloat16, jnp.float32

    def shape(dims, dtype):
        return jax.ShapeDtypeStruct(dims, dtype)

    whole, anywhere = pl.BlockSpec(memory_space=VMEM), pl.BlockSpec(memory_space=pl.ANY)
    mix_rows = mixed_part.shape[1]
    block, steps = (LINES, mix_rows, width), (LINES - 1, mix_rows, width)
    pack = (shards, rows, pack_cols)
    return pl.pallas_call(
        back_kernel,
        name="back",
        out_shape=[
            shape((mixed_part.shape[1], width), low),
            shape((token_rows, width), f32),
            shape((rows, shards * q_cols), f32),
            shape((rows, shards * k_cols), f32),
            shape((rows, shards * k_cols), f32),
            shape((rows, pack_cols - main_cols), f32),
            shape((rows, width), f32),
            shape((experts, in_rows, in_cols), f32),
            shape((experts, down_rows, width), f32),
        ],
        in_specs=[whole] + [anywhere] * 3 + [whole] * 14,
        out_specs=[whole] * 7 + [anywhere] * 2,
        scratch_shapes=[
            VMEM(block, low),
            VMEM(block, low),
            VMEM(steps, low),
            VMEM(steps, low),
            VMEM((2, experts, in_rows, in_cols), low),
            VMEM((2, experts, in_rows, in_cols), low),
            VMEM((experts, in_rows, in_cols), low),
            VMEM((2, experts, down_rows, width), low),
            VMEM((2, experts, down_rows, width), low),
            VMEM((experts, down_rows, width), low),
            VMEM((token_rows, width), f32),
            VMEM((shards, token_rows, width), low),
            VMEM((seq_len, q_cols), low),
            VMEM((128, seq_len), f32),
            VMEM((2, seq_len, 128), f32),
            VMEM((2, seq_len, 128), f32),
            VMEM((seq_len, main_cols), low),
            VMEM((shards, token_rows, width), low),
            VMEM((2, token_rows, width), low),
            VMEM((token_rows, width), low),
            VMEM((shards, groups, rows, pack_cols), low),
            VMEM((LINES,) + pack, low),
            *[VMEM((LINES - 1,) + pack, low)] * 2,
            VMEM((shards, rows, pack_cols), low),
            VMEM((shards, rows, pack_cols), low),
            VMEM((groups, rows, width), low),
            VMEM((LINES, rows, width), low),
            *[VMEM((LINES - 1, rows, width), low)] * 2,
            VMEM((2, in_rows, in_cols), f32),
            VMEM((2, down_rows, width), f32),
            DMA((2, experts)),
            DMA((8,)),
            *scatter_sems(3),
            *scatter_sems(1),
            *scatter_sems(1),
            *square_sems(experts),
            *square_sems(experts),
            *square_sems(1),
            *square_sems(4),
            DMA((3,)),
            DMA((3,)),
        ],
        compiler_params=pltpu.CompilerParams(
            collective_id=2, has_side_effects=True, vmem_limit_bytes=62 * 2**20
        ),
    )(
        moe_in_grads, mixed_part, grad_in, grad_down, tokens, cot, resid, gain_two, gain_one, router_sum,
        all_tokens, weights, out_rows, qkv, heads_out, log_norm, seg_col, seg_row,
    )


def two_parts(values):
    high = values.astype(jnp.bfloat16)
    return high, (values - high.astype(jnp.float32)).astype(jnp.bfloat16)


def by_heads(
    tokens,
    segments,
    routes,
    gain_attn,
    gain_moe,
    query_weight,
    key_weight,
    value_weight,
    w_output,
    w_router,
    w_expert_in,
    w_expert_out,
    cotangent,
):
    shards = lax.axis_size("ctx")
    groups = lax.axis_size("exp")
    local_experts = EXPERTS // groups
    width = tokens.shape[2]
    rows = query_weight.shape[0]
    q_cols = query_weight.shape[1] // shards
    k_cols = key_weight.shape[1] // shards
    main_cols = q_cols + 2 * k_cols
    side = 128

    side_cols = jnp.concatenate(
        [
            w_router,
            gain_attn[:, None],
            gain_moe[:, None],
            jnp.zeros((rows, side - EXPERTS - 2), jnp.bfloat16),
        ],
        1,
    )
    seg_col, seg_row = segments[0][:, None], segments
    (
        all_moe,
        all_cot,
        all_routes,
        all_in,
        all_out,
        all_tokens,
        all_weights,
        out_rows,
        qkv,
        heads_out,
        log_norm,
        resid,
        side_rows,
    ) = front(
        tokens[0],
        side_cols,
        query_weight,
        key_weight,
        value_weight,
        w_output,
        routes[0].T,
        seg_col,
        seg_row,
        cotangent[0],
        w_expert_in,
        w_expert_out,
    )
    expert_in = all_in.reshape(local_experts, width, -1)
    expert_out = all_out.reshape(local_experts, FF, -1)
    gains = side_rows[EXPERTS : EXPERTS + 2].astype(jnp.float32)
    (
        grad_moe_in,
        mixed_first,
        mixed_rest,
        router_sum,
        in_first,
        down_first,
        in_rest,
        down_rest,
    ) = experts(all_moe, all_cot, all_routes, expert_in, expert_out, side_rows, resid)
    rest = in_rest.shape[0]
    (
        mixed_last,
        grad_tokens,
        query_sum,
        key_sum,
        value_sum,
        side_sum,
        output_sum,
        in_sum,
        down_sum,
    ) = back(
        grad_moe_in,
        mixed_rest,
        in_rest.reshape((rest,) + all_in.shape[1:]),
        down_rest.reshape((rest,) + all_out.shape[1:]),
        tokens[0],
        cotangent[0],
        resid,
        gains[1:2],
        gains[0:1],
        router_sum,
        all_tokens,
        all_weights,
        out_rows,
        qkv,
        heads_out,
        log_norm,
        seg_col,
        seg_row,
    )
    return (
        jnp.concatenate([mixed_first, mixed_last], 0)[None],
        grad_tokens[None],
        side_sum[:, EXPERTS],
        side_sum[:, EXPERTS + 1],
        query_sum,
        key_sum,
        value_sum,
        output_sum,
        side_sum[:, :EXPERTS],
        jnp.concatenate([in_first, in_sum], 0),
        jnp.concatenate([down_first, down_sum], 0),
    )


def solution(mesh):
    sizes = (mesh.shape["ctx"], mesh.shape["exp"])
    return jax.shard_map(
        by_heads if sizes == (4, 8) else local,
        mesh=mesh,
        in_specs=(
            P("exp", "ctx", None),
            P("exp", None),
            P("exp", "ctx", None),
            P(("ctx", "exp")),
            P(("ctx", "exp")),
            P(("ctx", "exp"), None),
            P(("ctx", "exp"), None),
            P(("ctx", "exp"), None),
            P(("ctx", "exp"), None),
            P(("ctx", "exp"), None),
            P("exp", "ctx", None),
            P("exp", "ctx", None),
            P("exp", "ctx", None),
        ),
        out_specs=(
            P("exp", "ctx", None),
            P("exp", "ctx", None),
            P(("ctx", "exp")),
            P(("ctx", "exp")),
            P(("ctx", "exp"), None),
            P(("ctx", "exp"), None),
            P(("ctx", "exp"), None),
            P(("ctx", "exp"), None),
            P(("ctx", "exp"), None),
            P("exp", "ctx", None),
            P("exp", "ctx", None),
        ),
        check_vma=False,
    )
```

```python
import math

import jax
import jax.numpy as jnp
from jax import lax
from jax.experimental import pallas as pl
from jax.experimental.pallas import tpu as pltpu
from jax.sharding import PartitionSpec as P

QUERY_HEADS = 16
KEY_VALUE_HEADS = 8
HEAD_SIZE = 64
EXPERTS = 32
TOPK = 8
FF = 512
CAP = 72


EPSILON = 1e-06
MASK_FILLER = -1e30


def rms_scale(values):
    return lax.rsqrt(jnp.mean(values * values, -1, keepdims=True) + EPSILON)


def inner_rows(left, right):
    return lax.dot_general(
        left, right, (((0,), (0,)), ((), ())), preferred_element_type=jnp.float32
    )


def outer_cols(left, right):
    return lax.dot_general(
        left, right, (((1,), (1,)), ((), ())), preferred_element_type=jnp.float32
    )


def allowed_block(query_pos, query_seg, seg_all, offset, key_total_count):
    key_pos = offset + jnp.arange(key_total_count, dtype=jnp.int32)
    key_seg = lax.dynamic_slice_in_dim(seg_all, offset, key_total_count)
    return (key_pos[None, :] <= query_pos[:, None]) & (key_seg[None, :] == query_seg[:, None])


def head_scores(heads_of_queries, key_segment_slice, factor):
    key_total_count = key_segment_slice.shape[0]
    heads_of_keys = key_segment_slice.reshape(key_total_count, KEY_VALUE_HEADS, -1)
    return (
        jnp.einsum(
            "ihgd,jhd->hgij", heads_of_queries, heads_of_keys, preferred_element_type=jnp.float32
        )
        * factor
    )


def slot_tables(pair_ids):
    pair_count = pair_ids.shape[0]
    member = (pair_ids[:, None] == jnp.arange(EXPERTS, dtype=jnp.int32)[None, :]).astype(jnp.int32)
    earlier = jnp.cumsum(member, 0) - member
    slot_place = jnp.sum(earlier * member, 1, dtype=jnp.int32)
    is_kept = slot_place < CAP
    slot_index = jnp.where(is_kept, pair_ids * CAP + slot_place, EXPERTS * CAP)
    slot_filler = (
        jnp.full((EXPERTS * CAP,), -1, jnp.int32)
        .at[slot_index]
        .set(jnp.arange(pair_count, dtype=jnp.int32), mode="drop")
    )
    return (slot_index, is_kept, slot_filler)


def local(
    tokens,
    segments,
    routes,
    gain_attn,
    gain_moe,
    query_weight,
    key_weight,
    value_weight,
    w_output,
    w_router,
    w_expert_in,
    w_expert_out,
    cotangent,
):
    shards = lax.axis_size("ctx")
    groups = lax.axis_size("exp")
    ctx_rank = lax.axis_index("ctx")
    gain_one, gain_two, full_query, full_key, full_value, full_output, full_router = (
        lax.all_gather(gain_attn, ("ctx", "exp"), axis=0, tiled=True),
        lax.all_gather(gain_moe, ("ctx", "exp"), axis=0, tiled=True),
        lax.all_gather(query_weight, ("ctx", "exp"), axis=0, tiled=True),
        lax.all_gather(key_weight, ("ctx", "exp"), axis=0, tiled=True),
        lax.all_gather(value_weight, ("ctx", "exp"), axis=0, tiled=True),
        lax.all_gather(w_output, ("ctx", "exp"), axis=0, tiled=True),
        lax.all_gather(w_router, ("ctx", "exp"), axis=0, tiled=True),
    )
    expert_in, expert_out = (
        lax.all_gather(w_expert_in, "ctx", axis=1, tiled=True),
        lax.all_gather(w_expert_out, "ctx", axis=1, tiled=True),
    )
    inputs = tokens[0].astype(jnp.float32)
    token_rows = inputs.shape[0]
    seq_len = token_rows * shards
    head_cluster = QUERY_HEADS // KEY_VALUE_HEADS
    factor = 1.0 / math.sqrt(HEAD_SIZE)
    kv_width = key_weight.shape[1]
    seg_all = segments[0]
    query_pos = ctx_rank * token_rows + jnp.arange(token_rows, dtype=jnp.int32)
    query_seg = lax.dynamic_slice_in_dim(seg_all, ctx_rank * token_rows, token_rows)
    scale_one = rms_scale(inputs)
    gain_one_f = gain_one.astype(jnp.float32)
    normalized_input = (inputs * scale_one * gain_one_f).astype(jnp.bfloat16)
    query_matrix = jnp.dot(normalized_input, full_query, preferred_element_type=jnp.float32).astype(
        jnp.bfloat16
    )
    key_rows = jnp.dot(normalized_input, full_key, preferred_element_type=jnp.float32).astype(
        jnp.bfloat16
    )
    value_rows = jnp.dot(normalized_input, full_value, preferred_element_type=jnp.float32).astype(
        jnp.bfloat16
    )
    heads_of_queries = query_matrix.reshape(token_rows, KEY_VALUE_HEADS, head_cluster, HEAD_SIZE)
    group_size = math.gcd(shards, max(1, 1024 // token_rows))
    key_range_width = group_size * token_rows
    turns_needed = ctx_rank // group_size + 1
    running_maximum = jnp.full(
        (KEY_VALUE_HEADS, head_cluster, token_rows), MASK_FILLER, jnp.float32
    )
    key_segment_slice = lax.all_gather(key_rows, "ctx", axis=0, tiled=True)
    value_segment_slice = lax.all_gather(value_rows, "ctx", axis=0, tiled=True)
    key_total_count = key_segment_slice.shape[0]
    scores = head_scores(heads_of_queries, key_segment_slice, factor)
    allowed = allowed_block(query_pos, query_seg, seg_all, jnp.int32(0), key_total_count)
    scores = jnp.where(allowed, scores, MASK_FILLER)
    new_max = jnp.maximum(running_maximum, jnp.max(scores, -1))
    weights = jnp.where(allowed, jnp.exp(scores - new_max[..., None]), 0.0)
    run_sum = jnp.sum(weights, -1)
    heads_of_values = value_segment_slice.reshape(key_total_count, KEY_VALUE_HEADS, HEAD_SIZE)
    run_acc = jnp.einsum(
        "hgij,jhd->ihgd",
        weights.astype(jnp.bfloat16),
        heads_of_values,
        preferred_element_type=jnp.float32,
    )
    running_maximum, run_sum, run_acc = (new_max, run_sum, run_acc)
    log_norm = running_maximum + jnp.log(run_sum)
    heads_out = run_acc / jnp.transpose(run_sum, (2, 0, 1))[..., None]
    attn_low = heads_out.reshape(token_rows, -1).astype(jnp.bfloat16)
    resid = inputs + jnp.dot(attn_low, full_output, preferred_element_type=jnp.float32)
    scale_two = rms_scale(resid)
    gain_two_f = gain_two.astype(jnp.float32)
    moe_in = (resid * scale_two * gain_two_f).astype(jnp.bfloat16)
    logits = jnp.dot(moe_in, full_router, preferred_element_type=jnp.float32)
    route_ids = routes[0]
    one_hot = (route_ids[:, :, None] == jnp.arange(EXPERTS, dtype=jnp.int32)[None, None, :]).astype(
        jnp.float32
    )
    chosen = jnp.sum(one_hot * logits[:, None, :], -1)
    gates = jax.nn.softmax(chosen, axis=-1)
    slot_index, is_kept, slot_filler = slot_tables(route_ids.reshape(-1))
    filled = slot_filler >= 0
    token_of = jnp.maximum(slot_filler, 0) // TOPK
    local_experts = EXPERTS // groups
    send_rows = jnp.where(
        filled[:, None], jnp.take(moe_in, token_of, axis=0), jnp.zeros((), jnp.bfloat16)
    )
    send_rows = send_rows.reshape(groups, local_experts, CAP, -1)
    received = lax.all_to_all(send_rows, "exp", split_axis=0, concat_axis=0, tiled=True)
    pre = jnp.einsum("sjcd,jdf->sjcf", received, expert_in, preferred_element_type=jnp.float32)
    gate_part = pre[..., :FF]
    up_part = pre[..., FF:]
    hidden = (jax.nn.silu(gate_part) * up_part).astype(jnp.bfloat16)
    expert_rows = jnp.einsum(
        "sjcf,jfd->sjcd", hidden, expert_out, preferred_element_type=jnp.float32
    ).astype(jnp.bfloat16)
    returned = lax.all_to_all(expert_rows, "exp", split_axis=0, concat_axis=0, tiled=True).reshape(
        EXPERTS * CAP, -1
    )
    safe_slot = jnp.minimum(slot_index, EXPERTS * CAP - 1)
    picked = jnp.where(
        is_kept[:, None], jnp.take(returned, safe_slot, axis=0), jnp.zeros((), jnp.bfloat16)
    )
    picked = picked.astype(jnp.float32).reshape(token_rows, TOPK, -1)
    branch = jnp.sum(gates[:, :, None] * picked, 1)
    mixed_out = (resid + branch).astype(jnp.bfloat16)
    grad_out = cotangent[0].astype(jnp.float32)
    grad_picked = jnp.sum(grad_out[:, None, :] * picked, -1)
    grad_chosen = gates * (grad_picked - jnp.sum(gates * grad_picked, -1, keepdims=True))
    grad_logits = jnp.sum(one_hot * grad_chosen[:, :, None], 1)
    slot_gate = jnp.where(filled, jnp.take(gates.reshape(-1), jnp.maximum(slot_filler, 0)), 0.0)
    grad_send = (slot_gate[:, None] * jnp.take(grad_out, token_of, axis=0)).astype(jnp.bfloat16)
    grad_send = grad_send.reshape(groups, local_experts, CAP, -1)
    grad_rows = lax.all_to_all(grad_send, "exp", split_axis=0, concat_axis=0, tiled=True)
    grad_hidden = jnp.einsum(
        "sjcd,jfd->sjcf", grad_rows, expert_out, preferred_element_type=jnp.float32
    )
    sigmoid_gate = jax.nn.sigmoid(gate_part)
    grad_gate = grad_hidden * up_part * sigmoid_gate * (1.0 + gate_part * (1.0 - sigmoid_gate))
    grad_up = grad_hidden * gate_part * sigmoid_gate
    grad_pre = jnp.concatenate([grad_gate, grad_up], -1).astype(jnp.bfloat16)
    grad_expert_out = jnp.einsum(
        "sjcf,sjcd->jfd", hidden, grad_rows, preferred_element_type=jnp.float32
    )
    grad_expert_in = jnp.einsum(
        "sjcd,sjcf->jdf", received, grad_pre, preferred_element_type=jnp.float32
    )
    grad_received = jnp.einsum(
        "sjcf,jdf->sjcd", grad_pre, expert_in, preferred_element_type=jnp.float32
    ).astype(jnp.bfloat16)
    grad_back = lax.all_to_all(
        grad_received, "exp", split_axis=0, concat_axis=0, tiled=True
    ).reshape(EXPERTS * CAP, -1)
    grad_pairs = jnp.where(
        is_kept[:, None], jnp.take(grad_back, safe_slot, axis=0), jnp.zeros((), jnp.bfloat16)
    )
    grad_pairs = grad_pairs.astype(jnp.float32).reshape(token_rows, TOPK, -1)
    grad_moe_in = (
        jnp.sum(grad_pairs, 1)
        + outer_cols(grad_logits.astype(jnp.bfloat16), full_router) * 0.0
        + lax.dot_general(
            grad_logits,
            full_router.astype(jnp.float32),
            (((1,), (1,)), ((), ())),
            precision=lax.Precision.HIGHEST,
            preferred_element_type=jnp.float32,
        )
    )
    grad_router = lax.dot_general(
        moe_in.astype(jnp.float32),
        grad_logits,
        (((0,), (0,)), ((), ())),
        precision=lax.Precision.HIGHEST,
        preferred_element_type=jnp.float32,
    )
    weighted_two = grad_moe_in * gain_two_f
    grad_gain_two = jnp.sum(grad_moe_in * resid * scale_two, 0)
    cube_two = scale_two * scale_two * scale_two
    grad_resid = (
        grad_out
        + scale_two * weighted_two
        - resid * cube_two * jnp.mean(weighted_two * resid, -1, keepdims=True)
    )
    grad_resid_low = grad_resid.astype(jnp.bfloat16)
    grad_output_w = inner_rows(attn_low, grad_resid_low)
    grad_heads = (
        outer_cols(grad_resid_low, full_output)
        .astype(jnp.bfloat16)
        .reshape(token_rows, KEY_VALUE_HEADS, head_cluster, HEAD_SIZE)
    )
    delta = jnp.transpose(jnp.sum(grad_heads.astype(jnp.float32) * heads_out, -1), (1, 2, 0))
    all_keys, all_values = (
        lax.all_gather(key_rows, "ctx", axis=0, tiled=True),
        lax.all_gather(value_rows, "ctx", axis=0, tiled=True),
    )

    def block_grads(offset):
        key_segment_slice = lax.dynamic_slice_in_dim(all_keys, offset, key_range_width)
        value_segment_slice = lax.dynamic_slice_in_dim(all_values, offset, key_range_width)
        scores = head_scores(heads_of_queries, key_segment_slice, factor)
        allowed = allowed_block(query_pos, query_seg, seg_all, offset, key_range_width)
        probs_full = jnp.where(allowed, jnp.exp(scores - log_norm[..., None]), 0.0)
        heads_of_keys = key_segment_slice.reshape(key_range_width, KEY_VALUE_HEADS, HEAD_SIZE)
        heads_of_values = value_segment_slice.reshape(key_range_width, KEY_VALUE_HEADS, HEAD_SIZE)
        grad_probs = jnp.einsum(
            "ihgd,jhd->hgij", grad_heads, heads_of_values, preferred_element_type=jnp.float32
        )
        grad_scores = (probs_full * (grad_probs - delta[..., None])).astype(jnp.bfloat16)
        query_part = jnp.einsum(
            "hgij,jhd->ihgd", grad_scores, heads_of_keys, preferred_element_type=jnp.float32
        )
        return (probs_full, grad_scores, query_part)

    query_begin_index = jnp.zeros(
        (token_rows, KEY_VALUE_HEADS, head_cluster, HEAD_SIZE), jnp.float32
    )

    def back_turn(turn, running):
        grad_query_acc, key_grad_buf = running
        offset = turn * key_range_width
        probs_full, grad_scores, query_part = block_grads(offset)
        grad_key_part = (
            jnp.einsum(
                "hgij,ihgd->jhd", grad_scores, heads_of_queries, preferred_element_type=jnp.float32
            )
            * factor
        )
        grad_value_part = jnp.einsum(
            "hgij,ihgd->jhd",
            probs_full.astype(jnp.bfloat16),
            grad_heads,
            preferred_element_type=jnp.float32,
        )
        joined = jnp.concatenate(
            [
                grad_key_part.reshape(key_range_width, -1),
                grad_value_part.reshape(key_range_width, -1),
            ],
            1,
        )
        key_grad_buf = lax.dynamic_update_slice_in_dim(key_grad_buf, joined, offset, 0)
        return (grad_query_acc + query_part, key_grad_buf)

    back_start = (query_begin_index, jnp.zeros((seq_len, 2 * kv_width), jnp.float32))
    grad_query_acc, key_grad_buf = lax.fori_loop(0, turns_needed, back_turn, back_start)
    own_grads = lax.psum_scatter(
        key_grad_buf.astype(jnp.bfloat16), "ctx", scatter_dimension=0, tiled=True
    ).astype(jnp.float32)
    grad_keys = own_grads[:, :kv_width].astype(jnp.bfloat16)
    grad_values = own_grads[:, kv_width:].astype(jnp.bfloat16)
    grad_query = (grad_query_acc * factor).reshape(token_rows, -1).astype(jnp.bfloat16)
    grad_query_w = inner_rows(normalized_input, grad_query)
    grad_key_w = inner_rows(normalized_input, grad_keys)
    grad_value_w = inner_rows(normalized_input, grad_values)
    grad_normed = (
        outer_cols(grad_query, full_query)
        + outer_cols(grad_keys, full_key)
        + outer_cols(grad_values, full_value)
    )
    weighted_one = grad_normed * gain_one_f
    grad_gain_one = jnp.sum(grad_normed * inputs * scale_one, 0)
    cube_one = scale_one * scale_one * scale_one
    grad_inputs = (
        grad_resid
        + scale_one * weighted_one
        - inputs * cube_one * jnp.mean(weighted_one * inputs, -1, keepdims=True)
    )
    dense_sums = (
        lax.psum_scatter(grad_gain_one, ("ctx", "exp"), scatter_dimension=0, tiled=True),
        lax.psum_scatter(grad_gain_two, ("ctx", "exp"), scatter_dimension=0, tiled=True),
        lax.psum_scatter(grad_query_w, ("ctx", "exp"), scatter_dimension=0, tiled=True),
        lax.psum_scatter(grad_key_w, ("ctx", "exp"), scatter_dimension=0, tiled=True),
        lax.psum_scatter(grad_value_w, ("ctx", "exp"), scatter_dimension=0, tiled=True),
        lax.psum_scatter(grad_output_w, ("ctx", "exp"), scatter_dimension=0, tiled=True),
        lax.psum_scatter(grad_router, ("ctx", "exp"), scatter_dimension=0, tiled=True),
    )
    expert_sums = (
        lax.psum_scatter(
            grad_expert_in.astype(jnp.bfloat16), "ctx", scatter_dimension=1, tiled=True
        ).astype(jnp.float32),
        lax.psum_scatter(
            grad_expert_out.astype(jnp.bfloat16), "ctx", scatter_dimension=1, tiled=True
        ).astype(jnp.float32),
    )
    return (mixed_out[None], grad_inputs[None]) + tuple(dense_sums) + tuple(expert_sums)


MESH = pl.DeviceIdType.MESH
VMEM = pltpu.VMEM
DMA = pltpu.SemaphoreType.DMA
COT_FIRST = 96
LINES = 4
GRANT = 56 * 2**20


def to_f32(value):
    return value.astype(jnp.float32)


def dot_rows(left, right):
    return jnp.dot(left, right, preferred_element_type=jnp.float32)


def remote(source, target, send, recv, to):
    return pltpu.make_async_remote_copy(
        src_ref=source,
        dst_ref=target,
        send_sem=send,
        recv_sem=recv,
        device_id=to,
        device_id_type=MESH,
    )


class Place:
    def __init__(self):
        ctx, exp = lax.axis_index("ctx"), lax.axis_index("exp")
        self.ctx, self.exp = ctx, exp
        self.y, self.half = ctx // 2, ctx % 2
        self.z, self.x = exp // 2, exp % 2
        other_half = ctx + 1 - 2 * (ctx % 2)
        self.up, self.down = (ctx, exp + 2), (ctx, exp - 2)
        self.across = (ctx, exp + 1 - 2 * (exp % 2))
        self.core = (other_half, exp)
        self.side = (lax.rem(ctx + 2, 4), exp)
        self.far = (lax.rem(other_half + 2, 4), exp)

    def greet(self, lines=True, square=True):
        barrier = pltpu.get_barrier_semaphore()
        count = jnp.int32(0)
        if square:
            for to in (self.core, self.side, self.far):
                pl.semaphore_signal(barrier, inc=1, device_id=to, device_id_type=MESH)
            count = count + 3
        if lines:
            pl.semaphore_signal(barrier, inc=1, device_id=self.across, device_id_type=MESH)

            @pl.when(self.z < LINES - 1)
            def _():
                pl.semaphore_signal(barrier, inc=1, device_id=self.up, device_id_type=MESH)

            @pl.when(self.z > 0)
            def _():
                pl.semaphore_signal(barrier, inc=1, device_id=self.down, device_id_type=MESH)

            count = count + 1 + jnp.where(self.z < LINES - 1, 1, 0) + jnp.where(self.z > 0, 1, 0)
        pl.semaphore_wait(barrier, count)


class ExpGather:
    def __init__(self, place, view, parts, send, recv):
        self.place, self.view, self.parts = place, view, parts
        self.send, self.recv = send, recv

    def copy(self, lane, line, part, to):
        index = line * 2 + self.place.x
        ref = self.view(index, part)
        return remote(ref, ref, self.send.at[lane, line, part], self.recv.at[index, part], to)

    def pass_on(self, line, part, up, down):
        place = self.place
        if up:

            @pl.when(place.z < LINES - 1)
            def _():
                self.copy(1, line, part, place.up).start()

        if down:

            @pl.when(place.z > 0)
            def _():
                self.copy(2, line, part, place.down).start()

        self.copy(0, line, part, place.across).start()

    def begin(self, part):
        self.pass_on(self.place.z, part, True, True)

    def arrived(self, index, part):
        ref = self.view(index, part)
        remote(
            ref, ref, self.send.at[0, 0, part], self.recv.at[index, part], self.place.across
        ).wait_recv()

    def relay(self, step, part):
        place = self.place

        @pl.when(place.z >= step)
        def _():
            line = place.z - step
            self.arrived(line * 2 + place.x, part)
            self.pass_on(line, part, True, False)

        @pl.when(place.z + step < LINES)
        def _():
            line = place.z + step
            self.arrived(line * 2 + place.x, part)
            self.pass_on(line, part, False, True)

    def relays(self):
        for step in range(1, LINES):
            for part in range(self.parts):
                self.relay(step, part)

    def across_arrived(self, line, part):
        self.arrived(line * 2 + 1 - self.place.x, part)

    def finish(self):
        place = self.place
        for part in range(self.parts):
            for line in range(LINES):
                self.across_arrived(line, part)
        for part in range(self.parts):
            for line in range(LINES):
                self.copy(0, line, part, place.across).wait_send()

                @pl.when((place.z >= line) & (place.z < LINES - 1))
                def _():
                    self.copy(1, line, part, place.up).wait_send()

                @pl.when((place.z <= line) & (place.z > 0))
                def _():
                    self.copy(2, line, part, place.down).wait_send()


def gather_sems(parts):
    return [DMA((3, LINES, parts)), DMA((2 * LINES, parts))]


def raised_slot(line):
    return max(line - 1, 0) if isinstance(line, int) else jnp.maximum(line - 1, 0)


def lowered_slot(line):
    return min(line, LINES - 2) if isinstance(line, int) else jnp.minimum(line, LINES - 2)


class ExpScatter:
    def __init__(self, place, outgoing, mine, crossed, raised, lowered, parts, sems):
        self.place, self.parts = place, parts
        self.outgoing, self.mine = outgoing, mine
        self.crossed, self.raised, self.lowered = crossed, raised, lowered
        self.cross_send, self.cross_recv, self.line_send, self.line_recv = sems

    def cross(self, line, part):
        place = self.place
        return remote(
            self.outgoing(line, part),
            self.crossed(line, part),
            self.cross_send.at[line, part],
            self.cross_recv.at[line, part],
            place.across,
        )

    def along(self, up, line, part):
        place = self.place
        side = 0 if up else 1
        return remote(
            self.mine(line, part),
            (self.raised if up else self.lowered)(line, part),
            self.line_send.at[side, line, part],
            self.line_recv.at[side, line, part],
            place.up if up else place.down,
        )

    def begin(self, line, part):
        self.cross(line, part).start()

    def fold(self, line, part):
        place = self.place

        @pl.when(place.z != line)
        def _():
            self.cross(line, part).wait_recv()
            ref = self.mine(line, part)
            ref[...] = (to_f32(ref[...]) + to_f32(self.crossed(line, part)[...])).astype(ref.dtype)

        for up in (True, False):
            towards = place.z < line if up else place.z > line
            inner = place.z > 0 if up else place.z < LINES - 1

            @pl.when(towards)
            def _():
                ref = self.mine(line, part)

                @pl.when(inner)
                def _():
                    self.along(up, line, part).wait_recv()
                    came = (self.raised if up else self.lowered)(line, part)
                    ref[...] = (to_f32(ref[...]) + to_f32(came[...])).astype(ref.dtype)

                self.along(up, line, part).start()

    def total(self, part):
        place = self.place
        line = place.z
        self.cross(line, part).wait_recv()
        value = to_f32(self.mine(line, part)[...]) + to_f32(self.crossed(line, part)[...])
        for up in (True, False):
            came = (self.raised if up else self.lowered)(line, part)
            some = line > 0 if up else line < LINES - 1

            @pl.when(some)
            def _():
                self.along(up, line, part).wait_recv()

            value = value + jnp.where(some, to_f32(came[...]), 0.0)
        return value

    def finish(self):
        place = self.place
        for part in range(self.parts):
            for line in range(LINES):
                self.cross(line, part).wait_send()
                for up in (True, False):

                    @pl.when(place.z < line if up else place.z > line)
                    def _():
                        self.along(up, line, part).wait_send()


def scatter_sems(parts):
    return [DMA((LINES, parts)), DMA((LINES, parts)), DMA((2, LINES, parts)), DMA((2, LINES, parts))]


class CtxGather:
    def __init__(self, place, view, parts, send, recv, own=None):
        self.place, self.view, self.parts = place, view, parts
        self.send, self.recv, self.own = send, recv, own

    def copy(self, lane, part):
        place = self.place
        index = lax.rem(place.ctx + 2, 4) if lane == 2 else place.ctx
        ref = self.view(index, part)
        source = ref if lane == 2 or self.own is None else self.own(part)
        to = place.side if lane == 1 else place.core
        return remote(source, ref, self.send.at[lane, part], self.recv.at[lane, part], to)

    def landed(self, lane, part):
        place = self.place
        index = (place.core, place.side, place.far)[lane][0]
        ref = self.view(index, part)
        return remote(ref, ref, self.send.at[lane, part], self.recv.at[lane, part], place.core)

    def begin(self, part):
        self.copy(1, part).start()
        self.copy(0, part).start()

    def relay(self, part):
        self.landed(1, part).wait_recv()
        self.copy(2, part).start()

    def arrived(self, part):
        self.landed(0, part).wait_recv()
        self.landed(2, part).wait_recv()

    def sent(self, part):
        for lane in range(3):
            self.copy(lane, part).wait_send()


def square_sems(parts):
    return [DMA((3, parts)), DMA((3, parts))]


class CtxScatter:
    def __init__(self, place, outgoing, mine, swapped, crossed, parts, send, recv):
        self.place, self.parts = place, parts
        self.outgoing, self.mine = outgoing, mine
        self.swapped, self.crossed = swapped, crossed
        self.send, self.recv = send, recv

    def swap(self, near, part):
        place = self.place
        y = place.y if near else 1 - place.y
        lane = 0 if near else 1
        return remote(
            self.outgoing(y, part),
            self.swapped(lane, part),
            self.send.at[lane, part],
            self.recv.at[lane, part],
            place.core,
        )

    def over(self, part):
        place = self.place
        return remote(
            self.mine(1 - place.y, part),
            self.crossed(part),
            self.send.at[2, part],
            self.recv.at[2, part],
            place.side,
        )

    def fold(self, part):
        self.swap(False, part).wait_recv()
        ref = self.mine(1 - self.place.y, part)
        ref[...] = (to_f32(ref[...]) + to_f32(self.swapped(1, part)[...])).astype(ref.dtype)
        self.over(part).start()

    def arrived(self, part):
        self.swap(True, part).wait_recv()
        self.over(part).wait_recv()

    def total(self, part, here=slice(None)):
        return (
            to_f32(self.mine(self.place.y, part)[here, :])
            + to_f32(self.swapped(0, part)[here, :])
            + to_f32(self.crossed(part)[here, :])
        )

    def finish(self):
        for part in range(self.parts):
            self.swap(False, part).wait_send()
            self.swap(True, part).wait_send()
            self.over(part).wait_send()


def front_kernel(
    tokens,
    side_cols,
    wq,
    wk,
    wv,
    wo,
    routes,
    seg_col,
    seg_row,
    cot,
    exp_in,
    exp_out,
    all_moe,
    all_cot,
    all_routes,
    all_in,
    all_out,
    all_tokens_hbm,
    weights_hbm,
    out_rows_hbm,
    qkv_hbm,
    heads_out_hbm,
    log_norm_hbm,
    resid_hbm,
    side_rows,
    packed,
    partial,
    swapped,
    crossed,
    stage,
    in_stage,
    out_stage,
    all_tokens,
    weights,
    out_rows,
    qkv,
    heads_out,
    log_norm,
    resid_out,
    keep_sem,
    local_sem,
    tok_send,
    tok_recv,
    mix_send,
    mix_recv,
    w_send,
    w_recv,
    o_send,
    o_recv,
    r_send,
    r_recv,
    c_send,
    c_recv,
    m_send,
    m_recv,
    i_send,
    i_recv,
    u_send,
    u_recv,
    s_send,
    s_recv,
):
    place = Place()
    ctx, exp = place.ctx, place.exp
    shards, rows = packed.shape[0], packed.shape[1]
    token_rows, width = tokens.shape
    q_cols = wq.shape[1] // shards
    k_cols = wk.shape[1] // shards
    main_cols = q_cols + 2 * k_cols
    factor = 1.0 / math.sqrt(HEAD_SIZE)
    keep = [
        pltpu.make_async_copy(cot.at[pl.ds(0, all_cot.shape[1])], all_cot.at[exp], local_sem.at[0]),
        pltpu.make_async_copy(exp_in, in_stage, local_sem.at[1]),
        pltpu.make_async_copy(exp_out, out_stage, local_sem.at[2]),
    ]
    for copy in keep:
        copy.start()
    all_tokens[ctx] = tokens[...]
    for shard in range(shards):
        packed[shard, :, :q_cols] = wq[:, shard * q_cols : (shard + 1) * q_cols]
        packed[shard, :, q_cols : q_cols + k_cols] = wk[:, shard * k_cols : (shard + 1) * k_cols]
        packed[shard, :, q_cols + k_cols : main_cols] = wv[:, shard * k_cols : (shard + 1) * k_cols]
        packed[shard, :, main_cols:] = side_cols[...]
    weights[ctx, exp] = packed[ctx]
    out_rows[exp] = wo[...]
    all_routes[exp] = routes[...]
    place.greet()

    mixes = []
    for lane, to in enumerate((place.core, place.side, place.far)):
        copy = remote(
            packed.at[to[0]],
            weights.at[ctx, exp],
            mix_send.at[lane],
            mix_recv.at[lane],
            to,
        )
        copy.start()
        mixes.append(copy)
    token_gather = CtxGather(
        place,
        lambda index, part: all_tokens.at[index, pl.ds(part * (token_rows // 2), token_rows // 2)],
        2,
        tok_send,
        tok_recv,
    )
    for part in range(2):
        token_gather.begin(part)
    route_gather = ExpGather(place, lambda index, part: all_routes.at[index], 1, r_send, r_recv)
    weight_gather = ExpGather(place, lambda index, part: weights.at[:, index], 1, w_send, w_recv)
    out_gather = ExpGather(place, lambda index, part: out_rows.at[index], 1, o_send, o_recv)
    for lane, copy in enumerate(mixes):
        source = (place.core, place.side, place.far)[lane][0]
        remote(
            packed.at[0], weights.at[source, exp], mix_send.at[lane], mix_recv.at[lane], place.core
        ).wait_recv()
    weight_gather.begin(0)
    route_gather.begin(0)
    out_gather.begin(0)
    local_experts = exp_in.shape[0]
    in_gather = CtxGather(
        place,
        lambda index, part: all_in.at[part, index],
        local_experts,
        i_send,
        i_recv,
        lambda part: in_stage.at[part],
    )
    down_gather = CtxGather(
        place,
        lambda index, part: all_out.at[part, index],
        local_experts,
        u_send,
        u_recv,
        lambda part: out_stage.at[part],
    )
    cot_gather = ExpGather(place, lambda index, part: all_cot.at[index], 1, c_send, c_recv)
    weight_gather.relay(1, 0)
    token_gather.relay(0)
    weight_gather.relay(2, 0)
    token_gather.relay(1)
    weight_gather.relay(3, 0)
    for copy in keep:
        copy.wait()
    keep = [
        pltpu.make_async_copy(in_stage, all_in.at[:, ctx], local_sem.at[1]),
        pltpu.make_async_copy(out_stage, all_out.at[:, ctx], local_sem.at[2]),
    ]
    for copy in keep:
        copy.start()
    half_experts = local_experts // 2
    for part in range(half_experts):
        in_gather.begin(part)
    for step in range(1, LINES):
        out_gather.relay(step, 0)
        route_gather.relay(step, 0)
    cot_gather.begin(0)
    for part in range(2):
        token_gather.arrived(part)
    weight_gather.finish()

    side = weights.shape[3] - main_cols
    same = (
        lax.broadcasted_iota(jnp.int32, (side, side), 0)
        == lax.broadcasted_iota(jnp.int32, (side, side), 1)
    ).astype(jnp.bfloat16)
    full = weights[...].reshape(width, weights.shape[3])
    side_t = outer_cols(same, full[:, main_cols:])
    side_rows[...] = side_t.astype(jnp.bfloat16)
    gain_one, gain_two = side_t[EXPERTS : EXPERTS + 1], side_t[EXPERTS + 1 : EXPERTS + 2]
    for block in range(shards):
        values = to_f32(all_tokens[block])
        normed = (values * rms_scale(values) * gain_one).astype(jnp.bfloat16)
        qkv[pl.ds(block * token_rows, token_rows), :] = dot_rows(normed, full[:, :main_cols]).astype(
            jnp.bfloat16
        )
    out_gather.finish()

    low = lax.broadcasted_iota(jnp.int32, (1, 2 * HEAD_SIZE), 1) < HEAD_SIZE

    def spread(first):
        plain = to_f32(qkv[:, first : first + k_cols])
        turned = pltpu.roll(plain, HEAD_SIZE, 1)
        zero = jnp.zeros((), jnp.float32)
        return [
            [
                jnp.where(low, plain, zero).astype(jnp.bfloat16),
                jnp.where(low, zero, turned).astype(jnp.bfloat16),
            ],
            [
                jnp.where(low, turned, zero).astype(jnp.bfloat16),
                jnp.where(low, zero, plain).astype(jnp.bfloat16),
            ],
        ]

    keys, values = spread(q_cols), spread(q_cols + k_cols)
    full_out = out_rows[...].reshape(q_cols, width)
    for block in range(shards - 1, -1, -1):
        here = pl.ds(block * token_rows, token_rows)
        count = (block + 1) * token_rows
        at_row = block * token_rows + lax.broadcasted_iota(jnp.int32, (token_rows, 1), 0)
        at_col = lax.broadcasted_iota(jnp.int32, (1, count), 1)
        bias = jnp.where(
            (at_col <= at_row) & (seg_col[here, :] == seg_row[:, :count]), 0.0, MASK_FILLER
        )
        lows = []
        norms = jnp.zeros((token_rows, 128), jnp.float32)
        at_lane = lax.broadcasted_iota(jnp.int32, (1, 128), 1)
        for pair in range(2):
            queries = qkv[here, pair * 128 : pair * 128 + 128]
            heads = jnp.zeros((token_rows, 128), jnp.float32)
            for head in range(2):
                scores = outer_cols(queries, keys[pair][head][:count]) * factor + bias
                top = jnp.max(scores, -1, keepdims=True)
                shares = jnp.exp(scores - top)
                total = jnp.sum(shares, -1, keepdims=True)
                norms = jnp.where(at_lane == 2 * pair + head, top + jnp.log(total), norms)
                heads = heads + dot_rows(
                    shares.astype(jnp.bfloat16), values[pair][head][:count]
                ) / total
            heads_out[here, pair * 128 : pair * 128 + 128] = heads
            lows.append(heads.astype(jnp.bfloat16))
        log_norm[here, :] = norms
        partial[block] = dot_rows(jnp.concatenate(lows, 1), full_out).astype(jnp.bfloat16)
        if block == 2:
            cot_gather.relay(1, 0)

    keep += [
        pltpu.make_async_copy(source, target, keep_sem.at[index])
        for index, (source, target) in enumerate(
            (
                (all_tokens, all_tokens_hbm),
                (weights, weights_hbm),
                (out_rows, out_rows_hbm),
                (qkv, qkv_hbm),
                (heads_out, heads_out_hbm),
                (log_norm, log_norm_hbm),
            )
        )
    ]
    for copy in keep[2:]:
        copy.start()

    half_rows = token_rows // 2
    branch = CtxScatter(
        place,
        lambda y, part: partial.at[2 * y + 1 - place.half, pl.ds(part * half_rows, half_rows)],
        lambda y, part: partial.at[2 * y + place.half, pl.ds(part * half_rows, half_rows)],
        lambda lane, part: swapped.at[lane, pl.ds(part * half_rows, half_rows)],
        lambda part: crossed.at[pl.ds(part * half_rows, half_rows)],
        2,
        s_send,
        s_recv,
    )
    for part in range(2):
        branch.swap(False, part).start()
    for part in range(2):
        branch.swap(True, part).start()
    cot_gather.relay(2, 0)
    for part in range(2):
        branch.fold(part)
    for part in range(half_experts, local_experts):
        in_gather.begin(part)
    for part in range(local_experts):
        down_gather.begin(part)
    moe_parts = 4
    moe_rows = token_rows // moe_parts
    moe_gather = ExpGather(
        place,
        lambda index, part: all_moe.at[index, pl.ds(part * moe_rows, moe_rows)],
        moe_parts,
        m_send,
        m_recv,
    )
    for part in range(2):
        here = pl.ds(part * half_rows, half_rows)
        branch.arrived(part)
        resid = to_f32(tokens[here, :]) + branch.total(part)
        resid_out[here, :] = resid
        stage[here, :] = (resid * rms_scale(resid) * gain_two).astype(jnp.bfloat16)
        copy = pltpu.make_async_copy(
            stage.at[here], all_moe.at[exp, here], local_sem.at[3 + part]
        )
        copy.start()
        copy.wait()
        for piece in range(2):
            moe_gather.begin(2 * part + piece)
    keep.append(pltpu.make_async_copy(resid_out, resid_hbm, keep_sem.at[6]))
    keep[-1].start()
    cot_gather.relay(3, 0)
    for part in range(half_experts):
        in_gather.relay(part)
    moe_gather.relays()
    for part in range(half_experts, local_experts):
        in_gather.relay(part)
    for part in range(local_experts):
        down_gather.relay(part)
    moe_gather.finish()
    cot_gather.finish()
    route_gather.finish()
    for copy in keep:
        copy.wait()
    branch.finish()
    for part in range(2):
        token_gather.sent(part)
    for copy in mixes:
        copy.wait_send()
    for part in range(local_experts):
        in_gather.arrived(part)
        in_gather.sent(part)
        down_gather.arrived(part)
        down_gather.sent(part)


def front(tokens, side_cols, wq, wk, wv, wo, routes, seg_col, seg_row, cot, exp_in, exp_out):
    shards, groups = lax.axis_size("ctx"), lax.axis_size("exp")
    token_rows, width = tokens.shape
    rows = wq.shape[0]
    q_cols, k_cols = wq.shape[1] // shards, wk.shape[1] // shards
    pack_cols = q_cols + 2 * k_cols + side_cols.shape[1]
    seq_len = token_rows * shards
    low, f32 = jnp.bfloat16, jnp.float32
    experts, in_rows, in_cols = exp_in.shape
    out_count = exp_out.shape[1]

    def shape(dims, dtype):
        return jax.ShapeDtypeStruct(dims, dtype)

    whole, anywhere = pl.BlockSpec(memory_space=VMEM), pl.BlockSpec(memory_space=pl.ANY)
    return pl.pallas_call(
        front_kernel,
        name="front",
        out_shape=[
            shape((groups, token_rows, width), low),
            shape((groups, COT_FIRST, width), low),
            shape((groups,) + routes.shape, jnp.int32),
            shape((experts, shards, in_rows, in_cols), low),
            shape((experts, shards, out_count, width), low),
            shape((shards, token_rows, width), low),
            shape((shards, groups, rows, pack_cols), low),
            shape((groups, rows, width), low),
            shape((seq_len, q_cols + 2 * k_cols), low),
            shape((seq_len, q_cols), f32),
            shape((seq_len, 128), f32),
            shape((token_rows, width), f32),
            shape((side_cols.shape[1], width), low),
        ],
        in_specs=[whole] * 10 + [anywhere] * 2,
        out_specs=[anywhere] * 2 + [whole] + [anywhere] * 9 + [whole],
        scratch_shapes=[
            VMEM((shards, rows, pack_cols), low),
            VMEM((shards, token_rows, width), low),
            VMEM((2, token_rows, width), low),
            VMEM((token_rows, width), low),
            VMEM((token_rows, width), low),
            VMEM(exp_in.shape, low),
            VMEM(exp_out.shape, low),
            VMEM((shards, token_rows, width), low),
            VMEM((shards, groups, rows, pack_cols), low),
            VMEM((groups, rows, width), low),
            VMEM((seq_len, q_cols + 2 * k_cols), low),
            VMEM((seq_len, q_cols), f32),
            VMEM((seq_len, 128), f32),
            VMEM((token_rows, width), f32),
            DMA((7,)),
            DMA((5,)),
            *square_sems(2),
            DMA((3,)),
            DMA((3,)),
            *gather_sems(1),
            *gather_sems(1),
            *gather_sems(1),
            *gather_sems(1),
            *gather_sems(4),
            *square_sems(experts),
            *square_sems(experts),
            *square_sems(2),
        ],
        compiler_params=pltpu.CompilerParams(
            collective_id=0, has_side_effects=True, vmem_limit_bytes=GRANT
        ),
    )(tokens, side_cols, wq, wk, wv, wo, routes, seg_col, seg_row, cot, exp_in, exp_out)


def experts_kernel(
    all_moe,
    all_cot,
    own_cot,
    all_routes,
    all_in,
    all_out,
    side_rows,
    resid,
    grad_moe_in,
    mixed_first,
    mixed_rest,
    logit_grads,
    in_first,
    down_first,
    in_rest,
    down_rest,
    moe,
    cot,
    w_in,
    w_out,
    slot_rows,
    slot_cot,
    hidden,
    slopes,
    slot_out,
    pick,
    slot_gate,
    gates,
    moe_crossed,
    moe_raised,
    moe_lowered,
    mix_crossed,
    mix_raised,
    mix_lowered,
    sum_stage,
    resid_rows,
    load_sem,
    store_sem,
    put_sem,
    free_sem,
    moe_xs,
    moe_xr,
    moe_ls,
    moe_lr,
    mix_xs,
    mix_xr,
    mix_ls,
    mix_lr,
    in_send,
    in_recv,
    down_send,
    down_recv,
    c_send,
    c_recv,
):
    place = Place()
    groups, token_rows, width = moe.shape
    local_experts = w_in.shape[0]
    slots = pick.shape[1] // local_experts
    first = place.exp * local_experts
    early_rows = all_cot.shape[1]
    late_rows = token_rows - early_rows
    loads = [
        pltpu.make_async_copy(all_moe, moe, load_sem.at[0]),
        pltpu.make_async_copy(all_cot, cot.at[:, pl.ds(0, early_rows)], load_sem.at[1]),
        pltpu.make_async_copy(
            own_cot.at[pl.ds(early_rows, late_rows)],
            cot.at[place.exp, pl.ds(early_rows, late_rows)],
            load_sem.at[3 + 2 * local_experts],
        ),
    ]
    for expert in range(local_experts):
        loads.append(
            pltpu.make_async_copy(all_in.at[expert], w_in.at[expert], load_sem.at[2 + 2 * expert])
        )
        loads.append(
            pltpu.make_async_copy(all_out.at[expert], w_out.at[expert], load_sem.at[3 + 2 * expert])
        )
    loads.append(
        pltpu.make_async_copy(
            resid.at[pl.ds(0, mixed_first.shape[0])], resid_rows, load_sem.at[2 + 2 * local_experts]
        )
    )
    loads[2].start()
    loads[0].start()
    place.greet()

    at_expert = lax.broadcasted_iota(jnp.int32, (EXPERTS, 1), 0)
    at_lane = lax.broadcasted_iota(jnp.int32, (1, 128), 1)
    at_slot = lax.broadcasted_iota(jnp.int32, (slots, 1), 0)
    before = (
        lax.broadcasted_iota(jnp.int32, (token_rows, token_rows), 0)
        < lax.broadcasted_iota(jnp.int32, (token_rows, token_rows), 1)
    ).astype(jnp.bfloat16)
    router = side_rows[:EXPERTS, :]
    cot_parts = c_send.shape[2]
    cot_rows = late_rows // cot_parts
    cot_gather = ExpGather(
        place,
        lambda index, part: cot.at[index, pl.ds(early_rows + part * cot_rows, cot_rows)],
        cot_parts,
        c_send,
        c_recv,
    )
    loads[2].wait()
    for part in range(cot_parts):
        cot_gather.begin(part)
    loads[0].wait()
    loads[1].start()
    for copy in loads[3:]:
        copy.start()

    def dispatch(block, carry):
        routes = all_routes[block]
        member = routes[0:1, :] == at_expert
        for rank in range(1, TOPK):
            member = member | (routes[rank : rank + 1, :] == at_expert)
        tokens = moe[block]
        logits = outer_cols(router, tokens)
        top = jnp.max(jnp.where(member, logits, MASK_FILLER), 0, keepdims=True)
        weights = jnp.where(member, jnp.exp(logits - top), 0.0)
        shares = weights / jnp.sum(weights, 0, keepdims=True)
        gates[block] = shares
        ranks = dot_rows(jnp.where(member, 1.0, 0.0).astype(jnp.bfloat16), before)
        filled = jnp.where(member & (ranks < CAP), ranks, -1.0)
        columns = jnp.zeros((slots, 128), jnp.float32)
        for expert in range(local_experts):
            mine = at_expert == first + expert
            spot = jnp.sum(jnp.where(mine, filled, 0.0), 0, keepdims=True)
            share = jnp.sum(jnp.where(mine, shares, 0.0), 0, keepdims=True)
            chosen = spot == at_slot.astype(jnp.float32)
            here = pl.ds(expert * slots, slots)
            pick[block, here, :] = jnp.where(chosen, 1.0, 0.0).astype(jnp.bfloat16)
            column = jnp.sum(jnp.where(chosen, share, 0.0), 1, keepdims=True)
            columns = jnp.where(at_lane == expert, column, columns)
        slot_gate[block] = columns
        chosen = pick[block]
        rows = dot_rows(chosen, tokens).astype(jnp.bfloat16)
        for expert in range(local_experts):
            slot_rows[expert, block] = rows[expert * slots : (expert + 1) * slots]
        return carry

    lax.fori_loop(0, groups, dispatch, 0)
    for part in range(cot_parts):
        cot_gather.relay(1, part)
    loads[1].wait()
    for copy in loads[3:]:
        copy.wait()
    all_slots = groups * slots

    def flat(ref, expert):
        return ref[expert].reshape(all_slots, ref.shape[-1])

    def shaped(value):
        return value.reshape(groups, slots, value.shape[-1])

    def forward(expert, carry):
        rows = flat(slot_rows, expert)
        for first_col in range(0, FF, 256):
            gate_cols, up_cols = pl.ds(first_col, 256), pl.ds(FF + first_col, 256)
            gate_part = dot_rows(rows, w_in[expert, :, gate_cols])
            up_part = dot_rows(rows, w_in[expert, :, up_cols])
            sigmoid_gate = jax.nn.sigmoid(gate_part)
            silu = gate_part * sigmoid_gate
            hidden[expert, :, gate_cols] = (silu * up_part).astype(jnp.bfloat16)
            slopes[expert, :, gate_cols] = (
                up_part * sigmoid_gate * (1.0 + gate_part * (1.0 - sigmoid_gate))
            ).astype(jnp.bfloat16)
            slopes[expert, :, up_cols] = silu.astype(jnp.bfloat16)
        slot_out[expert] = dot_rows(hidden[expert], w_out[expert]).astype(jnp.bfloat16)
        return carry

    half_experts, most = local_experts // 2, local_experts - 1
    lax.fori_loop(0, most, forward, 0)
    for part in range(cot_parts):
        cot_gather.relay(2, part)
    lax.fori_loop(most, local_experts, forward, 0)

    def block_rows(ref, block):
        here = pl.ds(pl.multiple_of(block * slots, slots), slots)
        return jnp.concatenate([ref[expert, here, :] for expert in range(local_experts)], 0)

    def combine(block, carry):
        shares = gates[block]
        weighted = []
        for expert in range(local_experts):
            mine = at_expert == first + expert
            share = jnp.sum(jnp.where(mine, shares, 0.0), 0, keepdims=True)
            chosen = to_f32(pick[block, pl.ds(expert * slots, slots), :])
            weighted.append((chosen * share).astype(jnp.bfloat16))
        moe[block] = inner_rows(
            jnp.concatenate(weighted, 0), block_rows(slot_out, block)
        ).astype(jnp.bfloat16)
        return carry

    lax.fori_loop(0, groups, combine, 0)
    for part in range(cot_parts):
        cot_gather.relay(3, part)

    mix_rows = mixed_first.shape[0]
    rest_store = pltpu.make_async_copy(
        moe.at[:, pl.ds(mix_rows, token_rows - mix_rows)], mixed_rest, load_sem.at[0]
    )
    rest_store.start()
    mix_parts = mix_xs.shape[1]
    mix_size = mix_rows // mix_parts

    def mix_piece(ref, part):
        return ref.at[pl.ds(part * mix_size, mix_size)]

    mix = ExpScatter(
        place,
        lambda line, part: mix_piece(moe.at[line * 2 + 1 - place.x], part),
        lambda line, part: mix_piece(moe.at[line * 2 + place.x], part),
        lambda line, part: mix_piece(mix_crossed.at[line], part),
        lambda line, part: mix_piece(mix_raised.at[raised_slot(line)], part),
        lambda line, part: mix_piece(mix_lowered.at[lowered_slot(line)], part),
        mix_parts,
        (mix_xs, mix_xr, mix_ls, mix_lr),
    )
    mix_order = [
        (line, part) for pair in ((3, 0), (2, 1)) for part in range(mix_parts) for line in pair
    ]
    for line, part in mix_order:
        mix.begin(line, part)

    cot_gather.finish()

    def dispatch_back(block, carry):
        shares = gates[block]
        chosen = pick[block]
        cots = dot_rows(chosen, cot[block])
        dots = jnp.sum(cots * to_f32(block_rows(slot_out, block)), 1, keepdims=True)
        picked_grads = jnp.zeros_like(shares)
        for expert in range(local_experts):
            here = slice(expert * slots, (expert + 1) * slots)
            row = jnp.sum(to_f32(chosen[here]) * dots[here], 0, keepdims=True)
            picked_grads = jnp.where(at_expert == first + expert, row, picked_grads)
            share = slot_gate[block, :, expert : expert + 1]
            slot_cot[expert, block] = (share * cots[here]).astype(jnp.bfloat16)
        grads = shares * (picked_grads - jnp.sum(shares * picked_grads, 0, keepdims=True))
        high, low = two_parts(grads)
        logit_grads[block] = jnp.concatenate([high, low], 0)
        return carry

    lax.fori_loop(0, groups, dispatch_back, 0)

    def backward(expert, carry):
        grads = outer_cols(flat(slot_cot, expert), w_out[expert])
        slopes[expert, :, :FF] = (grads * to_f32(slopes[expert, :, :FF])).astype(jnp.bfloat16)
        slopes[expert, :, FF:] = (grads * to_f32(slopes[expert, :, FF:])).astype(jnp.bfloat16)
        slot_out[expert] = outer_cols(slopes[expert], w_in[expert]).astype(jnp.bfloat16)
        return carry

    lax.fori_loop(0, half_experts, backward, 0)
    for line, part in mix_order[:4]:
        mix.fold(line, part)
    lax.fori_loop(half_experts, local_experts, backward, 0)

    def combine_back(block, carry):
        left = jnp.concatenate([pick[block], logit_grads[block]], 0)
        right = jnp.concatenate([block_rows(slot_out, block), router, router], 0)
        cot[block] = inner_rows(left, right).astype(jnp.bfloat16)
        return carry

    lax.fori_loop(0, groups, combine_back, 0)
    for line, part in mix_order[4:]:
        mix.fold(line, part)
    moe_parts = moe_xs.shape[1]
    part_rows = token_rows // moe_parts

    def piece(ref, part):
        return ref.at[pl.ds(part * part_rows, part_rows)]

    back_sum = ExpScatter(
        place,
        lambda line, part: piece(cot.at[line * 2 + 1 - place.x], part),
        lambda line, part: piece(cot.at[line * 2 + place.x], part),
        lambda line, part: piece(moe_crossed.at[line], part),
        lambda line, part: piece(moe_raised.at[raised_slot(line)], part),
        lambda line, part: piece(moe_lowered.at[lowered_slot(line)], part),
        moe_parts,
        (moe_xs, moe_xr, moe_ls, moe_lr),
    )
    for pair in ((3, 0), (2, 1)):
        for part in range(moe_parts):
            for line in pair:
                back_sum.begin(line, part)

    for to in (place.core, place.side):
        pl.semaphore_signal(free_sem, inc=1, device_id=to, device_id_type=MESH)

    early = in_first.shape[0]
    in_rows, down_rows = in_first.shape[1], down_first.shape[1]
    into = CtxScatter(
        place,
        lambda y, part: w_in.at[part, pl.ds((2 * y + 1 - place.half) * in_rows, in_rows)],
        lambda y, part: w_in.at[part, pl.ds((2 * y + place.half) * in_rows, in_rows)],
        lambda lane, part: slot_out.at[part, pl.ds(lane * in_rows, in_rows)],
        lambda part: slot_out.at[early + part, pl.ds(2 * down_rows, in_rows)],
        early,
        in_send,
        in_recv,
    )
    downs = CtxScatter(
        place,
        lambda y, part: w_out.at[part, pl.ds((2 * y + 1 - place.half) * down_rows, down_rows)],
        lambda y, part: w_out.at[part, pl.ds((2 * y + place.half) * down_rows, down_rows)],
        lambda lane, part: slot_out.at[early + part, pl.ds(lane * down_rows, down_rows)],
        lambda part: slot_out.at[early + part, pl.ds(2 * down_rows + in_rows, down_rows)],
        early,
        down_send,
        down_recv,
    )
    rest_store.wait()
    pl.semaphore_wait(free_sem, 2)
    stores = []

    def store(source, target, sem):
        copy = pltpu.make_async_copy(source, target, sem)
        copy.start()
        stores.append(copy)

    folds = [(pair, part) for pair in ((3, 0), (2, 1)) for part in range(moe_parts)]

    def fold_next():
        if folds:
            pair, part = folds.pop(0)
            for line in pair:
                back_sum.fold(line, part)

    for expert in range(local_experts):
        w_out[expert] = inner_rows(hidden[expert], flat(slot_cot, expert)).astype(jnp.bfloat16)
        if expert < early:
            downs.swap(False, expert).start()
            downs.swap(True, expert).start()
        else:
            store(w_out.at[expert], down_rest.at[expert - early], store_sem.at[0, expert])
        fold_next()
        w_in[expert] = inner_rows(flat(slot_rows, expert), slopes[expert]).astype(jnp.bfloat16)
        if expert < early:
            into.swap(False, expert).start()
            into.swap(True, expert).start()
        else:
            store(w_in.at[expert], in_rest.at[expert - early], store_sem.at[1, expert])
        if expert > 0 and expert <= early:
            downs.fold(expert - 1)
            into.fold(expert - 1)
        fold_next()
    while folds:
        fold_next()

    staged = [None, None]
    stage_rows = sum_stage.shape[1]

    def put(slot, value, target, sem):
        if staged[slot] is not None:
            staged[slot].wait()
        sum_stage[slot] = value
        staged[slot] = pltpu.make_async_copy(sum_stage.at[slot], target, sem)
        staged[slot].start()

    def finish_expert(part):
        into.arrived(part)
        downs.arrived(part)
        slot = 0
        for scatter, target, kind in ((downs, down_first, 0), (into, in_first, 1)):
            for step in range(target.shape[1] // stage_rows):
                here = pl.ds(step * stage_rows, stage_rows)
                put(slot, scatter.total(part, here), target.at[part, here], put_sem.at[slot])
                slot = 1 - slot

    for part in range(early - 1):
        finish_expert(part)
    for part in range(mix_parts):
        here = pl.ds(part * mix_size, mix_size)
        mixed_first[here, :] = (resid_rows[here, :] + mix.total(part)).astype(jnp.bfloat16)
    for part in range(moe_parts):
        here = pl.ds(part * part_rows, part_rows)
        put(part % 2, back_sum.total(part), grad_moe_in.at[here], put_sem.at[part % 2])
    finish_expert(early - 1)
    for copy in staged:
        copy.wait()
    for copy in stores:
        copy.wait()
    for scatter in (mix, back_sum, into, downs):
        scatter.finish()


MIX_FIRST = 128
EARLY = 2
MOE_PARTS = 4


def experts(all_moe, all_cot, own_cot, all_routes, all_in, all_out, side_rows, resid):
    groups, token_rows, width = all_moe.shape
    local_experts, in_cols = all_in.shape[0], all_in.shape[2]
    shards = lax.axis_size("ctx")
    in_rows, down_rows = width // shards, FF // shards
    slots = -(-CAP // 16) * 16
    low, f32 = jnp.bfloat16, jnp.float32

    def shape(dims, dtype):
        return jax.ShapeDtypeStruct(dims, dtype)

    whole, anywhere = pl.BlockSpec(memory_space=VMEM), pl.BlockSpec(memory_space=pl.ANY)
    rest, rest_rows = local_experts - EARLY, token_rows - MIX_FIRST
    slot_block = (local_experts, groups, slots)
    block, steps = (LINES, token_rows, width), (LINES - 1, token_rows, width)
    short, short_steps = (LINES, MIX_FIRST, width), (LINES - 1, MIX_FIRST, width)
    return pl.pallas_call(
        experts_kernel,
        name="experts",
        out_shape=[
            shape((token_rows, width), f32),
            shape((MIX_FIRST, width), low),
            shape((groups, rest_rows, width), low),
            shape((groups, 2 * EXPERTS, token_rows), low),
            shape((EARLY, in_rows, in_cols), f32),
            shape((EARLY, down_rows, width), f32),
            shape((rest, width, in_cols), low),
            shape((rest, FF, width), low),
        ],
        in_specs=[anywhere] * 3
        + [whole]
        + [anywhere] * 2
        + [whole, anywhere],
        out_specs=[anywhere, whole, anywhere, whole] + [anywhere] * 4,
        scratch_shapes=[
            VMEM(all_moe.shape, low),
            VMEM(all_moe.shape, low),
            VMEM(all_in.shape, low),
            VMEM(all_out.shape, low),
            VMEM(slot_block + (width,), low),
            VMEM(slot_block + (width,), low),
            VMEM((local_experts, groups * slots, FF), low),
            VMEM((local_experts, groups * slots, 2 * FF), low),
            VMEM((local_experts, groups * slots, width), low),
            VMEM((groups, local_experts * slots, token_rows), low),
            VMEM((groups, slots, 128), f32),
            VMEM((groups, EXPERTS, token_rows), f32),
            VMEM(block, low),
            VMEM(steps, low),
            VMEM(steps, low),
            VMEM(short, low),
            VMEM(short_steps, low),
            VMEM(short_steps, low),
            VMEM((2, token_rows // MOE_PARTS, width), f32),
            VMEM((MIX_FIRST, width), f32),
            DMA((4 + 2 * local_experts,)),
            DMA((2, local_experts)),
            DMA((2,)),
            pltpu.SemaphoreType.REGULAR,
            *scatter_sems(MOE_PARTS),
            *scatter_sems(2),
            *square_sems(EARLY),
            *square_sems(EARLY),
            *gather_sems(2),
        ],
        compiler_params=pltpu.CompilerParams(
            collective_id=1, has_side_effects=True, vmem_limit_bytes=63 * 2**20
        ),
    )(all_moe, all_cot, own_cot, all_routes, all_in, all_out, side_rows, resid)


def back_kernel(
    moe_in_grads,
    mixed_part,
    grad_in,
    grad_down,
    tokens,
    cot,
    resid,
    gain_two,
    gain_one,
    logit_grads,
    all_moe_hbm,
    all_tokens_hbm,
    weights_hbm,
    out_rows_hbm,
    qkv_hbm,
    heads_out_hbm,
    log_norm_hbm,
    seg_col_hbm,
    seg_row,
    mixed_out,
    grad_tokens,
    query_sum,
    key_sum,
    value_sum,
    side_sum,
    output_sum,
    in_sum,
    down_sum,
    mix_mine,
    mix_crossed,
    mix_raised,
    mix_lowered,
    in_mine,
    in_swapped,
    in_crossed,
    down_mine,
    down_swapped,
    down_crossed,
    grad_resid,
    all_resid,
    head_grads,
    turned,
    key_grads,
    value_grads,
    qkv_grads,
    normed_part,
    normed_swapped,
    normed_crossed,
    sums,
    sums_crossed,
    sums_raised,
    sums_lowered,
    sums_own,
    sums_all,
    out_grads,
    out_crossed,
    out_raised,
    out_lowered,
    in_stage,
    down_stage,
    store_sem,
    all_moe,
    all_tokens,
    weights,
    out_rows,
    qkv,
    heads_out,
    log_norm,
    seg_col,
    late_sem,
    local_sem,
    mix_xs,
    mix_xr,
    mix_ls,
    mix_lr,
    sum_xs,
    sum_xr,
    sum_ls,
    sum_lr,
    out_xs,
    out_xr,
    out_ls,
    out_lr,
    in_send,
    in_recv,
    down_send,
    down_recv,
    normed_send,
    normed_recv,
    resid_send,
    resid_recv,
    last_send,
    last_recv,
):
    place = Place()
    ctx, exp = place.ctx, place.exp
    token_rows, width = tokens.shape
    shards, groups, rows, pack_cols = weights.shape
    local_experts = grad_in.shape[0]
    q_cols = heads_out.shape[1]
    main_cols = qkv.shape[1]
    k_cols = (main_cols - q_cols) // 2
    factor = 1.0 / math.sqrt(HEAD_SIZE)
    order = (3, 0, 2, 1)

    loads = []

    def load(source, target):
        copy = pltpu.make_async_copy(source, target, local_sem.at[len(loads)])
        copy.start()
        loads.append(copy)

    for y in range(2):
        load(grad_in.at[:, 2 * y + place.half], in_mine.at[y])
        load(grad_down.at[:, 2 * y + place.half], down_mine.at[y])
    for line in order:
        load(mixed_part.at[line * 2 + place.x], mix_mine.at[line])
    place.greet()

    def piece(ref, count, part):
        size = ref.shape[0] // count
        return ref.at[pl.ds(part * size, size)]

    moe_parts, mix_parts = 4, mix_xs.shape[1]
    mix = ExpScatter(
        place,
        lambda line, part: piece(mixed_part.at[line * 2 + 1 - place.x], mix_parts, part),
        lambda line, part: piece(mix_mine.at[line], mix_parts, part),
        lambda line, part: piece(mix_crossed.at[line], mix_parts, part),
        lambda line, part: piece(mix_raised.at[raised_slot(line)], mix_parts, part),
        lambda line, part: piece(mix_lowered.at[lowered_slot(line)], mix_parts, part),
        mix_parts,
        (mix_xs, mix_xr, mix_ls, mix_lr),
    )
    into = CtxScatter(
        place,
        lambda y, part: grad_in.at[part, 2 * y + 1 - place.half],
        lambda y, part: in_mine.at[y, part],
        lambda lane, part: in_swapped.at[lane, part],
        lambda part: in_crossed.at[part],
        local_experts,
        in_send,
        in_recv,
    )
    downs = CtxScatter(
        place,
        lambda y, part: grad_down.at[part, 2 * y + 1 - place.half],
        lambda y, part: down_mine.at[y, part],
        lambda lane, part: down_swapped.at[lane, part],
        lambda part: down_crossed.at[part],
        local_experts,
        down_send,
        down_recv,
    )
    for near in (False, True):
        for part in range(local_experts):
            into.swap(near, part).start()
        for part in range(local_experts):
            downs.swap(near, part).start()
    gain_one_row, gain_two_row = gain_one[...], gain_two[...]
    moe_rows = token_rows // moe_parts
    gain_two_sum = jnp.zeros((1, width), jnp.float32)
    resid_gather = CtxGather(
        place,
        lambda index, part: all_resid.at[index, pl.ds(part * moe_rows, moe_rows)],
        moe_parts,
        resid_send,
        resid_recv,
    )
    for part in range(moe_parts):
        here = pl.ds(part * moe_rows, moe_rows)
        grad_moe_in = moe_in_grads[here, :]
        values = resid[here, :]
        scale = rms_scale(values)
        weighted = grad_moe_in * gain_two_row
        gain_two_sum = gain_two_sum + jnp.sum(grad_moe_in * values * scale, 0, keepdims=True)
        grads = (
            to_f32(cot[here, :])
            + scale * weighted
            - values * (scale * scale * scale) * jnp.mean(weighted * values, -1, keepdims=True)
        )
        grad_resid[here, :] = grads
        all_resid[ctx, here, :] = grads.astype(jnp.bfloat16)
        resid_gather.begin(part)
    for pair in ((3, 0), (2, 1)):
        for part in range(mix_parts):
            for line in pair:
                mix.begin(line, part)
    for copy in loads:
        copy.wait()
    late = []
    for index, (source, target) in enumerate(
        (
            (all_moe_hbm, all_moe),
            (qkv_hbm, qkv),
            (log_norm_hbm, log_norm),
            (out_rows_hbm, out_rows),
            (heads_out_hbm, heads_out),
            (seg_col_hbm, seg_col),
            (weights_hbm, weights),
            (all_tokens_hbm, all_tokens),
        )
    ):
        late.append(pltpu.make_async_copy(source, target, late_sem.at[index]))
        late[-1].start()

    low = lax.broadcasted_iota(jnp.int32, (1, 2 * HEAD_SIZE), 1) < HEAD_SIZE

    def spread(first):
        plain = to_f32(qkv[:, first : first + k_cols])
        other = pltpu.roll(plain, HEAD_SIZE, 1)
        zero = jnp.zeros((), jnp.float32)
        return [
            [
                jnp.where(low, plain, zero).astype(jnp.bfloat16),
                jnp.where(low, zero, other).astype(jnp.bfloat16),
            ],
            [
                jnp.where(low, other, zero).astype(jnp.bfloat16),
                jnp.where(low, zero, plain).astype(jnp.bfloat16),
            ],
        ]

    def add_router(block, total):
        return total + dot_rows(logit_grads[block], all_moe[block])

    for part in range(moe_parts // 2):
        resid_gather.relay(part)
    for copy in late:
        copy.wait()
    full = weights[...].reshape(width, pack_cols)
    full_out = out_rows[...].reshape(q_cols, width)
    keys, values = spread(q_cols), spread(q_cols + k_cols)
    norm_rows = log_norm[...].T
    router_grads = lax.fori_loop(
        0, groups, add_router, jnp.zeros((2 * EXPERTS, width), jnp.float32)
    )
    router_sum = router_grads[:EXPERTS] + router_grads[EXPERTS:]
    for part in range(moe_parts // 2, moe_parts):
        resid_gather.relay(part)
    mix.fold(3, 0)
    mix.fold(0, 0)
    for part in range(moe_parts):
        resid_gather.arrived(part)
    for part in range(local_experts):
        into.fold(part)
        downs.fold(part)
    at_lane = lax.broadcasted_iota(jnp.int32, (1, 128), 1)
    for block in range(shards):
        here = pl.ds(block * token_rows, token_rows)
        grads = outer_cols(all_resid[block], full_out).astype(jnp.bfloat16)
        head_grads[here, :] = grads
        products = to_f32(grads) * heads_out[here, :]
        deltas = jnp.zeros((token_rows, 128), jnp.float32)
        for pair in range(2):
            both = products[:, pair * 128 : pair * 128 + 128]
            first = jnp.sum(jnp.where(low, both, 0.0), -1, keepdims=True)
            second = jnp.sum(jnp.where(low, 0.0, both), -1, keepdims=True)
            deltas = jnp.where(at_lane == 2 * pair, first, deltas)
            deltas = jnp.where(at_lane == 2 * pair + 1, second, deltas)
        turned[:, here] = deltas.T
    attn_low = heads_out[...].astype(jnp.bfloat16)
    flat_resid = all_resid[...].reshape(shards * token_rows, width)
    out_grads[...] = (
        inner_rows(attn_low, flat_resid).astype(jnp.bfloat16).reshape(groups, rows, width)
    )
    out_scatter = ExpScatter(
        place,
        lambda line, part: out_grads.at[line * 2 + 1 - place.x],
        lambda line, part: out_grads.at[line * 2 + place.x],
        lambda line, part: out_crossed.at[line],
        lambda line, part: out_raised.at[raised_slot(line)],
        lambda line, part: out_lowered.at[lowered_slot(line)],
        1,
        (out_xs, out_xr, out_ls, out_lr),
    )
    for line in order:
        out_scatter.begin(line, 0)
    mix_order = [
        (line, part) for pair in ((3, 0), (2, 1)) for part in range(mix_parts) for line in pair
    ]
    key_grads[...] = jnp.zeros_like(key_grads)
    value_grads[...] = jnp.zeros_like(value_grads)
    for block in range(shards):
        here = pl.ds(block * token_rows, token_rows)
        count = (block + 1) * token_rows
        at_col = block * token_rows + lax.broadcasted_iota(jnp.int32, (1, token_rows), 1)
        at_row = lax.broadcasted_iota(jnp.int32, (count, 1), 0)
        bias = jnp.where(
            (at_row <= at_col) & (seg_col[:count, :] == seg_row[:, here]), 0.0, MASK_FILLER
        )
        for pair in range(2):
            lanes = slice(pair * 128, pair * 128 + 128)
            queries = qkv[here, lanes]
            grads = head_grads[here, lanes]
            query_grad = jnp.zeros((token_rows, 128), jnp.float32)
            for head in range(2):
                row = 2 * pair + head
                mine = low if head == 0 else jnp.logical_not(low)
                own_queries = jnp.where(mine, queries, jnp.zeros((), jnp.bfloat16))
                own_grads = jnp.where(mine, grads, jnp.zeros((), jnp.bfloat16))
                key, value = keys[pair][head][:count], values[pair][head][:count]
                scores = outer_cols(key, queries) * factor + bias
                probs = jnp.exp(scores - norm_rows[row : row + 1, block * token_rows : count])
                grad_probs = outer_cols(value, grads)
                grad_scores = (probs * (grad_probs - turned[row : row + 1, here])).astype(
                    jnp.bfloat16
                )
                value_grads[pair, :count, :] += dot_rows(probs.astype(jnp.bfloat16), own_grads)
                key_grads[pair, :count, :] += dot_rows(grad_scores, own_queries)
                query_grad = query_grad + inner_rows(grad_scores, key)
            qkv_grads[here, lanes] = (query_grad * factor).astype(jnp.bfloat16)
        if block > 0:
            for line in mix_order[4 * block - 2 : 4 * block + 2]:
                mix.fold(*line)

    def fold_heads(first, second):
        return jnp.where(
            low,
            first + pltpu.roll(first, HEAD_SIZE, 1),
            second + pltpu.roll(second, HEAD_SIZE, 1),
        )

    qkv_grads[:, q_cols : q_cols + k_cols] = (
        fold_heads(key_grads[0], key_grads[1]) * factor
    ).astype(jnp.bfloat16)
    qkv_grads[:, q_cols + k_cols :] = fold_heads(value_grads[0], value_grads[1]).astype(
        jnp.bfloat16
    )

    normed_scatter = CtxScatter(
        place,
        lambda y, part: normed_part.at[2 * y + 1 - place.half],
        lambda y, part: normed_part.at[2 * y + place.half],
        lambda lane, part: normed_swapped.at[lane],
        lambda part: normed_crossed,
        1,
        normed_send,
        normed_recv,
    )
    gain_one_sum = jnp.zeros((1, width), jnp.float32)
    main_sum = jnp.zeros((width, main_cols), jnp.float32)
    for block in range(shards):
        here = pl.ds(block * token_rows, token_rows)
        grads = outer_cols(qkv_grads[here, :], full[:, :main_cols])
        normed_part[block] = grads.astype(jnp.bfloat16)
        own = to_f32(all_tokens[block])
        scaled = own * rms_scale(own)
        gain_one_sum = gain_one_sum + jnp.sum(grads * scaled, 0, keepdims=True)
        normed = (scaled * gain_one_row).astype(jnp.bfloat16)
        main_sum = main_sum + inner_rows(normed, qkv_grads[here, :])
    normed_scatter.swap(False, 0).start()
    normed_scatter.swap(True, 0).start()
    at_sub = lax.broadcasted_iota(jnp.int32, (128, 1), 0)
    gain_rows = jnp.where(
        at_sub == EXPERTS, gain_one_sum, jnp.where(at_sub == EXPERTS + 1, gain_two_sum, 0.0)
    )
    side = jnp.concatenate([router_sum, gain_rows[EXPERTS:, :]], 0).T
    sums[:, :, :, :main_cols] = main_sum.astype(jnp.bfloat16).reshape(
        shards, groups, rows, main_cols
    )
    sums[:, :, :, main_cols:] = side.astype(jnp.bfloat16).reshape(
        shards, groups, rows, pack_cols - main_cols
    )
    sum_scatter = ExpScatter(
        place,
        lambda line, part: sums.at[:, line * 2 + 1 - place.x],
        lambda line, part: sums.at[:, line * 2 + place.x],
        lambda line, part: sums_crossed.at[line],
        lambda line, part: sums_raised.at[raised_slot(line)],
        lambda line, part: sums_lowered.at[lowered_slot(line)],
        1,
        (sum_xs, sum_xr, sum_ls, sum_lr),
    )
    for line in order:
        sum_scatter.begin(line, 0)
    normed_scatter.fold(0)
    for line in order:
        out_scatter.fold(line, 0)
    size = mixed_out.shape[0] // mix_parts
    for part in range(mix_parts):
        mixed_out[pl.ds(part * size, size), :] = (
            resid[pl.ds(token_rows - (mix_parts - part) * size, size), :] + mix.total(part)
        ).astype(jnp.bfloat16)
    for line in order:
        sum_scatter.fold(line, 0)
    output_sum[...] = out_scatter.total(0)
    stores = []
    for part in range(local_experts):
        slot = part % 2
        if part >= 2:
            for copy in stores[2 * (part - 2) : 2 * (part - 1)]:
                copy.wait()
        into.arrived(part)
        downs.arrived(part)
        in_stage[slot] = into.total(part)
        down_stage[slot] = downs.total(part)
        for kind, (source, target) in enumerate(
            ((in_stage.at[slot], in_sum.at[part]), (down_stage.at[slot], down_sum.at[part]))
        ):
            copy = pltpu.make_async_copy(source, target, store_sem.at[kind, part])
            copy.start()
            stores.append(copy)
    sums_own[...] = sum_scatter.total(0).astype(jnp.bfloat16)
    sums_all[ctx] = sums_own[ctx]
    copies = []
    for lane, to in enumerate((place.core, place.side, place.far)):
        copy = remote(
            sums_own.at[to[0]], sums_all.at[ctx], last_send.at[lane], last_recv.at[lane], to
        )
        copy.start()
        copies.append(copy)
    normed_scatter.arrived(0)
    grad_normed = normed_scatter.total(0)
    own = to_f32(tokens[...])
    scale = rms_scale(own)
    weighted = grad_normed * gain_one_row
    grad_tokens[...] = (
        grad_resid[...]
        + scale * weighted
        - own * (scale * scale * scale) * jnp.mean(weighted * own, -1, keepdims=True)
    )
    for lane, to in enumerate((place.core, place.side, place.far)):
        remote(
            sums_own.at[0], sums_all.at[to[0]], last_send.at[lane], last_recv.at[lane], to
        ).wait_recv()
    side = jnp.zeros((rows, pack_cols - main_cols), jnp.float32)
    for shard in range(shards):
        came = to_f32(sums_all[shard])
        query_sum[:, shard * q_cols : (shard + 1) * q_cols] = came[:, :q_cols]
        key_sum[:, shard * k_cols : (shard + 1) * k_cols] = came[:, q_cols : q_cols + k_cols]
        value_sum[:, shard * k_cols : (shard + 1) * k_cols] = came[:, q_cols + k_cols : main_cols]
        side = side + came[:, main_cols:]
    side_sum[...] = side
    for copy in stores[-4:]:
        copy.wait()
    for copy in copies:
        copy.wait_send()
    for scatter in (mix, into, downs, out_scatter, normed_scatter, sum_scatter):
        scatter.finish()
    for part in range(moe_parts):
        resid_gather.sent(part)


def back(
    moe_in_grads, mixed_part, grad_in, grad_down, tokens, cot, resid, gain_two, gain_one, logit_grads,
    all_moe, all_tokens, weights, out_rows, qkv, heads_out, log_norm, seg_col, seg_row,
):
    token_rows, width = tokens.shape
    shards, groups, rows, pack_cols = weights.shape
    seq_len = shards * token_rows
    q_cols, main_cols = heads_out.shape[1], qkv.shape[1]
    k_cols = (main_cols - q_cols) // 2
    experts, _, in_rows, in_cols = grad_in.shape
    down_rows = grad_down.shape[2]
    low, f32 = jnp.bfloat16, jnp.float32

    def shape(dims, dtype):
        return jax.ShapeDtypeStruct(dims, dtype)

    whole, anywhere = pl.BlockSpec(memory_space=VMEM), pl.BlockSpec(memory_space=pl.ANY)
    mix_rows = mixed_part.shape[1]
    block, steps = (LINES, mix_rows, width), (LINES - 1, mix_rows, width)
    pack = (shards, rows, pack_cols)
    return pl.pallas_call(
        back_kernel,
        name="back",
        out_shape=[
            shape((mixed_part.shape[1], width), low),
            shape((token_rows, width), f32),
            shape((rows, shards * q_cols), f32),
            shape((rows, shards * k_cols), f32),
            shape((rows, shards * k_cols), f32),
            shape((rows, pack_cols - main_cols), f32),
            shape((rows, width), f32),
            shape((experts, in_rows, in_cols), f32),
            shape((experts, down_rows, width), f32),
        ],
        in_specs=[whole] + [anywhere] * 3 + [whole] * 6 + [anywhere] * 8 + [whole],
        out_specs=[whole] * 7 + [anywhere] * 2,
        scratch_shapes=[
            VMEM(block, low),
            VMEM(block, low),
            VMEM(steps, low),
            VMEM(steps, low),
            VMEM((2, experts, in_rows, in_cols), low),
            VMEM((2, experts, in_rows, in_cols), low),
            VMEM((experts, in_rows, in_cols), low),
            VMEM((2, experts, down_rows, width), low),
            VMEM((2, experts, down_rows, width), low),
            VMEM((experts, down_rows, width), low),
            VMEM((token_rows, width), f32),
            VMEM((shards, token_rows, width), low),
            VMEM((seq_len, q_cols), low),
            VMEM((128, seq_len), f32),
            VMEM((2, seq_len, 128), f32),
            VMEM((2, seq_len, 128), f32),
            VMEM((seq_len, main_cols), low),
            VMEM((shards, token_rows, width), low),
            VMEM((2, token_rows, width), low),
            VMEM((token_rows, width), low),
            VMEM((shards, groups, rows, pack_cols), low),
            VMEM((LINES,) + pack, low),
            *[VMEM((LINES - 1,) + pack, low)] * 2,
            VMEM((shards, rows, pack_cols), low),
            VMEM((shards, rows, pack_cols), low),
            VMEM((groups, rows, width), low),
            VMEM((LINES, rows, width), low),
            *[VMEM((LINES - 1, rows, width), low)] * 2,
            VMEM((2, in_rows, in_cols), f32),
            VMEM((2, down_rows, width), f32),
            DMA((2, experts)),
            VMEM(all_moe.shape, low),
            VMEM(all_tokens.shape, low),
            VMEM(weights.shape, low),
            VMEM(out_rows.shape, low),
            VMEM(qkv.shape, low),
            VMEM(heads_out.shape, f32),
            VMEM(log_norm.shape, f32),
            VMEM(seg_col.shape, jnp.int32),
            DMA((8,)),
            DMA((8,)),
            *scatter_sems(2),
            *scatter_sems(1),
            *scatter_sems(1),
            *square_sems(experts),
            *square_sems(experts),
            *square_sems(1),
            *square_sems(4),
            DMA((3,)),
            DMA((3,)),
        ],
        compiler_params=pltpu.CompilerParams(
            collective_id=2, has_side_effects=True, vmem_limit_bytes=62 * 2**20
        ),
    )(
        moe_in_grads, mixed_part, grad_in, grad_down, tokens, cot, resid, gain_two, gain_one, logit_grads,
        all_moe, all_tokens, weights, out_rows, qkv, heads_out, log_norm, seg_col, seg_row,
    )


def two_parts(values):
    high = values.astype(jnp.bfloat16)
    return high, (values - high.astype(jnp.float32)).astype(jnp.bfloat16)


def by_heads(
    tokens,
    segments,
    routes,
    gain_attn,
    gain_moe,
    query_weight,
    key_weight,
    value_weight,
    w_output,
    w_router,
    w_expert_in,
    w_expert_out,
    cotangent,
):
    shards = lax.axis_size("ctx")
    groups = lax.axis_size("exp")
    local_experts = EXPERTS // groups
    width = tokens.shape[2]
    rows = query_weight.shape[0]
    q_cols = query_weight.shape[1] // shards
    k_cols = key_weight.shape[1] // shards
    main_cols = q_cols + 2 * k_cols
    side = 128

    side_cols = jnp.concatenate(
        [
            w_router,
            gain_attn[:, None],
            gain_moe[:, None],
            jnp.zeros((rows, side - EXPERTS - 2), jnp.bfloat16),
        ],
        1,
    )
    seg_col, seg_row = segments[0][:, None], segments
    (
        all_moe,
        all_cot,
        all_routes,
        all_in,
        all_out,
        all_tokens,
        all_weights,
        out_rows,
        qkv,
        heads_out,
        log_norm,
        resid,
        side_rows,
    ) = front(
        tokens[0],
        side_cols,
        query_weight,
        key_weight,
        value_weight,
        w_output,
        routes[0].T,
        seg_col,
        seg_row,
        cotangent[0],
        w_expert_in,
        w_expert_out,
    )
    expert_in = all_in.reshape(local_experts, width, -1)
    expert_out = all_out.reshape(local_experts, FF, -1)
    gains = side_rows[EXPERTS : EXPERTS + 2].astype(jnp.float32)
    (
        grad_moe_in,
        mixed_first,
        mixed_rest,
        logit_grads,
        in_first,
        down_first,
        in_rest,
        down_rest,
    ) = experts(all_moe, all_cot, cotangent[0], all_routes, expert_in, expert_out, side_rows, resid)
    rest = in_rest.shape[0]
    (
        mixed_last,
        grad_tokens,
        query_sum,
        key_sum,
        value_sum,
        side_sum,
        output_sum,
        in_sum,
        down_sum,
    ) = back(
        grad_moe_in,
        mixed_rest,
        in_rest.reshape((rest,) + all_in.shape[1:]),
        down_rest.reshape((rest,) + all_out.shape[1:]),
        tokens[0],
        cotangent[0],
        resid,
        gains[1:2],
        gains[0:1],
        logit_grads,
        all_moe,
        all_tokens,
        all_weights,
        out_rows,
        qkv,
        heads_out,
        log_norm,
        seg_col,
        seg_row,
    )
    return (
        jnp.concatenate([mixed_first, mixed_last], 0)[None],
        grad_tokens[None],
        side_sum[:, EXPERTS],
        side_sum[:, EXPERTS + 1],
        query_sum,
        key_sum,
        value_sum,
        output_sum,
        side_sum[:, :EXPERTS],
        jnp.concatenate([in_first, in_sum], 0),
        jnp.concatenate([down_first, down_sum], 0),
    )


def solution(mesh):
    sizes = (mesh.shape["ctx"], mesh.shape["exp"])
    return jax.shard_map(
        by_heads if sizes == (4, 8) else local,
        mesh=mesh,
        in_specs=(
            P("exp", "ctx", None),
            P("exp", None),
            P("exp", "ctx", None),
            P(("ctx", "exp")),
            P(("ctx", "exp")),
            P(("ctx", "exp"), None),
            P(("ctx", "exp"), None),
            P(("ctx", "exp"), None),
            P(("ctx", "exp"), None),
            P(("ctx", "exp"), None),
            P("exp", "ctx", None),
            P("exp", "ctx", None),
            P("exp", "ctx", None),
        ),
        out_specs=(
            P("exp", "ctx", None),
            P("exp", "ctx", None),
            P(("ctx", "exp")),
            P(("ctx", "exp")),
            P(("ctx", "exp"), None),
            P(("ctx", "exp"), None),
            P(("ctx", "exp"), None),
            P(("ctx", "exp"), None),
            P(("ctx", "exp"), None),
            P("exp", "ctx", None),
            P("exp", "ctx", None),
        ),
        check_vma=False,
    )
```

```python
import math

import jax
import jax.numpy as jnp
from jax import lax
from jax.experimental import pallas as pl
from jax.experimental.pallas import tpu as pltpu
from jax.sharding import PartitionSpec as P

QUERY_HEADS = 16
KEY_VALUE_HEADS = 8
HEAD_SIZE = 64
EXPERTS = 32
TOPK = 8
FF = 512
CAP = 72


EPSILON = 1e-06
MASK_FILLER = -1e30


def rms_scale(values):
    return lax.rsqrt(jnp.mean(values * values, -1, keepdims=True) + EPSILON)


def inner_rows(left, right):
    return lax.dot_general(
        left, right, (((0,), (0,)), ((), ())), preferred_element_type=jnp.float32
    )


def outer_cols(left, right):
    return lax.dot_general(
        left, right, (((1,), (1,)), ((), ())), preferred_element_type=jnp.float32
    )


def allowed_block(query_pos, query_seg, seg_all, offset, key_total_count):
    key_pos = offset + jnp.arange(key_total_count, dtype=jnp.int32)
    key_seg = lax.dynamic_slice_in_dim(seg_all, offset, key_total_count)
    return (key_pos[None, :] <= query_pos[:, None]) & (key_seg[None, :] == query_seg[:, None])


def head_scores(heads_of_queries, key_segment_slice, factor):
    key_total_count = key_segment_slice.shape[0]
    heads_of_keys = key_segment_slice.reshape(key_total_count, KEY_VALUE_HEADS, -1)
    return (
        jnp.einsum(
            "ihgd,jhd->hgij", heads_of_queries, heads_of_keys, preferred_element_type=jnp.float32
        )
        * factor
    )


def slot_tables(pair_ids):
    pair_count = pair_ids.shape[0]
    member = (pair_ids[:, None] == jnp.arange(EXPERTS, dtype=jnp.int32)[None, :]).astype(jnp.int32)
    earlier = jnp.cumsum(member, 0) - member
    slot_place = jnp.sum(earlier * member, 1, dtype=jnp.int32)
    is_kept = slot_place < CAP
    slot_index = jnp.where(is_kept, pair_ids * CAP + slot_place, EXPERTS * CAP)
    slot_filler = (
        jnp.full((EXPERTS * CAP,), -1, jnp.int32)
        .at[slot_index]
        .set(jnp.arange(pair_count, dtype=jnp.int32), mode="drop")
    )
    return (slot_index, is_kept, slot_filler)


def local(
    tokens,
    segments,
    routes,
    gain_attn,
    gain_moe,
    query_weight,
    key_weight,
    value_weight,
    w_output,
    w_router,
    w_expert_in,
    w_expert_out,
    cotangent,
):
    shards = lax.axis_size("ctx")
    groups = lax.axis_size("exp")
    ctx_rank = lax.axis_index("ctx")
    gain_one, gain_two, full_query, full_key, full_value, full_output, full_router = (
        lax.all_gather(gain_attn, ("ctx", "exp"), axis=0, tiled=True),
        lax.all_gather(gain_moe, ("ctx", "exp"), axis=0, tiled=True),
        lax.all_gather(query_weight, ("ctx", "exp"), axis=0, tiled=True),
        lax.all_gather(key_weight, ("ctx", "exp"), axis=0, tiled=True),
        lax.all_gather(value_weight, ("ctx", "exp"), axis=0, tiled=True),
        lax.all_gather(w_output, ("ctx", "exp"), axis=0, tiled=True),
        lax.all_gather(w_router, ("ctx", "exp"), axis=0, tiled=True),
    )
    expert_in, expert_out = (
        lax.all_gather(w_expert_in, "ctx", axis=1, tiled=True),
        lax.all_gather(w_expert_out, "ctx", axis=1, tiled=True),
    )
    inputs = tokens[0].astype(jnp.float32)
    token_rows = inputs.shape[0]
    seq_len = token_rows * shards
    head_cluster = QUERY_HEADS // KEY_VALUE_HEADS
    factor = 1.0 / math.sqrt(HEAD_SIZE)
    kv_width = key_weight.shape[1]
    seg_all = segments[0]
    query_pos = ctx_rank * token_rows + jnp.arange(token_rows, dtype=jnp.int32)
    query_seg = lax.dynamic_slice_in_dim(seg_all, ctx_rank * token_rows, token_rows)
    scale_one = rms_scale(inputs)
    gain_one_f = gain_one.astype(jnp.float32)
    normalized_input = (inputs * scale_one * gain_one_f).astype(jnp.bfloat16)
    query_matrix = jnp.dot(normalized_input, full_query, preferred_element_type=jnp.float32).astype(
        jnp.bfloat16
    )
    key_rows = jnp.dot(normalized_input, full_key, preferred_element_type=jnp.float32).astype(
        jnp.bfloat16
    )
    value_rows = jnp.dot(normalized_input, full_value, preferred_element_type=jnp.float32).astype(
        jnp.bfloat16
    )
    heads_of_queries = query_matrix.reshape(token_rows, KEY_VALUE_HEADS, head_cluster, HEAD_SIZE)
    group_size = math.gcd(shards, max(1, 1024 // token_rows))
    key_range_width = group_size * token_rows
    turns_needed = ctx_rank // group_size + 1
    running_maximum = jnp.full(
        (KEY_VALUE_HEADS, head_cluster, token_rows), MASK_FILLER, jnp.float32
    )
    key_segment_slice = lax.all_gather(key_rows, "ctx", axis=0, tiled=True)
    value_segment_slice = lax.all_gather(value_rows, "ctx", axis=0, tiled=True)
    key_total_count = key_segment_slice.shape[0]
    scores = head_scores(heads_of_queries, key_segment_slice, factor)
    allowed = allowed_block(query_pos, query_seg, seg_all, jnp.int32(0), key_total_count)
    scores = jnp.where(allowed, scores, MASK_FILLER)
    new_max = jnp.maximum(running_maximum, jnp.max(scores, -1))
    weights = jnp.where(allowed, jnp.exp(scores - new_max[..., None]), 0.0)
    run_sum = jnp.sum(weights, -1)
    heads_of_values = value_segment_slice.reshape(key_total_count, KEY_VALUE_HEADS, HEAD_SIZE)
    run_acc = jnp.einsum(
        "hgij,jhd->ihgd",
        weights.astype(jnp.bfloat16),
        heads_of_values,
        preferred_element_type=jnp.float32,
    )
    running_maximum, run_sum, run_acc = (new_max, run_sum, run_acc)
    log_norm = running_maximum + jnp.log(run_sum)
    heads_out = run_acc / jnp.transpose(run_sum, (2, 0, 1))[..., None]
    attn_low = heads_out.reshape(token_rows, -1).astype(jnp.bfloat16)
    resid = inputs + jnp.dot(attn_low, full_output, preferred_element_type=jnp.float32)
    scale_two = rms_scale(resid)
    gain_two_f = gain_two.astype(jnp.float32)
    moe_in = (resid * scale_two * gain_two_f).astype(jnp.bfloat16)
    logits = jnp.dot(moe_in, full_router, preferred_element_type=jnp.float32)
    route_ids = routes[0]
    one_hot = (route_ids[:, :, None] == jnp.arange(EXPERTS, dtype=jnp.int32)[None, None, :]).astype(
        jnp.float32
    )
    chosen = jnp.sum(one_hot * logits[:, None, :], -1)
    gates = jax.nn.softmax(chosen, axis=-1)
    slot_index, is_kept, slot_filler = slot_tables(route_ids.reshape(-1))
    filled = slot_filler >= 0
    token_of = jnp.maximum(slot_filler, 0) // TOPK
    local_experts = EXPERTS // groups
    send_rows = jnp.where(
        filled[:, None], jnp.take(moe_in, token_of, axis=0), jnp.zeros((), jnp.bfloat16)
    )
    send_rows = send_rows.reshape(groups, local_experts, CAP, -1)
    received = lax.all_to_all(send_rows, "exp", split_axis=0, concat_axis=0, tiled=True)
    pre = jnp.einsum("sjcd,jdf->sjcf", received, expert_in, preferred_element_type=jnp.float32)
    gate_part = pre[..., :FF]
    up_part = pre[..., FF:]
    hidden = (jax.nn.silu(gate_part) * up_part).astype(jnp.bfloat16)
    expert_rows = jnp.einsum(
        "sjcf,jfd->sjcd", hidden, expert_out, preferred_element_type=jnp.float32
    ).astype(jnp.bfloat16)
    returned = lax.all_to_all(expert_rows, "exp", split_axis=0, concat_axis=0, tiled=True).reshape(
        EXPERTS * CAP, -1
    )
    safe_slot = jnp.minimum(slot_index, EXPERTS * CAP - 1)
    picked = jnp.where(
        is_kept[:, None], jnp.take(returned, safe_slot, axis=0), jnp.zeros((), jnp.bfloat16)
    )
    picked = picked.astype(jnp.float32).reshape(token_rows, TOPK, -1)
    branch = jnp.sum(gates[:, :, None] * picked, 1)
    mixed_out = (resid + branch).astype(jnp.bfloat16)
    grad_out = cotangent[0].astype(jnp.float32)
    grad_picked = jnp.sum(grad_out[:, None, :] * picked, -1)
    grad_chosen = gates * (grad_picked - jnp.sum(gates * grad_picked, -1, keepdims=True))
    grad_logits = jnp.sum(one_hot * grad_chosen[:, :, None], 1)
    slot_gate = jnp.where(filled, jnp.take(gates.reshape(-1), jnp.maximum(slot_filler, 0)), 0.0)
    grad_send = (slot_gate[:, None] * jnp.take(grad_out, token_of, axis=0)).astype(jnp.bfloat16)
    grad_send = grad_send.reshape(groups, local_experts, CAP, -1)
    grad_rows = lax.all_to_all(grad_send, "exp", split_axis=0, concat_axis=0, tiled=True)
    grad_hidden = jnp.einsum(
        "sjcd,jfd->sjcf", grad_rows, expert_out, preferred_element_type=jnp.float32
    )
    sigmoid_gate = jax.nn.sigmoid(gate_part)
    grad_gate = grad_hidden * up_part * sigmoid_gate * (1.0 + gate_part * (1.0 - sigmoid_gate))
    grad_up = grad_hidden * gate_part * sigmoid_gate
    grad_pre = jnp.concatenate([grad_gate, grad_up], -1).astype(jnp.bfloat16)
    grad_expert_out = jnp.einsum(
        "sjcf,sjcd->jfd", hidden, grad_rows, preferred_element_type=jnp.float32
    )
    grad_expert_in = jnp.einsum(
        "sjcd,sjcf->jdf", received, grad_pre, preferred_element_type=jnp.float32
    )
    grad_received = jnp.einsum(
        "sjcf,jdf->sjcd", grad_pre, expert_in, preferred_element_type=jnp.float32
    ).astype(jnp.bfloat16)
    grad_back = lax.all_to_all(
        grad_received, "exp", split_axis=0, concat_axis=0, tiled=True
    ).reshape(EXPERTS * CAP, -1)
    grad_pairs = jnp.where(
        is_kept[:, None], jnp.take(grad_back, safe_slot, axis=0), jnp.zeros((), jnp.bfloat16)
    )
    grad_pairs = grad_pairs.astype(jnp.float32).reshape(token_rows, TOPK, -1)
    grad_moe_in = (
        jnp.sum(grad_pairs, 1)
        + outer_cols(grad_logits.astype(jnp.bfloat16), full_router) * 0.0
        + lax.dot_general(
            grad_logits,
            full_router.astype(jnp.float32),
            (((1,), (1,)), ((), ())),
            precision=lax.Precision.HIGHEST,
            preferred_element_type=jnp.float32,
        )
    )
    grad_router = lax.dot_general(
        moe_in.astype(jnp.float32),
        grad_logits,
        (((0,), (0,)), ((), ())),
        precision=lax.Precision.HIGHEST,
        preferred_element_type=jnp.float32,
    )
    weighted_two = grad_moe_in * gain_two_f
    grad_gain_two = jnp.sum(grad_moe_in * resid * scale_two, 0)
    cube_two = scale_two * scale_two * scale_two
    grad_resid = (
        grad_out
        + scale_two * weighted_two
        - resid * cube_two * jnp.mean(weighted_two * resid, -1, keepdims=True)
    )
    grad_resid_low = grad_resid.astype(jnp.bfloat16)
    grad_output_w = inner_rows(attn_low, grad_resid_low)
    grad_heads = (
        outer_cols(grad_resid_low, full_output)
        .astype(jnp.bfloat16)
        .reshape(token_rows, KEY_VALUE_HEADS, head_cluster, HEAD_SIZE)
    )
    delta = jnp.transpose(jnp.sum(grad_heads.astype(jnp.float32) * heads_out, -1), (1, 2, 0))
    all_keys, all_values = (
        lax.all_gather(key_rows, "ctx", axis=0, tiled=True),
        lax.all_gather(value_rows, "ctx", axis=0, tiled=True),
    )

    def block_grads(offset):
        key_segment_slice = lax.dynamic_slice_in_dim(all_keys, offset, key_range_width)
        value_segment_slice = lax.dynamic_slice_in_dim(all_values, offset, key_range_width)
        scores = head_scores(heads_of_queries, key_segment_slice, factor)
        allowed = allowed_block(query_pos, query_seg, seg_all, offset, key_range_width)
        probs_full = jnp.where(allowed, jnp.exp(scores - log_norm[..., None]), 0.0)
        heads_of_keys = key_segment_slice.reshape(key_range_width, KEY_VALUE_HEADS, HEAD_SIZE)
        heads_of_values = value_segment_slice.reshape(key_range_width, KEY_VALUE_HEADS, HEAD_SIZE)
        grad_probs = jnp.einsum(
            "ihgd,jhd->hgij", grad_heads, heads_of_values, preferred_element_type=jnp.float32
        )
        grad_scores = (probs_full * (grad_probs - delta[..., None])).astype(jnp.bfloat16)
        query_part = jnp.einsum(
            "hgij,jhd->ihgd", grad_scores, heads_of_keys, preferred_element_type=jnp.float32
        )
        return (probs_full, grad_scores, query_part)

    query_begin_index = jnp.zeros(
        (token_rows, KEY_VALUE_HEADS, head_cluster, HEAD_SIZE), jnp.float32
    )

    def back_turn(turn, running):
        grad_query_acc, key_grad_buf = running
        offset = turn * key_range_width
        probs_full, grad_scores, query_part = block_grads(offset)
        grad_key_part = (
            jnp.einsum(
                "hgij,ihgd->jhd", grad_scores, heads_of_queries, preferred_element_type=jnp.float32
            )
            * factor
        )
        grad_value_part = jnp.einsum(
            "hgij,ihgd->jhd",
            probs_full.astype(jnp.bfloat16),
            grad_heads,
            preferred_element_type=jnp.float32,
        )
        joined = jnp.concatenate(
            [
                grad_key_part.reshape(key_range_width, -1),
                grad_value_part.reshape(key_range_width, -1),
            ],
            1,
        )
        key_grad_buf = lax.dynamic_update_slice_in_dim(key_grad_buf, joined, offset, 0)
        return (grad_query_acc + query_part, key_grad_buf)

    back_start = (query_begin_index, jnp.zeros((seq_len, 2 * kv_width), jnp.float32))
    grad_query_acc, key_grad_buf = lax.fori_loop(0, turns_needed, back_turn, back_start)
    own_grads = lax.psum_scatter(
        key_grad_buf.astype(jnp.bfloat16), "ctx", scatter_dimension=0, tiled=True
    ).astype(jnp.float32)
    grad_keys = own_grads[:, :kv_width].astype(jnp.bfloat16)
    grad_values = own_grads[:, kv_width:].astype(jnp.bfloat16)
    grad_query = (grad_query_acc * factor).reshape(token_rows, -1).astype(jnp.bfloat16)
    grad_query_w = inner_rows(normalized_input, grad_query)
    grad_key_w = inner_rows(normalized_input, grad_keys)
    grad_value_w = inner_rows(normalized_input, grad_values)
    grad_normed = (
        outer_cols(grad_query, full_query)
        + outer_cols(grad_keys, full_key)
        + outer_cols(grad_values, full_value)
    )
    weighted_one = grad_normed * gain_one_f
    grad_gain_one = jnp.sum(grad_normed * inputs * scale_one, 0)
    cube_one = scale_one * scale_one * scale_one
    grad_inputs = (
        grad_resid
        + scale_one * weighted_one
        - inputs * cube_one * jnp.mean(weighted_one * inputs, -1, keepdims=True)
    )
    dense_sums = (
        lax.psum_scatter(grad_gain_one, ("ctx", "exp"), scatter_dimension=0, tiled=True),
        lax.psum_scatter(grad_gain_two, ("ctx", "exp"), scatter_dimension=0, tiled=True),
        lax.psum_scatter(grad_query_w, ("ctx", "exp"), scatter_dimension=0, tiled=True),
        lax.psum_scatter(grad_key_w, ("ctx", "exp"), scatter_dimension=0, tiled=True),
        lax.psum_scatter(grad_value_w, ("ctx", "exp"), scatter_dimension=0, tiled=True),
        lax.psum_scatter(grad_output_w, ("ctx", "exp"), scatter_dimension=0, tiled=True),
        lax.psum_scatter(grad_router, ("ctx", "exp"), scatter_dimension=0, tiled=True),
    )
    expert_sums = (
        lax.psum_scatter(
            grad_expert_in.astype(jnp.bfloat16), "ctx", scatter_dimension=1, tiled=True
        ).astype(jnp.float32),
        lax.psum_scatter(
            grad_expert_out.astype(jnp.bfloat16), "ctx", scatter_dimension=1, tiled=True
        ).astype(jnp.float32),
    )
    return (mixed_out[None], grad_inputs[None]) + tuple(dense_sums) + tuple(expert_sums)


MESH = pl.DeviceIdType.MESH
VMEM = pltpu.VMEM
DMA = pltpu.SemaphoreType.DMA
COT_LATE = 64
COLUMN = 32
ORDER = (3, 0, 2, 1)
CUTS = ((0, 64), (64, 64), (128, 64), (192, 32))
LINES = 4
GRANT = 56 * 2**20


def to_f32(value):
    return value.astype(jnp.float32)


def dot_rows(left, right):
    return jnp.dot(left, right, preferred_element_type=jnp.float32)


def remote(source, target, send, recv, to):
    return pltpu.make_async_remote_copy(
        src_ref=source,
        dst_ref=target,
        send_sem=send,
        recv_sem=recv,
        device_id=to,
        device_id_type=MESH,
    )


class Place:
    def __init__(self):
        ctx, exp = lax.axis_index("ctx"), lax.axis_index("exp")
        self.ctx, self.exp = ctx, exp
        self.y, self.half = ctx // 2, ctx % 2
        self.z, self.x = exp // 2, exp % 2
        other_half = ctx + 1 - 2 * (ctx % 2)
        self.up, self.down = (ctx, exp + 2), (ctx, exp - 2)
        self.across = (ctx, exp + 1 - 2 * (exp % 2))
        self.core = (other_half, exp)
        self.side = (lax.rem(ctx + 2, 4), exp)
        self.far = (lax.rem(other_half + 2, 4), exp)

    def greet(self, lines=True, square=True):
        barrier = pltpu.get_barrier_semaphore()
        count = jnp.int32(0)
        if square:
            for to in (self.core, self.side, self.far):
                pl.semaphore_signal(barrier, inc=1, device_id=to, device_id_type=MESH)
            count = count + 3
        if lines:
            pl.semaphore_signal(barrier, inc=1, device_id=self.across, device_id_type=MESH)

            @pl.when(self.z < LINES - 1)
            def _():
                pl.semaphore_signal(barrier, inc=1, device_id=self.up, device_id_type=MESH)

            @pl.when(self.z > 0)
            def _():
                pl.semaphore_signal(barrier, inc=1, device_id=self.down, device_id_type=MESH)

            count = count + 1 + jnp.where(self.z < LINES - 1, 1, 0) + jnp.where(self.z > 0, 1, 0)
        pl.semaphore_wait(barrier, count)


class ExpGather:
    def __init__(self, place, view, parts, send, recv):
        self.place, self.view, self.parts = place, view, parts
        self.send, self.recv = send, recv

    def copy(self, lane, line, part, to):
        index = line * 2 + self.place.x
        ref = self.view(index, part)
        return remote(ref, ref, self.send.at[lane, line, part], self.recv.at[index, part], to)

    def pass_on(self, line, part, up, down):
        place = self.place
        if up:

            @pl.when(place.z < LINES - 1)
            def _():
                self.copy(1, line, part, place.up).start()

        if down:

            @pl.when(place.z > 0)
            def _():
                self.copy(2, line, part, place.down).start()

        self.copy(0, line, part, place.across).start()

    def begin(self, part):
        self.pass_on(self.place.z, part, True, True)

    def arrived(self, index, part):
        ref = self.view(index, part)
        remote(
            ref, ref, self.send.at[0, 0, part], self.recv.at[index, part], self.place.across
        ).wait_recv()

    def relay(self, step, part):
        place = self.place

        @pl.when(place.z >= step)
        def _():
            line = place.z - step
            self.arrived(line * 2 + place.x, part)
            self.pass_on(line, part, True, False)

        @pl.when(place.z + step < LINES)
        def _():
            line = place.z + step
            self.arrived(line * 2 + place.x, part)
            self.pass_on(line, part, False, True)

    def relays(self):
        for step in range(1, LINES):
            for part in range(self.parts):
                self.relay(step, part)

    def across_arrived(self, line, part):
        self.arrived(line * 2 + 1 - self.place.x, part)

    def finish(self):
        for part in range(self.parts):
            for line in range(LINES):
                self.across_arrived(line, part)
        self.sent()

    def sent(self):
        place = self.place
        for part in range(self.parts):
            for line in range(LINES):
                self.copy(0, line, part, place.across).wait_send()

                @pl.when((place.z >= line) & (place.z < LINES - 1))
                def _():
                    self.copy(1, line, part, place.up).wait_send()

                @pl.when((place.z <= line) & (place.z > 0))
                def _():
                    self.copy(2, line, part, place.down).wait_send()


def gather_sems(parts):
    return [DMA((3, LINES, parts)), DMA((2 * LINES, parts))]


def raised_slot(line):
    return max(line - 1, 0) if isinstance(line, int) else jnp.maximum(line - 1, 0)


def lowered_slot(line):
    return min(line, LINES - 2) if isinstance(line, int) else jnp.minimum(line, LINES - 2)


class ExpScatter:
    def __init__(self, place, outgoing, mine, crossed, raised, lowered, parts, sems):
        self.place, self.parts = place, parts
        self.outgoing, self.mine = outgoing, mine
        self.crossed, self.raised, self.lowered = crossed, raised, lowered
        self.cross_send, self.cross_recv, self.line_send, self.line_recv = sems

    def cross(self, line, part):
        place = self.place
        return remote(
            self.outgoing(line, part),
            self.crossed(line, part),
            self.cross_send.at[line, part],
            self.cross_recv.at[line, part],
            place.across,
        )

    def along(self, up, line, part):
        place = self.place
        side = 0 if up else 1
        return remote(
            self.mine(line, part),
            (self.raised if up else self.lowered)(line, part),
            self.line_send.at[side, line, part],
            self.line_recv.at[side, line, part],
            place.up if up else place.down,
        )

    def begin(self, line, part):
        self.cross(line, part).start()

    def fold(self, part):
        place = self.place
        for line in ORDER:

            @pl.when(place.z != line)
            def _():
                self.cross(line, part).wait_recv()
                ref = self.mine(line, part)
                ref[...] = (to_f32(ref[...]) + to_f32(self.crossed(line, part)[...])).astype(
                    ref.dtype
                )

    def hop(self, stage, part):
        place = self.place
        for up in (True, False):
            here = stage if up else LINES - 1 - stage
            lines = range(LINES - 1, here, -1) if up else range(here)

            @pl.when(place.z == here)
            def _():
                for line in lines:
                    if stage > 0:
                        self.along(up, line, part).wait_recv()
                        ref = self.mine(line, part)
                        came = (self.raised if up else self.lowered)(line, part)
                        ref[...] = (to_f32(ref[...]) + to_f32(came[...])).astype(ref.dtype)
                    self.along(up, line, part).start()

    def total(self, part):
        place = self.place
        line = place.z
        self.cross(line, part).wait_recv()
        value = to_f32(self.mine(line, part)[...]) + to_f32(self.crossed(line, part)[...])
        for up in (True, False):
            came = (self.raised if up else self.lowered)(line, part)
            some = line > 0 if up else line < LINES - 1

            @pl.when(some)
            def _():
                self.along(up, line, part).wait_recv()

            value = value + jnp.where(some, to_f32(came[...]), 0.0)
        return value

    def finish(self):
        place = self.place
        for part in range(self.parts):
            for line in range(LINES):
                self.cross(line, part).wait_send()
                for up in (True, False):

                    @pl.when(place.z < line if up else place.z > line)
                    def _():
                        self.along(up, line, part).wait_send()


def scatter_sems(parts):
    return [DMA((LINES, parts)), DMA((LINES, parts)), DMA((2, LINES, parts)), DMA((2, LINES, parts))]


class ColumnGather:
    def __init__(self, place, view, send, recv):
        self.place, self.view, self.send, self.recv = place, view, send, recv

    def copy(self, lane, index, to):
        ref = self.view(index)
        return remote(ref, ref, self.send.at[lane, index], self.recv.at[index], to)

    def pass_on(self, index, up, down):
        place = self.place
        if up:

            @pl.when(place.z < LINES - 1)
            def _():
                self.copy(1, index, place.up).start()

        if down:

            @pl.when(place.z > 0)
            def _():
                self.copy(2, index, place.down).start()

    def arrived(self, index):
        ref = self.view(index)
        remote(
            ref, ref, self.send.at[0, index], self.recv.at[index], self.place.across
        ).wait_recv()

    def begin(self):
        self.copy(0, self.place.exp, self.place.across).start()
        self.pass_on(self.place.exp, True, True)

    def turn(self):
        other = self.place.across[1]
        self.arrived(other)
        self.pass_on(other, True, True)

    def relay(self, step):
        place = self.place
        for column in (place.x, 1 - place.x):

            @pl.when(place.z >= step)
            def _():
                index = (place.z - step) * 2 + column
                self.arrived(index)
                self.pass_on(index, True, False)

            @pl.when(place.z + step < LINES)
            def _():
                index = (place.z + step) * 2 + column
                self.arrived(index)
                self.pass_on(index, False, True)

    def sent(self):
        place = self.place
        self.copy(0, place.exp, place.across).wait_send()
        for line in range(LINES):
            for column in range(2):
                index = line * 2 + column

                @pl.when((place.z >= line) & (place.z < LINES - 1))
                def _():
                    self.copy(1, index, place.up).wait_send()

                @pl.when((place.z <= line) & (place.z > 0))
                def _():
                    self.copy(2, index, place.down).wait_send()


def column_sems():
    return [DMA((3, 2 * LINES)), DMA((2 * LINES,))]


class ColumnScatter:
    def __init__(self, place, mine, came, crossed, sems):
        self.place, self.mine, self.came, self.crossed = place, mine, came, crossed
        self.line_send, self.line_recv, self.cross_send, self.cross_recv = sems

    def along(self, up, line, far):
        place = self.place
        side = 0 if up else 1
        slot = raised_slot(line) if up else lowered_slot(line)
        return remote(
            self.mine(line, far),
            self.came(side, far, slot),
            self.line_send.at[side, far, line],
            self.line_recv.at[side, far, line],
            place.up if up else place.down,
        )

    def cross(self):
        return remote(
            self.mine(self.place.z, 1),
            self.crossed,
            self.cross_send.at[0],
            self.cross_recv.at[0],
            self.place.across,
        )

    def hop(self, stage):
        place = self.place
        for up in (True, False):
            here = stage if up else LINES - 1 - stage
            lines = range(LINES - 1, here, -1) if up else range(here)

            @pl.when(place.z == here)
            def _():
                for line in lines:
                    for far in (1, 0):
                        if stage > 0:
                            self.along(up, line, far).wait_recv()
                            ref = self.mine(line, far)
                            slot = raised_slot(line) if up else lowered_slot(line)
                            came = self.came(0 if up else 1, far, slot)
                            ref[...] = (to_f32(ref[...]) + to_f32(came[...])).astype(ref.dtype)
                        self.along(up, line, far).start()

    def line_total(self, far):
        line = self.place.z
        value = to_f32(self.mine(line, far)[...])
        for up in (True, False):
            some = line > 0 if up else line < LINES - 1

            @pl.when(some)
            def _():
                self.along(up, line, far).wait_recv()

            slot = raised_slot(line) if up else lowered_slot(line)
            came = self.came(0 if up else 1, far, slot)
            value = value + jnp.where(some, to_f32(came[...]), 0.0)
        return value

    def turn(self):
        ref = self.mine(self.place.z, 1)
        ref[...] = self.line_total(1).astype(ref.dtype)
        self.cross().start()

    def total(self):
        value = self.line_total(0)
        self.cross().wait_recv()
        return value + to_f32(self.crossed[...])

    def finish(self):
        place = self.place
        self.cross().wait_send()
        for line in range(LINES):
            for far in range(2):
                for up in (True, False):

                    @pl.when(place.z < line if up else place.z > line)
                    def _():
                        self.along(up, line, far).wait_send()


def column_sum_sems():
    return [DMA((2, 2, LINES)), DMA((2, 2, LINES)), DMA((1,)), DMA((1,))]


class CtxGather:
    def __init__(self, place, view, parts, send, recv, own=None):
        self.place, self.view, self.parts = place, view, parts
        self.send, self.recv, self.own = send, recv, own

    def copy(self, lane, part):
        place = self.place
        index = lax.rem(place.ctx + 2, 4) if lane == 2 else place.ctx
        ref = self.view(index, part)
        source = ref if lane == 2 or self.own is None else self.own(part)
        to = place.side if lane == 1 else place.core
        return remote(source, ref, self.send.at[lane, part], self.recv.at[lane, part], to)

    def landed(self, lane, part):
        place = self.place
        index = (place.core, place.side, place.far)[lane][0]
        ref = self.view(index, part)
        return remote(ref, ref, self.send.at[lane, part], self.recv.at[lane, part], place.core)

    def begin(self, part):
        self.copy(1, part).start()
        self.copy(0, part).start()

    def relay(self, part):
        self.landed(1, part).wait_recv()
        self.copy(2, part).start()

    def arrived(self, part):
        self.landed(0, part).wait_recv()
        self.landed(2, part).wait_recv()

    def sent(self, part):
        for lane in range(3):
            self.copy(lane, part).wait_send()


def square_sems(parts):
    return [DMA((3, parts)), DMA((3, parts))]


class CtxScatter:
    def __init__(self, place, outgoing, mine, swapped, crossed, parts, send, recv):
        self.place, self.parts = place, parts
        self.outgoing, self.mine = outgoing, mine
        self.swapped, self.crossed = swapped, crossed
        self.send, self.recv = send, recv

    def swap(self, near, part):
        place = self.place
        y = place.y if near else 1 - place.y
        lane = 0 if near else 1
        return remote(
            self.outgoing(y, part),
            self.swapped(lane, part),
            self.send.at[lane, part],
            self.recv.at[lane, part],
            place.core,
        )

    def over(self, part):
        place = self.place
        return remote(
            self.mine(1 - place.y, part),
            self.crossed(part),
            self.send.at[2, part],
            self.recv.at[2, part],
            place.side,
        )

    def fold(self, part):
        self.swap(False, part).wait_recv()
        ref = self.mine(1 - self.place.y, part)
        ref[...] = (to_f32(ref[...]) + to_f32(self.swapped(1, part)[...])).astype(ref.dtype)
        self.over(part).start()

    def arrived(self, part):
        self.swap(True, part).wait_recv()
        self.over(part).wait_recv()

    def total(self, part, here=slice(None)):
        return (
            to_f32(self.mine(self.place.y, part)[here, :])
            + to_f32(self.swapped(0, part)[here, :])
            + to_f32(self.crossed(part)[here, :])
        )

    def finish(self):
        for part in range(self.parts):
            self.swap(False, part).wait_send()
            self.swap(True, part).wait_send()
            self.over(part).wait_send()


def ahead_kernel(
    tokens,
    side_cols,
    wq,
    wk,
    wv,
    wo,
    routes,
    seg_row,
    cot_hbm,
    in_hbm,
    out_hbm,
    grad_moe_in,
    mixed_part,
    logit_grads,
    in_first,
    down_first,
    in_rest,
    down_rest,
    moe_hbm,
    tokens_hbm,
    weights_hbm,
    out_rows_hbm,
    qkv_hbm,
    heads_hbm,
    norm_rows,
    resid_hbm,
    side_rows,
    moe,
    cot,
    w_in,
    w_out,
    slot_rows,
    slot_cot,
    hidden,
    slopes,
    slot_out,
    pick,
    slot_gate,
    gates,
    all_routes,
    resid_rows,
    moe_crossed,
    moe_raised,
    moe_lowered,
    column_came,
    column_crossed,
    sum_stage,
    load_sem,
    keep_sem,
    store_sem,
    put_sem,
    free_sem,
    tok_send,
    tok_recv,
    swap_send,
    swap_recv,
    w_send,
    w_recv,
    o_send,
    o_recv,
    r_send,
    r_recv,
    c_send,
    c_recv,
    cc_send,
    cc_recv,
    l_send,
    l_recv,
    m_send,
    m_recv,
    mc_send,
    mc_recv,
    i_send,
    i_recv,
    u_send,
    u_recv,
    s_send,
    s_recv,
    moe_xs,
    moe_xr,
    moe_ls,
    moe_lr,
    column_ls,
    column_lr,
    column_xs,
    column_xr,
    in_send,
    in_recv,
    down_send,
    down_recv,
):
    place = Place()
    ctx, exp = place.ctx, place.exp
    groups, token_rows, width = moe.shape
    shards = width // in_hbm.shape[1]
    rows = wq.shape[0]
    q_cols, k_cols = wq.shape[1] // shards, wk.shape[1] // shards
    main_cols = q_cols + 2 * k_cols
    pack_cols = main_cols + side_cols.shape[1]
    local_experts = w_in.shape[0]
    in_rows, down_rows = in_hbm.shape[1], out_hbm.shape[1]
    slots = pick.shape[1] // local_experts
    first = exp * local_experts
    factor = 1.0 / math.sqrt(HEAD_SIZE)

    def token_block(index):
        return slot_rows.at[index, pl.ds(0, token_rows)]

    def partial(index, start, size):
        return slot_rows.at[index, pl.ds(token_rows + start, size)]

    def out_part(index):
        return slot_rows.at[
            index // LINES, pl.ds(2 * token_rows + lax.rem(index, LINES) * rows, rows)
        ]

    def weight_part(index):
        return slot_cot.at[:, pl.ds(index * rows, rows), pl.ds(0, pack_cols)]

    def packed(shard):
        return slot_cot.at[shard, pl.ds(2 * token_rows, rows), pl.ds(0, pack_cols)]

    def swap_space(lane, start, size):
        return slot_cot.at[lane, pl.ds(token_rows + start, size)]

    def qkv_cols(low, count):
        return slopes[:, :token_rows, low : low + count].reshape(shards * token_rows, count)

    own_in = pltpu.make_async_copy(
        in_hbm, w_in.at[:, pl.ds(ctx * in_rows, in_rows)], load_sem.at[0]
    )
    own_out = pltpu.make_async_copy(
        out_hbm, w_out.at[:, pl.ds(ctx * down_rows, down_rows)], load_sem.at[1]
    )
    own_cot = pltpu.make_async_copy(cot_hbm, cot.at[exp], load_sem.at[2])
    for copy in (own_cot, own_in, own_out):
        copy.start()
    token_block(ctx)[...] = tokens[...]
    for shard in range(shards):
        target = packed(shard)
        target[:, :q_cols] = wq[:, shard * q_cols : (shard + 1) * q_cols]
        target[:, q_cols : q_cols + k_cols] = wk[:, shard * k_cols : (shard + 1) * k_cols]
        target[:, q_cols + k_cols : main_cols] = wv[:, shard * k_cols : (shard + 1) * k_cols]
        target[:, main_cols:] = side_cols[...]

    def weight_slot(shard):
        return slot_cot.at[shard, pl.ds(exp * rows, rows), pl.ds(0, pack_cols)]

    weight_slot(ctx)[...] = packed(ctx)[...]
    out_part(exp)[...] = wo[...]
    all_routes[exp] = routes[...]
    place.greet()

    mixes = []
    for lane, to in enumerate((place.core, place.side, place.far)):
        copy = remote(
            packed(to[0]),
            weight_slot(ctx),
            swap_send.at[lane],
            swap_recv.at[lane],
            to,
        )
        copy.start()
        mixes.append(copy)
    half_rows = token_rows // 2
    token_gather = CtxGather(
        place,
        lambda index, part: slot_rows.at[index, pl.ds(part * half_rows, half_rows)],
        2,
        tok_send,
        tok_recv,
    )
    for part in range(2):
        token_gather.begin(part)
    route_gather = ExpGather(place, lambda index, part: all_routes.at[index], 1, r_send, r_recv)
    weight_gather = ExpGather(place, lambda index, part: weight_part(index), 1, w_send, w_recv)
    out_gather = ExpGather(place, lambda index, part: out_part(index), 1, o_send, o_recv)
    for lane, copy in enumerate(mixes):
        source = (place.core, place.side, place.far)[lane][0]
        remote(
            packed(0), weight_slot(source), swap_send.at[lane], swap_recv.at[lane], place.core
        ).wait_recv()
    weight_gather.begin(0)
    route_gather.begin(0)
    out_gather.begin(0)
    in_gather = CtxGather(
        place,
        lambda index, part: w_in.at[part, pl.ds(index * in_rows, in_rows)],
        local_experts,
        i_send,
        i_recv,
    )
    down_gather = CtxGather(
        place,
        lambda index, part: w_out.at[part, pl.ds(index * down_rows, down_rows)],
        local_experts,
        u_send,
        u_recv,
    )
    cot_parts = c_send.shape[2]
    late_rows = COT_LATE
    cot_rows = (token_rows - late_rows - COLUMN) // cot_parts
    cot_gather = ExpGather(
        place,
        lambda index, part: cot.at[index, pl.ds(part * cot_rows, cot_rows)],
        cot_parts,
        c_send,
        c_recv,
    )
    late_gather = ExpGather(
        place,
        lambda index, part: cot.at[index, pl.ds(token_rows - COLUMN - late_rows, late_rows)],
        1,
        l_send,
        l_recv,
    )
    column_rows = pl.ds(token_rows - COLUMN, COLUMN)
    cot_column = ColumnGather(place, lambda index: cot.at[index, column_rows], cc_send, cc_recv)
    own_in.wait()
    half_experts = local_experts // 2
    for part in range(half_experts):
        in_gather.begin(part)
    weight_gather.relay(1, 0)
    token_gather.relay(0)
    weight_gather.relay(2, 0)
    token_gather.relay(1)
    weight_gather.relay(3, 0)
    own_cot.wait()
    own_out.wait()
    for step in range(1, LINES):
        out_gather.relay(step, 0)
        route_gather.relay(step, 0)
    cot_column.begin()
    for part in range(cot_parts):
        cot_gather.begin(part)
    for part in range(2):
        token_gather.arrived(part)
    weight_gather.finish()

    side = pack_cols - main_cols
    same = (
        lax.broadcasted_iota(jnp.int32, (side, side), 0)
        == lax.broadcasted_iota(jnp.int32, (side, side), 1)
    ).astype(jnp.bfloat16)
    full = slot_cot[:, :token_rows, :pack_cols].reshape(width, pack_cols)
    side_t = outer_cols(same, full[:, main_cols:])
    side_rows[...] = side_t.astype(jnp.bfloat16)
    gain_one, gain_two = side_t[EXPERTS : EXPERTS + 1], side_t[EXPERTS + 1 : EXPERTS + 2]
    for block in range(shards):
        values = to_f32(token_block(block)[...])
        normed = (values * rms_scale(values) * gain_one).astype(jnp.bfloat16)
        slopes[block, :token_rows, :main_cols] = dot_rows(normed, full[:, :main_cols]).astype(
            jnp.bfloat16
        )

    low = lax.broadcasted_iota(jnp.int32, (1, 2 * HEAD_SIZE), 1) < HEAD_SIZE

    def spread(start):
        plain = to_f32(qkv_cols(start, k_cols))
        turned = pltpu.roll(plain, HEAD_SIZE, 1)
        zero = jnp.zeros((), jnp.float32)
        return [
            [
                jnp.where(low, plain, zero).astype(jnp.bfloat16),
                jnp.where(low, zero, turned).astype(jnp.bfloat16),
            ],
            [
                jnp.where(low, turned, zero).astype(jnp.bfloat16),
                jnp.where(low, zero, plain).astype(jnp.bfloat16),
            ],
        ]

    keys, values = spread(q_cols), spread(q_cols + k_cols)
    parts = slot_rows.shape[1] - 2 * token_rows
    attn_low = {}
    keep = []
    for block in range(shards - 1, -1, -1):
        count = (block + 1) * token_rows
        at_row = block * token_rows + lax.broadcasted_iota(jnp.int32, (token_rows, 1), 0)
        at_col = lax.broadcasted_iota(jnp.int32, (1, count), 1)
        documents = seg_row[:, block * token_rows : count].astype(jnp.float32)
        own_document = jnp.broadcast_to(documents, (128, token_rows)).T[:, :1]
        bias = jnp.where(
            (at_col <= at_row) & (own_document == seg_row[:, :count].astype(jnp.float32)),
            0.0,
            MASK_FILLER,
        )
        lows = []
        norms = jnp.zeros((token_rows, 128), jnp.float32)
        at_lane = lax.broadcasted_iota(jnp.int32, (1, 128), 1)
        for pair in range(2):
            queries = slopes[block, :token_rows, pair * 128 : pair * 128 + 128]
            heads = jnp.zeros((token_rows, 128), jnp.float32)
            for head in range(2):
                scores = outer_cols(queries, keys[pair][head][:count]) * factor + bias
                top = jnp.max(scores, -1, keepdims=True)
                shares = jnp.exp(scores - top)
                total = jnp.sum(shares, -1, keepdims=True)
                norms = jnp.where(at_lane == 2 * pair + head, top + jnp.log(total), norms)
                heads = heads + dot_rows(
                    shares.astype(jnp.bfloat16), values[pair][head][:count]
                ) / total
            start = block * q_cols + pair * 128
            resid_rows[:, start : start + 128] = heads
            lows.append(heads.astype(jnp.bfloat16))
        norm_rows[:, block * token_rows : count] = norms.T[:8]
        attn_low[block] = jnp.concatenate(lows, 1)
        keep.append(
            pltpu.make_async_copy(
                resid_rows.at[:, pl.ds(block * q_cols, q_cols)],
                heads_hbm.at[pl.ds(block * token_rows, token_rows)],
                keep_sem.at[len(keep)],
            )
        )
        keep[-1].start()
        if block == 2:
            cot_column.turn()
            for part in range(cot_parts):
                cot_gather.relay(1, part)

    out_gather.finish()
    full_out = jnp.concatenate(
        [slot_rows[part, 2 * token_rows :, :] for part in range(q_cols // parts)], 0
    )
    for block in range(shards):
        partial(block, 0, token_rows)[...] = dot_rows(attn_low[block], full_out).astype(
            jnp.bfloat16
        )
    stored = len(keep)
    here = pl.ds(0, token_rows)
    for source, target in (
        (slot_rows.at[:, here], tokens_hbm),
        (slot_cot.at[:, here, pl.ds(0, pack_cols)], weights_hbm),
        (slopes.at[:, here, pl.ds(0, main_cols)], qkv_hbm),
        (slot_rows.at[pl.ds(0, q_cols // parts), pl.ds(2 * token_rows, parts)], out_rows_hbm),
    ):
        keep.append(pltpu.make_async_copy(source, target, keep_sem.at[len(keep)]))
        keep[-1].start()

    branch = CtxScatter(
        place,
        lambda y, part: partial(2 * y + 1 - place.half, part * half_rows, half_rows),
        lambda y, part: partial(2 * y + place.half, part * half_rows, half_rows),
        lambda lane, part: swap_space(lane, part * half_rows, half_rows),
        lambda part: swap_space(2, part * half_rows, half_rows),
        2,
        s_send,
        s_recv,
    )
    for part in range(2):
        branch.swap(False, part).start()
    for part in range(2):
        branch.swap(True, part).start()
    cot_column.relay(1)
    for part in range(cot_parts):
        cot_gather.relay(2, part)
    for part in range(2):
        branch.fold(part)
    for part in range(half_experts, local_experts):
        in_gather.begin(part)
    for part in range(local_experts):
        down_gather.begin(part)
    gather_parts = len(CUTS)
    moe_gather = ExpGather(
        place,
        lambda index, part: moe.at[index, pl.ds(*CUTS[part])],
        gather_parts,
        m_send,
        m_recv,
    )
    moe_column = ColumnGather(place, lambda index: moe.at[index, column_rows], mc_send, mc_recv)
    cot_column.relay(2)
    for copy in keep[:stored]:
        copy.wait()
    for part in range(2):
        here = pl.ds(part * half_rows, half_rows)
        branch.arrived(part)
        resid = to_f32(tokens[here, :]) + branch.total(part)
        resid_rows[here, :] = resid
        moe[exp, here, :] = (resid * rms_scale(resid) * gain_two).astype(jnp.bfloat16)
        if part == 1:
            moe_column.begin()
        for piece, (start, size) in enumerate(CUTS):
            if start // half_rows == part:
                moe_gather.begin(piece)
    keep.append(pltpu.make_async_copy(resid_rows, resid_hbm, keep_sem.at[len(keep)]))
    keep[-1].start()
    cot_column.relay(3)
    for part in range(cot_parts):
        cot_gather.relay(3, part)
    for part in range(half_experts):
        in_gather.relay(part)
    moe_column.turn()
    for step in range(1, LINES):
        for part in range(gather_parts):
            moe_gather.relay(step, part)
        moe_column.relay(step)
    late_gather.begin(0)
    for part in range(half_experts, local_experts):
        in_gather.relay(part)
    route_gather.finish()
    branch.finish()
    for part in range(2):
        token_gather.sent(part)
    for copy in mixes:
        copy.wait_send()
    for copy in keep[stored:]:
        copy.wait()

    at_expert = lax.broadcasted_iota(jnp.int32, (EXPERTS, 1), 0)
    at_lane = lax.broadcasted_iota(jnp.int32, (1, 128), 1)
    at_slot = lax.broadcasted_iota(jnp.int32, (slots, 1), 0)
    before = (
        lax.broadcasted_iota(jnp.int32, (token_rows, token_rows), 0)
        < lax.broadcasted_iota(jnp.int32, (token_rows, token_rows), 1)
    ).astype(jnp.bfloat16)
    router = side_rows[:EXPERTS, :]
    all_slots = groups * slots
    def block_of(line, far):
        return line * 2 + (1 - place.x if far else place.x)

    def slot_range(line, far):
        start = (far * LINES + line) * slots
        return pl.ds(start if isinstance(line, int) else pl.multiple_of(start, slots), slots)

    def dispatch(line, far):
        block = block_of(line, far)
        routes = all_routes[block]
        member = routes[0:1, :] == at_expert
        for rank in range(1, TOPK):
            member = member | (routes[rank : rank + 1, :] == at_expert)
        tokens = moe[block]
        logits = outer_cols(router, tokens)
        top = jnp.max(jnp.where(member, logits, MASK_FILLER), 0, keepdims=True)
        weights = jnp.where(member, jnp.exp(logits - top), 0.0)
        shares = weights / jnp.sum(weights, 0, keepdims=True)
        gates[block] = shares
        ranks = dot_rows(jnp.where(member, 1.0, 0.0).astype(jnp.bfloat16), before)
        filled = jnp.where(member & (ranks < CAP), ranks, -1.0)
        columns = jnp.zeros((slots, 128), jnp.float32)
        for expert in range(local_experts):
            mine = at_expert == first + expert
            spot = jnp.sum(jnp.where(mine, filled, 0.0), 0, keepdims=True)
            share = jnp.sum(jnp.where(mine, shares, 0.0), 0, keepdims=True)
            chosen = spot == at_slot.astype(jnp.float32)
            here = pl.ds(expert * slots, slots)
            pick[block, here, :] = jnp.where(chosen, 1.0, 0.0).astype(jnp.bfloat16)
            column = jnp.sum(jnp.where(chosen, share, 0.0), 1, keepdims=True)
            columns = jnp.where(at_lane == expert, column, columns)
        slot_gate[block] = columns
        chosen = pick[block]
        rows = dot_rows(chosen, tokens).astype(jnp.bfloat16)
        here = slot_range(line, far)
        for expert in range(local_experts):
            slot_rows[expert, here, :] = rows[expert * slots : (expert + 1) * slots]

    half_slots = all_slots // 2

    def each(count, body, far):
        def step(index, carry):
            body(index, far)
            return carry

        lax.fori_loop(0, count, step, 0)

    def near_line(step, carry):
        dispatch(place.z ^ step, 0)
        return carry

    def far_line(step, carry):
        line = place.z ^ step
        for part in range(gather_parts):
            moe_gather.across_arrived(line, part)
        dispatch(line, 1)
        return carry

    lax.fori_loop(0, LINES, near_line, 0)
    for part in range(local_experts):
        down_gather.relay(part)
    for part in range(local_experts):
        in_gather.arrived(part)
        down_gather.arrived(part)
    def forward(expert, far):
        half = pl.ds(far * half_slots, half_slots)
        rows = slot_rows[expert, half, :]
        for first_col in range(0, FF, 256):
            gate_cols, up_cols = pl.ds(first_col, 256), pl.ds(FF + first_col, 256)
            gate_part = dot_rows(rows, w_in[expert, :, gate_cols])
            up_part = dot_rows(rows, w_in[expert, :, up_cols])
            sigmoid_gate = jax.nn.sigmoid(gate_part)
            silu = gate_part * sigmoid_gate
            hidden[expert, half, gate_cols] = (silu * up_part).astype(jnp.bfloat16)
            slopes[expert, half, gate_cols] = (
                up_part * sigmoid_gate * (1.0 + gate_part * (1.0 - sigmoid_gate))
            ).astype(jnp.bfloat16)
            slopes[expert, half, up_cols] = silu.astype(jnp.bfloat16)
        slot_out[expert, half, :] = dot_rows(hidden[expert, half, :], w_out[expert]).astype(
            jnp.bfloat16
        )

    each(local_experts, forward, 0)
    lax.fori_loop(0, LINES, far_line, 0)
    moe_gather.sent()
    moe_column.sent()
    moe_store = pltpu.make_async_copy(moe, moe_hbm, load_sem.at[0])
    moe_store.start()
    late_gather.relay(1, 0)
    each(local_experts, forward, 1)
    late_gather.relay(2, 0)
    moe_store.wait()

    def block_rows(line, far):
        here = slot_range(line, far)
        return jnp.concatenate([slot_out[expert, here, :] for expert in range(local_experts)], 0)

    def combine(line, far):
        block = block_of(line, far)
        shares = gates[block]
        weighted = []
        for expert in range(local_experts):
            mine = at_expert == first + expert
            share = jnp.sum(jnp.where(mine, shares, 0.0), 0, keepdims=True)
            chosen = to_f32(pick[block, pl.ds(expert * slots, slots), :])
            weighted.append((chosen * share).astype(jnp.bfloat16))
        moe[block] = inner_rows(
            jnp.concatenate(weighted, 0), block_rows(line, far)
        ).astype(jnp.bfloat16)

    each(LINES, combine, 0)
    late_gather.relay(3, 0)
    each(LINES, combine, 1)
    part_store = pltpu.make_async_copy(moe, mixed_part, load_sem.at[0])
    part_store.start()

    cot_gather.finish()
    cot_column.sent()
    late_gather.finish()

    def dispatch_back(line, far):
        block = block_of(line, far)
        shares = gates[block]
        chosen = pick[block]
        cots = dot_rows(chosen, cot[block])
        dots = jnp.sum(cots * to_f32(block_rows(line, far)), 1, keepdims=True)
        picked_grads = jnp.zeros_like(shares)
        there = slot_range(line, far)
        for expert in range(local_experts):
            here = slice(expert * slots, (expert + 1) * slots)
            row = jnp.sum(to_f32(chosen[here]) * dots[here], 0, keepdims=True)
            picked_grads = jnp.where(at_expert == first + expert, row, picked_grads)
            share = slot_gate[block, :, expert : expert + 1]
            slot_cot[expert, there, :] = (share * cots[here]).astype(jnp.bfloat16)
        grads = shares * (picked_grads - jnp.sum(shares * picked_grads, 0, keepdims=True))
        high, low = two_parts(grads)
        logit_grads[block] = jnp.concatenate([high, low], 0)

    def backward(expert, far):
        half = pl.ds(far * half_slots, half_slots)
        grads = outer_cols(slot_cot[expert, half, :], w_out[expert])
        slopes[expert, half, :FF] = (grads * to_f32(slopes[expert, half, :FF])).astype(jnp.bfloat16)
        slopes[expert, half, FF:] = (grads * to_f32(slopes[expert, half, FF:])).astype(jnp.bfloat16)
        slot_out[expert, half, :] = outer_cols(slopes[expert, half, :], w_in[expert]).astype(
            jnp.bfloat16
        )

    def combine_back(line, far):
        block = block_of(line, far)
        left = jnp.concatenate([pick[block], logit_grads[block]], 0)
        right = jnp.concatenate([block_rows(line, far), router, router], 0)
        cot[block] = inner_rows(left, right).astype(jnp.bfloat16)

    moe_parts = len(CUTS)

    def piece(ref, part):
        return ref.at[pl.ds(*CUTS[part])]

    back_sum = ExpScatter(
        place,
        lambda line, part: piece(cot.at[line * 2 + 1 - place.x], part),
        lambda line, part: piece(cot.at[line * 2 + place.x], part),
        lambda line, part: piece(moe_crossed.at[line], part),
        lambda line, part: piece(moe_raised.at[raised_slot(line)], part),
        lambda line, part: piece(moe_lowered.at[lowered_slot(line)], part),
        moe_parts,
        (moe_xs, moe_xr, moe_ls, moe_lr),
    )
    column_sum = ColumnScatter(
        place,
        lambda line, far: cot.at[block_of(line, far), column_rows],
        lambda side, far, slot: column_came.at[side, far, slot],
        column_crossed,
        (column_ls, column_lr, column_xs, column_xr),
    )
    each(LINES, dispatch_back, 1)
    each(local_experts, backward, 1)
    each(LINES, combine_back, 1)
    for part in range(moe_parts):
        for line in ORDER:
            back_sum.begin(line, part)
    each(LINES, dispatch_back, 0)
    each(local_experts, backward, 0)
    each(LINES, combine_back, 0)

    for to in (place.core, place.side):
        pl.semaphore_signal(free_sem, inc=1, device_id=to, device_id_type=MESH)

    early = in_first.shape[0]
    for part in range(local_experts):
        in_gather.sent(part)
        down_gather.sent(part)
    into = CtxScatter(
        place,
        lambda y, part: w_in.at[part, pl.ds((2 * y + 1 - place.half) * in_rows, in_rows)],
        lambda y, part: w_in.at[part, pl.ds((2 * y + place.half) * in_rows, in_rows)],
        lambda lane, part: slot_out.at[part, pl.ds(lane * in_rows, in_rows)],
        lambda part: slot_out.at[early + part, pl.ds(2 * down_rows, in_rows)],
        early,
        in_send,
        in_recv,
    )
    downs = CtxScatter(
        place,
        lambda y, part: w_out.at[part, pl.ds((2 * y + 1 - place.half) * down_rows, down_rows)],
        lambda y, part: w_out.at[part, pl.ds((2 * y + place.half) * down_rows, down_rows)],
        lambda lane, part: slot_out.at[early + part, pl.ds(lane * down_rows, down_rows)],
        lambda part: slot_out.at[early + part, pl.ds(2 * down_rows + in_rows, down_rows)],
        early,
        down_send,
        down_recv,
    )
    part_store.wait()
    pl.semaphore_wait(free_sem, 2)
    stores = []

    def store(source, target, sem):
        copy = pltpu.make_async_copy(source, target, sem)
        copy.start()
        stores.append(copy)

    column_sum.hop(0)
    for expert in range(local_experts):
        w_out[expert] = inner_rows(hidden[expert], slot_cot[expert]).astype(jnp.bfloat16)
        if expert < early:
            downs.swap(False, expert).start()
            downs.swap(True, expert).start()
        else:
            store(w_out.at[expert], down_rest.at[expert - early], store_sem.at[0, expert])
        w_in[expert] = inner_rows(slot_rows[expert], slopes[expert]).astype(jnp.bfloat16)
        if expert < early:
            into.swap(False, expert).start()
            into.swap(True, expert).start()
        else:
            store(w_in.at[expert], in_rest.at[expert - early], store_sem.at[1, expert])
        if expert > 0 and expert <= early:
            downs.fold(expert - 1)
            into.fold(expert - 1)
        if expert == 1:
            back_sum.fold(0)
            back_sum.hop(0, 0)
            column_sum.hop(1)
    for part in range(1, moe_parts + 2):
        if part == 1:
            column_sum.hop(2)
        if part == 2:
            column_sum.turn()
        if part >= 2:
            back_sum.hop(2, part - 2)
        if part <= moe_parts:
            back_sum.hop(1, part - 1)
        if part < moe_parts:
            back_sum.fold(part)
            back_sum.hop(0, part)

    staged = [None, None]
    stage_rows = sum_stage.shape[1]

    def put(slot, value, target, sem):
        if staged[slot] is not None:
            staged[slot].wait()
        stage = sum_stage.at[slot, pl.ds(0, value.shape[0])]
        stage[...] = value
        staged[slot] = pltpu.make_async_copy(stage, target, sem)
        staged[slot].start()

    def finish_expert(part):
        into.arrived(part)
        downs.arrived(part)
        slot = 0
        for scatter, target, kind in ((downs, down_first, 0), (into, in_first, 1)):
            for step in range(target.shape[1] // stage_rows):
                here = pl.ds(step * stage_rows, stage_rows)
                put(slot, scatter.total(part, here), target.at[part, here], put_sem.at[slot])
                slot = 1 - slot

    for part in range(early - 1):
        finish_expert(part)
    for part in range(moe_parts):
        here = pl.ds(*CUTS[part])
        put(part % 2, back_sum.total(part), grad_moe_in.at[here], put_sem.at[part % 2])
    put(moe_parts % 2, column_sum.total(), grad_moe_in.at[column_rows], put_sem.at[moe_parts % 2])
    finish_expert(early - 1)
    for copy in staged:
        copy.wait()
    for copy in stores:
        copy.wait()
    for scatter in (back_sum, column_sum, into, downs):
        scatter.finish()


EARLY = 2


def ahead(tokens, side_cols, wq, wk, wv, wo, routes, seg_row, cot, exp_in, exp_out):
    shards, groups = lax.axis_size("ctx"), lax.axis_size("exp")
    token_rows, width = tokens.shape
    rows = wq.shape[0]
    q_cols, k_cols = wq.shape[1] // shards, wk.shape[1] // shards
    main_cols = q_cols + 2 * k_cols
    pack_cols = main_cols + side_cols.shape[1]
    seq_len = token_rows * shards
    low, f32 = jnp.bfloat16, jnp.float32
    local_experts, in_rows, in_cols = exp_in.shape
    down_rows = exp_out.shape[1]
    slots = -(-CAP // 16) * 16
    arena = (local_experts, groups * slots)

    def shape(dims, dtype):
        return jax.ShapeDtypeStruct(dims, dtype)

    whole, anywhere = pl.BlockSpec(memory_space=VMEM), pl.BlockSpec(memory_space=pl.ANY)
    rest = local_experts - EARLY
    block, steps = (LINES, token_rows, width), (LINES - 1, token_rows, width)
    out_parts = groups * slots - 2 * token_rows
    return pl.pallas_call(
        ahead_kernel,
        name="ahead",
        out_shape=[
            shape((token_rows, width), f32),
            shape((groups, token_rows, width), low),
            shape((groups, 2 * EXPERTS, token_rows), low),
            shape((EARLY, in_rows, in_cols), f32),
            shape((EARLY, down_rows, width), f32),
            shape((rest, width, in_cols), low),
            shape((rest, FF, width), low),
            shape((groups, token_rows, width), low),
            shape((shards, token_rows, width), low),
            shape((shards, groups * rows, pack_cols), low),
            shape((q_cols // out_parts, out_parts, width), low),
            shape((shards, token_rows, main_cols), low),
            shape((seq_len, q_cols), f32),
            shape((8, seq_len), f32),
            shape((token_rows, width), f32),
            shape((side_cols.shape[1], width), low),
        ],
        in_specs=[whole] * 8 + [anywhere] * 3,
        out_specs=[anywhere, anywhere, whole]
        + [anywhere] * 10
        + [whole, anywhere, whole],
        scratch_shapes=[
            VMEM((groups, token_rows, width), low),
            VMEM((groups, token_rows, width), low),
            VMEM((local_experts, width, in_cols), low),
            VMEM((local_experts, FF, width), low),
            VMEM(arena + (width,), low),
            VMEM(arena + (width,), low),
            VMEM(arena + (FF,), low),
            VMEM(arena + (2 * FF,), low),
            VMEM(arena + (width,), low),
            VMEM((groups, local_experts * slots, token_rows), low),
            VMEM((groups, slots, 128), f32),
            VMEM((groups, EXPERTS, token_rows), f32),
            VMEM((groups,) + routes.shape, jnp.int32),
            VMEM((token_rows, width), f32),
            VMEM(block, low),
            VMEM(steps, low),
            VMEM(steps, low),
            VMEM((2, 2, LINES - 1, COLUMN, width), low),
            VMEM((COLUMN, width), low),
            VMEM((2, max(size for _, size in CUTS), width), f32),
            DMA((3,)),
            DMA((shards + 5,)),
            DMA((2, local_experts)),
            DMA((2,)),
            pltpu.SemaphoreType.REGULAR,
            *square_sems(2),
            DMA((3,)),
            DMA((3,)),
            *gather_sems(1),
            *gather_sems(1),
            *gather_sems(1),
            *gather_sems(2),
            *column_sems(),
            *gather_sems(1),
            *gather_sems(len(CUTS)),
            *column_sems(),
            *square_sems(local_experts),
            *square_sems(local_experts),
            *square_sems(2),
            *scatter_sems(len(CUTS)),
            *column_sum_sems(),
            *square_sems(EARLY),
            *square_sems(EARLY),
        ],
        compiler_params=pltpu.CompilerParams(
            collective_id=0, has_side_effects=True, vmem_limit_bytes=63 * 2**20
        ),
    )(tokens, side_cols, wq, wk, wv, wo, routes, seg_row, cot, exp_in, exp_out)


def back_kernel(
    moe_in_grads,
    mixed_part,
    grad_in,
    grad_down,
    tokens,
    cot,
    resid,
    gain_two,
    gain_one,
    logit_grads,
    all_moe_hbm,
    all_tokens_hbm,
    weights_hbm,
    out_rows_hbm,
    qkv_hbm,
    heads_out_hbm,
    norm_rows,
    seg_row,
    mixed_out,
    grad_tokens,
    query_sum,
    key_sum,
    value_sum,
    side_sum,
    output_sum,
    in_sum,
    down_sum,
    mix_mine,
    mix_crossed,
    mix_raised,
    mix_lowered,
    column_mine,
    column_came,
    column_crossed,
    in_mine,
    in_swapped,
    in_crossed,
    down_mine,
    down_swapped,
    down_crossed,
    grad_resid,
    all_resid,
    head_grads,
    turned,
    key_grads,
    value_grads,
    qkv_grads,
    normed_part,
    normed_swapped,
    normed_crossed,
    sums,
    sums_crossed,
    sums_raised,
    sums_lowered,
    sums_own,
    sums_all,
    out_grads,
    out_crossed,
    out_raised,
    out_lowered,
    in_stage,
    down_stage,
    store_sem,
    all_moe,
    all_tokens,
    weights,
    out_rows,
    qkv,
    heads_out,
    late_sem,
    local_sem,
    mix_xs,
    mix_xr,
    mix_ls,
    mix_lr,
    column_ls,
    column_lr,
    column_xs,
    column_xr,
    sum_xs,
    sum_xr,
    sum_ls,
    sum_lr,
    out_xs,
    out_xr,
    out_ls,
    out_lr,
    in_send,
    in_recv,
    down_send,
    down_recv,
    normed_send,
    normed_recv,
    resid_send,
    resid_recv,
    last_send,
    last_recv,
):
    place = Place()
    ctx, exp = place.ctx, place.exp
    token_rows, width = tokens.shape
    shards, groups, rows, pack_cols = weights.shape
    local_experts = grad_in.shape[0]
    q_cols = heads_out.shape[1]
    main_cols = qkv.shape[1]
    k_cols = (main_cols - q_cols) // 2
    factor = 1.0 / math.sqrt(HEAD_SIZE)

    loads = []

    def load(source, target):
        copy = pltpu.make_async_copy(source, target, local_sem.at[len(loads)])
        copy.start()
        loads.append(copy)

    for y in range(2):
        load(grad_in.at[:, 2 * y + place.half], in_mine.at[y])
        load(grad_down.at[:, 2 * y + place.half], down_mine.at[y])
    mix_rows = sum(size for _, size in CUTS)
    for line in ORDER:
        load(mixed_part.at[line * 2 + place.x, pl.ds(0, mix_rows)], mix_mine.at[line])
    load(mixed_part.at[:, pl.ds(mix_rows, COLUMN)], column_mine)
    place.greet()

    def piece(ref, count, part):
        size = ref.shape[0] // count
        return ref.at[pl.ds(part * size, size)]

    moe_parts, mix_parts = 4, len(CUTS)

    def cut(ref, part):
        return ref.at[pl.ds(*CUTS[part])]

    mix = ExpScatter(
        place,
        lambda line, part: cut(mixed_part.at[line * 2 + 1 - place.x], part),
        lambda line, part: cut(mix_mine.at[line], part),
        lambda line, part: cut(mix_crossed.at[line], part),
        lambda line, part: cut(mix_raised.at[raised_slot(line)], part),
        lambda line, part: cut(mix_lowered.at[lowered_slot(line)], part),
        mix_parts,
        (mix_xs, mix_xr, mix_ls, mix_lr),
    )
    column_sum = ColumnScatter(
        place,
        lambda line, far: column_mine.at[line * 2 + (1 - place.x if far else place.x)],
        lambda side, far, slot: column_came.at[side, far, slot],
        column_crossed,
        (column_ls, column_lr, column_xs, column_xr),
    )
    into = CtxScatter(
        place,
        lambda y, part: grad_in.at[part, 2 * y + 1 - place.half],
        lambda y, part: in_mine.at[y, part],
        lambda lane, part: in_swapped.at[lane, part],
        lambda part: in_crossed.at[part],
        local_experts,
        in_send,
        in_recv,
    )
    downs = CtxScatter(
        place,
        lambda y, part: grad_down.at[part, 2 * y + 1 - place.half],
        lambda y, part: down_mine.at[y, part],
        lambda lane, part: down_swapped.at[lane, part],
        lambda part: down_crossed.at[part],
        local_experts,
        down_send,
        down_recv,
    )
    for near in (False, True):
        for part in range(local_experts):
            into.swap(near, part).start()
        for part in range(local_experts):
            downs.swap(near, part).start()
    gain_one_row, gain_two_row = gain_one[...], gain_two[...]
    moe_rows = token_rows // moe_parts
    gain_two_sum = jnp.zeros((1, width), jnp.float32)
    resid_gather = CtxGather(
        place,
        lambda index, part: all_resid.at[index, pl.ds(part * moe_rows, moe_rows)],
        moe_parts,
        resid_send,
        resid_recv,
    )
    for part in range(moe_parts):
        here = pl.ds(part * moe_rows, moe_rows)
        grad_moe_in = moe_in_grads[here, :]
        values = resid[here, :]
        scale = rms_scale(values)
        weighted = grad_moe_in * gain_two_row
        gain_two_sum = gain_two_sum + jnp.sum(grad_moe_in * values * scale, 0, keepdims=True)
        grads = (
            to_f32(cot[here, :])
            + scale * weighted
            - values * (scale * scale * scale) * jnp.mean(weighted * values, -1, keepdims=True)
        )
        grad_resid[here, :] = grads
        all_resid[ctx, here, :] = grads.astype(jnp.bfloat16)
        resid_gather.begin(part)
    for part in range(mix_parts):
        for line in ORDER:
            mix.begin(line, part)
    for copy in loads:
        copy.wait()
    column_sum.hop(0)
    late = []
    for index, (source, target) in enumerate(
        (
            (all_moe_hbm, all_moe),
            (qkv_hbm, qkv),
            (out_rows_hbm, out_rows),
            (heads_out_hbm, heads_out),
            (weights_hbm, weights),
            (all_tokens_hbm, all_tokens),
        )
    ):
        late.append(pltpu.make_async_copy(source, target, late_sem.at[index]))
        late[-1].start()

    low = lax.broadcasted_iota(jnp.int32, (1, 2 * HEAD_SIZE), 1) < HEAD_SIZE

    def spread(first):
        plain = to_f32(qkv[:, first : first + k_cols])
        other = pltpu.roll(plain, HEAD_SIZE, 1)
        zero = jnp.zeros((), jnp.float32)
        return [
            [
                jnp.where(low, plain, zero).astype(jnp.bfloat16),
                jnp.where(low, zero, other).astype(jnp.bfloat16),
            ],
            [
                jnp.where(low, other, zero).astype(jnp.bfloat16),
                jnp.where(low, zero, plain).astype(jnp.bfloat16),
            ],
        ]

    def add_router(block, total):
        return total + dot_rows(logit_grads[block], all_moe[block])

    for part in range(moe_parts // 2):
        resid_gather.relay(part)
    for copy in late:
        copy.wait()
    full = weights[...].reshape(width, pack_cols)
    full_out = out_rows[...].reshape(q_cols, width)
    keys, values = spread(q_cols), spread(q_cols + k_cols)
    documents = seg_row[...].astype(jnp.float32)
    columns = jnp.broadcast_to(documents, (128, documents.shape[1])).T[:, :1]
    router_grads = lax.fori_loop(
        0, groups, add_router, jnp.zeros((2 * EXPERTS, width), jnp.float32)
    )
    router_sum = router_grads[:EXPERTS] + router_grads[EXPERTS:]
    for part in range(moe_parts // 2, moe_parts):
        resid_gather.relay(part)
    column_sum.hop(1)
    mix.fold(0)
    mix.hop(0, 0)
    for part in range(moe_parts):
        resid_gather.arrived(part)
    for part in range(local_experts):
        into.fold(part)
        downs.fold(part)
    at_lane = lax.broadcasted_iota(jnp.int32, (1, 128), 1)
    for block in range(shards):
        here = pl.ds(block * token_rows, token_rows)
        grads = outer_cols(all_resid[block], full_out).astype(jnp.bfloat16)
        head_grads[here, :] = grads
        products = to_f32(grads) * heads_out[here, :]
        deltas = jnp.zeros((token_rows, 128), jnp.float32)
        for pair in range(2):
            both = products[:, pair * 128 : pair * 128 + 128]
            first = jnp.sum(jnp.where(low, both, 0.0), -1, keepdims=True)
            second = jnp.sum(jnp.where(low, 0.0, both), -1, keepdims=True)
            deltas = jnp.where(at_lane == 2 * pair, first, deltas)
            deltas = jnp.where(at_lane == 2 * pair + 1, second, deltas)
        turned[:, here] = deltas.T
    attn_low = heads_out[...].astype(jnp.bfloat16)
    flat_resid = all_resid[...].reshape(shards * token_rows, width)
    out_grads[...] = (
        inner_rows(attn_low, flat_resid).astype(jnp.bfloat16).reshape(groups, rows, width)
    )
    out_scatter = ExpScatter(
        place,
        lambda line, part: out_grads.at[line * 2 + 1 - place.x],
        lambda line, part: out_grads.at[line * 2 + place.x],
        lambda line, part: out_crossed.at[line],
        lambda line, part: out_raised.at[raised_slot(line)],
        lambda line, part: out_lowered.at[lowered_slot(line)],
        1,
        (out_xs, out_xr, out_ls, out_lr),
    )
    for line in ORDER:
        out_scatter.begin(line, 0)
    column_sum.hop(2)
    mix.hop(1, 0)
    key_grads[...] = jnp.zeros_like(key_grads)
    value_grads[...] = jnp.zeros_like(value_grads)
    for block in range(shards):
        here = pl.ds(block * token_rows, token_rows)
        count = (block + 1) * token_rows
        at_col = block * token_rows + lax.broadcasted_iota(jnp.int32, (1, token_rows), 1)
        at_row = lax.broadcasted_iota(jnp.int32, (count, 1), 0)
        bias = jnp.where(
            (at_row <= at_col)
            & (columns[:count] == documents[:, block * token_rows : count]),
            0.0,
            MASK_FILLER,
        )
        for pair in range(2):
            lanes = slice(pair * 128, pair * 128 + 128)
            queries = qkv[here, lanes]
            grads = head_grads[here, lanes]
            query_grad = jnp.zeros((token_rows, 128), jnp.float32)
            for head in range(2):
                row = 2 * pair + head
                mine = low if head == 0 else jnp.logical_not(low)
                own_queries = jnp.where(mine, queries, jnp.zeros((), jnp.bfloat16))
                own_grads = jnp.where(mine, grads, jnp.zeros((), jnp.bfloat16))
                key, value = keys[pair][head][:count], values[pair][head][:count]
                scores = outer_cols(key, queries) * factor + bias
                probs = jnp.exp(scores - norm_rows[row : row + 1, block * token_rows : count])
                grad_probs = outer_cols(value, grads)
                grad_scores = (probs * (grad_probs - turned[row : row + 1, here])).astype(
                    jnp.bfloat16
                )
                value_grads[pair, :count, :] += dot_rows(probs.astype(jnp.bfloat16), own_grads)
                key_grads[pair, :count, :] += dot_rows(grad_scores, own_queries)
                query_grad = query_grad + inner_rows(grad_scores, key)
            qkv_grads[here, lanes] = (query_grad * factor).astype(jnp.bfloat16)
        if block == 1:
            mix.fold(1)
            mix.hop(0, 1)
            column_sum.turn()
        if block == 3:
            mix.hop(2, 0)
            mix.hop(1, 1)

    def fold_heads(first, second):
        return jnp.where(
            low,
            first + pltpu.roll(first, HEAD_SIZE, 1),
            second + pltpu.roll(second, HEAD_SIZE, 1),
        )

    qkv_grads[:, q_cols : q_cols + k_cols] = (
        fold_heads(key_grads[0], key_grads[1]) * factor
    ).astype(jnp.bfloat16)
    qkv_grads[:, q_cols + k_cols :] = fold_heads(value_grads[0], value_grads[1]).astype(
        jnp.bfloat16
    )

    normed_scatter = CtxScatter(
        place,
        lambda y, part: normed_part.at[2 * y + 1 - place.half],
        lambda y, part: normed_part.at[2 * y + place.half],
        lambda lane, part: normed_swapped.at[lane],
        lambda part: normed_crossed,
        1,
        normed_send,
        normed_recv,
    )
    gain_one_sum = jnp.zeros((1, width), jnp.float32)
    main_sum = jnp.zeros((width, main_cols), jnp.float32)
    for block in range(shards):
        here = pl.ds(block * token_rows, token_rows)
        grads = outer_cols(qkv_grads[here, :], full[:, :main_cols])
        normed_part[block] = grads.astype(jnp.bfloat16)
        own = to_f32(all_tokens[block])
        scaled = own * rms_scale(own)
        gain_one_sum = gain_one_sum + jnp.sum(grads * scaled, 0, keepdims=True)
        normed = (scaled * gain_one_row).astype(jnp.bfloat16)
        main_sum = main_sum + inner_rows(normed, qkv_grads[here, :])
    normed_scatter.swap(False, 0).start()
    normed_scatter.swap(True, 0).start()
    at_sub = lax.broadcasted_iota(jnp.int32, (128, 1), 0)
    gain_rows = jnp.where(
        at_sub == EXPERTS, gain_one_sum, jnp.where(at_sub == EXPERTS + 1, gain_two_sum, 0.0)
    )
    side = jnp.concatenate([router_sum, gain_rows[EXPERTS:, :]], 0).T
    sums[:, :, :, :main_cols] = main_sum.astype(jnp.bfloat16).reshape(
        shards, groups, rows, main_cols
    )
    sums[:, :, :, main_cols:] = side.astype(jnp.bfloat16).reshape(
        shards, groups, rows, pack_cols - main_cols
    )
    sum_scatter = ExpScatter(
        place,
        lambda line, part: sums.at[:, line * 2 + 1 - place.x],
        lambda line, part: sums.at[:, line * 2 + place.x],
        lambda line, part: sums_crossed.at[line],
        lambda line, part: sums_raised.at[raised_slot(line)],
        lambda line, part: sums_lowered.at[lowered_slot(line)],
        1,
        (sum_xs, sum_xr, sum_ls, sum_lr),
    )
    for line in ORDER:
        sum_scatter.begin(line, 0)
    normed_scatter.fold(0)
    mix.fold(2)
    mix.hop(0, 2)
    mix.hop(2, 1)
    out_scatter.fold(0)
    out_scatter.hop(0, 0)
    mix.hop(1, 2)
    mix.fold(3)
    mix.hop(0, 3)
    sum_scatter.fold(0)
    sum_scatter.hop(0, 0)
    out_scatter.hop(1, 0)
    mix.hop(2, 2)
    mix.hop(1, 3)
    sum_scatter.hop(1, 0)
    out_scatter.hop(2, 0)
    stores = []
    for part in range(local_experts):
        slot = part % 2
        if part >= 2:
            for copy in stores[2 * (part - 2) : 2 * (part - 1)]:
                copy.wait()
        into.arrived(part)
        downs.arrived(part)
        in_stage[slot] = into.total(part)
        down_stage[slot] = downs.total(part)
        for kind, (source, target) in enumerate(
            ((in_stage.at[slot], in_sum.at[part]), (down_stage.at[slot], down_sum.at[part]))
        ):
            copy = pltpu.make_async_copy(source, target, store_sem.at[kind, part])
            copy.start()
            stores.append(copy)
    sum_scatter.hop(2, 0)
    mix.hop(2, 3)
    output_sum[...] = out_scatter.total(0)
    sums_own[...] = sum_scatter.total(0).astype(jnp.bfloat16)
    sums_all[ctx] = sums_own[ctx]
    copies = []
    for lane, to in enumerate((place.core, place.side, place.far)):
        copy = remote(
            sums_own.at[to[0]], sums_all.at[ctx], last_send.at[lane], last_recv.at[lane], to
        )
        copy.start()
        copies.append(copy)
    normed_scatter.arrived(0)
    grad_normed = normed_scatter.total(0)
    own = to_f32(tokens[...])
    scale = rms_scale(own)
    weighted = grad_normed * gain_one_row
    grad_tokens[...] = (
        grad_resid[...]
        + scale * weighted
        - own * (scale * scale * scale) * jnp.mean(weighted * own, -1, keepdims=True)
    )
    for part in range(mix_parts):
        here = pl.ds(*CUTS[part])
        mixed_out[here, :] = (resid[here, :] + mix.total(part)).astype(jnp.bfloat16)
    here = pl.ds(mix_rows, COLUMN)
    mixed_out[here, :] = (resid[here, :] + column_sum.total()).astype(jnp.bfloat16)
    for lane, to in enumerate((place.core, place.side, place.far)):
        remote(
            sums_own.at[0], sums_all.at[to[0]], last_send.at[lane], last_recv.at[lane], to
        ).wait_recv()
    side = jnp.zeros((rows, pack_cols - main_cols), jnp.float32)
    for shard in range(shards):
        came = to_f32(sums_all[shard])
        query_sum[:, shard * q_cols : (shard + 1) * q_cols] = came[:, :q_cols]
        key_sum[:, shard * k_cols : (shard + 1) * k_cols] = came[:, q_cols : q_cols + k_cols]
        value_sum[:, shard * k_cols : (shard + 1) * k_cols] = came[:, q_cols + k_cols : main_cols]
        side = side + came[:, main_cols:]
    side_sum[...] = side
    for copy in stores[-4:]:
        copy.wait()
    for copy in copies:
        copy.wait_send()
    for scatter in (mix, column_sum, into, downs, out_scatter, normed_scatter, sum_scatter):
        scatter.finish()
    for part in range(moe_parts):
        resid_gather.sent(part)


def back(
    moe_in_grads, mixed_part, grad_in, grad_down, tokens, cot, resid, gain_two, gain_one, logit_grads,
    all_moe, all_tokens, weights, out_rows, qkv, heads_out, norm_rows, seg_row,
):
    token_rows, width = tokens.shape
    shards, groups, rows, pack_cols = weights.shape
    seq_len = shards * token_rows
    q_cols, main_cols = heads_out.shape[1], qkv.shape[1]
    k_cols = (main_cols - q_cols) // 2
    experts, _, in_rows, in_cols = grad_in.shape
    down_rows = grad_down.shape[2]
    low, f32 = jnp.bfloat16, jnp.float32

    def shape(dims, dtype):
        return jax.ShapeDtypeStruct(dims, dtype)

    whole, anywhere = pl.BlockSpec(memory_space=VMEM), pl.BlockSpec(memory_space=pl.ANY)
    mix_rows = sum(size for _, size in CUTS)
    block, steps = (LINES, mix_rows, width), (LINES - 1, mix_rows, width)
    pack = (shards, rows, pack_cols)
    return pl.pallas_call(
        back_kernel,
        name="back",
        out_shape=[
            shape((token_rows, width), low),
            shape((token_rows, width), f32),
            shape((rows, shards * q_cols), f32),
            shape((rows, shards * k_cols), f32),
            shape((rows, shards * k_cols), f32),
            shape((rows, pack_cols - main_cols), f32),
            shape((rows, width), f32),
            shape((experts, in_rows, in_cols), f32),
            shape((experts, down_rows, width), f32),
        ],
        in_specs=[whole] + [anywhere] * 3 + [whole] * 6 + [anywhere] * 6 + [whole] * 2,
        out_specs=[whole] * 7 + [anywhere] * 2,
        scratch_shapes=[
            VMEM(block, low),
            VMEM(block, low),
            VMEM(steps, low),
            VMEM(steps, low),
            VMEM((groups, COLUMN, width), low),
            VMEM((2, 2, LINES - 1, COLUMN, width), low),
            VMEM((COLUMN, width), low),
            VMEM((2, experts, in_rows, in_cols), low),
            VMEM((2, experts, in_rows, in_cols), low),
            VMEM((experts, in_rows, in_cols), low),
            VMEM((2, experts, down_rows, width), low),
            VMEM((2, experts, down_rows, width), low),
            VMEM((experts, down_rows, width), low),
            VMEM((token_rows, width), f32),
            VMEM((shards, token_rows, width), low),
            VMEM((seq_len, q_cols), low),
            VMEM((128, seq_len), f32),
            VMEM((2, seq_len, 128), f32),
            VMEM((2, seq_len, 128), f32),
            VMEM((seq_len, main_cols), low),
            VMEM((shards, token_rows, width), low),
            VMEM((2, token_rows, width), low),
            VMEM((token_rows, width), low),
            VMEM((shards, groups, rows, pack_cols), low),
            VMEM((LINES,) + pack, low),
            *[VMEM((LINES - 1,) + pack, low)] * 2,
            VMEM((shards, rows, pack_cols), low),
            VMEM((shards, rows, pack_cols), low),
            VMEM((groups, rows, width), low),
            VMEM((LINES, rows, width), low),
            *[VMEM((LINES - 1, rows, width), low)] * 2,
            VMEM((2, in_rows, in_cols), f32),
            VMEM((2, down_rows, width), f32),
            DMA((2, experts)),
            VMEM(all_moe.shape, low),
            VMEM(all_tokens.shape, low),
            VMEM(weights.shape, low),
            VMEM(out_rows.shape, low),
            VMEM(qkv.shape, low),
            VMEM(heads_out.shape, f32),
            DMA((6,)),
            DMA((9,)),
            *scatter_sems(len(CUTS)),
            *column_sum_sems(),
            *scatter_sems(1),
            *scatter_sems(1),
            *square_sems(experts),
            *square_sems(experts),
            *square_sems(1),
            *square_sems(4),
            DMA((3,)),
            DMA((3,)),
        ],
        compiler_params=pltpu.CompilerParams(
            collective_id=1, has_side_effects=True, vmem_limit_bytes=62 * 2**20
        ),
    )(
        moe_in_grads, mixed_part, grad_in, grad_down, tokens, cot, resid, gain_two, gain_one, logit_grads,
        all_moe, all_tokens, weights, out_rows, qkv, heads_out, norm_rows, seg_row,
    )


def two_parts(values):
    high = values.astype(jnp.bfloat16)
    return high, (values - high.astype(jnp.float32)).astype(jnp.bfloat16)


def by_heads(
    tokens,
    segments,
    routes,
    gain_attn,
    gain_moe,
    query_weight,
    key_weight,
    value_weight,
    w_output,
    w_router,
    w_expert_in,
    w_expert_out,
    cotangent,
):
    shards = lax.axis_size("ctx")
    groups = lax.axis_size("exp")
    width = tokens.shape[2]
    rows = query_weight.shape[0]
    q_cols = query_weight.shape[1] // shards
    k_cols = key_weight.shape[1] // shards
    main_cols = q_cols + 2 * k_cols
    side = 128

    side_cols = jnp.concatenate(
        [
            w_router,
            gain_attn[:, None],
            gain_moe[:, None],
            jnp.zeros((rows, side - EXPERTS - 2), jnp.bfloat16),
        ],
        1,
    )
    (
        grad_moe_in,
        mixed_part,
        logit_grads,
        in_first,
        down_first,
        in_rest,
        down_rest,
        all_moe,
        all_tokens,
        all_weights,
        out_rows,
        qkv,
        heads_out,
        norm_rows,
        resid,
        side_rows,
    ) = ahead(
        tokens[0],
        side_cols,
        query_weight,
        key_weight,
        value_weight,
        w_output,
        routes[0].T,
        segments,
        cotangent[0],
        w_expert_in,
        w_expert_out,
    )
    gains = side_rows[EXPERTS : EXPERTS + 2].astype(jnp.float32)
    rest = in_rest.shape[0]
    (
        mixed_out,
        grad_tokens,
        query_sum,
        key_sum,
        value_sum,
        side_sum,
        output_sum,
        in_sum,
        down_sum,
    ) = back(
        grad_moe_in,
        mixed_part,
        in_rest.reshape((rest, shards, -1, width)),
        down_rest.reshape((rest, shards, -1, width)),
        tokens[0],
        cotangent[0],
        resid,
        gains[1:2],
        gains[0:1],
        logit_grads,
        all_moe,
        all_tokens,
        all_weights.reshape(shards, groups, rows, main_cols + side),
        out_rows.reshape(groups, rows, width),
        qkv.reshape(-1, main_cols),
        heads_out,
        norm_rows,
        segments,
    )
    return (
        mixed_out[None],
        grad_tokens[None],
        side_sum[:, EXPERTS],
        side_sum[:, EXPERTS + 1],
        query_sum,
        key_sum,
        value_sum,
        output_sum,
        side_sum[:, :EXPERTS],
        jnp.concatenate([in_first, in_sum], 0),
        jnp.concatenate([down_first, down_sum], 0),
    )


def solution(mesh):
    sizes = (mesh.shape["ctx"], mesh.shape["exp"])
    return jax.shard_map(
        by_heads if sizes == (4, 8) else local,
        mesh=mesh,
        in_specs=(
            P("exp", "ctx", None),
            P("exp", None),
            P("exp", "ctx", None),
            P(("ctx", "exp")),
            P(("ctx", "exp")),
            P(("ctx", "exp"), None),
            P(("ctx", "exp"), None),
            P(("ctx", "exp"), None),
            P(("ctx", "exp"), None),
            P(("ctx", "exp"), None),
            P("exp", "ctx", None),
            P("exp", "ctx", None),
            P("exp", "ctx", None),
        ),
        out_specs=(
            P("exp", "ctx", None),
            P("exp", "ctx", None),
            P(("ctx", "exp")),
            P(("ctx", "exp")),
            P(("ctx", "exp"), None),
            P(("ctx", "exp"), None),
            P(("ctx", "exp"), None),
            P(("ctx", "exp"), None),
            P(("ctx", "exp"), None),
            P("exp", "ctx", None),
            P("exp", "ctx", None),
        ),
        check_vma=False,
    )
```

```python
import functools
import math

import jax
import jax.numpy as jnp
from jax import lax
from jax.experimental import pallas as pl
from jax.experimental.pallas import tpu as pltpu
from jax.sharding import PartitionSpec as P

QUERY_HEADS = 16
KEY_VALUE_HEADS = 8
HEAD_SIZE = 64
EXPERTS = 32
TOPK = 8
FF = 512
CAP = 72


EPSILON = 1e-06
MASK_FILLER = -1e30


def rms_scale(values):
    return lax.rsqrt(jnp.mean(values * values, -1, keepdims=True) + EPSILON)


def inner_rows(left, right):
    return lax.dot_general(
        left, right, (((0,), (0,)), ((), ())), preferred_element_type=jnp.float32
    )


def outer_cols(left, right):
    return lax.dot_general(
        left, right, (((1,), (1,)), ((), ())), preferred_element_type=jnp.float32
    )


def allowed_block(query_pos, query_seg, seg_all, offset, key_total_count):
    key_pos = offset + jnp.arange(key_total_count, dtype=jnp.int32)
    key_seg = lax.dynamic_slice_in_dim(seg_all, offset, key_total_count)
    return (key_pos[None, :] <= query_pos[:, None]) & (key_seg[None, :] == query_seg[:, None])


def head_scores(heads_of_queries, key_segment_slice, factor):
    key_total_count = key_segment_slice.shape[0]
    heads_of_keys = key_segment_slice.reshape(key_total_count, KEY_VALUE_HEADS, -1)
    return (
        jnp.einsum(
            "ihgd,jhd->hgij", heads_of_queries, heads_of_keys, preferred_element_type=jnp.float32
        )
        * factor
    )


def slot_tables(pair_ids):
    pair_count = pair_ids.shape[0]
    member = (pair_ids[:, None] == jnp.arange(EXPERTS, dtype=jnp.int32)[None, :]).astype(jnp.int32)
    earlier = jnp.cumsum(member, 0) - member
    slot_place = jnp.sum(earlier * member, 1, dtype=jnp.int32)
    is_kept = slot_place < CAP
    slot_index = jnp.where(is_kept, pair_ids * CAP + slot_place, EXPERTS * CAP)
    slot_filler = (
        jnp.full((EXPERTS * CAP,), -1, jnp.int32)
        .at[slot_index]
        .set(jnp.arange(pair_count, dtype=jnp.int32), mode="drop")
    )
    return (slot_index, is_kept, slot_filler)


def local(
    tokens,
    segments,
    routes,
    gain_attn,
    gain_moe,
    query_weight,
    key_weight,
    value_weight,
    w_output,
    w_router,
    w_expert_in,
    w_expert_out,
    cotangent,
):
    shards = lax.axis_size("ctx")
    groups = lax.axis_size("exp")
    ctx_rank = lax.axis_index("ctx")
    gain_one, gain_two, full_query, full_key, full_value, full_output, full_router = (
        lax.all_gather(gain_attn, ("ctx", "exp"), axis=0, tiled=True),
        lax.all_gather(gain_moe, ("ctx", "exp"), axis=0, tiled=True),
        lax.all_gather(query_weight, ("ctx", "exp"), axis=0, tiled=True),
        lax.all_gather(key_weight, ("ctx", "exp"), axis=0, tiled=True),
        lax.all_gather(value_weight, ("ctx", "exp"), axis=0, tiled=True),
        lax.all_gather(w_output, ("ctx", "exp"), axis=0, tiled=True),
        lax.all_gather(w_router, ("ctx", "exp"), axis=0, tiled=True),
    )
    expert_in, expert_out = (
        lax.all_gather(w_expert_in, "ctx", axis=1, tiled=True),
        lax.all_gather(w_expert_out, "ctx", axis=1, tiled=True),
    )
    inputs = tokens[0].astype(jnp.float32)
    token_rows = inputs.shape[0]
    seq_len = token_rows * shards
    head_cluster = QUERY_HEADS // KEY_VALUE_HEADS
    factor = 1.0 / math.sqrt(HEAD_SIZE)
    kv_width = key_weight.shape[1]
    seg_all = segments[0]
    query_pos = ctx_rank * token_rows + jnp.arange(token_rows, dtype=jnp.int32)
    query_seg = lax.dynamic_slice_in_dim(seg_all, ctx_rank * token_rows, token_rows)
    scale_one = rms_scale(inputs)
    gain_one_f = gain_one.astype(jnp.float32)
    normalized_input = (inputs * scale_one * gain_one_f).astype(jnp.bfloat16)
    query_matrix = jnp.dot(normalized_input, full_query, preferred_element_type=jnp.float32).astype(
        jnp.bfloat16
    )
    key_rows = jnp.dot(normalized_input, full_key, preferred_element_type=jnp.float32).astype(
        jnp.bfloat16
    )
    value_rows = jnp.dot(normalized_input, full_value, preferred_element_type=jnp.float32).astype(
        jnp.bfloat16
    )
    heads_of_queries = query_matrix.reshape(token_rows, KEY_VALUE_HEADS, head_cluster, HEAD_SIZE)
    group_size = math.gcd(shards, max(1, 1024 // token_rows))
    key_range_width = group_size * token_rows
    turns_needed = ctx_rank // group_size + 1
    running_maximum = jnp.full(
        (KEY_VALUE_HEADS, head_cluster, token_rows), MASK_FILLER, jnp.float32
    )
    key_segment_slice = lax.all_gather(key_rows, "ctx", axis=0, tiled=True)
    value_segment_slice = lax.all_gather(value_rows, "ctx", axis=0, tiled=True)
    key_total_count = key_segment_slice.shape[0]
    scores = head_scores(heads_of_queries, key_segment_slice, factor)
    allowed = allowed_block(query_pos, query_seg, seg_all, jnp.int32(0), key_total_count)
    scores = jnp.where(allowed, scores, MASK_FILLER)
    new_max = jnp.maximum(running_maximum, jnp.max(scores, -1))
    weights = jnp.where(allowed, jnp.exp(scores - new_max[..., None]), 0.0)
    run_sum = jnp.sum(weights, -1)
    heads_of_values = value_segment_slice.reshape(key_total_count, KEY_VALUE_HEADS, HEAD_SIZE)
    run_acc = jnp.einsum(
        "hgij,jhd->ihgd",
        weights.astype(jnp.bfloat16),
        heads_of_values,
        preferred_element_type=jnp.float32,
    )
    running_maximum, run_sum, run_acc = (new_max, run_sum, run_acc)
    log_norm = running_maximum + jnp.log(run_sum)
    heads_out = run_acc / jnp.transpose(run_sum, (2, 0, 1))[..., None]
    attn_low = heads_out.reshape(token_rows, -1).astype(jnp.bfloat16)
    resid = inputs + jnp.dot(attn_low, full_output, preferred_element_type=jnp.float32)
    scale_two = rms_scale(resid)
    gain_two_f = gain_two.astype(jnp.float32)
    moe_in = (resid * scale_two * gain_two_f).astype(jnp.bfloat16)
    logits = jnp.dot(moe_in, full_router, preferred_element_type=jnp.float32)
    route_ids = routes[0]
    one_hot = (route_ids[:, :, None] == jnp.arange(EXPERTS, dtype=jnp.int32)[None, None, :]).astype(
        jnp.float32
    )
    chosen = jnp.sum(one_hot * logits[:, None, :], -1)
    gates = jax.nn.softmax(chosen, axis=-1)
    slot_index, is_kept, slot_filler = slot_tables(route_ids.reshape(-1))
    filled = slot_filler >= 0
    token_of = jnp.maximum(slot_filler, 0) // TOPK
    local_experts = EXPERTS // groups
    send_rows = jnp.where(
        filled[:, None], jnp.take(moe_in, token_of, axis=0), jnp.zeros((), jnp.bfloat16)
    )
    send_rows = send_rows.reshape(groups, local_experts, CAP, -1)
    received = lax.all_to_all(send_rows, "exp", split_axis=0, concat_axis=0, tiled=True)
    pre = jnp.einsum("sjcd,jdf->sjcf", received, expert_in, preferred_element_type=jnp.float32)
    gate_part = pre[..., :FF]
    up_part = pre[..., FF:]
    hidden = (jax.nn.silu(gate_part) * up_part).astype(jnp.bfloat16)
    expert_rows = jnp.einsum(
        "sjcf,jfd->sjcd", hidden, expert_out, preferred_element_type=jnp.float32
    ).astype(jnp.bfloat16)
    returned = lax.all_to_all(expert_rows, "exp", split_axis=0, concat_axis=0, tiled=True).reshape(
        EXPERTS * CAP, -1
    )
    safe_slot = jnp.minimum(slot_index, EXPERTS * CAP - 1)
    picked = jnp.where(
        is_kept[:, None], jnp.take(returned, safe_slot, axis=0), jnp.zeros((), jnp.bfloat16)
    )
    picked = picked.astype(jnp.float32).reshape(token_rows, TOPK, -1)
    branch = jnp.sum(gates[:, :, None] * picked, 1)
    mixed_out = (resid + branch).astype(jnp.bfloat16)
    grad_out = cotangent[0].astype(jnp.float32)
    grad_picked = jnp.sum(grad_out[:, None, :] * picked, -1)
    grad_chosen = gates * (grad_picked - jnp.sum(gates * grad_picked, -1, keepdims=True))
    grad_logits = jnp.sum(one_hot * grad_chosen[:, :, None], 1)
    slot_gate = jnp.where(filled, jnp.take(gates.reshape(-1), jnp.maximum(slot_filler, 0)), 0.0)
    grad_send = (slot_gate[:, None] * jnp.take(grad_out, token_of, axis=0)).astype(jnp.bfloat16)
    grad_send = grad_send.reshape(groups, local_experts, CAP, -1)
    grad_rows = lax.all_to_all(grad_send, "exp", split_axis=0, concat_axis=0, tiled=True)
    grad_hidden = jnp.einsum(
        "sjcd,jfd->sjcf", grad_rows, expert_out, preferred_element_type=jnp.float32
    )
    sigmoid_gate = jax.nn.sigmoid(gate_part)
    grad_gate = grad_hidden * up_part * sigmoid_gate * (1.0 + gate_part * (1.0 - sigmoid_gate))
    grad_up = grad_hidden * gate_part * sigmoid_gate
    grad_pre = jnp.concatenate([grad_gate, grad_up], -1).astype(jnp.bfloat16)
    grad_expert_out = jnp.einsum(
        "sjcf,sjcd->jfd", hidden, grad_rows, preferred_element_type=jnp.float32
    )
    grad_expert_in = jnp.einsum(
        "sjcd,sjcf->jdf", received, grad_pre, preferred_element_type=jnp.float32
    )
    grad_received = jnp.einsum(
        "sjcf,jdf->sjcd", grad_pre, expert_in, preferred_element_type=jnp.float32
    ).astype(jnp.bfloat16)
    grad_back = lax.all_to_all(
        grad_received, "exp", split_axis=0, concat_axis=0, tiled=True
    ).reshape(EXPERTS * CAP, -1)
    grad_pairs = jnp.where(
        is_kept[:, None], jnp.take(grad_back, safe_slot, axis=0), jnp.zeros((), jnp.bfloat16)
    )
    grad_pairs = grad_pairs.astype(jnp.float32).reshape(token_rows, TOPK, -1)
    grad_moe_in = (
        jnp.sum(grad_pairs, 1)
        + outer_cols(grad_logits.astype(jnp.bfloat16), full_router) * 0.0
        + lax.dot_general(
            grad_logits,
            full_router.astype(jnp.float32),
            (((1,), (1,)), ((), ())),
            precision=lax.Precision.HIGHEST,
            preferred_element_type=jnp.float32,
        )
    )
    grad_router = lax.dot_general(
        moe_in.astype(jnp.float32),
        grad_logits,
        (((0,), (0,)), ((), ())),
        precision=lax.Precision.HIGHEST,
        preferred_element_type=jnp.float32,
    )
    weighted_two = grad_moe_in * gain_two_f
    grad_gain_two = jnp.sum(grad_moe_in * resid * scale_two, 0)
    cube_two = scale_two * scale_two * scale_two
    grad_resid = (
        grad_out
        + scale_two * weighted_two
        - resid * cube_two * jnp.mean(weighted_two * resid, -1, keepdims=True)
    )
    grad_resid_low = grad_resid.astype(jnp.bfloat16)
    grad_output_w = inner_rows(attn_low, grad_resid_low)
    grad_heads = (
        outer_cols(grad_resid_low, full_output)
        .astype(jnp.bfloat16)
        .reshape(token_rows, KEY_VALUE_HEADS, head_cluster, HEAD_SIZE)
    )
    delta = jnp.transpose(jnp.sum(grad_heads.astype(jnp.float32) * heads_out, -1), (1, 2, 0))
    all_keys, all_values = (
        lax.all_gather(key_rows, "ctx", axis=0, tiled=True),
        lax.all_gather(value_rows, "ctx", axis=0, tiled=True),
    )

    def block_grads(offset):
        key_segment_slice = lax.dynamic_slice_in_dim(all_keys, offset, key_range_width)
        value_segment_slice = lax.dynamic_slice_in_dim(all_values, offset, key_range_width)
        scores = head_scores(heads_of_queries, key_segment_slice, factor)
        allowed = allowed_block(query_pos, query_seg, seg_all, offset, key_range_width)
        probs_full = jnp.where(allowed, jnp.exp(scores - log_norm[..., None]), 0.0)
        heads_of_keys = key_segment_slice.reshape(key_range_width, KEY_VALUE_HEADS, HEAD_SIZE)
        heads_of_values = value_segment_slice.reshape(key_range_width, KEY_VALUE_HEADS, HEAD_SIZE)
        grad_probs = jnp.einsum(
            "ihgd,jhd->hgij", grad_heads, heads_of_values, preferred_element_type=jnp.float32
        )
        grad_scores = (probs_full * (grad_probs - delta[..., None])).astype(jnp.bfloat16)
        query_part = jnp.einsum(
            "hgij,jhd->ihgd", grad_scores, heads_of_keys, preferred_element_type=jnp.float32
        )
        return (probs_full, grad_scores, query_part)

    query_begin_index = jnp.zeros(
        (token_rows, KEY_VALUE_HEADS, head_cluster, HEAD_SIZE), jnp.float32
    )

    def back_turn(turn, running):
        grad_query_acc, key_grad_buf = running
        offset = turn * key_range_width
        probs_full, grad_scores, query_part = block_grads(offset)
        grad_key_part = (
            jnp.einsum(
                "hgij,ihgd->jhd", grad_scores, heads_of_queries, preferred_element_type=jnp.float32
            )
            * factor
        )
        grad_value_part = jnp.einsum(
            "hgij,ihgd->jhd",
            probs_full.astype(jnp.bfloat16),
            grad_heads,
            preferred_element_type=jnp.float32,
        )
        joined = jnp.concatenate(
            [
                grad_key_part.reshape(key_range_width, -1),
                grad_value_part.reshape(key_range_width, -1),
            ],
            1,
        )
        key_grad_buf = lax.dynamic_update_slice_in_dim(key_grad_buf, joined, offset, 0)
        return (grad_query_acc + query_part, key_grad_buf)

    back_start = (query_begin_index, jnp.zeros((seq_len, 2 * kv_width), jnp.float32))
    grad_query_acc, key_grad_buf = lax.fori_loop(0, turns_needed, back_turn, back_start)
    own_grads = lax.psum_scatter(
        key_grad_buf.astype(jnp.bfloat16), "ctx", scatter_dimension=0, tiled=True
    ).astype(jnp.float32)
    grad_keys = own_grads[:, :kv_width].astype(jnp.bfloat16)
    grad_values = own_grads[:, kv_width:].astype(jnp.bfloat16)
    grad_query = (grad_query_acc * factor).reshape(token_rows, -1).astype(jnp.bfloat16)
    grad_query_w = inner_rows(normalized_input, grad_query)
    grad_key_w = inner_rows(normalized_input, grad_keys)
    grad_value_w = inner_rows(normalized_input, grad_values)
    grad_normed = (
        outer_cols(grad_query, full_query)
        + outer_cols(grad_keys, full_key)
        + outer_cols(grad_values, full_value)
    )
    weighted_one = grad_normed * gain_one_f
    grad_gain_one = jnp.sum(grad_normed * inputs * scale_one, 0)
    cube_one = scale_one * scale_one * scale_one
    grad_inputs = (
        grad_resid
        + scale_one * weighted_one
        - inputs * cube_one * jnp.mean(weighted_one * inputs, -1, keepdims=True)
    )
    dense_sums = (
        lax.psum_scatter(grad_gain_one, ("ctx", "exp"), scatter_dimension=0, tiled=True),
        lax.psum_scatter(grad_gain_two, ("ctx", "exp"), scatter_dimension=0, tiled=True),
        lax.psum_scatter(grad_query_w, ("ctx", "exp"), scatter_dimension=0, tiled=True),
        lax.psum_scatter(grad_key_w, ("ctx", "exp"), scatter_dimension=0, tiled=True),
        lax.psum_scatter(grad_value_w, ("ctx", "exp"), scatter_dimension=0, tiled=True),
        lax.psum_scatter(grad_output_w, ("ctx", "exp"), scatter_dimension=0, tiled=True),
        lax.psum_scatter(grad_router, ("ctx", "exp"), scatter_dimension=0, tiled=True),
    )
    expert_sums = (
        lax.psum_scatter(
            grad_expert_in.astype(jnp.bfloat16), "ctx", scatter_dimension=1, tiled=True
        ).astype(jnp.float32),
        lax.psum_scatter(
            grad_expert_out.astype(jnp.bfloat16), "ctx", scatter_dimension=1, tiled=True
        ).astype(jnp.float32),
    )
    return (mixed_out[None], grad_inputs[None]) + tuple(dense_sums) + tuple(expert_sums)


MESH = pl.DeviceIdType.MESH
VMEM = pltpu.VMEM
DMA = pltpu.SemaphoreType.DMA
COT_LATE = 64
COLUMN = 32
ORDER = (3, 0, 2, 1)
MIX_CUTS = ((0, 64), (64, 64), (128, 64), (192, 32))
CUTS = ((0, 64), (64, 64), (128, 64), (192, 32))
LINES = 4
GRANT = 56 * 2**20


def to_f32(value):
    return value.astype(jnp.float32)


def dot_rows(left, right):
    return jnp.dot(left, right, preferred_element_type=jnp.float32)


def remote(source, target, send, recv, to):
    return pltpu.make_async_remote_copy(
        src_ref=source,
        dst_ref=target,
        send_sem=send,
        recv_sem=recv,
        device_id=to,
        device_id_type=MESH,
    )


class Place:
    def __init__(self):
        ctx, exp = lax.axis_index("ctx"), lax.axis_index("exp")
        self.ctx, self.exp = ctx, exp
        self.y, self.half = ctx // 2, ctx % 2
        self.z, self.x = exp // 2, exp % 2
        other_half = ctx + 1 - 2 * (ctx % 2)
        self.up, self.down = (ctx, exp + 2), (ctx, exp - 2)
        self.across = (ctx, exp + 1 - 2 * (exp % 2))
        self.core = (other_half, exp)
        self.side = (lax.rem(ctx + 2, 4), exp)
        self.far = (lax.rem(other_half + 2, 4), exp)

    def greet(self, lines=True, square=True):
        barrier = pltpu.get_barrier_semaphore()
        count = jnp.int32(0)
        if square:
            for to in (self.core, self.side, self.far):
                pl.semaphore_signal(barrier, inc=1, device_id=to, device_id_type=MESH)
            count = count + 3
        if lines:
            pl.semaphore_signal(barrier, inc=1, device_id=self.across, device_id_type=MESH)

            @pl.when(self.z < LINES - 1)
            def _():
                pl.semaphore_signal(barrier, inc=1, device_id=self.up, device_id_type=MESH)

            @pl.when(self.z > 0)
            def _():
                pl.semaphore_signal(barrier, inc=1, device_id=self.down, device_id_type=MESH)

            count = count + 1 + jnp.where(self.z < LINES - 1, 1, 0) + jnp.where(self.z > 0, 1, 0)
        pl.semaphore_wait(barrier, count)


class ExpGather:
    def __init__(self, place, view, parts, send, recv):
        self.place, self.view, self.parts = place, view, parts
        self.send, self.recv = send, recv

    def copy(self, lane, line, part, to):
        index = line * 2 + self.place.x
        ref = self.view(index, part)
        return remote(ref, ref, self.send.at[lane, line, part], self.recv.at[index, part], to)

    def pass_on(self, line, part, up, down):
        place = self.place
        if up:

            @pl.when(place.z < LINES - 1)
            def _():
                self.copy(1, line, part, place.up).start()

        if down:

            @pl.when(place.z > 0)
            def _():
                self.copy(2, line, part, place.down).start()

        self.copy(0, line, part, place.across).start()

    def begin(self, part):
        self.pass_on(self.place.z, part, True, True)

    def arrived(self, index, part):
        ref = self.view(index, part)
        remote(
            ref, ref, self.send.at[0, 0, part], self.recv.at[index, part], self.place.across
        ).wait_recv()

    def relay(self, step, part):
        place = self.place

        @pl.when(place.z >= step)
        def _():
            line = place.z - step
            self.arrived(line * 2 + place.x, part)
            self.pass_on(line, part, True, False)

        @pl.when(place.z + step < LINES)
        def _():
            line = place.z + step
            self.arrived(line * 2 + place.x, part)
            self.pass_on(line, part, False, True)

    def relays(self):
        for step in range(1, LINES):
            for part in range(self.parts):
                self.relay(step, part)

    def across_arrived(self, line, part):
        self.arrived(line * 2 + 1 - self.place.x, part)

    def finish(self):
        for part in range(self.parts):
            for line in range(LINES):
                self.across_arrived(line, part)
        self.sent()

    def sent(self):
        place = self.place
        for part in range(self.parts):
            for line in range(LINES):
                self.copy(0, line, part, place.across).wait_send()

                @pl.when((place.z >= line) & (place.z < LINES - 1))
                def _():
                    self.copy(1, line, part, place.up).wait_send()

                @pl.when((place.z <= line) & (place.z > 0))
                def _():
                    self.copy(2, line, part, place.down).wait_send()


def gather_sems(parts):
    return [DMA((3, LINES, parts)), DMA((2 * LINES, parts))]


def raised_slot(line):
    return max(line - 1, 0) if isinstance(line, int) else jnp.maximum(line - 1, 0)


def lowered_slot(line):
    return min(line, LINES - 2) if isinstance(line, int) else jnp.minimum(line, LINES - 2)


class ExpScatter:
    def __init__(self, place, outgoing, mine, crossed, raised, lowered, parts, sems, done=0):
        self.place, self.parts = place, parts
        self.done = done
        self.outgoing, self.mine = outgoing, mine
        self.crossed, self.raised, self.lowered = crossed, raised, lowered
        self.cross_send, self.cross_recv, self.line_send, self.line_recv = sems

    def cross(self, line, part):
        place = self.place
        return remote(
            self.outgoing(line, part),
            self.crossed(line, part),
            self.cross_send.at[line, part],
            self.cross_recv.at[line, part],
            place.across,
        )

    def along(self, up, line, part):
        place = self.place
        side = 0 if up else 1
        return remote(
            self.mine(line, part),
            (self.raised if up else self.lowered)(line, part),
            self.line_send.at[side, line, part],
            self.line_recv.at[side, line, part],
            place.up if up else place.down,
        )

    def begin(self, line, part):
        self.cross(line, part).start()

    def fold(self, part):
        place = self.place
        for line in ORDER:

            @pl.when(place.z != line)
            def _():
                self.cross(line, part).wait_recv()
                ref = self.mine(line, part)
                ref[...] = (to_f32(ref[...]) + to_f32(self.crossed(line, part)[...])).astype(
                    ref.dtype
                )

    def hop(self, stage, part):
        place = self.place
        for up in (True, False):
            here = stage if up else LINES - 1 - stage
            lines = range(LINES - 1, here, -1) if up else range(here)

            @pl.when(place.z == here)
            def _():
                for line in lines:
                    if stage > 0:
                        self.along(up, line, part).wait_recv()
                        ref = self.mine(line, part)
                        came = (self.raised if up else self.lowered)(line, part)
                        ref[...] = (to_f32(ref[...]) + to_f32(came[...])).astype(ref.dtype)
                    self.along(up, line, part).start()

    def total(self, part):
        place = self.place
        line = place.z
        value = to_f32(self.mine(line, part)[...])
        if part >= self.done:
            self.cross(line, part).wait_recv()
            value = value + to_f32(self.crossed(line, part)[...])
        for up in (True, False):
            came = (self.raised if up else self.lowered)(line, part)
            some = line > 0 if up else line < LINES - 1

            @pl.when(some)
            def _():
                self.along(up, line, part).wait_recv()

            value = value + jnp.where(some, to_f32(came[...]), 0.0)
        return value

    def finish(self):
        place = self.place
        for part in range(self.parts):
            for line in range(LINES):
                if part >= self.done:
                    self.cross(line, part).wait_send()
                for up in (True, False):

                    @pl.when(place.z < line if up else place.z > line)
                    def _():
                        self.along(up, line, part).wait_send()


def scatter_sems(parts):
    return [DMA((LINES, parts)), DMA((LINES, parts)), DMA((2, LINES, parts)), DMA((2, LINES, parts))]


class ColumnGather:
    def __init__(self, place, view, send, recv):
        self.place, self.view, self.send, self.recv = place, view, send, recv

    def copy(self, lane, index, to):
        ref = self.view(index)
        return remote(ref, ref, self.send.at[lane, index], self.recv.at[index], to)

    def pass_on(self, index, up, down):
        place = self.place
        if up:

            @pl.when(place.z < LINES - 1)
            def _():
                self.copy(1, index, place.up).start()

        if down:

            @pl.when(place.z > 0)
            def _():
                self.copy(2, index, place.down).start()

    def arrived(self, index):
        ref = self.view(index)
        remote(
            ref, ref, self.send.at[0, index], self.recv.at[index], self.place.across
        ).wait_recv()

    def begin(self):
        self.copy(0, self.place.exp, self.place.across).start()
        self.pass_on(self.place.exp, True, True)

    def turn(self):
        other = self.place.across[1]
        self.arrived(other)
        self.pass_on(other, True, True)

    def relay(self, step):
        place = self.place
        for column in (place.x, 1 - place.x):

            @pl.when(place.z >= step)
            def _():
                index = (place.z - step) * 2 + column
                self.arrived(index)
                self.pass_on(index, True, False)

            @pl.when(place.z + step < LINES)
            def _():
                index = (place.z + step) * 2 + column
                self.arrived(index)
                self.pass_on(index, False, True)

    def sent(self):
        place = self.place
        self.copy(0, place.exp, place.across).wait_send()
        for line in range(LINES):
            for column in range(2):
                index = line * 2 + column

                @pl.when((place.z >= line) & (place.z < LINES - 1))
                def _():
                    self.copy(1, index, place.up).wait_send()

                @pl.when((place.z <= line) & (place.z > 0))
                def _():
                    self.copy(2, index, place.down).wait_send()


def column_sems():
    return [DMA((3, 2 * LINES)), DMA((2 * LINES,))]


class ColumnScatter:
    def __init__(self, place, mine, came, crossed, sems):
        self.place, self.mine, self.came, self.crossed = place, mine, came, crossed
        self.line_send, self.line_recv, self.cross_send, self.cross_recv = sems

    def along(self, up, line, far):
        place = self.place
        side = 0 if up else 1
        slot = raised_slot(line) if up else lowered_slot(line)
        return remote(
            self.mine(line, far),
            self.came(side, far, slot),
            self.line_send.at[side, far, line],
            self.line_recv.at[side, far, line],
            place.up if up else place.down,
        )

    def cross(self):
        return remote(
            self.mine(self.place.z, 1),
            self.crossed,
            self.cross_send.at[0],
            self.cross_recv.at[0],
            self.place.across,
        )

    def hop(self, stage):
        place = self.place
        for up in (True, False):
            here = stage if up else LINES - 1 - stage
            lines = range(LINES - 1, here, -1) if up else range(here)

            @pl.when(place.z == here)
            def _():
                for line in lines:
                    for far in (1, 0):
                        if stage > 0:
                            self.along(up, line, far).wait_recv()
                            ref = self.mine(line, far)
                            slot = raised_slot(line) if up else lowered_slot(line)
                            came = self.came(0 if up else 1, far, slot)
                            ref[...] = (to_f32(ref[...]) + to_f32(came[...])).astype(ref.dtype)
                        self.along(up, line, far).start()

    def line_total(self, far):
        line = self.place.z
        value = to_f32(self.mine(line, far)[...])
        for up in (True, False):
            some = line > 0 if up else line < LINES - 1

            @pl.when(some)
            def _():
                self.along(up, line, far).wait_recv()

            slot = raised_slot(line) if up else lowered_slot(line)
            came = self.came(0 if up else 1, far, slot)
            value = value + jnp.where(some, to_f32(came[...]), 0.0)
        return value

    def turn(self):
        ref = self.mine(self.place.z, 1)
        ref[...] = self.line_total(1).astype(ref.dtype)
        self.cross().start()

    def total(self):
        value = self.line_total(0)
        self.cross().wait_recv()
        return value + to_f32(self.crossed[...])

    def finish(self):
        place = self.place
        self.cross().wait_send()
        for line in range(LINES):
            for far in range(2):
                for up in (True, False):

                    @pl.when(place.z < line if up else place.z > line)
                    def _():
                        self.along(up, line, far).wait_send()


def column_sum_sems():
    return [DMA((2, 2, LINES)), DMA((2, 2, LINES)), DMA((1,)), DMA((1,))]


class CtxGather:
    def __init__(self, place, view, parts, send, recv, own=None):
        self.place, self.view, self.parts = place, view, parts
        self.send, self.recv, self.own = send, recv, own

    def copy(self, lane, part):
        place = self.place
        index = lax.rem(place.ctx + 2, 4) if lane == 2 else place.ctx
        ref = self.view(index, part)
        source = ref if lane == 2 or self.own is None else self.own(part)
        to = place.side if lane == 1 else place.core
        return remote(source, ref, self.send.at[lane, part], self.recv.at[lane, part], to)

    def landed(self, lane, part):
        place = self.place
        index = (place.core, place.side, place.far)[lane][0]
        ref = self.view(index, part)
        return remote(ref, ref, self.send.at[lane, part], self.recv.at[lane, part], place.core)

    def begin(self, part):
        self.copy(1, part).start()
        self.copy(0, part).start()

    def relay(self, part):
        self.landed(1, part).wait_recv()
        self.copy(2, part).start()

    def arrived(self, part):
        self.landed(0, part).wait_recv()
        self.landed(2, part).wait_recv()

    def sent(self, part):
        for lane in range(3):
            self.copy(lane, part).wait_send()


def square_sems(parts):
    return [DMA((3, parts)), DMA((3, parts))]


class CtxScatter:
    def __init__(self, place, outgoing, mine, swapped, crossed, parts, send, recv):
        self.place, self.parts = place, parts
        self.outgoing, self.mine = outgoing, mine
        self.swapped, self.crossed = swapped, crossed
        self.send, self.recv = send, recv

    def swap(self, near, part):
        place = self.place
        y = place.y if near else 1 - place.y
        lane = 0 if near else 1
        return remote(
            self.outgoing(y, part),
            self.swapped(lane, part),
            self.send.at[lane, part],
            self.recv.at[lane, part],
            place.core,
        )

    def over(self, part):
        place = self.place
        return remote(
            self.mine(1 - place.y, part),
            self.crossed(part),
            self.send.at[2, part],
            self.recv.at[2, part],
            place.side,
        )

    def fold(self, part):
        self.swap(False, part).wait_recv()
        ref = self.mine(1 - self.place.y, part)
        ref[...] = (to_f32(ref[...]) + to_f32(self.swapped(1, part)[...])).astype(ref.dtype)
        self.over(part).start()

    def arrived(self, part):
        self.swap(True, part).wait_recv()
        self.over(part).wait_recv()

    def total(self, part, here=slice(None)):
        return (
            to_f32(self.mine(self.place.y, part)[here, :])
            + to_f32(self.swapped(0, part)[here, :])
            + to_f32(self.crossed(part)[here, :])
        )

    def finish(self):
        for part in range(self.parts):
            self.swap(False, part).wait_send()
            self.swap(True, part).wait_send()
            self.over(part).wait_send()


def ahead_kernel(
    tokens,
    gain_attn,
    gain_moe,
    w_router,
    wq,
    wk,
    wv,
    wo,
    routes,
    seg_row,
    cot_hbm,
    in_hbm,
    out_hbm,
    grad_moe_in,
    mixed_part,
    logit_grads,
    in_first,
    down_first,
    in_rest,
    down_rest,
    moe_hbm,
    tokens_hbm,
    weights_hbm,
    out_rows_hbm,
    qkv_hbm,
    heads_hbm,
    norm_rows,
    resid_hbm,
    side_rows,
    moe,
    cot,
    w_in,
    w_out,
    slot_rows,
    slot_cot,
    hidden,
    slopes,
    slot_out,
    pick,
    slot_gate,
    gates,
    all_routes,
    resid_rows,
    moe_crossed,
    moe_raised,
    moe_lowered,
    column_came,
    column_crossed,
    sum_stage,
    load_sem,
    keep_sem,
    store_sem,
    put_sem,
    free_sem,
    tok_send,
    tok_recv,
    swap_send,
    swap_recv,
    w_send,
    w_recv,
    o_send,
    o_recv,
    r_send,
    r_recv,
    c_send,
    c_recv,
    cc_send,
    cc_recv,
    l_send,
    l_recv,
    m_send,
    m_recv,
    mc_send,
    mc_recv,
    i_send,
    i_recv,
    u_send,
    u_recv,
    s_send,
    s_recv,
    moe_xs,
    moe_xr,
    moe_ls,
    moe_lr,
    column_ls,
    column_lr,
    column_xs,
    column_xr,
    cross_sem,
    mix_send,
    mix_recv,
    in_send,
    in_recv,
    down_send,
    down_recv,
):
    place = Place()
    ctx, exp = place.ctx, place.exp
    groups, token_rows, width = moe.shape
    shards = width // in_hbm.shape[1]
    rows = wq.shape[0]
    q_cols, k_cols = wq.shape[1] // shards, wk.shape[1] // shards
    main_cols = q_cols + 2 * k_cols
    side = side_rows.shape[0]
    pack_cols = main_cols + side
    local_experts = w_in.shape[0]
    in_rows, down_rows = in_hbm.shape[1], out_hbm.shape[1]
    slots = pick.shape[1] // local_experts
    first = exp * local_experts
    factor = 1.0 / math.sqrt(HEAD_SIZE)

    def token_block(index):
        return slot_rows.at[index, pl.ds(0, token_rows)]

    def partial(index, start, size):
        return slot_rows.at[index, pl.ds(token_rows + start, size)]

    def out_part(index):
        return slot_rows.at[
            index // LINES, pl.ds(2 * token_rows + lax.rem(index, LINES) * rows, rows)
        ]

    sources = (ctx, place.core[0], place.side[0], place.far[0])

    def weight_part(index, part):
        return slot_cot.at[sources[part], pl.ds(index * rows, rows), pl.ds(0, pack_cols)]

    def packed(shard):
        return slot_cot.at[shard, pl.ds(2 * token_rows, rows), pl.ds(0, pack_cols)]

    def swap_space(lane, start, size):
        return slot_cot.at[lane, pl.ds(token_rows + start, size)]

    def qkv_cols(low, count):
        return slopes[:, :token_rows, low : low + count].reshape(shards * token_rows, count)

    own_in = pltpu.make_async_copy(
        in_hbm, w_in.at[:, pl.ds(ctx * in_rows, in_rows)], load_sem.at[0]
    )
    own_out = pltpu.make_async_copy(
        out_hbm, w_out.at[:, pl.ds(ctx * down_rows, down_rows)], load_sem.at[1]
    )
    own_cot = pltpu.make_async_copy(cot_hbm, cot.at[exp], load_sem.at[2])
    for copy in (own_cot, own_in, own_out):
        copy.start()
    token_block(ctx)[...] = tokens[...]
    diagonal = lax.broadcasted_iota(jnp.int32, (rows, rows), 0) == lax.broadcasted_iota(
        jnp.int32, (rows, rows), 1
    )
    gain_cols = [
        jnp.sum(jnp.where(diagonal, to_f32(gain[...]), 0.0), 1, keepdims=True)
        for gain in (gain_attn, gain_moe)
    ]
    lane = lax.broadcasted_iota(jnp.int32, (1, side - EXPERTS), 1)
    gain_cols = jnp.where(
        lane == 0, gain_cols[0], jnp.where(lane == 1, gain_cols[1], 0.0)
    ).astype(jnp.bfloat16)
    for shard in range(shards):
        target = packed(shard)
        target[:, :q_cols] = wq[:, shard * q_cols : (shard + 1) * q_cols]
        target[:, q_cols : q_cols + k_cols] = wk[:, shard * k_cols : (shard + 1) * k_cols]
        target[:, q_cols + k_cols : main_cols] = wv[:, shard * k_cols : (shard + 1) * k_cols]
        target[:, main_cols : main_cols + EXPERTS] = w_router[...]
        target[:, main_cols + EXPERTS :] = gain_cols

    def weight_slot(shard):
        return slot_cot.at[shard, pl.ds(exp * rows, rows), pl.ds(0, pack_cols)]

    weight_slot(ctx)[...] = packed(ctx)[...]
    out_part(exp)[...] = wo[...]
    all_routes[exp] = routes[...]
    place.greet()

    mixes = []
    for lane, to in enumerate((place.core, place.side, place.far)):
        copy = remote(
            packed(to[0]),
            weight_slot(ctx),
            swap_send.at[lane],
            swap_recv.at[lane],
            to,
        )
        copy.start()
        mixes.append(copy)
    half_rows = token_rows // 2
    token_gather = CtxGather(
        place,
        lambda index, part: slot_rows.at[index, pl.ds(part * half_rows, half_rows)],
        2,
        tok_send,
        tok_recv,
    )
    for part in range(2):
        token_gather.begin(part)
    route_gather = ExpGather(place, lambda index, part: all_routes.at[index], 1, r_send, r_recv)
    weight_gather = ExpGather(place, weight_part, shards, w_send, w_recv)
    out_gather = ExpGather(place, lambda index, part: out_part(index), 1, o_send, o_recv)
    weight_gather.begin(0)
    for lane, copy in enumerate(mixes):
        remote(
            packed(0),
            weight_slot(sources[1 + lane]),
            swap_send.at[lane],
            swap_recv.at[lane],
            place.core,
        ).wait_recv()
        weight_gather.begin(1 + lane)
    route_gather.begin(0)
    out_gather.begin(0)
    in_gather = CtxGather(
        place,
        lambda index, part: w_in.at[part, pl.ds(index * in_rows, in_rows)],
        local_experts,
        i_send,
        i_recv,
    )
    down_gather = CtxGather(
        place,
        lambda index, part: w_out.at[part, pl.ds(index * down_rows, down_rows)],
        local_experts,
        u_send,
        u_recv,
    )
    cot_parts = c_send.shape[2]
    late_rows = COT_LATE
    cot_rows = (token_rows - late_rows - COLUMN) // cot_parts
    cot_gather = ExpGather(
        place,
        lambda index, part: cot.at[index, pl.ds(part * cot_rows, cot_rows)],
        cot_parts,
        c_send,
        c_recv,
    )
    late_gather = ExpGather(
        place,
        lambda index, part: cot.at[index, pl.ds(token_rows - COLUMN - late_rows, late_rows)],
        1,
        l_send,
        l_recv,
    )
    column_rows = pl.ds(token_rows - COLUMN, COLUMN)
    cot_column = ColumnGather(place, lambda index: cot.at[index, column_rows], cc_send, cc_recv)
    own_in.wait()
    half_experts = local_experts // 2
    for part in range(half_experts):
        in_gather.begin(part)
    for step in range(1, LINES):
        for part in range(shards):
            weight_gather.relay(step, part)
        if step < LINES - 1:
            token_gather.relay(step - 1)
    own_cot.wait()
    own_out.wait()
    for step in range(1, LINES):
        out_gather.relay(step, 0)
        route_gather.relay(step, 0)
    cot_column.begin()
    for part in range(cot_parts):
        cot_gather.begin(part)
    for part in range(2):
        token_gather.arrived(part)
    weight_gather.finish()

    same = (
        lax.broadcasted_iota(jnp.int32, (side, side), 0)
        == lax.broadcasted_iota(jnp.int32, (side, side), 1)
    ).astype(jnp.bfloat16)
    full = slot_cot[:, :token_rows, :pack_cols].reshape(width, pack_cols)
    side_t = outer_cols(same, full[:, main_cols:])
    side_rows[...] = side_t.astype(jnp.bfloat16)
    gain_one, gain_two = side_t[EXPERTS : EXPERTS + 1], side_t[EXPERTS + 1 : EXPERTS + 2]
    for block in range(shards):
        values = to_f32(token_block(block)[...])
        normed = (values * rms_scale(values) * gain_one).astype(jnp.bfloat16)
        slopes[block, :token_rows, :main_cols] = dot_rows(normed, full[:, :main_cols]).astype(
            jnp.bfloat16
        )

    low = lax.broadcasted_iota(jnp.int32, (1, 2 * HEAD_SIZE), 1) < HEAD_SIZE

    def spread(start):
        plain = to_f32(qkv_cols(start, k_cols))
        turned = pltpu.roll(plain, HEAD_SIZE, 1)
        zero = jnp.zeros((), jnp.float32)
        return [
            [
                jnp.where(low, plain, zero).astype(jnp.bfloat16),
                jnp.where(low, zero, turned).astype(jnp.bfloat16),
            ],
            [
                jnp.where(low, turned, zero).astype(jnp.bfloat16),
                jnp.where(low, zero, plain).astype(jnp.bfloat16),
            ],
        ]

    keys, values = spread(q_cols), spread(q_cols + k_cols)
    parts = slot_rows.shape[1] - 2 * token_rows
    attn_low = {}
    keep = []
    for block in range(shards - 1, -1, -1):
        count = (block + 1) * token_rows
        at_row = block * token_rows + lax.broadcasted_iota(jnp.int32, (token_rows, 1), 0)
        at_col = lax.broadcasted_iota(jnp.int32, (1, count), 1)
        documents = seg_row[:, block * token_rows : count].astype(jnp.float32)
        own_document = jnp.broadcast_to(documents, (128, token_rows)).T[:, :1]
        bias = jnp.where(
            (at_col <= at_row) & (own_document == seg_row[:, :count].astype(jnp.float32)),
            0.0,
            MASK_FILLER,
        )
        lows = []
        norms = jnp.zeros((token_rows, 128), jnp.float32)
        at_lane = lax.broadcasted_iota(jnp.int32, (1, 128), 1)
        for pair in range(2):
            queries = slopes[block, :token_rows, pair * 128 : pair * 128 + 128]
            heads = jnp.zeros((token_rows, 128), jnp.float32)
            for head in range(2):
                scores = outer_cols(queries, keys[pair][head][:count]) * factor + bias
                top = jnp.max(scores, -1, keepdims=True)
                shares = jnp.exp(scores - top)
                total = jnp.sum(shares, -1, keepdims=True)
                norms = jnp.where(at_lane == 2 * pair + head, top + jnp.log(total), norms)
                heads = heads + dot_rows(
                    shares.astype(jnp.bfloat16), values[pair][head][:count]
                ) / total
            start = block * q_cols + pair * 128
            resid_rows[:, start : start + 128] = heads
            lows.append(heads.astype(jnp.bfloat16))
        norm_rows[:, block * token_rows : count] = norms.T[:8]
        attn_low[block] = jnp.concatenate(lows, 1)
        keep.append(
            pltpu.make_async_copy(
                resid_rows.at[:, pl.ds(block * q_cols, q_cols)],
                heads_hbm.at[pl.ds(block * token_rows, token_rows)],
                keep_sem.at[len(keep)],
            )
        )
        keep[-1].start()
        if block == 2:
            cot_column.turn()
            for part in range(cot_parts):
                cot_gather.relay(1, part)

    out_gather.finish()
    full_out = jnp.concatenate(
        [slot_rows[part, 2 * token_rows :, :] for part in range(q_cols // parts)], 0
    )
    for block in range(shards):
        partial(block, 0, token_rows)[...] = dot_rows(attn_low[block], full_out).astype(
            jnp.bfloat16
        )
    stored = len(keep)
    here = pl.ds(0, token_rows)
    for source, target in (
        (slot_rows.at[:, here], tokens_hbm),
        (slot_cot.at[:, here, pl.ds(0, pack_cols)], weights_hbm),
        (slopes.at[:, here, pl.ds(0, main_cols)], qkv_hbm),
        (slot_rows.at[pl.ds(0, q_cols // parts), pl.ds(2 * token_rows, parts)], out_rows_hbm),
    ):
        keep.append(pltpu.make_async_copy(source, target, keep_sem.at[len(keep)]))
        keep[-1].start()

    branch = CtxScatter(
        place,
        lambda y, part: partial(2 * y + 1 - place.half, part * half_rows, half_rows),
        lambda y, part: partial(2 * y + place.half, part * half_rows, half_rows),
        lambda lane, part: swap_space(lane, part * half_rows, half_rows),
        lambda part: swap_space(2, part * half_rows, half_rows),
        2,
        s_send,
        s_recv,
    )
    for part in range(2):
        branch.swap(False, part).start()
    for part in range(2):
        branch.swap(True, part).start()
    cot_column.relay(1)
    for part in range(cot_parts):
        cot_gather.relay(2, part)
    for part in range(2):
        branch.fold(part)
    for part in range(half_experts, local_experts):
        in_gather.begin(part)
    for part in range(local_experts):
        down_gather.begin(part)
    gather_parts = len(CUTS)
    moe_gather = ExpGather(
        place,
        lambda index, part: moe.at[index, pl.ds(*CUTS[part])],
        gather_parts,
        m_send,
        m_recv,
    )
    moe_column = ColumnGather(place, lambda index: moe.at[index, column_rows], mc_send, mc_recv)
    cot_column.relay(2)
    for copy in keep[:stored]:
        copy.wait()
    for part in range(2):
        here = pl.ds(part * half_rows, half_rows)
        branch.arrived(part)
        resid = to_f32(tokens[here, :]) + branch.total(part)
        resid_rows[here, :] = resid
        moe[exp, here, :] = (resid * rms_scale(resid) * gain_two).astype(jnp.bfloat16)
        if part == 1:
            moe_column.begin()
        for piece, (start, size) in enumerate(CUTS):
            if start // half_rows == part:
                moe_gather.begin(piece)
    keep.append(pltpu.make_async_copy(resid_rows, resid_hbm, keep_sem.at[len(keep)]))
    keep[-1].start()
    cot_column.relay(3)
    for part in range(cot_parts):
        cot_gather.relay(3, part)
    for part in range(half_experts):
        in_gather.relay(part)
    moe_column.turn()
    for step in range(1, LINES):
        for part in range(gather_parts):
            moe_gather.relay(step, part)
        moe_column.relay(step)
    late_gather.begin(0)
    for part in range(half_experts, local_experts):
        in_gather.relay(part)
    route_gather.finish()
    branch.finish()
    for part in range(2):
        token_gather.sent(part)
    for copy in mixes:
        copy.wait_send()
    for copy in keep[stored:]:
        copy.wait()

    at_expert = lax.broadcasted_iota(jnp.int32, (EXPERTS, 1), 0)
    at_lane = lax.broadcasted_iota(jnp.int32, (1, 128), 1)
    at_slot = lax.broadcasted_iota(jnp.int32, (slots, 1), 0)
    before = (
        lax.broadcasted_iota(jnp.int32, (token_rows, token_rows), 0)
        < lax.broadcasted_iota(jnp.int32, (token_rows, token_rows), 1)
    ).astype(jnp.bfloat16)
    router = side_rows[:EXPERTS, :]
    all_slots = groups * slots
    def block_of(line, far):
        return line * 2 + (1 - place.x if far else place.x)

    def slot_range(line, far):
        start = (far * LINES + line) * slots
        return pl.ds(start if isinstance(line, int) else pl.multiple_of(start, slots), slots)

    def dispatch(line, far):
        block = block_of(line, far)
        routes = all_routes[block]
        member = routes[0:1, :] == at_expert
        for rank in range(1, TOPK):
            member = member | (routes[rank : rank + 1, :] == at_expert)
        tokens = moe[block]
        logits = outer_cols(router, tokens)
        top = jnp.max(jnp.where(member, logits, MASK_FILLER), 0, keepdims=True)
        weights = jnp.where(member, jnp.exp(logits - top), 0.0)
        shares = weights / jnp.sum(weights, 0, keepdims=True)
        gates[block] = shares
        ranks = dot_rows(jnp.where(member, 1.0, 0.0).astype(jnp.bfloat16), before)
        filled = jnp.where(member & (ranks < CAP), ranks, -1.0)
        columns = jnp.zeros((slots, 128), jnp.float32)
        for expert in range(local_experts):
            mine = at_expert == first + expert
            spot = jnp.sum(jnp.where(mine, filled, 0.0), 0, keepdims=True)
            share = jnp.sum(jnp.where(mine, shares, 0.0), 0, keepdims=True)
            chosen = spot == at_slot.astype(jnp.float32)
            here = pl.ds(expert * slots, slots)
            pick[block, here, :] = jnp.where(chosen, 1.0, 0.0).astype(jnp.bfloat16)
            column = jnp.sum(jnp.where(chosen, share, 0.0), 1, keepdims=True)
            columns = jnp.where(at_lane == expert, column, columns)
        slot_gate[block] = columns
        chosen = pick[block]
        rows = dot_rows(chosen, tokens).astype(jnp.bfloat16)
        here = slot_range(line, far)
        for expert in range(local_experts):
            slot_rows[expert, here, :] = rows[expert * slots : (expert + 1) * slots]

    half_slots = all_slots // 2

    def each(count, body, far):
        def step(index, carry):
            body(index, far)
            return carry

        lax.fori_loop(0, count, step, 0)

    def near_line(step, carry):
        dispatch(place.z ^ step, 0)
        return carry

    def far_line(step, carry):
        line = place.z ^ step
        for part in range(gather_parts):
            moe_gather.across_arrived(line, part)
        dispatch(line, 1)
        return carry

    lax.fori_loop(0, LINES, near_line, 0)
    for part in range(local_experts):
        down_gather.relay(part)
    for part in range(local_experts):
        in_gather.arrived(part)
        down_gather.arrived(part)
    def forward(expert, far):
        half = pl.ds(far * half_slots, half_slots)
        rows = slot_rows[expert, half, :]
        for first_col in range(0, FF, 256):
            gate_cols, up_cols = pl.ds(first_col, 256), pl.ds(FF + first_col, 256)
            gate_part = dot_rows(rows, w_in[expert, :, gate_cols])
            up_part = dot_rows(rows, w_in[expert, :, up_cols])
            sigmoid_gate = jax.nn.sigmoid(gate_part)
            silu = gate_part * sigmoid_gate
            hidden[expert, half, gate_cols] = (silu * up_part).astype(jnp.bfloat16)
            slopes[expert, half, gate_cols] = (
                up_part * sigmoid_gate * (1.0 + gate_part * (1.0 - sigmoid_gate))
            ).astype(jnp.bfloat16)
            slopes[expert, half, up_cols] = silu.astype(jnp.bfloat16)
        slot_out[expert, half, :] = dot_rows(hidden[expert, half, :], w_out[expert]).astype(
            jnp.bfloat16
        )

    each(local_experts, forward, 0)
    lax.fori_loop(0, LINES, far_line, 0)
    moe_gather.sent()
    moe_column.sent()
    moe_store = pltpu.make_async_copy(moe, moe_hbm, load_sem.at[0])
    moe_store.start()
    late_gather.relay(1, 0)
    each(local_experts, forward, 1)
    late_gather.relay(2, 0)
    moe_store.wait()

    def block_rows(line, far):
        here = slot_range(line, far)
        return jnp.concatenate([slot_out[expert, here, :] for expert in range(local_experts)], 0)

    def combine(line, far):
        block = block_of(line, far)
        shares = gates[block]
        weighted = []
        for expert in range(local_experts):
            mine = at_expert == first + expert
            share = jnp.sum(jnp.where(mine, shares, 0.0), 0, keepdims=True)
            chosen = to_f32(pick[block, pl.ds(expert * slots, slots), :])
            weighted.append((chosen * share).astype(jnp.bfloat16))
        moe[block] = inner_rows(
            jnp.concatenate(weighted, 0), block_rows(line, far)
        ).astype(jnp.bfloat16)

    each(LINES, combine, 0)
    late_gather.relay(3, 0)
    each(LINES, combine, 1)
    mix_rows = pl.ds(*MIX_CUTS[0])
    later_rows = pl.ds(MIX_CUTS[0][1], token_rows - MIX_CUTS[0][1])
    part_store = pltpu.make_async_copy(
        moe.at[:, later_rows], mixed_part.at[:, later_rows], load_sem.at[0]
    )
    part_store.start()

    cot_gather.finish()
    cot_column.sent()
    late_gather.finish()

    def dispatch_back(line, far):
        block = block_of(line, far)
        shares = gates[block]
        chosen = pick[block]
        cots = dot_rows(chosen, cot[block])
        dots = jnp.sum(cots * to_f32(block_rows(line, far)), 1, keepdims=True)
        picked_grads = jnp.zeros_like(shares)
        there = slot_range(line, far)
        for expert in range(local_experts):
            here = slice(expert * slots, (expert + 1) * slots)
            row = jnp.sum(to_f32(chosen[here]) * dots[here], 0, keepdims=True)
            picked_grads = jnp.where(at_expert == first + expert, row, picked_grads)
            share = slot_gate[block, :, expert : expert + 1]
            slot_cot[expert, there, :] = (share * cots[here]).astype(jnp.bfloat16)
        grads = shares * (picked_grads - jnp.sum(shares * picked_grads, 0, keepdims=True))
        high, low = two_parts(grads)
        logit_grads[block] = jnp.concatenate([high, low], 0)

    def backward(expert, far):
        half = pl.ds(far * half_slots, half_slots)
        grads = outer_cols(slot_cot[expert, half, :], w_out[expert])
        slopes[expert, half, :FF] = (grads * to_f32(slopes[expert, half, :FF])).astype(jnp.bfloat16)
        slopes[expert, half, FF:] = (grads * to_f32(slopes[expert, half, FF:])).astype(jnp.bfloat16)
        slot_out[expert, half, :] = outer_cols(slopes[expert, half, :], w_in[expert]).astype(
            jnp.bfloat16
        )

    def combine_back(line, far):
        block = block_of(line, far)
        left = jnp.concatenate([pick[block], logit_grads[block]], 0)
        right = jnp.concatenate([block_rows(line, far), router, router], 0)
        cot[block] = inner_rows(left, right).astype(jnp.bfloat16)

    moe_parts = len(CUTS)

    def piece(ref, part):
        return ref.at[pl.ds(*CUTS[part])]

    back_sum = ExpScatter(
        place,
        lambda line, part: piece(cot.at[line * 2 + 1 - place.x], part),
        lambda line, part: piece(cot.at[line * 2 + place.x], part),
        lambda line, part: piece(moe_crossed.at[line], part),
        lambda line, part: piece(moe_raised.at[raised_slot(line)], part),
        lambda line, part: piece(moe_lowered.at[lowered_slot(line)], part),
        moe_parts,
        (moe_xs, moe_xr, moe_ls, moe_lr),
    )
    column_sum = ColumnScatter(
        place,
        lambda line, far: cot.at[block_of(line, far), column_rows],
        lambda side, far, slot: column_came.at[side, far, slot],
        column_crossed,
        (column_ls, column_lr, column_xs, column_xr),
    )
    each(LINES, dispatch_back, 1)
    each(local_experts, backward, 1)
    each(LINES, combine_back, 1)
    for part in range(moe_parts):
        for line in ORDER:
            back_sum.begin(line, part)
    each(LINES, dispatch_back, 0)
    each(local_experts, backward, 0)
    each(LINES, combine_back, 0)

    for to in (place.core, place.side):
        pl.semaphore_signal(free_sem, inc=1, device_id=to, device_id_type=MESH)

    early = in_first.shape[0]
    for part in range(local_experts):
        in_gather.sent(part)
        down_gather.sent(part)
    into = CtxScatter(
        place,
        lambda y, part: w_in.at[part, pl.ds((2 * y + 1 - place.half) * in_rows, in_rows)],
        lambda y, part: w_in.at[part, pl.ds((2 * y + place.half) * in_rows, in_rows)],
        lambda lane, part: slot_out.at[part, pl.ds(lane * in_rows, in_rows)],
        lambda part: slot_out.at[early + part, pl.ds(2 * down_rows, in_rows)],
        early,
        in_send,
        in_recv,
    )
    downs = CtxScatter(
        place,
        lambda y, part: w_out.at[part, pl.ds((2 * y + 1 - place.half) * down_rows, down_rows)],
        lambda y, part: w_out.at[part, pl.ds((2 * y + place.half) * down_rows, down_rows)],
        lambda lane, part: slot_out.at[early + part, pl.ds(lane * down_rows, down_rows)],
        lambda part: slot_out.at[early + part, pl.ds(2 * down_rows + in_rows, down_rows)],
        early,
        down_send,
        down_recv,
    )
    part_store.wait()
    pl.semaphore_wait(free_sem, 2)
    stores = []

    def store(source, target, sem):
        copy = pltpu.make_async_copy(source, target, sem)
        copy.start()
        stores.append(copy)

    column_sum.hop(0)
    for expert in range(local_experts):
        w_out[expert] = inner_rows(hidden[expert], slot_cot[expert]).astype(jnp.bfloat16)
        if expert < early:
            downs.swap(False, expert).start()
            downs.swap(True, expert).start()
        else:
            store(w_out.at[expert], down_rest.at[expert - early], store_sem.at[0, expert])
        w_in[expert] = inner_rows(slot_rows[expert], slopes[expert]).astype(jnp.bfloat16)
        if expert < early:
            into.swap(False, expert).start()
            into.swap(True, expert).start()
        else:
            store(w_in.at[expert], in_rest.at[expert - early], store_sem.at[1, expert])
        if expert > 0 and expert <= early:
            downs.fold(expert - 1)
            into.fold(expert - 1)
        if expert == 1:
            back_sum.fold(0)
            back_sum.hop(0, 0)
            column_sum.hop(1)
    pl.semaphore_signal(cross_sem, inc=1, device_id=place.across, device_id_type=MESH)

    def mix_cross(line):
        return remote(
            moe.at[line * 2 + 1 - place.x, mix_rows],
            slot_rows.at[line, mix_rows],
            mix_send.at[line],
            mix_recv.at[line],
            place.across,
        )

    for part in range(1, moe_parts + 2):
        if part == 1:
            column_sum.hop(2)
        if part == moe_parts - 1:
            pl.semaphore_wait(cross_sem, 1)
            for line in ORDER:
                mix_cross(line).start()
        if part == 2:
            column_sum.turn()
        if part >= 2:
            back_sum.hop(2, part - 2)
        if part <= moe_parts:
            back_sum.hop(1, part - 1)
        if part < moe_parts:
            back_sum.fold(part)
            back_sum.hop(0, part)

    staged = [None, None]
    stage_rows = sum_stage.shape[1]

    def put(slot, value, target, sem):
        if staged[slot] is not None:
            staged[slot].wait()
        stage = sum_stage.at[slot, pl.ds(0, value.shape[0])]
        stage[...] = value
        staged[slot] = pltpu.make_async_copy(stage, target, sem)
        staged[slot].start()

    def finish_expert(part):
        for kind, (scatter, target) in enumerate(((downs, down_first), (into, in_first))):
            scatter.arrived(part)
            held = scatter.mine(place.y, part)
            held[...] = scatter.total(part).astype(jnp.bfloat16)
            store(held, target.at[part], store_sem.at[kind, part])

    for part in range(early - 1):
        finish_expert(part)
    mix_stores = []
    for part in range(moe_parts):
        here = pl.ds(*CUTS[part])
        put(part % 2, back_sum.total(part), grad_moe_in.at[here], put_sem.at[part % 2])
    put(moe_parts % 2, column_sum.total(), grad_moe_in.at[column_rows], put_sem.at[moe_parts % 2])
    finish_expert(early - 1)
    for line in ORDER:
        mix_cross(line).wait_recv()
        block = line * 2 + place.x
        moe[block, mix_rows, :] = (
            to_f32(moe[block, mix_rows, :]) + to_f32(slot_rows[line, mix_rows, :])
        ).astype(jnp.bfloat16)
        mix_stores.append(
            pltpu.make_async_copy(
                moe.at[block, mix_rows], mixed_part.at[block, mix_rows], load_sem.at[1 + line]
            )
        )
        mix_stores[-1].start()
    for line in ORDER:
        mix_cross(line).wait_send()
    for copy in mix_stores:
        copy.wait()
    for copy in staged:
        copy.wait()
    for copy in stores:
        copy.wait()
    for scatter in (back_sum, column_sum, into, downs):
        scatter.finish()


EARLY = 2


def ahead(
    tokens, gain_attn, gain_moe, w_router, wq, wk, wv, wo, routes, seg_row, cot, exp_in, exp_out
):
    shards, groups = lax.axis_size("ctx"), lax.axis_size("exp")
    token_rows, width = tokens.shape
    rows = wq.shape[0]
    q_cols, k_cols = wq.shape[1] // shards, wk.shape[1] // shards
    main_cols = q_cols + 2 * k_cols
    side = 128
    pack_cols = main_cols + side
    seq_len = token_rows * shards
    low, f32 = jnp.bfloat16, jnp.float32
    local_experts, in_rows, in_cols = exp_in.shape
    down_rows = exp_out.shape[1]
    slots = -(-CAP // 16) * 16
    arena = (local_experts, groups * slots)

    def shape(dims, dtype):
        return jax.ShapeDtypeStruct(dims, dtype)

    whole, anywhere = pl.BlockSpec(memory_space=VMEM), pl.BlockSpec(memory_space=pl.ANY)
    rest = local_experts - EARLY
    block, steps = (LINES, token_rows, width), (LINES - 1, token_rows, width)
    out_parts = groups * slots - 2 * token_rows
    return pl.pallas_call(
        ahead_kernel,
        name="ahead",
        out_shape=[
            shape((token_rows, width), f32),
            shape((groups, token_rows, width), low),
            shape((groups, 2 * EXPERTS, token_rows), low),
            shape((EARLY, in_rows, in_cols), low),
            shape((EARLY, down_rows, width), low),
            shape((rest, width, in_cols), low),
            shape((rest, FF, width), low),
            shape((groups, token_rows, width), low),
            shape((shards, token_rows, width), low),
            shape((shards, groups * rows, pack_cols), low),
            shape((q_cols // out_parts, out_parts, width), low),
            shape((shards, token_rows, main_cols), low),
            shape((seq_len, q_cols), f32),
            shape((8, seq_len), f32),
            shape((token_rows, width), f32),
            shape((side, width), low),
        ],
        in_specs=[whole] * 10 + [anywhere] * 3,
        out_specs=[anywhere, anywhere, whole]
        + [anywhere] * 10
        + [whole, anywhere, whole],
        scratch_shapes=[
            VMEM((groups, token_rows, width), low),
            VMEM((groups, token_rows, width), low),
            VMEM((local_experts, width, in_cols), low),
            VMEM((local_experts, FF, width), low),
            VMEM(arena + (width,), low),
            VMEM(arena + (width,), low),
            VMEM(arena + (FF,), low),
            VMEM(arena + (2 * FF,), low),
            VMEM(arena + (width,), low),
            VMEM((groups, local_experts * slots, token_rows), low),
            VMEM((groups, slots, 128), f32),
            VMEM((groups, EXPERTS, token_rows), f32),
            VMEM((groups,) + routes.shape, jnp.int32),
            VMEM((token_rows, width), f32),
            VMEM(block, low),
            VMEM(steps, low),
            VMEM(steps, low),
            VMEM((2, 2, LINES - 1, COLUMN, width), low),
            VMEM((COLUMN, width), low),
            VMEM((2, max(size for _, size in CUTS), width), f32),
            DMA((1 + LINES,)),
            DMA((shards + 5,)),
            DMA((2, local_experts)),
            DMA((2,)),
            pltpu.SemaphoreType.REGULAR,
            *square_sems(2),
            DMA((3,)),
            DMA((3,)),
            *gather_sems(shards),
            *gather_sems(1),
            *gather_sems(1),
            *gather_sems(2),
            *column_sems(),
            *gather_sems(1),
            *gather_sems(len(CUTS)),
            *column_sems(),
            *square_sems(local_experts),
            *square_sems(local_experts),
            *square_sems(2),
            *scatter_sems(len(CUTS)),
            *column_sum_sems(),
            pltpu.SemaphoreType.REGULAR,
            DMA((LINES,)),
            DMA((LINES,)),
            *square_sems(EARLY),
            *square_sems(EARLY),
        ],
        compiler_params=pltpu.CompilerParams(
            collective_id=0, has_side_effects=True, vmem_limit_bytes=63 * 2**20
        ),
    )(tokens, gain_attn, gain_moe, w_router, wq, wk, wv, wo, routes, seg_row, cot, exp_in, exp_out)


def back_kernel(
    moe_in_grads,
    mixed_part,
    grad_in,
    grad_down,
    in_first,
    down_first,
    tokens,
    cot,
    resid,
    side_rows,
    logit_grads,
    all_moe_hbm,
    all_tokens_hbm,
    weights_hbm,
    out_rows_hbm,
    qkv_hbm,
    heads_out_hbm,
    norm_rows,
    seg_row,
    mixed_out,
    grad_tokens,
    query_sum,
    key_sum,
    value_sum,
    side_sum,
    output_sum,
    in_sum,
    down_sum,
    mix_mine,
    mix_crossed,
    mix_raised,
    mix_lowered,
    column_mine,
    column_came,
    column_crossed,
    in_mine,
    in_swapped,
    in_crossed,
    down_mine,
    down_swapped,
    down_crossed,
    grad_resid,
    all_resid,
    head_grads,
    turned,
    key_grads,
    value_grads,
    qkv_grads,
    normed_part,
    normed_swapped,
    normed_crossed,
    sums,
    sums_crossed,
    sums_raised,
    sums_lowered,
    sums_own,
    sums_all,
    out_grads,
    out_crossed,
    out_raised,
    out_lowered,
    in_stage,
    down_stage,
    store_sem,
    all_moe,
    all_tokens,
    weights,
    out_rows,
    qkv,
    heads_out,
    late_sem,
    early_sem,
    local_sem,
    mix_xs,
    mix_xr,
    mix_ls,
    mix_lr,
    column_ls,
    column_lr,
    column_xs,
    column_xr,
    sum_xs,
    sum_xr,
    sum_ls,
    sum_lr,
    out_xs,
    out_xr,
    out_ls,
    out_lr,
    in_send,
    in_recv,
    down_send,
    down_recv,
    normed_send,
    normed_recv,
    resid_send,
    resid_recv,
    last_send,
    last_recv,
):
    place = Place()
    ctx, exp = place.ctx, place.exp
    token_rows, width = tokens.shape
    shards, groups, rows, pack_cols = weights.shape
    local_experts = grad_in.shape[0]
    q_cols = heads_out.shape[1]
    main_cols = qkv.shape[1]
    k_cols = (main_cols - q_cols) // 2
    factor = 1.0 / math.sqrt(HEAD_SIZE)

    loads = []

    def load(source, target):
        copy = pltpu.make_async_copy(source, target, local_sem.at[len(loads)])
        copy.start()
        loads.append(copy)

    for y in range(2):
        load(grad_in.at[:, 2 * y + place.half], in_mine.at[y])
        load(grad_down.at[:, 2 * y + place.half], down_mine.at[y])
    mix_rows = sum(size for _, size in MIX_CUTS)
    for line in ORDER:
        load(mixed_part.at[line * 2 + place.x, pl.ds(0, mix_rows)], mix_mine.at[line])
    load(mixed_part.at[:, pl.ds(mix_rows, COLUMN)], column_mine)
    place.greet()

    def piece(ref, count, part):
        size = ref.shape[0] // count
        return ref.at[pl.ds(part * size, size)]

    moe_parts, mix_parts = 4, len(MIX_CUTS)

    def cut(ref, part):
        return ref.at[pl.ds(*MIX_CUTS[part])]

    mix = ExpScatter(
        place,
        lambda line, part: cut(mixed_part.at[line * 2 + 1 - place.x], part),
        lambda line, part: cut(mix_mine.at[line], part),
        lambda line, part: cut(mix_crossed.at[line], part),
        lambda line, part: cut(mix_raised.at[raised_slot(line)], part),
        lambda line, part: cut(mix_lowered.at[lowered_slot(line)], part),
        mix_parts,
        (mix_xs, mix_xr, mix_ls, mix_lr),
        1,
    )
    column_sum = ColumnScatter(
        place,
        lambda line, far: column_mine.at[line * 2 + (1 - place.x if far else place.x)],
        lambda side, far, slot: column_came.at[side, far, slot],
        column_crossed,
        (column_ls, column_lr, column_xs, column_xr),
    )
    into = CtxScatter(
        place,
        lambda y, part: grad_in.at[part, 2 * y + 1 - place.half],
        lambda y, part: in_mine.at[y, part],
        lambda lane, part: in_swapped.at[lane, part],
        lambda part: in_crossed.at[part],
        local_experts,
        in_send,
        in_recv,
    )
    downs = CtxScatter(
        place,
        lambda y, part: grad_down.at[part, 2 * y + 1 - place.half],
        lambda y, part: down_mine.at[y, part],
        lambda lane, part: down_swapped.at[lane, part],
        lambda part: down_crossed.at[part],
        local_experts,
        down_send,
        down_recv,
    )
    for near in (False, True):
        for part in range(local_experts):
            into.swap(near, part).start()
        for part in range(local_experts):
            downs.swap(near, part).start()
    early_loads = [
        pltpu.make_async_copy(source, target, early_sem.at[index])
        for index, (source, target) in enumerate(((in_first, in_stage), (down_first, down_stage)))
    ]
    for copy in early_loads:
        copy.start()
    gain_one_row = to_f32(side_rows[EXPERTS : EXPERTS + 1, :])
    gain_two_row = to_f32(side_rows[EXPERTS + 1 : EXPERTS + 2, :])
    moe_rows = token_rows // moe_parts
    gain_two_sum = jnp.zeros((1, width), jnp.float32)
    resid_gather = CtxGather(
        place,
        lambda index, part: all_resid.at[index, pl.ds(part * moe_rows, moe_rows)],
        moe_parts,
        resid_send,
        resid_recv,
    )
    for part in range(moe_parts):
        here = pl.ds(part * moe_rows, moe_rows)
        grad_moe_in = moe_in_grads[here, :]
        values = resid[here, :]
        scale = rms_scale(values)
        weighted = grad_moe_in * gain_two_row
        gain_two_sum = gain_two_sum + jnp.sum(grad_moe_in * values * scale, 0, keepdims=True)
        grads = (
            to_f32(cot[here, :])
            + scale * weighted
            - values * (scale * scale * scale) * jnp.mean(weighted * values, -1, keepdims=True)
        )
        grad_resid[here, :] = grads
        all_resid[ctx, here, :] = grads.astype(jnp.bfloat16)
        resid_gather.begin(part)
    for part in range(1, mix_parts):
        for line in ORDER:
            mix.begin(line, part)
    for copy in loads:
        copy.wait()
    column_sum.hop(0)
    late = []
    for index, (source, target) in enumerate(
        (
            (all_moe_hbm, all_moe),
            (qkv_hbm, qkv),
            (out_rows_hbm, out_rows),
            (heads_out_hbm, heads_out),
            (weights_hbm, weights),
            (all_tokens_hbm, all_tokens),
        )
    ):
        late.append(pltpu.make_async_copy(source, target, late_sem.at[index]))
        late[-1].start()

    low = lax.broadcasted_iota(jnp.int32, (1, 2 * HEAD_SIZE), 1) < HEAD_SIZE

    def spread(first):
        plain = to_f32(qkv[:, first : first + k_cols])
        other = pltpu.roll(plain, HEAD_SIZE, 1)
        zero = jnp.zeros((), jnp.float32)
        return [
            [
                jnp.where(low, plain, zero).astype(jnp.bfloat16),
                jnp.where(low, zero, other).astype(jnp.bfloat16),
            ],
            [
                jnp.where(low, other, zero).astype(jnp.bfloat16),
                jnp.where(low, zero, plain).astype(jnp.bfloat16),
            ],
        ]

    for copy in early_loads:
        copy.wait()
    early_stores = [
        pltpu.make_async_copy(source, target, early_sem.at[index])
        for index, (source, target) in enumerate(
            (
                (in_stage, in_sum.at[pl.ds(0, EARLY)]),
                (down_stage, down_sum.at[pl.ds(0, EARLY)]),
            )
        )
    ]
    for copy in early_stores:
        copy.start()

    def add_router(block, total):
        return total + dot_rows(logit_grads[block], all_moe[block])

    for part in range(moe_parts // 2):
        resid_gather.relay(part)
    for copy in late:
        copy.wait()
    full = weights[...].reshape(width, pack_cols)
    full_out = out_rows[...].reshape(q_cols, width)
    keys, values = spread(q_cols), spread(q_cols + k_cols)
    documents = seg_row[...].astype(jnp.float32)
    columns = jnp.broadcast_to(documents, (128, documents.shape[1])).T[:, :1]
    router_grads = lax.fori_loop(
        0, groups, add_router, jnp.zeros((2 * EXPERTS, width), jnp.float32)
    )
    router_sum = router_grads[:EXPERTS] + router_grads[EXPERTS:]
    for part in range(moe_parts // 2, moe_parts):
        resid_gather.relay(part)
    column_sum.hop(1)
    mix.hop(0, 0)
    for part in range(moe_parts):
        resid_gather.arrived(part)
    for part in range(local_experts):
        into.fold(part)
        downs.fold(part)
    at_lane = lax.broadcasted_iota(jnp.int32, (1, 128), 1)
    for block in range(shards):
        here = pl.ds(block * token_rows, token_rows)
        grads = outer_cols(all_resid[block], full_out).astype(jnp.bfloat16)
        head_grads[here, :] = grads
        products = to_f32(grads) * heads_out[here, :]
        deltas = jnp.zeros((token_rows, 128), jnp.float32)
        for pair in range(2):
            both = products[:, pair * 128 : pair * 128 + 128]
            first = jnp.sum(jnp.where(low, both, 0.0), -1, keepdims=True)
            second = jnp.sum(jnp.where(low, 0.0, both), -1, keepdims=True)
            deltas = jnp.where(at_lane == 2 * pair, first, deltas)
            deltas = jnp.where(at_lane == 2 * pair + 1, second, deltas)
        turned[:, here] = deltas.T
    attn_low = heads_out[...].astype(jnp.bfloat16)
    flat_resid = all_resid[...].reshape(shards * token_rows, width)
    out_grads[...] = (
        inner_rows(attn_low, flat_resid).astype(jnp.bfloat16).reshape(groups, rows, width)
    )
    out_scatter = ExpScatter(
        place,
        lambda line, part: out_grads.at[line * 2 + 1 - place.x],
        lambda line, part: out_grads.at[line * 2 + place.x],
        lambda line, part: out_crossed.at[line],
        lambda line, part: out_raised.at[raised_slot(line)],
        lambda line, part: out_lowered.at[lowered_slot(line)],
        1,
        (out_xs, out_xr, out_ls, out_lr),
    )
    for line in ORDER:
        out_scatter.begin(line, 0)
    column_sum.hop(2)
    mix.hop(1, 0)
    key_grads[...] = jnp.zeros_like(key_grads)
    value_grads[...] = jnp.zeros_like(value_grads)
    for block in range(shards):
        here = pl.ds(block * token_rows, token_rows)
        count = (block + 1) * token_rows
        at_col = block * token_rows + lax.broadcasted_iota(jnp.int32, (1, token_rows), 1)
        at_row = lax.broadcasted_iota(jnp.int32, (count, 1), 0)
        bias = jnp.where(
            (at_row <= at_col)
            & (columns[:count] == documents[:, block * token_rows : count]),
            0.0,
            MASK_FILLER,
        )
        for pair in range(2):
            lanes = slice(pair * 128, pair * 128 + 128)
            queries = qkv[here, lanes]
            grads = head_grads[here, lanes]
            query_grad = jnp.zeros((token_rows, 128), jnp.float32)
            for head in range(2):
                row = 2 * pair + head
                mine = low if head == 0 else jnp.logical_not(low)
                own_queries = jnp.where(mine, queries, jnp.zeros((), jnp.bfloat16))
                own_grads = jnp.where(mine, grads, jnp.zeros((), jnp.bfloat16))
                key, value = keys[pair][head][:count], values[pair][head][:count]
                scores = outer_cols(key, queries) * factor + bias
                probs = jnp.exp(scores - norm_rows[row : row + 1, block * token_rows : count])
                grad_probs = outer_cols(value, grads)
                grad_scores = (probs * (grad_probs - turned[row : row + 1, here])).astype(
                    jnp.bfloat16
                )
                value_grads[pair, :count, :] += dot_rows(probs.astype(jnp.bfloat16), own_grads)
                key_grads[pair, :count, :] += dot_rows(grad_scores, own_queries)
                query_grad = query_grad + inner_rows(grad_scores, key)
            qkv_grads[here, lanes] = (query_grad * factor).astype(jnp.bfloat16)
        if block == 1:
            mix.fold(1)
            mix.hop(0, 1)
            column_sum.turn()
        if block == 3:
            mix.hop(2, 0)
            mix.hop(1, 1)

    def fold_heads(first, second):
        return jnp.where(
            low,
            first + pltpu.roll(first, HEAD_SIZE, 1),
            second + pltpu.roll(second, HEAD_SIZE, 1),
        )

    qkv_grads[:, q_cols : q_cols + k_cols] = (
        fold_heads(key_grads[0], key_grads[1]) * factor
    ).astype(jnp.bfloat16)
    qkv_grads[:, q_cols + k_cols :] = fold_heads(value_grads[0], value_grads[1]).astype(
        jnp.bfloat16
    )

    normed_scatter = CtxScatter(
        place,
        lambda y, part: normed_part.at[2 * y + 1 - place.half],
        lambda y, part: normed_part.at[2 * y + place.half],
        lambda lane, part: normed_swapped.at[lane],
        lambda part: normed_crossed,
        1,
        normed_send,
        normed_recv,
    )
    gain_one_sum = jnp.zeros((1, width), jnp.float32)
    main_sum = jnp.zeros((width, main_cols), jnp.float32)
    for block in range(shards):
        here = pl.ds(block * token_rows, token_rows)
        grads = outer_cols(qkv_grads[here, :], full[:, :main_cols])
        normed_part[block] = grads.astype(jnp.bfloat16)
        own = to_f32(all_tokens[block])
        scaled = own * rms_scale(own)
        gain_one_sum = gain_one_sum + jnp.sum(grads * scaled, 0, keepdims=True)
        normed = (scaled * gain_one_row).astype(jnp.bfloat16)
        main_sum = main_sum + inner_rows(normed, qkv_grads[here, :])
    normed_scatter.swap(False, 0).start()
    normed_scatter.swap(True, 0).start()
    at_sub = lax.broadcasted_iota(jnp.int32, (128, 1), 0)
    gain_rows = jnp.where(
        at_sub == EXPERTS, gain_one_sum, jnp.where(at_sub == EXPERTS + 1, gain_two_sum, 0.0)
    )
    side = jnp.concatenate([router_sum, gain_rows[EXPERTS:, :]], 0).T
    sums[:, :, :, :main_cols] = main_sum.astype(jnp.bfloat16).reshape(
        shards, groups, rows, main_cols
    )
    sums[:, :, :, main_cols:] = side.astype(jnp.bfloat16).reshape(
        shards, groups, rows, pack_cols - main_cols
    )
    sum_scatter = ExpScatter(
        place,
        lambda line, part: sums.at[:, line * 2 + 1 - place.x],
        lambda line, part: sums.at[:, line * 2 + place.x],
        lambda line, part: sums_crossed.at[line],
        lambda line, part: sums_raised.at[raised_slot(line)],
        lambda line, part: sums_lowered.at[lowered_slot(line)],
        1,
        (sum_xs, sum_xr, sum_ls, sum_lr),
    )
    for line in ORDER:
        sum_scatter.begin(line, 0)
    normed_scatter.fold(0)
    mix.fold(2)
    mix.hop(0, 2)
    mix.hop(2, 1)
    out_scatter.fold(0)
    out_scatter.hop(0, 0)
    mix.hop(1, 2)
    mix.fold(3)
    mix.hop(0, 3)
    sum_scatter.fold(0)
    sum_scatter.hop(0, 0)
    out_scatter.hop(1, 0)
    mix.hop(2, 2)
    mix.hop(1, 3)
    sum_scatter.hop(1, 0)
    out_scatter.hop(2, 0)
    for copy in early_stores:
        copy.wait()
    stores = []
    for part in range(local_experts):
        for kind, (scatter, held, target) in enumerate(
            ((into, in_mine, in_sum), (downs, down_mine, down_sum))
        ):
            scatter.arrived(part)
            held[place.y, part] = scatter.total(part).astype(jnp.bfloat16)
            copy = pltpu.make_async_copy(
                held.at[place.y, part], target.at[EARLY + part], store_sem.at[kind, part]
            )
            copy.start()
            stores.append(copy)
    sum_scatter.hop(2, 0)
    mix.hop(2, 3)
    output_sum[...] = out_scatter.total(0)
    sums_own[...] = sum_scatter.total(0).astype(jnp.bfloat16)
    sums_all[ctx] = sums_own[ctx]
    copies = []
    for lane, to in enumerate((place.core, place.side, place.far)):
        copy = remote(
            sums_own.at[to[0]], sums_all.at[ctx], last_send.at[lane], last_recv.at[lane], to
        )
        copy.start()
        copies.append(copy)
    normed_scatter.arrived(0)
    grad_normed = normed_scatter.total(0)
    own = to_f32(tokens[...])
    scale = rms_scale(own)
    weighted = grad_normed * gain_one_row
    grad_tokens[...] = (
        grad_resid[...]
        + scale * weighted
        - own * (scale * scale * scale) * jnp.mean(weighted * own, -1, keepdims=True)
    )
    for part in range(mix_parts):
        here = pl.ds(*MIX_CUTS[part])
        mixed_out[here, :] = (resid[here, :] + mix.total(part)).astype(jnp.bfloat16)
    here = pl.ds(mix_rows, COLUMN)
    mixed_out[here, :] = (resid[here, :] + column_sum.total()).astype(jnp.bfloat16)
    for lane, to in enumerate((place.core, place.side, place.far)):
        remote(
            sums_own.at[0], sums_all.at[to[0]], last_send.at[lane], last_recv.at[lane], to
        ).wait_recv()
    side = jnp.zeros((rows, pack_cols - main_cols), jnp.float32)
    for shard in range(shards):
        came = to_f32(sums_all[shard])
        query_sum[:, shard * q_cols : (shard + 1) * q_cols] = came[:, :q_cols]
        key_sum[:, shard * k_cols : (shard + 1) * k_cols] = came[:, q_cols : q_cols + k_cols]
        value_sum[:, shard * k_cols : (shard + 1) * k_cols] = came[:, q_cols + k_cols : main_cols]
        side = side + came[:, main_cols:]
    side_sum[...] = side
    for copy in stores:
        copy.wait()
    for copy in copies:
        copy.wait_send()
    for scatter in (mix, column_sum, into, downs, out_scatter, normed_scatter, sum_scatter):
        scatter.finish()
    for part in range(moe_parts):
        resid_gather.sent(part)


def back(
    moe_in_grads, mixed_part, grad_in, grad_down, in_first, down_first, tokens, cot, resid, side_rows, logit_grads,
    all_moe, all_tokens, weights, out_rows, qkv, heads_out, norm_rows, seg_row,
):
    token_rows, width = tokens.shape
    shards, groups, rows, pack_cols = weights.shape
    seq_len = shards * token_rows
    q_cols, main_cols = heads_out.shape[1], qkv.shape[1]
    k_cols = (main_cols - q_cols) // 2
    experts, _, in_rows, in_cols = grad_in.shape
    down_rows = grad_down.shape[2]
    low, f32 = jnp.bfloat16, jnp.float32

    def shape(dims, dtype):
        return jax.ShapeDtypeStruct(dims, dtype)

    whole, anywhere = pl.BlockSpec(memory_space=VMEM), pl.BlockSpec(memory_space=pl.ANY)
    mix_rows = sum(size for _, size in MIX_CUTS)
    block, steps = (LINES, mix_rows, width), (LINES - 1, mix_rows, width)
    pack = (shards, rows, pack_cols)
    return pl.pallas_call(
        back_kernel,
        name="back",
        out_shape=[
            shape((token_rows, width), low),
            shape((token_rows, width), f32),
            shape((rows, shards * q_cols), f32),
            shape((rows, shards * k_cols), f32),
            shape((rows, shards * k_cols), f32),
            shape((rows, pack_cols - main_cols), f32),
            shape((rows, width), f32),
            shape((EARLY + experts, in_rows, in_cols), low),
            shape((EARLY + experts, down_rows, width), low),
        ],
        in_specs=[whole] + [anywhere] * 5 + [whole] * 5 + [anywhere] * 6 + [whole] * 2,
        out_specs=[whole] * 7 + [anywhere] * 2,
        scratch_shapes=[
            VMEM(block, low),
            VMEM(block, low),
            VMEM(steps, low),
            VMEM(steps, low),
            VMEM((groups, COLUMN, width), low),
            VMEM((2, 2, LINES - 1, COLUMN, width), low),
            VMEM((COLUMN, width), low),
            VMEM((2, experts, in_rows, in_cols), low),
            VMEM((2, experts, in_rows, in_cols), low),
            VMEM((experts, in_rows, in_cols), low),
            VMEM((2, experts, down_rows, width), low),
            VMEM((2, experts, down_rows, width), low),
            VMEM((experts, down_rows, width), low),
            VMEM((token_rows, width), f32),
            VMEM((shards, token_rows, width), low),
            VMEM((seq_len, q_cols), low),
            VMEM((128, seq_len), f32),
            VMEM((2, seq_len, 128), f32),
            VMEM((2, seq_len, 128), f32),
            VMEM((seq_len, main_cols), low),
            VMEM((shards, token_rows, width), low),
            VMEM((2, token_rows, width), low),
            VMEM((token_rows, width), low),
            VMEM((shards, groups, rows, pack_cols), low),
            VMEM((LINES,) + pack, low),
            *[VMEM((LINES - 1,) + pack, low)] * 2,
            VMEM((shards, rows, pack_cols), low),
            VMEM((shards, rows, pack_cols), low),
            VMEM((groups, rows, width), low),
            VMEM((LINES, rows, width), low),
            *[VMEM((LINES - 1, rows, width), low)] * 2,
            VMEM((EARLY, in_rows, in_cols), low),
            VMEM((EARLY, down_rows, width), low),
            DMA((2, experts)),
            VMEM(all_moe.shape, low),
            VMEM(all_tokens.shape, low),
            VMEM(weights.shape, low),
            VMEM(out_rows.shape, low),
            VMEM(qkv.shape, low),
            VMEM(heads_out.shape, f32),
            DMA((6,)),
            DMA((2,)),
            DMA((9,)),
            *scatter_sems(len(MIX_CUTS)),
            *column_sum_sems(),
            *scatter_sems(1),
            *scatter_sems(1),
            *square_sems(experts),
            *square_sems(experts),
            *square_sems(1),
            *square_sems(4),
            DMA((3,)),
            DMA((3,)),
        ],
        compiler_params=pltpu.CompilerParams(
            collective_id=1, has_side_effects=True, vmem_limit_bytes=62 * 2**20
        ),
    )(
        moe_in_grads, mixed_part, grad_in, grad_down, in_first, down_first, tokens, cot, resid, side_rows, logit_grads,
        all_moe, all_tokens, weights, out_rows, qkv, heads_out, norm_rows, seg_row,
    )


def two_parts(values):
    high = values.astype(jnp.bfloat16)
    return high, (values - high.astype(jnp.float32)).astype(jnp.bfloat16)


def finish_kernel(pieces, *refs):
    count = len(pieces)
    kinds = max(kind for kind, _ in pieces) + 1
    sources, targets = refs[:kinds], refs[kinds : 2 * kinds]
    held, ready = refs[2 * kinds : 2 * kinds + count], refs[2 * kinds + count : -2]
    load_sem, store_sem = refs[-2:]
    loads, stores = [], []
    for index, (kind, at) in enumerate(pieces):
        source = sources[kind] if at is None else sources[kind].at[at]
        loads.append(pltpu.make_async_copy(source, held[index], load_sem.at[index]))
        loads[-1].start()
    wide = 0
    for index, (kind, at) in enumerate(pieces):
        loads[index].wait()
        target = targets[kind] if at is None else targets[kind].at[at]
        value = held[index]
        if sources[kind].dtype != targets[kind].dtype:
            ready[wide][...] = to_f32(value[...])
            value = ready[wide]
            wide += 1
        stores.append(pltpu.make_async_copy(value, target, store_sem.at[index]))
        stores[-1].start()
    for copy in stores:
        copy.wait()


def finish(*arrays):
    wide = [array.ndim == 3 for array in arrays]
    pieces, held, ready = [], [], []
    for kind, array in enumerate(arrays):
        places = range(array.shape[0]) if wide[kind] else [None]
        for at in places:
            pieces.append((kind, at))
            dims = array.shape[1:] if wide[kind] else array.shape
            held.append(VMEM(dims, array.dtype))
            if wide[kind]:
                ready.append(VMEM(dims, jnp.float32))
    anywhere = pl.BlockSpec(memory_space=pl.ANY)
    return pl.pallas_call(
        functools.partial(finish_kernel, tuple(pieces)),
        name="finish",
        out_shape=[
            jax.ShapeDtypeStruct(array.shape, jnp.float32 if wide[kind] else array.dtype)
            for kind, array in enumerate(arrays)
        ],
        in_specs=[anywhere] * len(arrays),
        out_specs=[anywhere] * len(arrays),
        scratch_shapes=held + ready + [DMA((len(pieces),)), DMA((len(pieces),))],
        compiler_params=pltpu.CompilerParams(vmem_limit_bytes=GRANT),
    )(*arrays)


def by_heads(
    tokens,
    segments,
    routes,
    gain_attn,
    gain_moe,
    query_weight,
    key_weight,
    value_weight,
    w_output,
    w_router,
    w_expert_in,
    w_expert_out,
    cotangent,
):
    shards = lax.axis_size("ctx")
    groups = lax.axis_size("exp")
    width = tokens.shape[2]
    rows = query_weight.shape[0]
    q_cols = query_weight.shape[1] // shards
    k_cols = key_weight.shape[1] // shards
    main_cols = q_cols + 2 * k_cols
    side = 128

    (
        grad_moe_in,
        mixed_part,
        logit_grads,
        in_first,
        down_first,
        in_rest,
        down_rest,
        all_moe,
        all_tokens,
        all_weights,
        out_rows,
        qkv,
        heads_out,
        norm_rows,
        resid,
        side_rows,
    ) = ahead(
        tokens[0],
        gain_attn[None],
        gain_moe[None],
        w_router,
        query_weight,
        key_weight,
        value_weight,
        w_output,
        routes[0].T,
        segments,
        cotangent[0],
        w_expert_in,
        w_expert_out,
    )
    rest = in_rest.shape[0]
    (
        mixed_out,
        grad_tokens,
        query_sum,
        key_sum,
        value_sum,
        side_sum,
        output_sum,
        in_sum,
        down_sum,
    ) = back(
        grad_moe_in,
        mixed_part,
        in_rest.reshape((rest, shards, -1, width)),
        down_rest.reshape((rest, shards, -1, width)),
        in_first,
        down_first,
        tokens[0],
        cotangent[0],
        resid,
        side_rows,
        logit_grads,
        all_moe,
        all_tokens,
        all_weights.reshape(shards, groups, rows, main_cols + side),
        out_rows.reshape(groups, rows, width),
        qkv.reshape(-1, main_cols),
        heads_out,
        norm_rows,
        segments,
    )
    in_sum, down_sum, grad_tokens, mixed_out, query_sum, output_sum, key_sum, value_sum = finish(
        in_sum, down_sum, grad_tokens, mixed_out, query_sum, output_sum, key_sum, value_sum
    )
    return (
        mixed_out[None],
        grad_tokens[None],
        side_sum[:, EXPERTS],
        side_sum[:, EXPERTS + 1],
        query_sum,
        key_sum,
        value_sum,
        output_sum,
        side_sum[:, :EXPERTS],
        in_sum,
        down_sum,
    )


def solution(mesh):
    sizes = (mesh.shape["ctx"], mesh.shape["exp"])
    return jax.shard_map(
        by_heads if sizes == (4, 8) else local,
        mesh=mesh,
        in_specs=(
            P("exp", "ctx", None),
            P("exp", None),
            P("exp", "ctx", None),
            P(("ctx", "exp")),
            P(("ctx", "exp")),
            P(("ctx", "exp"), None),
            P(("ctx", "exp"), None),
            P(("ctx", "exp"), None),
            P(("ctx", "exp"), None),
            P(("ctx", "exp"), None),
            P("exp", "ctx", None),
            P("exp", "ctx", None),
            P("exp", "ctx", None),
        ),
        out_specs=(
            P("exp", "ctx", None),
            P("exp", "ctx", None),
            P(("ctx", "exp")),
            P(("ctx", "exp")),
            P(("ctx", "exp"), None),
            P(("ctx", "exp"), None),
            P(("ctx", "exp"), None),
            P(("ctx", "exp"), None),
            P(("ctx", "exp"), None),
            P("exp", "ctx", None),
            P("exp", "ctx", None),
        ),
        check_vma=False,
    )
```

```python
import functools
import math

import jax
import jax.numpy as jnp
from jax import lax
from jax.experimental import pallas as pl
from jax.experimental.pallas import tpu as pltpu
from jax.sharding import PartitionSpec as P

QUERY_HEADS = 16
KEY_VALUE_HEADS = 8
HEAD_SIZE = 64
EXPERTS = 32
TOPK = 8
FF = 512
CAP = 72


EPSILON = 1e-06
MASK_FILLER = -1e30


def rms_scale(values):
    return lax.rsqrt(jnp.mean(values * values, -1, keepdims=True) + EPSILON)


def inner_rows(left, right):
    return lax.dot_general(
        left, right, (((0,), (0,)), ((), ())), preferred_element_type=jnp.float32
    )


def outer_cols(left, right):
    return lax.dot_general(
        left, right, (((1,), (1,)), ((), ())), preferred_element_type=jnp.float32
    )


def allowed_block(query_pos, query_seg, seg_all, offset, key_total_count):
    key_pos = offset + jnp.arange(key_total_count, dtype=jnp.int32)
    key_seg = lax.dynamic_slice_in_dim(seg_all, offset, key_total_count)
    return (key_pos[None, :] <= query_pos[:, None]) & (key_seg[None, :] == query_seg[:, None])


def head_scores(heads_of_queries, key_segment_slice, factor):
    key_total_count = key_segment_slice.shape[0]
    heads_of_keys = key_segment_slice.reshape(key_total_count, KEY_VALUE_HEADS, -1)
    return (
        jnp.einsum(
            "ihgd,jhd->hgij", heads_of_queries, heads_of_keys, preferred_element_type=jnp.float32
        )
        * factor
    )


def slot_tables(pair_ids):
    pair_count = pair_ids.shape[0]
    member = (pair_ids[:, None] == jnp.arange(EXPERTS, dtype=jnp.int32)[None, :]).astype(jnp.int32)
    earlier = jnp.cumsum(member, 0) - member
    slot_place = jnp.sum(earlier * member, 1, dtype=jnp.int32)
    is_kept = slot_place < CAP
    slot_index = jnp.where(is_kept, pair_ids * CAP + slot_place, EXPERTS * CAP)
    slot_filler = (
        jnp.full((EXPERTS * CAP,), -1, jnp.int32)
        .at[slot_index]
        .set(jnp.arange(pair_count, dtype=jnp.int32), mode="drop")
    )
    return (slot_index, is_kept, slot_filler)


def local(
    tokens,
    segments,
    routes,
    gain_attn,
    gain_moe,
    query_weight,
    key_weight,
    value_weight,
    w_output,
    w_router,
    w_expert_in,
    w_expert_out,
    cotangent,
):
    shards = lax.axis_size("ctx")
    groups = lax.axis_size("exp")
    ctx_rank = lax.axis_index("ctx")
    gain_one, gain_two, full_query, full_key, full_value, full_output, full_router = (
        lax.all_gather(gain_attn, ("ctx", "exp"), axis=0, tiled=True),
        lax.all_gather(gain_moe, ("ctx", "exp"), axis=0, tiled=True),
        lax.all_gather(query_weight, ("ctx", "exp"), axis=0, tiled=True),
        lax.all_gather(key_weight, ("ctx", "exp"), axis=0, tiled=True),
        lax.all_gather(value_weight, ("ctx", "exp"), axis=0, tiled=True),
        lax.all_gather(w_output, ("ctx", "exp"), axis=0, tiled=True),
        lax.all_gather(w_router, ("ctx", "exp"), axis=0, tiled=True),
    )
    expert_in, expert_out = (
        lax.all_gather(w_expert_in, "ctx", axis=1, tiled=True),
        lax.all_gather(w_expert_out, "ctx", axis=1, tiled=True),
    )
    inputs = tokens[0].astype(jnp.float32)
    token_rows = inputs.shape[0]
    seq_len = token_rows * shards
    head_cluster = QUERY_HEADS // KEY_VALUE_HEADS
    factor = 1.0 / math.sqrt(HEAD_SIZE)
    kv_width = key_weight.shape[1]
    seg_all = segments[0]
    query_pos = ctx_rank * token_rows + jnp.arange(token_rows, dtype=jnp.int32)
    query_seg = lax.dynamic_slice_in_dim(seg_all, ctx_rank * token_rows, token_rows)
    scale_one = rms_scale(inputs)
    gain_one_f = gain_one.astype(jnp.float32)
    normalized_input = (inputs * scale_one * gain_one_f).astype(jnp.bfloat16)
    query_matrix = jnp.dot(normalized_input, full_query, preferred_element_type=jnp.float32).astype(
        jnp.bfloat16
    )
    key_rows = jnp.dot(normalized_input, full_key, preferred_element_type=jnp.float32).astype(
        jnp.bfloat16
    )
    value_rows = jnp.dot(normalized_input, full_value, preferred_element_type=jnp.float32).astype(
        jnp.bfloat16
    )
    heads_of_queries = query_matrix.reshape(token_rows, KEY_VALUE_HEADS, head_cluster, HEAD_SIZE)
    group_size = math.gcd(shards, max(1, 1024 // token_rows))
    key_range_width = group_size * token_rows
    turns_needed = ctx_rank // group_size + 1
    running_maximum = jnp.full(
        (KEY_VALUE_HEADS, head_cluster, token_rows), MASK_FILLER, jnp.float32
    )
    key_segment_slice = lax.all_gather(key_rows, "ctx", axis=0, tiled=True)
    value_segment_slice = lax.all_gather(value_rows, "ctx", axis=0, tiled=True)
    key_total_count = key_segment_slice.shape[0]
    scores = head_scores(heads_of_queries, key_segment_slice, factor)
    allowed = allowed_block(query_pos, query_seg, seg_all, jnp.int32(0), key_total_count)
    scores = jnp.where(allowed, scores, MASK_FILLER)
    new_max = jnp.maximum(running_maximum, jnp.max(scores, -1))
    weights = jnp.where(allowed, jnp.exp(scores - new_max[..., None]), 0.0)
    run_sum = jnp.sum(weights, -1)
    heads_of_values = value_segment_slice.reshape(key_total_count, KEY_VALUE_HEADS, HEAD_SIZE)
    run_acc = jnp.einsum(
        "hgij,jhd->ihgd",
        weights.astype(jnp.bfloat16),
        heads_of_values,
        preferred_element_type=jnp.float32,
    )
    running_maximum, run_sum, run_acc = (new_max, run_sum, run_acc)
    log_norm = running_maximum + jnp.log(run_sum)
    heads_out = run_acc / jnp.transpose(run_sum, (2, 0, 1))[..., None]
    attn_low = heads_out.reshape(token_rows, -1).astype(jnp.bfloat16)
    resid = inputs + jnp.dot(attn_low, full_output, preferred_element_type=jnp.float32)
    scale_two = rms_scale(resid)
    gain_two_f = gain_two.astype(jnp.float32)
    moe_in = (resid * scale_two * gain_two_f).astype(jnp.bfloat16)
    logits = jnp.dot(moe_in, full_router, preferred_element_type=jnp.float32)
    route_ids = routes[0]
    one_hot = (route_ids[:, :, None] == jnp.arange(EXPERTS, dtype=jnp.int32)[None, None, :]).astype(
        jnp.float32
    )
    chosen = jnp.sum(one_hot * logits[:, None, :], -1)
    gates = jax.nn.softmax(chosen, axis=-1)
    slot_index, is_kept, slot_filler = slot_tables(route_ids.reshape(-1))
    filled = slot_filler >= 0
    token_of = jnp.maximum(slot_filler, 0) // TOPK
    local_experts = EXPERTS // groups
    send_rows = jnp.where(
        filled[:, None], jnp.take(moe_in, token_of, axis=0), jnp.zeros((), jnp.bfloat16)
    )
    send_rows = send_rows.reshape(groups, local_experts, CAP, -1)
    received = lax.all_to_all(send_rows, "exp", split_axis=0, concat_axis=0, tiled=True)
    pre = jnp.einsum("sjcd,jdf->sjcf", received, expert_in, preferred_element_type=jnp.float32)
    gate_part = pre[..., :FF]
    up_part = pre[..., FF:]
    hidden = (jax.nn.silu(gate_part) * up_part).astype(jnp.bfloat16)
    expert_rows = jnp.einsum(
        "sjcf,jfd->sjcd", hidden, expert_out, preferred_element_type=jnp.float32
    ).astype(jnp.bfloat16)
    returned = lax.all_to_all(expert_rows, "exp", split_axis=0, concat_axis=0, tiled=True).reshape(
        EXPERTS * CAP, -1
    )
    safe_slot = jnp.minimum(slot_index, EXPERTS * CAP - 1)
    picked = jnp.where(
        is_kept[:, None], jnp.take(returned, safe_slot, axis=0), jnp.zeros((), jnp.bfloat16)
    )
    picked = picked.astype(jnp.float32).reshape(token_rows, TOPK, -1)
    branch = jnp.sum(gates[:, :, None] * picked, 1)
    mixed_out = (resid + branch).astype(jnp.bfloat16)
    grad_out = cotangent[0].astype(jnp.float32)
    grad_picked = jnp.sum(grad_out[:, None, :] * picked, -1)
    grad_chosen = gates * (grad_picked - jnp.sum(gates * grad_picked, -1, keepdims=True))
    grad_logits = jnp.sum(one_hot * grad_chosen[:, :, None], 1)
    slot_gate = jnp.where(filled, jnp.take(gates.reshape(-1), jnp.maximum(slot_filler, 0)), 0.0)
    grad_send = (slot_gate[:, None] * jnp.take(grad_out, token_of, axis=0)).astype(jnp.bfloat16)
    grad_send = grad_send.reshape(groups, local_experts, CAP, -1)
    grad_rows = lax.all_to_all(grad_send, "exp", split_axis=0, concat_axis=0, tiled=True)
    grad_hidden = jnp.einsum(
        "sjcd,jfd->sjcf", grad_rows, expert_out, preferred_element_type=jnp.float32
    )
    sigmoid_gate = jax.nn.sigmoid(gate_part)
    grad_gate = grad_hidden * up_part * sigmoid_gate * (1.0 + gate_part * (1.0 - sigmoid_gate))
    grad_up = grad_hidden * gate_part * sigmoid_gate
    grad_pre = jnp.concatenate([grad_gate, grad_up], -1).astype(jnp.bfloat16)
    grad_expert_out = jnp.einsum(
        "sjcf,sjcd->jfd", hidden, grad_rows, preferred_element_type=jnp.float32
    )
    grad_expert_in = jnp.einsum(
        "sjcd,sjcf->jdf", received, grad_pre, preferred_element_type=jnp.float32
    )
    grad_received = jnp.einsum(
        "sjcf,jdf->sjcd", grad_pre, expert_in, preferred_element_type=jnp.float32
    ).astype(jnp.bfloat16)
    grad_back = lax.all_to_all(
        grad_received, "exp", split_axis=0, concat_axis=0, tiled=True
    ).reshape(EXPERTS * CAP, -1)
    grad_pairs = jnp.where(
        is_kept[:, None], jnp.take(grad_back, safe_slot, axis=0), jnp.zeros((), jnp.bfloat16)
    )
    grad_pairs = grad_pairs.astype(jnp.float32).reshape(token_rows, TOPK, -1)
    grad_moe_in = (
        jnp.sum(grad_pairs, 1)
        + outer_cols(grad_logits.astype(jnp.bfloat16), full_router) * 0.0
        + lax.dot_general(
            grad_logits,
            full_router.astype(jnp.float32),
            (((1,), (1,)), ((), ())),
            precision=lax.Precision.HIGHEST,
            preferred_element_type=jnp.float32,
        )
    )
    grad_router = lax.dot_general(
        moe_in.astype(jnp.float32),
        grad_logits,
        (((0,), (0,)), ((), ())),
        precision=lax.Precision.HIGHEST,
        preferred_element_type=jnp.float32,
    )
    weighted_two = grad_moe_in * gain_two_f
    grad_gain_two = jnp.sum(grad_moe_in * resid * scale_two, 0)
    cube_two = scale_two * scale_two * scale_two
    grad_resid = (
        grad_out
        + scale_two * weighted_two
        - resid * cube_two * jnp.mean(weighted_two * resid, -1, keepdims=True)
    )
    grad_resid_low = grad_resid.astype(jnp.bfloat16)
    grad_output_w = inner_rows(attn_low, grad_resid_low)
    grad_heads = (
        outer_cols(grad_resid_low, full_output)
        .astype(jnp.bfloat16)
        .reshape(token_rows, KEY_VALUE_HEADS, head_cluster, HEAD_SIZE)
    )
    delta = jnp.transpose(jnp.sum(grad_heads.astype(jnp.float32) * heads_out, -1), (1, 2, 0))
    all_keys, all_values = (
        lax.all_gather(key_rows, "ctx", axis=0, tiled=True),
        lax.all_gather(value_rows, "ctx", axis=0, tiled=True),
    )

    def block_grads(offset):
        key_segment_slice = lax.dynamic_slice_in_dim(all_keys, offset, key_range_width)
        value_segment_slice = lax.dynamic_slice_in_dim(all_values, offset, key_range_width)
        scores = head_scores(heads_of_queries, key_segment_slice, factor)
        allowed = allowed_block(query_pos, query_seg, seg_all, offset, key_range_width)
        probs_full = jnp.where(allowed, jnp.exp(scores - log_norm[..., None]), 0.0)
        heads_of_keys = key_segment_slice.reshape(key_range_width, KEY_VALUE_HEADS, HEAD_SIZE)
        heads_of_values = value_segment_slice.reshape(key_range_width, KEY_VALUE_HEADS, HEAD_SIZE)
        grad_probs = jnp.einsum(
            "ihgd,jhd->hgij", grad_heads, heads_of_values, preferred_element_type=jnp.float32
        )
        grad_scores = (probs_full * (grad_probs - delta[..., None])).astype(jnp.bfloat16)
        query_part = jnp.einsum(
            "hgij,jhd->ihgd", grad_scores, heads_of_keys, preferred_element_type=jnp.float32
        )
        return (probs_full, grad_scores, query_part)

    query_begin_index = jnp.zeros(
        (token_rows, KEY_VALUE_HEADS, head_cluster, HEAD_SIZE), jnp.float32
    )

    def back_turn(turn, running):
        grad_query_acc, key_grad_buf = running
        offset = turn * key_range_width
        probs_full, grad_scores, query_part = block_grads(offset)
        grad_key_part = (
            jnp.einsum(
                "hgij,ihgd->jhd", grad_scores, heads_of_queries, preferred_element_type=jnp.float32
            )
            * factor
        )
        grad_value_part = jnp.einsum(
            "hgij,ihgd->jhd",
            probs_full.astype(jnp.bfloat16),
            grad_heads,
            preferred_element_type=jnp.float32,
        )
        joined = jnp.concatenate(
            [
                grad_key_part.reshape(key_range_width, -1),
                grad_value_part.reshape(key_range_width, -1),
            ],
            1,
        )
        key_grad_buf = lax.dynamic_update_slice_in_dim(key_grad_buf, joined, offset, 0)
        return (grad_query_acc + query_part, key_grad_buf)

    back_start = (query_begin_index, jnp.zeros((seq_len, 2 * kv_width), jnp.float32))
    grad_query_acc, key_grad_buf = lax.fori_loop(0, turns_needed, back_turn, back_start)
    own_grads = lax.psum_scatter(
        key_grad_buf.astype(jnp.bfloat16), "ctx", scatter_dimension=0, tiled=True
    ).astype(jnp.float32)
    grad_keys = own_grads[:, :kv_width].astype(jnp.bfloat16)
    grad_values = own_grads[:, kv_width:].astype(jnp.bfloat16)
    grad_query = (grad_query_acc * factor).reshape(token_rows, -1).astype(jnp.bfloat16)
    grad_query_w = inner_rows(normalized_input, grad_query)
    grad_key_w = inner_rows(normalized_input, grad_keys)
    grad_value_w = inner_rows(normalized_input, grad_values)
    grad_normed = (
        outer_cols(grad_query, full_query)
        + outer_cols(grad_keys, full_key)
        + outer_cols(grad_values, full_value)
    )
    weighted_one = grad_normed * gain_one_f
    grad_gain_one = jnp.sum(grad_normed * inputs * scale_one, 0)
    cube_one = scale_one * scale_one * scale_one
    grad_inputs = (
        grad_resid
        + scale_one * weighted_one
        - inputs * cube_one * jnp.mean(weighted_one * inputs, -1, keepdims=True)
    )
    dense_sums = (
        lax.psum_scatter(grad_gain_one, ("ctx", "exp"), scatter_dimension=0, tiled=True),
        lax.psum_scatter(grad_gain_two, ("ctx", "exp"), scatter_dimension=0, tiled=True),
        lax.psum_scatter(grad_query_w, ("ctx", "exp"), scatter_dimension=0, tiled=True),
        lax.psum_scatter(grad_key_w, ("ctx", "exp"), scatter_dimension=0, tiled=True),
        lax.psum_scatter(grad_value_w, ("ctx", "exp"), scatter_dimension=0, tiled=True),
        lax.psum_scatter(grad_output_w, ("ctx", "exp"), scatter_dimension=0, tiled=True),
        lax.psum_scatter(grad_router, ("ctx", "exp"), scatter_dimension=0, tiled=True),
    )
    expert_sums = (
        lax.psum_scatter(
            grad_expert_in.astype(jnp.bfloat16), "ctx", scatter_dimension=1, tiled=True
        ).astype(jnp.float32),
        lax.psum_scatter(
            grad_expert_out.astype(jnp.bfloat16), "ctx", scatter_dimension=1, tiled=True
        ).astype(jnp.float32),
    )
    return (mixed_out[None], grad_inputs[None]) + tuple(dense_sums) + tuple(expert_sums)


MESH = pl.DeviceIdType.MESH
VMEM = pltpu.VMEM
DMA = pltpu.SemaphoreType.DMA
COT_LATE = 32
COLUMN = 32
ORDER = (3, 0, 2, 1)
MIX_CUTS = ((0, 64), (64, 64), (128, 64), (192, 32))
CUTS = ((0, 64), (64, 64), (128, 64), (192, 32))
SUM_CUTS = ((0, 80), (80, 80), (160, 48), (208, 16))
LINES = 4
GRANT = 56 * 2**20


def to_f32(value):
    return value.astype(jnp.float32)


def dot_rows(left, right):
    return jnp.dot(left, right, preferred_element_type=jnp.float32)


def remote(source, target, send, recv, to):
    return pltpu.make_async_remote_copy(
        src_ref=source,
        dst_ref=target,
        send_sem=send,
        recv_sem=recv,
        device_id=to,
        device_id_type=MESH,
    )


class Place:
    def __init__(self):
        ctx, exp = lax.axis_index("ctx"), lax.axis_index("exp")
        self.ctx, self.exp = ctx, exp
        self.y, self.half = ctx // 2, ctx % 2
        self.z, self.x = exp // 2, exp % 2
        other_half = ctx + 1 - 2 * (ctx % 2)
        self.up, self.down = (ctx, exp + 2), (ctx, exp - 2)
        self.across = (ctx, exp + 1 - 2 * (exp % 2))
        self.core = (other_half, exp)
        self.side = (lax.rem(ctx + 2, 4), exp)
        self.far = (lax.rem(other_half + 2, 4), exp)

    def greet(self, lines=True, square=True):
        barrier = pltpu.get_barrier_semaphore()
        count = jnp.int32(0)
        if square:
            for to in (self.core, self.side, self.far):
                pl.semaphore_signal(barrier, inc=1, device_id=to, device_id_type=MESH)
            count = count + 3
        if lines:
            pl.semaphore_signal(barrier, inc=1, device_id=self.across, device_id_type=MESH)

            @pl.when(self.z < LINES - 1)
            def _():
                pl.semaphore_signal(barrier, inc=1, device_id=self.up, device_id_type=MESH)

            @pl.when(self.z > 0)
            def _():
                pl.semaphore_signal(barrier, inc=1, device_id=self.down, device_id_type=MESH)

            count = count + 1 + jnp.where(self.z < LINES - 1, 1, 0) + jnp.where(self.z > 0, 1, 0)
        pl.semaphore_wait(barrier, count)


class ExpGather:
    def __init__(self, place, view, parts, send, recv):
        self.place, self.view, self.parts = place, view, parts
        self.send, self.recv = send, recv

    def copy(self, lane, line, part, to):
        index = line * 2 + self.place.x
        ref = self.view(index, part)
        return remote(ref, ref, self.send.at[lane, line, part], self.recv.at[index, part], to)

    def pass_on(self, line, part, up, down):
        place = self.place
        if up:

            @pl.when(place.z < LINES - 1)
            def _():
                self.copy(1, line, part, place.up).start()

        if down:

            @pl.when(place.z > 0)
            def _():
                self.copy(2, line, part, place.down).start()

        self.copy(0, line, part, place.across).start()

    def begin(self, part):
        self.pass_on(self.place.z, part, True, True)

    def arrived(self, index, part):
        ref = self.view(index, part)
        remote(
            ref, ref, self.send.at[0, 0, part], self.recv.at[index, part], self.place.across
        ).wait_recv()

    def relay(self, step, part):
        place = self.place

        @pl.when(place.z >= step)
        def _():
            line = place.z - step
            self.arrived(line * 2 + place.x, part)
            self.pass_on(line, part, True, False)

        @pl.when(place.z + step < LINES)
        def _():
            line = place.z + step
            self.arrived(line * 2 + place.x, part)
            self.pass_on(line, part, False, True)

    def relays(self):
        for step in range(1, LINES):
            for part in range(self.parts):
                self.relay(step, part)

    def across_arrived(self, line, part):
        self.arrived(line * 2 + 1 - self.place.x, part)

    def finish(self):
        for part in range(self.parts):
            for line in range(LINES):
                self.across_arrived(line, part)
        self.sent()

    def sent(self):
        place = self.place
        for part in range(self.parts):
            for line in range(LINES):
                self.copy(0, line, part, place.across).wait_send()

                @pl.when((place.z >= line) & (place.z < LINES - 1))
                def _():
                    self.copy(1, line, part, place.up).wait_send()

                @pl.when((place.z <= line) & (place.z > 0))
                def _():
                    self.copy(2, line, part, place.down).wait_send()


def gather_sems(parts):
    return [DMA((3, LINES, parts)), DMA((2 * LINES, parts))]


def raised_slot(line):
    return max(line - 1, 0) if isinstance(line, int) else jnp.maximum(line - 1, 0)


def lowered_slot(line):
    return min(line, LINES - 2) if isinstance(line, int) else jnp.minimum(line, LINES - 2)


class ExpScatter:
    def __init__(self, place, outgoing, mine, crossed, raised, lowered, parts, sems, done=0):
        self.place, self.parts = place, parts
        self.done = done
        self.outgoing, self.mine = outgoing, mine
        self.crossed, self.raised, self.lowered = crossed, raised, lowered
        self.cross_send, self.cross_recv, self.line_send, self.line_recv = sems

    def cross(self, line, part):
        place = self.place
        return remote(
            self.outgoing(line, part),
            self.crossed(line, part),
            self.cross_send.at[line, part],
            self.cross_recv.at[line, part],
            place.across,
        )

    def along(self, up, line, part):
        place = self.place
        side = 0 if up else 1
        return remote(
            self.mine(line, part),
            (self.raised if up else self.lowered)(line, part),
            self.line_send.at[side, line, part],
            self.line_recv.at[side, line, part],
            place.up if up else place.down,
        )

    def begin(self, line, part):
        self.cross(line, part).start()

    def fold(self, part, owners=ORDER):
        place = self.place
        for line in owners:

            @pl.when(place.z != line)
            def _():
                self.cross(line, part).wait_recv()
                ref = self.mine(line, part)
                ref[...] = (to_f32(ref[...]) + to_f32(self.crossed(line, part)[...])).astype(
                    ref.dtype
                )

    def hop(self, stage, part, owners=ORDER):
        place = self.place
        for up in (True, False):
            here = stage if up else LINES - 1 - stage
            lines = range(LINES - 1, here, -1) if up else range(here)
            lines = [line for line in lines if line in owners]
            if not lines:
                continue

            @pl.when(place.z == here)
            def _():
                for line in lines:
                    if stage > 0:
                        self.along(up, line, part).wait_recv()
                        ref = self.mine(line, part)
                        came = (self.raised if up else self.lowered)(line, part)
                        ref[...] = (to_f32(ref[...]) + to_f32(came[...])).astype(ref.dtype)
                    self.along(up, line, part).start()

    def total(self, part):
        place = self.place
        line = place.z
        value = to_f32(self.mine(line, part)[...])
        if part >= self.done:
            self.cross(line, part).wait_recv()
            value = value + to_f32(self.crossed(line, part)[...])
        for up in (True, False):
            came = (self.raised if up else self.lowered)(line, part)
            some = line > 0 if up else line < LINES - 1

            @pl.when(some)
            def _():
                self.along(up, line, part).wait_recv()

            value = value + jnp.where(some, to_f32(came[...]), 0.0)
        return value

    def finish(self):
        place = self.place
        for part in range(self.parts):
            for line in range(LINES):
                if part >= self.done:
                    self.cross(line, part).wait_send()
                for up in (True, False):

                    @pl.when(place.z < line if up else place.z > line)
                    def _():
                        self.along(up, line, part).wait_send()


def scatter_sems(parts):
    return [DMA((LINES, parts)), DMA((LINES, parts)), DMA((2, LINES, parts)), DMA((2, LINES, parts))]


class ColumnGather:
    def __init__(self, place, view, send, recv):
        self.place, self.view, self.send, self.recv = place, view, send, recv

    def copy(self, lane, index, to):
        ref = self.view(index)
        return remote(ref, ref, self.send.at[lane, index], self.recv.at[index], to)

    def pass_on(self, index, up, down):
        place = self.place
        if up:

            @pl.when(place.z < LINES - 1)
            def _():
                self.copy(1, index, place.up).start()

        if down:

            @pl.when(place.z > 0)
            def _():
                self.copy(2, index, place.down).start()

    def arrived(self, index):
        ref = self.view(index)
        remote(
            ref, ref, self.send.at[0, index], self.recv.at[index], self.place.across
        ).wait_recv()

    def begin(self):
        self.copy(0, self.place.exp, self.place.across).start()
        self.pass_on(self.place.exp, True, True)

    def turn(self):
        other = self.place.across[1]
        self.arrived(other)
        self.pass_on(other, True, True)

    def relay(self, step):
        place = self.place
        for column in (place.x, 1 - place.x):

            @pl.when(place.z >= step)
            def _():
                index = (place.z - step) * 2 + column
                self.arrived(index)
                self.pass_on(index, True, False)

            @pl.when(place.z + step < LINES)
            def _():
                index = (place.z + step) * 2 + column
                self.arrived(index)
                self.pass_on(index, False, True)

    def sent(self):
        place = self.place
        self.copy(0, place.exp, place.across).wait_send()
        for line in range(LINES):
            for column in range(2):
                index = line * 2 + column

                @pl.when((place.z >= line) & (place.z < LINES - 1))
                def _():
                    self.copy(1, index, place.up).wait_send()

                @pl.when((place.z <= line) & (place.z > 0))
                def _():
                    self.copy(2, index, place.down).wait_send()


def column_sems():
    return [DMA((3, 2 * LINES)), DMA((2 * LINES,))]


class ColumnScatter:
    def __init__(self, place, mine, came, crossed, sems):
        self.place, self.mine, self.came, self.crossed = place, mine, came, crossed
        self.line_send, self.line_recv, self.cross_send, self.cross_recv = sems

    def along(self, up, line, far):
        place = self.place
        side = 0 if up else 1
        slot = raised_slot(line) if up else lowered_slot(line)
        return remote(
            self.mine(line, far),
            self.came(side, far, slot),
            self.line_send.at[side, far, line],
            self.line_recv.at[side, far, line],
            place.up if up else place.down,
        )

    def cross(self):
        return remote(
            self.mine(self.place.z, 1),
            self.crossed,
            self.cross_send.at[0],
            self.cross_recv.at[0],
            self.place.across,
        )

    def hop(self, stage):
        place = self.place
        for up in (True, False):
            here = stage if up else LINES - 1 - stage
            lines = range(LINES - 1, here, -1) if up else range(here)

            @pl.when(place.z == here)
            def _():
                for line in lines:
                    for far in (1, 0):
                        if stage > 0:
                            self.along(up, line, far).wait_recv()
                            ref = self.mine(line, far)
                            slot = raised_slot(line) if up else lowered_slot(line)
                            came = self.came(0 if up else 1, far, slot)
                            ref[...] = (to_f32(ref[...]) + to_f32(came[...])).astype(ref.dtype)
                        self.along(up, line, far).start()

    def line_total(self, far):
        line = self.place.z
        value = to_f32(self.mine(line, far)[...])
        for up in (True, False):
            some = line > 0 if up else line < LINES - 1

            @pl.when(some)
            def _():
                self.along(up, line, far).wait_recv()

            slot = raised_slot(line) if up else lowered_slot(line)
            came = self.came(0 if up else 1, far, slot)
            value = value + jnp.where(some, to_f32(came[...]), 0.0)
        return value

    def turn(self):
        ref = self.mine(self.place.z, 1)
        ref[...] = self.line_total(1).astype(ref.dtype)
        self.cross().start()

    def total(self):
        value = self.line_total(0)
        self.cross().wait_recv()
        return value + to_f32(self.crossed[...])

    def finish(self):
        place = self.place
        self.cross().wait_send()
        for line in range(LINES):
            for far in range(2):
                for up in (True, False):

                    @pl.when(place.z < line if up else place.z > line)
                    def _():
                        self.along(up, line, far).wait_send()


def column_sum_sems():
    return [DMA((2, 2, LINES)), DMA((2, 2, LINES)), DMA((1,)), DMA((1,))]


class CtxGather:
    def __init__(self, place, view, parts, send, recv, own=None):
        self.place, self.view, self.parts = place, view, parts
        self.send, self.recv, self.own = send, recv, own

    def copy(self, lane, part):
        place = self.place
        index = lax.rem(place.ctx + 2, 4) if lane == 2 else place.ctx
        ref = self.view(index, part)
        source = ref if lane == 2 or self.own is None else self.own(part)
        to = place.side if lane == 1 else place.core
        return remote(source, ref, self.send.at[lane, part], self.recv.at[lane, part], to)

    def landed(self, lane, part):
        place = self.place
        index = (place.core, place.side, place.far)[lane][0]
        ref = self.view(index, part)
        return remote(ref, ref, self.send.at[lane, part], self.recv.at[lane, part], place.core)

    def begin(self, part):
        self.copy(1, part).start()
        self.copy(0, part).start()

    def relay(self, part):
        self.landed(1, part).wait_recv()
        self.copy(2, part).start()

    def arrived(self, part):
        self.landed(0, part).wait_recv()
        self.landed(2, part).wait_recv()

    def sent(self, part):
        for lane in range(3):
            self.copy(lane, part).wait_send()


def square_sems(parts):
    return [DMA((3, parts)), DMA((3, parts))]


class CtxScatter:
    def __init__(self, place, outgoing, mine, swapped, crossed, parts, send, recv):
        self.place, self.parts = place, parts
        self.outgoing, self.mine = outgoing, mine
        self.swapped, self.crossed = swapped, crossed
        self.send, self.recv = send, recv

    def swap(self, near, part):
        place = self.place
        y = place.y if near else 1 - place.y
        lane = 0 if near else 1
        return remote(
            self.outgoing(y, part),
            self.swapped(lane, part),
            self.send.at[lane, part],
            self.recv.at[lane, part],
            place.core,
        )

    def over(self, part):
        place = self.place
        return remote(
            self.mine(1 - place.y, part),
            self.crossed(part),
            self.send.at[2, part],
            self.recv.at[2, part],
            place.side,
        )

    def fold(self, part):
        self.swap(False, part).wait_recv()
        ref = self.mine(1 - self.place.y, part)
        ref[...] = (to_f32(ref[...]) + to_f32(self.swapped(1, part)[...])).astype(ref.dtype)
        self.over(part).start()

    def arrived(self, part):
        self.swap(True, part).wait_recv()
        self.over(part).wait_recv()

    def total(self, part, here=slice(None)):
        return (
            to_f32(self.mine(self.place.y, part)[here, :])
            + to_f32(self.swapped(0, part)[here, :])
            + to_f32(self.crossed(part)[here, :])
        )

    def finish(self):
        for part in range(self.parts):
            self.swap(False, part).wait_send()
            self.swap(True, part).wait_send()
            self.over(part).wait_send()


def ahead_kernel(
    tokens,
    gain_attn,
    gain_moe,
    w_router,
    wq,
    wk,
    wv,
    wo,
    routes,
    seg_row,
    cot_hbm,
    in_hbm,
    out_hbm,
    grad_moe_in,
    mixed_part,
    logit_grads,
    in_first,
    down_first,
    in_rest,
    down_rest,
    moe_hbm,
    tokens_hbm,
    weights_hbm,
    out_rows_hbm,
    qkv_hbm,
    heads_hbm,
    norm_rows,
    resid_hbm,
    side_rows,
    moe,
    cot,
    w_in,
    w_out,
    slot_rows,
    slot_cot,
    hidden,
    slopes,
    slot_out,
    pick,
    slot_gate,
    gates,
    all_routes,
    resid_rows,
    moe_crossed,
    moe_raised,
    moe_lowered,
    column_came,
    column_crossed,
    sum_stage,
    load_sem,
    keep_sem,
    store_sem,
    put_sem,
    free_sem,
    tok_send,
    tok_recv,
    swap_send,
    swap_recv,
    w_send,
    w_recv,
    o_send,
    o_recv,
    r_send,
    r_recv,
    c_send,
    c_recv,
    cc_send,
    cc_recv,
    l_send,
    l_recv,
    m_send,
    m_recv,
    mc_send,
    mc_recv,
    i_send,
    i_recv,
    u_send,
    u_recv,
    s_send,
    s_recv,
    moe_xs,
    moe_xr,
    moe_ls,
    moe_lr,
    column_ls,
    column_lr,
    column_xs,
    column_xr,
    cross_sem,
    step_sem,
    mix_send,
    mix_recv,
    in_send,
    in_recv,
    down_send,
    down_recv,
):
    place = Place()
    ctx, exp = place.ctx, place.exp
    groups, token_rows, width = moe.shape
    shards = width // in_hbm.shape[1]
    rows = wq.shape[0]
    q_cols, k_cols = wq.shape[1] // shards, wk.shape[1] // shards
    main_cols = q_cols + 2 * k_cols
    side = side_rows.shape[0]
    pack_cols = main_cols + side
    local_experts = w_in.shape[0]
    in_rows, down_rows = in_hbm.shape[1], out_hbm.shape[1]
    slots = pick.shape[1] // local_experts
    first = exp * local_experts
    factor = 1.0 / math.sqrt(HEAD_SIZE)

    def token_block(index):
        return slot_rows.at[index, pl.ds(0, token_rows)]

    def partial(index, start, size):
        return slot_rows.at[index, pl.ds(token_rows + start, size)]

    def out_part(index):
        return slot_rows.at[
            index // LINES, pl.ds(2 * token_rows + lax.rem(index, LINES) * rows, rows)
        ]

    sources = (ctx, place.core[0], place.side[0], place.far[0])

    def weight_part(index, part):
        return slot_cot.at[sources[part], pl.ds(index * rows, rows), pl.ds(0, pack_cols)]

    def packed(shard):
        return slot_cot.at[shard, pl.ds(2 * token_rows, rows), pl.ds(0, pack_cols)]

    def swap_space(lane, start, size):
        return slot_cot.at[lane, pl.ds(token_rows + start, size)]

    def qkv_cols(low, count):
        return slopes[:, :token_rows, low : low + count].reshape(shards * token_rows, count)

    own_in = pltpu.make_async_copy(
        in_hbm, w_in.at[:, pl.ds(ctx * in_rows, in_rows)], load_sem.at[0]
    )
    own_out = pltpu.make_async_copy(
        out_hbm, w_out.at[:, pl.ds(ctx * down_rows, down_rows)], load_sem.at[1]
    )
    own_cot = pltpu.make_async_copy(cot_hbm, cot.at[exp], load_sem.at[2])
    for copy in (own_cot, own_in, own_out):
        copy.start()
    token_block(ctx)[...] = tokens[...]
    diagonal = lax.broadcasted_iota(jnp.int32, (rows, rows), 0) == lax.broadcasted_iota(
        jnp.int32, (rows, rows), 1
    )
    gain_cols = [
        jnp.sum(jnp.where(diagonal, to_f32(gain[...]), 0.0), 1, keepdims=True)
        for gain in (gain_attn, gain_moe)
    ]
    lane = lax.broadcasted_iota(jnp.int32, (1, side - EXPERTS), 1)
    gain_cols = jnp.where(
        lane == 0, gain_cols[0], jnp.where(lane == 1, gain_cols[1], 0.0)
    ).astype(jnp.bfloat16)
    for shard in range(shards):
        target = packed(shard)
        target[:, :q_cols] = wq[:, shard * q_cols : (shard + 1) * q_cols]
        target[:, q_cols : q_cols + k_cols] = wk[:, shard * k_cols : (shard + 1) * k_cols]
        target[:, q_cols + k_cols : main_cols] = wv[:, shard * k_cols : (shard + 1) * k_cols]
        target[:, main_cols : main_cols + EXPERTS] = w_router[...]
        target[:, main_cols + EXPERTS :] = gain_cols

    def weight_slot(shard):
        return slot_cot.at[shard, pl.ds(exp * rows, rows), pl.ds(0, pack_cols)]

    weight_slot(ctx)[...] = packed(ctx)[...]
    out_part(exp)[...] = wo[...]
    all_routes[exp] = routes[...]
    place.greet()

    mixes = []
    for lane, to in enumerate((place.core, place.side, place.far)):
        copy = remote(
            packed(to[0]),
            weight_slot(ctx),
            swap_send.at[lane],
            swap_recv.at[lane],
            to,
        )
        copy.start()
        mixes.append(copy)
    half_rows = token_rows // 2
    token_gather = CtxGather(
        place,
        lambda index, part: slot_rows.at[index, pl.ds(part * half_rows, half_rows)],
        2,
        tok_send,
        tok_recv,
    )
    for part in range(2):
        token_gather.begin(part)
    cot_parts = c_send.shape[2]
    late_rows = COT_LATE
    cot_rows = (token_rows - late_rows - COLUMN) // cot_parts
    cot_gather = ExpGather(
        place,
        lambda index, part: cot.at[index, pl.ds(part * cot_rows, cot_rows)],
        cot_parts,
        c_send,
        c_recv,
    )
    own_cot.wait()
    cot_gather.begin(0)
    route_gather = ExpGather(place, lambda index, part: all_routes.at[index], 1, r_send, r_recv)
    weight_gather = ExpGather(place, weight_part, shards, w_send, w_recv)
    out_gather = ExpGather(place, lambda index, part: out_part(index), 1, o_send, o_recv)
    weight_gather.begin(0)
    for lane, copy in enumerate(mixes):
        remote(
            packed(0),
            weight_slot(sources[1 + lane]),
            swap_send.at[lane],
            swap_recv.at[lane],
            place.core,
        ).wait_recv()
        weight_gather.begin(1 + lane)
    route_gather.begin(0)
    out_gather.begin(0)
    in_gather = CtxGather(
        place,
        lambda index, part: w_in.at[part, pl.ds(index * in_rows, in_rows)],
        local_experts,
        i_send,
        i_recv,
    )
    down_gather = CtxGather(
        place,
        lambda index, part: w_out.at[part, pl.ds(index * down_rows, down_rows)],
        local_experts,
        u_send,
        u_recv,
    )
    late_gather = ExpGather(
        place,
        lambda index, part: cot.at[index, pl.ds(token_rows - COLUMN - late_rows, late_rows)],
        1,
        l_send,
        l_recv,
    )
    column_rows = pl.ds(token_rows - COLUMN, COLUMN)
    cot_column = ColumnGather(place, lambda index: cot.at[index, column_rows], cc_send, cc_recv)
    own_in.wait()
    own_out.wait()
    half_experts = local_experts // 2
    wanted = [
        (gather, part) for part in range(local_experts) for gather in (in_gather, down_gather)
    ]
    ahead_of_branch = 3
    for gather, part in wanted[:ahead_of_branch]:
        gather.begin(part)
    for step in range(1, LINES):
        for part in range(shards):
            weight_gather.relay(step, part)
        if step < LINES - 1:
            token_gather.relay(step - 1)
    cot_gather.relay(1, 0)
    for step in range(1, LINES):
        out_gather.relay(step, 0)
        route_gather.relay(step, 0)
    cot_column.begin()
    for part in range(1, cot_parts):
        cot_gather.begin(part)
    cot_gather.relay(2, 0)
    for part in range(2):
        token_gather.arrived(part)
    weight_gather.finish()

    same = (
        lax.broadcasted_iota(jnp.int32, (side, side), 0)
        == lax.broadcasted_iota(jnp.int32, (side, side), 1)
    ).astype(jnp.bfloat16)
    full = slot_cot[:, :token_rows, :pack_cols].reshape(width, pack_cols)
    side_t = outer_cols(same, full[:, main_cols:])
    side_rows[...] = side_t.astype(jnp.bfloat16)
    gain_one, gain_two = side_t[EXPERTS : EXPERTS + 1], side_t[EXPERTS + 1 : EXPERTS + 2]
    for block in range(shards):
        values = to_f32(token_block(block)[...])
        normed = (values * rms_scale(values) * gain_one).astype(jnp.bfloat16)
        slopes[block, :token_rows, :main_cols] = dot_rows(normed, full[:, :main_cols]).astype(
            jnp.bfloat16
        )

    low = lax.broadcasted_iota(jnp.int32, (1, 2 * HEAD_SIZE), 1) < HEAD_SIZE

    def spread(start):
        plain = to_f32(qkv_cols(start, k_cols))
        turned = pltpu.roll(plain, HEAD_SIZE, 1)
        zero = jnp.zeros((), jnp.float32)
        return [
            [
                jnp.where(low, plain, zero).astype(jnp.bfloat16),
                jnp.where(low, zero, turned).astype(jnp.bfloat16),
            ],
            [
                jnp.where(low, turned, zero).astype(jnp.bfloat16),
                jnp.where(low, zero, plain).astype(jnp.bfloat16),
            ],
        ]

    keys, values = spread(q_cols), spread(q_cols + k_cols)
    parts = slot_rows.shape[1] - 2 * token_rows
    keep = []
    for block in range(shards - 1, -1, -1):
        count = (block + 1) * token_rows
        at_row = block * token_rows + lax.broadcasted_iota(jnp.int32, (token_rows, 1), 0)
        at_col = lax.broadcasted_iota(jnp.int32, (1, count), 1)
        documents = seg_row[:, block * token_rows : count].astype(jnp.float32)
        own_document = jnp.broadcast_to(documents, (128, token_rows)).T[:, :1]
        bias = jnp.where(
            (at_col <= at_row) & (own_document == seg_row[:, :count].astype(jnp.float32)),
            0.0,
            MASK_FILLER,
        )
        lows = []
        norms = jnp.zeros((token_rows, 128), jnp.float32)
        at_lane = lax.broadcasted_iota(jnp.int32, (1, 128), 1)
        for pair in range(2):
            queries = slopes[block, :token_rows, pair * 128 : pair * 128 + 128]
            heads = jnp.zeros((token_rows, 128), jnp.float32)
            for head in range(2):
                scores = outer_cols(queries, keys[pair][head][:count]) * factor + bias
                top = jnp.max(scores, -1, keepdims=True)
                shares = jnp.exp(scores - top)
                total = jnp.sum(shares, -1, keepdims=True)
                norms = jnp.where(at_lane == 2 * pair + head, top + jnp.log(total), norms)
                heads = heads + dot_rows(
                    shares.astype(jnp.bfloat16), values[pair][head][:count]
                ) / total
            start = block * q_cols + pair * 128
            resid_rows[:, start : start + 128] = heads
            lows.append(heads.astype(jnp.bfloat16))
        norm_rows[:, block * token_rows : count] = norms.T[:8]
        slopes[block, token_rows : 2 * token_rows, :q_cols] = jnp.concatenate(lows, 1)
        keep.append(
            pltpu.make_async_copy(
                resid_rows.at[:, pl.ds(block * q_cols, q_cols)],
                heads_hbm.at[pl.ds(block * token_rows, token_rows)],
                keep_sem.at[len(keep)],
            )
        )
        keep[-1].start()
        if block == 2:
            cot_column.turn()
            for part in range(1, cot_parts):
                cot_gather.relay(1, part)
            cot_gather.relay(3, 0)
        pl.semaphore_signal(step_sem, inc=1)
        pl.semaphore_wait(step_sem, 1)

    out_gather.finish()
    full_out = jnp.concatenate(
        [slot_rows[part, 2 * token_rows :, :] for part in range(q_cols // parts)], 0
    )
    for block in range(shards):
        partial(block, 0, token_rows)[...] = dot_rows(
            slopes[block, token_rows : 2 * token_rows, :q_cols], full_out
        ).astype(
            jnp.bfloat16
        )
    stored = len(keep)
    here = pl.ds(0, token_rows)
    for source, target in (
        (slot_rows.at[:, here], tokens_hbm),
        (slot_cot.at[:, here, pl.ds(0, pack_cols)], weights_hbm),
        (slopes.at[:, here, pl.ds(0, main_cols)], qkv_hbm),
        (slot_rows.at[pl.ds(0, q_cols // parts), pl.ds(2 * token_rows, parts)], out_rows_hbm),
    ):
        keep.append(pltpu.make_async_copy(source, target, keep_sem.at[len(keep)]))
        keep[-1].start()

    branch = CtxScatter(
        place,
        lambda y, part: partial(2 * y + 1 - place.half, part * half_rows, half_rows),
        lambda y, part: partial(2 * y + place.half, part * half_rows, half_rows),
        lambda lane, part: swap_space(lane, part * half_rows, half_rows),
        lambda part: swap_space(2, part * half_rows, half_rows),
        2,
        s_send,
        s_recv,
    )
    for part in range(2):
        branch.swap(False, part).start()
    for part in range(2):
        branch.swap(True, part).start()
    cot_column.relay(1)
    for part in range(1, cot_parts):
        cot_gather.relay(2, part)
    for part in range(2):
        branch.fold(part)
    for gather, part in wanted[ahead_of_branch:]:
        gather.begin(part)
    gather_parts = len(CUTS)
    moe_gather = ExpGather(
        place,
        lambda index, part: moe.at[index, pl.ds(*CUTS[part])],
        gather_parts,
        m_send,
        m_recv,
    )
    moe_column = ColumnGather(place, lambda index: moe.at[index, column_rows], mc_send, mc_recv)
    cot_column.relay(2)
    for copy in keep[:stored]:
        copy.wait()
    for part in range(2):
        here = pl.ds(part * half_rows, half_rows)
        branch.arrived(part)
        resid = to_f32(tokens[here, :]) + branch.total(part)
        resid_rows[here, :] = resid
        moe[exp, here, :] = (resid * rms_scale(resid) * gain_two).astype(jnp.bfloat16)
        if part == 1:
            moe_column.begin()
        for piece, (start, size) in enumerate(CUTS):
            if start // half_rows == part:
                moe_gather.begin(piece)
    keep.append(pltpu.make_async_copy(resid_rows, resid_hbm, keep_sem.at[len(keep)]))
    keep[-1].start()
    cot_column.relay(3)
    for part in range(1, cot_parts):
        cot_gather.relay(3, part)
    moe_column.turn()
    for step in range(1, LINES):
        for part in range(gather_parts):
            moe_gather.relay(step, part)
        moe_column.relay(step)
        if step == 1:
            for gather, part in wanted[:ahead_of_branch]:
                gather.relay(part)
    late_gather.begin(0)
    route_gather.finish()
    branch.finish()
    for part in range(2):
        token_gather.sent(part)
    for copy in mixes:
        copy.wait_send()
    for copy in keep[stored:]:
        copy.wait()

    at_expert = lax.broadcasted_iota(jnp.int32, (EXPERTS, 1), 0)
    at_lane = lax.broadcasted_iota(jnp.int32, (1, 128), 1)
    at_slot = lax.broadcasted_iota(jnp.int32, (slots, 1), 0)
    before = (
        lax.broadcasted_iota(jnp.int32, (token_rows, token_rows), 0)
        < lax.broadcasted_iota(jnp.int32, (token_rows, token_rows), 1)
    ).astype(jnp.bfloat16)
    router = side_rows[:EXPERTS, :]
    all_slots = groups * slots
    def block_of(line, far):
        return line * 2 + (1 - place.x if far else place.x)

    def slot_range(line, far):
        start = (far * LINES + line) * slots
        return pl.ds(start if isinstance(line, int) else pl.multiple_of(start, slots), slots)

    def dispatch(line, far):
        block = block_of(line, far)
        routes = all_routes[block]
        member = routes[0:1, :] == at_expert
        for rank in range(1, TOPK):
            member = member | (routes[rank : rank + 1, :] == at_expert)
        tokens = moe[block]
        logits = outer_cols(router, tokens)
        top = jnp.max(jnp.where(member, logits, MASK_FILLER), 0, keepdims=True)
        weights = jnp.where(member, jnp.exp(logits - top), 0.0)
        shares = weights / jnp.sum(weights, 0, keepdims=True)
        gates[block] = shares
        ranks = dot_rows(jnp.where(member, 1.0, 0.0).astype(jnp.bfloat16), before)
        filled = jnp.where(member & (ranks < CAP), ranks, -1.0)
        columns = jnp.zeros((slots, 128), jnp.float32)
        for expert in range(local_experts):
            mine = at_expert == first + expert
            spot = jnp.sum(jnp.where(mine, filled, 0.0), 0, keepdims=True)
            share = jnp.sum(jnp.where(mine, shares, 0.0), 0, keepdims=True)
            chosen = spot == at_slot.astype(jnp.float32)
            here = pl.ds(expert * slots, slots)
            pick[block, here, :] = jnp.where(chosen, 1.0, 0.0).astype(jnp.bfloat16)
            column = jnp.sum(jnp.where(chosen, share, 0.0), 1, keepdims=True)
            columns = jnp.where(at_lane == expert, column, columns)
        slot_gate[block] = columns
        chosen = pick[block]
        rows = dot_rows(chosen, tokens).astype(jnp.bfloat16)
        here = slot_range(line, far)
        for expert in range(local_experts):
            slot_rows[expert, here, :] = rows[expert * slots : (expert + 1) * slots]

    half_slots = all_slots // 2

    def each(count, body, far):
        def step(index, carry):
            body(index, far)
            return carry

        lax.fori_loop(0, count, step, 0)

    def near_line(step, carry):
        dispatch(place.z ^ step, 0)
        return carry

    def far_line(step, carry):
        line = place.z ^ step
        for part in range(gather_parts):
            moe_gather.across_arrived(line, part)
        dispatch(line, 1)
        return carry

    lax.fori_loop(0, LINES, near_line, 0)
    def forward(expert, far):
        half = pl.ds(far * half_slots, half_slots)
        rows = slot_rows[expert, half, :]
        for first_col in range(0, FF, 256):
            gate_cols, up_cols = pl.ds(first_col, 256), pl.ds(FF + first_col, 256)
            gate_part = dot_rows(rows, w_in[expert, :, gate_cols])
            up_part = dot_rows(rows, w_in[expert, :, up_cols])
            sigmoid_gate = jax.nn.sigmoid(gate_part)
            silu = gate_part * sigmoid_gate
            hidden[expert, half, gate_cols] = (silu * up_part).astype(jnp.bfloat16)
            slopes[expert, half, gate_cols] = (
                up_part * sigmoid_gate * (1.0 + gate_part * (1.0 - sigmoid_gate))
            ).astype(jnp.bfloat16)
            slopes[expert, half, up_cols] = silu.astype(jnp.bfloat16)
        slot_out[expert, half, :] = dot_rows(hidden[expert, half, :], w_out[expert]).astype(
            jnp.bfloat16
        )

    def pass_weights(expert):
        for gather, part in wanted[ahead_of_branch:]:
            if part == expert:
                gather.relay(part)

    def need(expert):
        in_gather.arrived(expert)
        down_gather.arrived(expert)

    last = local_experts - 1
    for expert in range(last):
        if expert + 1 < last:
            pass_weights(expert + 1)
        need(expert)
        forward(expert, 0)
    lax.fori_loop(0, LINES, far_line, 0)
    moe_gather.sent()
    moe_column.sent()
    moe_store = pltpu.make_async_copy(moe, moe_hbm, load_sem.at[0])
    moe_store.start()
    late_gather.relay(1, 0)
    each(half_experts, forward, 1)
    pass_weights(last)
    for expert in range(half_experts, last):
        forward(expert, 1)
    need(last)
    forward(last, 0)
    late_gather.relay(2, 0)
    forward(last, 1)
    moe_store.wait()

    def block_rows(line, far):
        here = slot_range(line, far)
        return jnp.concatenate([slot_out[expert, here, :] for expert in range(local_experts)], 0)

    def combine(line, far):
        block = block_of(line, far)
        shares = gates[block]
        weighted = []
        for expert in range(local_experts):
            mine = at_expert == first + expert
            share = jnp.sum(jnp.where(mine, shares, 0.0), 0, keepdims=True)
            chosen = to_f32(pick[block, pl.ds(expert * slots, slots), :])
            weighted.append((chosen * share).astype(jnp.bfloat16))
        moe[block] = inner_rows(
            jnp.concatenate(weighted, 0), block_rows(line, far)
        ).astype(jnp.bfloat16)

    each(LINES, combine, 0)
    late_gather.relay(3, 0)
    each(LINES, combine, 1)
    mix_rows = pl.ds(*MIX_CUTS[0])
    later_rows = pl.ds(MIX_CUTS[0][1], token_rows - MIX_CUTS[0][1])
    part_store = pltpu.make_async_copy(
        moe.at[:, later_rows], mixed_part.at[:, later_rows], load_sem.at[0]
    )
    part_store.start()

    cot_gather.finish()
    cot_column.sent()
    late_gather.finish()

    def dispatch_back(line, far):
        block = block_of(line, far)
        shares = gates[block]
        chosen = pick[block]
        cots = dot_rows(chosen, cot[block])
        dots = jnp.sum(cots * to_f32(block_rows(line, far)), 1, keepdims=True)
        picked_grads = jnp.zeros_like(shares)
        there = slot_range(line, far)
        for expert in range(local_experts):
            here = slice(expert * slots, (expert + 1) * slots)
            row = jnp.sum(to_f32(chosen[here]) * dots[here], 0, keepdims=True)
            picked_grads = jnp.where(at_expert == first + expert, row, picked_grads)
            share = slot_gate[block, :, expert : expert + 1]
            slot_cot[expert, there, :] = (share * cots[here]).astype(jnp.bfloat16)
        grads = shares * (picked_grads - jnp.sum(shares * picked_grads, 0, keepdims=True))
        high, low = two_parts(grads)
        logit_grads[block] = jnp.concatenate([high, low], 0)

    def backward(expert, far):
        half = pl.ds(far * half_slots, half_slots)
        grads = outer_cols(slot_cot[expert, half, :], w_out[expert])
        slopes[expert, half, :FF] = (grads * to_f32(slopes[expert, half, :FF])).astype(jnp.bfloat16)
        slopes[expert, half, FF:] = (grads * to_f32(slopes[expert, half, FF:])).astype(jnp.bfloat16)
        slot_out[expert, half, :] = outer_cols(slopes[expert, half, :], w_in[expert]).astype(
            jnp.bfloat16
        )

    def combine_back(line, far):
        block = block_of(line, far)
        left = jnp.concatenate([pick[block], logit_grads[block]], 0)
        right = jnp.concatenate([block_rows(line, far), router, router], 0)
        cot[block] = inner_rows(left, right).astype(jnp.bfloat16)

    moe_parts = len(SUM_CUTS)

    def piece(ref, part):
        return ref.at[pl.ds(*SUM_CUTS[part])]

    back_sum = ExpScatter(
        place,
        lambda line, part: piece(cot.at[line * 2 + 1 - place.x], part),
        lambda line, part: piece(cot.at[line * 2 + place.x], part),
        lambda line, part: piece(moe_crossed.at[line], part),
        lambda line, part: piece(moe_raised.at[raised_slot(line)], part),
        lambda line, part: piece(moe_lowered.at[lowered_slot(line)], part),
        moe_parts,
        (moe_xs, moe_xr, moe_ls, moe_lr),
    )
    column_sum = ColumnScatter(
        place,
        lambda line, far: cot.at[block_of(line, far), column_rows],
        lambda side, far, slot: column_came.at[side, far, slot],
        column_crossed,
        (column_ls, column_lr, column_xs, column_xr),
    )
    each(LINES, dispatch_back, 1)
    each(local_experts, backward, 1)
    each(LINES, combine_back, 1)
    units = [(part, owners) for owners in (ORDER[:2], ORDER[2:]) for part in range(moe_parts)]
    for part, owners in units:
        for line in owners:
            back_sum.begin(line, part)
    each(LINES, dispatch_back, 0)
    each(local_experts, backward, 0)
    each(LINES, combine_back, 0)

    for to in (place.core, place.side):
        pl.semaphore_signal(free_sem, inc=1, device_id=to, device_id_type=MESH)

    early = in_first.shape[0]
    for part in range(local_experts):
        in_gather.sent(part)
        down_gather.sent(part)
    into = CtxScatter(
        place,
        lambda y, part: w_in.at[part, pl.ds((2 * y + 1 - place.half) * in_rows, in_rows)],
        lambda y, part: w_in.at[part, pl.ds((2 * y + place.half) * in_rows, in_rows)],
        lambda lane, part: slot_out.at[part, pl.ds(lane * in_rows, in_rows)],
        lambda part: slot_out.at[early + part, pl.ds(2 * down_rows, in_rows)],
        early,
        in_send,
        in_recv,
    )
    downs = CtxScatter(
        place,
        lambda y, part: w_out.at[part, pl.ds((2 * y + 1 - place.half) * down_rows, down_rows)],
        lambda y, part: w_out.at[part, pl.ds((2 * y + place.half) * down_rows, down_rows)],
        lambda lane, part: slot_out.at[early + part, pl.ds(lane * down_rows, down_rows)],
        lambda part: slot_out.at[early + part, pl.ds(2 * down_rows + in_rows, down_rows)],
        early,
        down_send,
        down_recv,
    )
    part_store.wait()
    pl.semaphore_wait(free_sem, 2)
    stores = []

    def store(source, target, sem):
        copy = pltpu.make_async_copy(source, target, sem)
        copy.start()
        stores.append(copy)

    column_sum.hop(0)
    for expert in range(local_experts):
        w_out[expert] = inner_rows(hidden[expert], slot_cot[expert]).astype(jnp.bfloat16)
        if expert < early:
            downs.swap(False, expert).start()
            downs.swap(True, expert).start()
        else:
            store(w_out.at[expert], down_rest.at[expert - early], store_sem.at[0, expert])
        w_in[expert] = inner_rows(slot_rows[expert], slopes[expert]).astype(jnp.bfloat16)
        if expert < early:
            into.swap(False, expert).start()
            into.swap(True, expert).start()
        else:
            store(w_in.at[expert], in_rest.at[expert - early], store_sem.at[1, expert])
        if expert > 0 and expert <= early:
            downs.fold(expert - 1)
            into.fold(expert - 1)
        if expert == 1:
            back_sum.fold(*units[0])
            back_sum.hop(0, *units[0])
            column_sum.hop(1)
    pl.semaphore_signal(cross_sem, inc=1, device_id=place.across, device_id_type=MESH)

    def mix_cross(line):
        return remote(
            moe.at[line * 2 + 1 - place.x, mix_rows],
            slot_rows.at[line, mix_rows],
            mix_send.at[line],
            mix_recv.at[line],
            place.across,
        )

    for unit in range(1, len(units) + 2):
        if unit == 2:
            column_sum.hop(2)
        if unit == 3:
            column_sum.turn()
        if unit == len(units) - 1:
            pl.semaphore_wait(cross_sem, 1)
            for line in ORDER:
                mix_cross(line).start()
        if unit >= 2:
            back_sum.hop(2, *units[unit - 2])
        if unit <= len(units):
            back_sum.hop(1, *units[unit - 1])
        if unit < len(units):
            back_sum.fold(*units[unit])
            back_sum.hop(0, *units[unit])

    staged = [None, None]
    stage_rows = sum_stage.shape[1]

    def put(slot, value, target, sem):
        if staged[slot] is not None:
            staged[slot].wait()
        stage = sum_stage.at[slot, pl.ds(0, value.shape[0])]
        stage[...] = value
        staged[slot] = pltpu.make_async_copy(stage, target, sem)
        staged[slot].start()

    def finish_expert(part):
        for kind, (scatter, target) in enumerate(((downs, down_first), (into, in_first))):
            scatter.arrived(part)
            held = scatter.mine(place.y, part)
            held[...] = scatter.total(part).astype(jnp.bfloat16)
            store(held, target.at[part], store_sem.at[kind, part])

    for part in range(early - 1):
        finish_expert(part)
    mix_stores = []
    for part in range(moe_parts):
        here = pl.ds(*SUM_CUTS[part])
        put(part % 2, back_sum.total(part), grad_moe_in.at[here], put_sem.at[part % 2])
    put(moe_parts % 2, column_sum.total(), grad_moe_in.at[column_rows], put_sem.at[moe_parts % 2])
    finish_expert(early - 1)
    for line in ORDER:
        mix_cross(line).wait_recv()
        block = line * 2 + place.x
        moe[block, mix_rows, :] = (
            to_f32(moe[block, mix_rows, :]) + to_f32(slot_rows[line, mix_rows, :])
        ).astype(jnp.bfloat16)
        mix_stores.append(
            pltpu.make_async_copy(
                moe.at[block, mix_rows], mixed_part.at[block, mix_rows], load_sem.at[1 + line]
            )
        )
        mix_stores[-1].start()
    for line in ORDER:
        mix_cross(line).wait_send()
    for copy in mix_stores:
        copy.wait()
    for copy in staged:
        copy.wait()
    for copy in stores:
        copy.wait()
    for scatter in (back_sum, column_sum, into, downs):
        scatter.finish()


EARLY = 2


def ahead(
    tokens, gain_attn, gain_moe, w_router, wq, wk, wv, wo, routes, seg_row, cot, exp_in, exp_out
):
    shards, groups = lax.axis_size("ctx"), lax.axis_size("exp")
    token_rows, width = tokens.shape
    rows = wq.shape[0]
    q_cols, k_cols = wq.shape[1] // shards, wk.shape[1] // shards
    main_cols = q_cols + 2 * k_cols
    side = 128
    pack_cols = main_cols + side
    seq_len = token_rows * shards
    low, f32 = jnp.bfloat16, jnp.float32
    local_experts, in_rows, in_cols = exp_in.shape
    down_rows = exp_out.shape[1]
    slots = -(-CAP // 16) * 16
    arena = (local_experts, groups * slots)

    def shape(dims, dtype):
        return jax.ShapeDtypeStruct(dims, dtype)

    whole, anywhere = pl.BlockSpec(memory_space=VMEM), pl.BlockSpec(memory_space=pl.ANY)
    rest = local_experts - EARLY
    block, steps = (LINES, token_rows, width), (LINES - 1, token_rows, width)
    out_parts = groups * slots - 2 * token_rows
    return pl.pallas_call(
        ahead_kernel,
        name="ahead",
        out_shape=[
            shape((token_rows, width), f32),
            shape((groups, token_rows, width), low),
            shape((groups, 2 * EXPERTS, token_rows), low),
            shape((EARLY, in_rows, in_cols), low),
            shape((EARLY, down_rows, width), low),
            shape((rest, width, in_cols), low),
            shape((rest, FF, width), low),
            shape((groups, token_rows, width), low),
            shape((shards, token_rows, width), low),
            shape((shards, groups * rows, pack_cols), low),
            shape((q_cols // out_parts, out_parts, width), low),
            shape((shards, token_rows, main_cols), low),
            shape((seq_len, q_cols), f32),
            shape((8, seq_len), f32),
            shape((token_rows, width), f32),
            shape((side, width), low),
        ],
        in_specs=[whole] * 10 + [anywhere] * 3,
        out_specs=[anywhere, anywhere, whole]
        + [anywhere] * 10
        + [whole, anywhere, whole],
        scratch_shapes=[
            VMEM((groups, token_rows, width), low),
            VMEM((groups, token_rows, width), low),
            VMEM((local_experts, width, in_cols), low),
            VMEM((local_experts, FF, width), low),
            VMEM(arena + (width,), low),
            VMEM(arena + (width,), low),
            VMEM(arena + (FF,), low),
            VMEM(arena + (2 * FF,), low),
            VMEM(arena + (width,), low),
            VMEM((groups, local_experts * slots, token_rows), low),
            VMEM((groups, slots, 128), f32),
            VMEM((groups, EXPERTS, token_rows), f32),
            VMEM((groups,) + routes.shape, jnp.int32),
            VMEM((token_rows, width), f32),
            VMEM(block, low),
            VMEM(steps, low),
            VMEM(steps, low),
            VMEM((2, 2, LINES - 1, COLUMN, width), low),
            VMEM((COLUMN, width), low),
            VMEM((2, max(size for _, size in SUM_CUTS), width), f32),
            DMA((1 + LINES,)),
            DMA((shards + 5,)),
            DMA((2, local_experts)),
            DMA((2,)),
            pltpu.SemaphoreType.REGULAR,
            *square_sems(2),
            DMA((3,)),
            DMA((3,)),
            *gather_sems(shards),
            *gather_sems(1),
            *gather_sems(1),
            *gather_sems(2),
            *column_sems(),
            *gather_sems(1),
            *gather_sems(len(CUTS)),
            *column_sems(),
            *square_sems(local_experts),
            *square_sems(local_experts),
            *square_sems(2),
            *scatter_sems(len(SUM_CUTS)),
            *column_sum_sems(),
            pltpu.SemaphoreType.REGULAR,
            pltpu.SemaphoreType.REGULAR,
            DMA((LINES,)),
            DMA((LINES,)),
            *square_sems(EARLY),
            *square_sems(EARLY),
        ],
        compiler_params=pltpu.CompilerParams(
            collective_id=0, has_side_effects=True, vmem_limit_bytes=63 * 2**20
        ),
    )(tokens, gain_attn, gain_moe, w_router, wq, wk, wv, wo, routes, seg_row, cot, exp_in, exp_out)


def back_kernel(
    moe_in_grads,
    mixed_part,
    grad_in,
    grad_down,
    in_first,
    down_first,
    tokens,
    cot,
    resid,
    side_rows,
    logit_grads,
    all_moe_hbm,
    all_tokens_hbm,
    weights_hbm,
    out_rows_hbm,
    qkv_hbm,
    heads_out_hbm,
    norm_rows,
    seg_row,
    mixed_out,
    grad_tokens,
    query_sum,
    key_sum,
    value_sum,
    side_sum,
    output_sum,
    in_sum,
    down_sum,
    mix_mine,
    mix_crossed,
    mix_raised,
    mix_lowered,
    column_mine,
    column_came,
    column_crossed,
    in_mine,
    in_swapped,
    in_crossed,
    down_mine,
    down_swapped,
    down_crossed,
    grad_resid,
    all_resid,
    head_grads,
    turned,
    key_grads,
    value_grads,
    qkv_grads,
    normed_part,
    normed_swapped,
    normed_crossed,
    sums,
    sums_crossed,
    sums_raised,
    sums_lowered,
    sums_own,
    sums_all,
    out_grads,
    out_crossed,
    out_raised,
    out_lowered,
    in_stage,
    down_stage,
    store_sem,
    all_moe,
    all_tokens,
    weights,
    out_rows,
    qkv,
    heads_out,
    late_sem,
    early_sem,
    local_sem,
    mix_xs,
    mix_xr,
    mix_ls,
    mix_lr,
    column_ls,
    column_lr,
    column_xs,
    column_xr,
    sum_xs,
    sum_xr,
    sum_ls,
    sum_lr,
    out_xs,
    out_xr,
    out_ls,
    out_lr,
    in_send,
    in_recv,
    down_send,
    down_recv,
    normed_send,
    normed_recv,
    resid_send,
    resid_recv,
    last_send,
    last_recv,
):
    place = Place()
    ctx, exp = place.ctx, place.exp
    token_rows, width = tokens.shape
    shards, groups, rows, pack_cols = weights.shape
    local_experts = grad_in.shape[0]
    q_cols = heads_out.shape[1]
    main_cols = qkv.shape[1]
    k_cols = (main_cols - q_cols) // 2
    factor = 1.0 / math.sqrt(HEAD_SIZE)

    loads = []

    def load(source, target):
        copy = pltpu.make_async_copy(source, target, local_sem.at[len(loads)])
        copy.start()
        loads.append(copy)

    for y in range(2):
        load(grad_in.at[:, 2 * y + place.half], in_mine.at[y])
        load(grad_down.at[:, 2 * y + place.half], down_mine.at[y])
    mix_rows = sum(size for _, size in MIX_CUTS)
    for line in ORDER:
        load(mixed_part.at[line * 2 + place.x, pl.ds(0, mix_rows)], mix_mine.at[line])
    load(mixed_part.at[:, pl.ds(mix_rows, COLUMN)], column_mine)
    place.greet()

    def piece(ref, count, part):
        size = ref.shape[0] // count
        return ref.at[pl.ds(part * size, size)]

    moe_parts, mix_parts = 4, len(MIX_CUTS)

    def cut(ref, part):
        return ref.at[pl.ds(*MIX_CUTS[part])]

    mix = ExpScatter(
        place,
        lambda line, part: cut(mixed_part.at[line * 2 + 1 - place.x], part),
        lambda line, part: cut(mix_mine.at[line], part),
        lambda line, part: cut(mix_crossed.at[line], part),
        lambda line, part: cut(mix_raised.at[raised_slot(line)], part),
        lambda line, part: cut(mix_lowered.at[lowered_slot(line)], part),
        mix_parts,
        (mix_xs, mix_xr, mix_ls, mix_lr),
        1,
    )
    column_sum = ColumnScatter(
        place,
        lambda line, far: column_mine.at[line * 2 + (1 - place.x if far else place.x)],
        lambda side, far, slot: column_came.at[side, far, slot],
        column_crossed,
        (column_ls, column_lr, column_xs, column_xr),
    )
    into = CtxScatter(
        place,
        lambda y, part: grad_in.at[part, 2 * y + 1 - place.half],
        lambda y, part: in_mine.at[y, part],
        lambda lane, part: in_swapped.at[lane, part],
        lambda part: in_crossed.at[part],
        local_experts,
        in_send,
        in_recv,
    )
    downs = CtxScatter(
        place,
        lambda y, part: grad_down.at[part, 2 * y + 1 - place.half],
        lambda y, part: down_mine.at[y, part],
        lambda lane, part: down_swapped.at[lane, part],
        lambda part: down_crossed.at[part],
        local_experts,
        down_send,
        down_recv,
    )
    for near in (False, True):
        for part in range(local_experts):
            into.swap(near, part).start()
        for part in range(local_experts):
            downs.swap(near, part).start()
    early_loads = [
        pltpu.make_async_copy(source, target, early_sem.at[index])
        for index, (source, target) in enumerate(((in_first, in_stage), (down_first, down_stage)))
    ]
    for copy in early_loads:
        copy.start()
    gain_one_row = to_f32(side_rows[EXPERTS : EXPERTS + 1, :])
    gain_two_row = to_f32(side_rows[EXPERTS + 1 : EXPERTS + 2, :])
    moe_rows = token_rows // moe_parts
    gain_two_sum = jnp.zeros((1, width), jnp.float32)
    resid_gather = CtxGather(
        place,
        lambda index, part: all_resid.at[index, pl.ds(part * moe_rows, moe_rows)],
        moe_parts,
        resid_send,
        resid_recv,
    )
    for part in range(moe_parts):
        here = pl.ds(part * moe_rows, moe_rows)
        grad_moe_in = moe_in_grads[here, :]
        values = resid[here, :]
        scale = rms_scale(values)
        weighted = grad_moe_in * gain_two_row
        gain_two_sum = gain_two_sum + jnp.sum(grad_moe_in * values * scale, 0, keepdims=True)
        grads = (
            to_f32(cot[here, :])
            + scale * weighted
            - values * (scale * scale * scale) * jnp.mean(weighted * values, -1, keepdims=True)
        )
        grad_resid[here, :] = grads
        all_resid[ctx, here, :] = grads.astype(jnp.bfloat16)
        resid_gather.begin(part)
    for part in range(1, mix_parts - 1):
        for line in ORDER:
            mix.begin(line, part)
    for copy in loads:
        copy.wait()
    column_sum.hop(0)
    late = []
    for index, (source, target) in enumerate(
        (
            (all_moe_hbm, all_moe),
            (qkv_hbm, qkv),
            (out_rows_hbm, out_rows),
            (heads_out_hbm, heads_out),
            (weights_hbm, weights),
            (all_tokens_hbm, all_tokens),
        )
    ):
        late.append(pltpu.make_async_copy(source, target, late_sem.at[index]))
        late[-1].start()

    low = lax.broadcasted_iota(jnp.int32, (1, 2 * HEAD_SIZE), 1) < HEAD_SIZE

    def spread(first):
        plain = to_f32(qkv[:, first : first + k_cols])
        other = pltpu.roll(plain, HEAD_SIZE, 1)
        zero = jnp.zeros((), jnp.float32)
        return [
            [
                jnp.where(low, plain, zero).astype(jnp.bfloat16),
                jnp.where(low, zero, other).astype(jnp.bfloat16),
            ],
            [
                jnp.where(low, other, zero).astype(jnp.bfloat16),
                jnp.where(low, zero, plain).astype(jnp.bfloat16),
            ],
        ]

    for copy in early_loads:
        copy.wait()
    early_stores = [
        pltpu.make_async_copy(source, target, early_sem.at[index])
        for index, (source, target) in enumerate(
            (
                (in_stage, in_sum.at[pl.ds(0, EARLY)]),
                (down_stage, down_sum.at[pl.ds(0, EARLY)]),
            )
        )
    ]
    for copy in early_stores:
        copy.start()

    def add_router(block, total):
        return total + dot_rows(logit_grads[block], all_moe[block])

    for part in range(moe_parts // 2):
        resid_gather.relay(part)
    for copy in late:
        copy.wait()
    full = weights[...].reshape(width, pack_cols)
    full_out = out_rows[...].reshape(q_cols, width)
    keys, values = spread(q_cols), spread(q_cols + k_cols)
    documents = seg_row[...].astype(jnp.float32)
    columns = jnp.broadcast_to(documents, (128, documents.shape[1])).T[:, :1]
    router_grads = lax.fori_loop(
        0, groups, add_router, jnp.zeros((2 * EXPERTS, width), jnp.float32)
    )
    router_sum = router_grads[:EXPERTS] + router_grads[EXPERTS:]
    for part in range(moe_parts // 2, moe_parts):
        resid_gather.relay(part)
    column_sum.hop(1)
    mix.hop(0, 0)
    for part in range(moe_parts):
        resid_gather.arrived(part)
    for part in range(local_experts):
        into.fold(part)
        downs.fold(part)
    at_lane = lax.broadcasted_iota(jnp.int32, (1, 128), 1)
    for block in range(shards):
        here = pl.ds(block * token_rows, token_rows)
        grads = outer_cols(all_resid[block], full_out).astype(jnp.bfloat16)
        head_grads[here, :] = grads
        products = to_f32(grads) * heads_out[here, :]
        deltas = jnp.zeros((token_rows, 128), jnp.float32)
        for pair in range(2):
            both = products[:, pair * 128 : pair * 128 + 128]
            first = jnp.sum(jnp.where(low, both, 0.0), -1, keepdims=True)
            second = jnp.sum(jnp.where(low, 0.0, both), -1, keepdims=True)
            deltas = jnp.where(at_lane == 2 * pair, first, deltas)
            deltas = jnp.where(at_lane == 2 * pair + 1, second, deltas)
        turned[:, here] = deltas.T
    attn_low = heads_out[...].astype(jnp.bfloat16)
    flat_resid = all_resid[...].reshape(shards * token_rows, width)
    out_grads[...] = (
        inner_rows(attn_low, flat_resid).astype(jnp.bfloat16).reshape(groups, rows, width)
    )
    out_scatter = ExpScatter(
        place,
        lambda line, part: out_grads.at[line * 2 + 1 - place.x],
        lambda line, part: out_grads.at[line * 2 + place.x],
        lambda line, part: out_crossed.at[line],
        lambda line, part: out_raised.at[raised_slot(line)],
        lambda line, part: out_lowered.at[lowered_slot(line)],
        1,
        (out_xs, out_xr, out_ls, out_lr),
    )
    for line in ORDER:
        out_scatter.begin(line, 0)
    column_sum.hop(2)
    mix.hop(1, 0)
    key_grads[...] = jnp.zeros_like(key_grads)
    value_grads[...] = jnp.zeros_like(value_grads)
    for block in range(shards):
        here = pl.ds(block * token_rows, token_rows)
        count = (block + 1) * token_rows
        at_col = block * token_rows + lax.broadcasted_iota(jnp.int32, (1, token_rows), 1)
        at_row = lax.broadcasted_iota(jnp.int32, (count, 1), 0)
        bias = jnp.where(
            (at_row <= at_col)
            & (columns[:count] == documents[:, block * token_rows : count]),
            0.0,
            MASK_FILLER,
        )
        for pair in range(2):
            lanes = slice(pair * 128, pair * 128 + 128)
            queries = qkv[here, lanes]
            grads = head_grads[here, lanes]
            query_grad = jnp.zeros((token_rows, 128), jnp.float32)
            for head in range(2):
                row = 2 * pair + head
                mine = low if head == 0 else jnp.logical_not(low)
                own_queries = jnp.where(mine, queries, jnp.zeros((), jnp.bfloat16))
                own_grads = jnp.where(mine, grads, jnp.zeros((), jnp.bfloat16))
                key, value = keys[pair][head][:count], values[pair][head][:count]
                scores = outer_cols(key, queries) * factor + bias
                probs = jnp.exp(scores - norm_rows[row : row + 1, block * token_rows : count])
                grad_probs = outer_cols(value, grads)
                grad_scores = (probs * (grad_probs - turned[row : row + 1, here])).astype(
                    jnp.bfloat16
                )
                value_grads[pair, :count, :] += dot_rows(probs.astype(jnp.bfloat16), own_grads)
                key_grads[pair, :count, :] += dot_rows(grad_scores, own_queries)
                query_grad = query_grad + inner_rows(grad_scores, key)
            qkv_grads[here, lanes] = (query_grad * factor).astype(jnp.bfloat16)
        if block == 1:
            mix.fold(1)
            mix.hop(0, 1)
            column_sum.turn()
        if block == 3:
            mix.hop(2, 0)
            mix.hop(1, 1)

    def fold_heads(first, second):
        return jnp.where(
            low,
            first + pltpu.roll(first, HEAD_SIZE, 1),
            second + pltpu.roll(second, HEAD_SIZE, 1),
        )

    qkv_grads[:, q_cols : q_cols + k_cols] = (
        fold_heads(key_grads[0], key_grads[1]) * factor
    ).astype(jnp.bfloat16)
    qkv_grads[:, q_cols + k_cols :] = fold_heads(value_grads[0], value_grads[1]).astype(
        jnp.bfloat16
    )

    normed_scatter = CtxScatter(
        place,
        lambda y, part: normed_part.at[2 * y + 1 - place.half],
        lambda y, part: normed_part.at[2 * y + place.half],
        lambda lane, part: normed_swapped.at[lane],
        lambda part: normed_crossed,
        1,
        normed_send,
        normed_recv,
    )
    gain_one_sum = jnp.zeros((1, width), jnp.float32)
    main_sum = jnp.zeros((width, main_cols), jnp.float32)
    for block in range(shards):
        here = pl.ds(block * token_rows, token_rows)
        grads = outer_cols(qkv_grads[here, :], full[:, :main_cols])
        normed_part[block] = grads.astype(jnp.bfloat16)
        own = to_f32(all_tokens[block])
        scaled = own * rms_scale(own)
        gain_one_sum = gain_one_sum + jnp.sum(grads * scaled, 0, keepdims=True)
        normed = (scaled * gain_one_row).astype(jnp.bfloat16)
        main_sum = main_sum + inner_rows(normed, qkv_grads[here, :])
    normed_scatter.swap(False, 0).start()
    normed_scatter.swap(True, 0).start()
    at_sub = lax.broadcasted_iota(jnp.int32, (128, 1), 0)
    gain_rows = jnp.where(
        at_sub == EXPERTS, gain_one_sum, jnp.where(at_sub == EXPERTS + 1, gain_two_sum, 0.0)
    )
    side = jnp.concatenate([router_sum, gain_rows[EXPERTS:, :]], 0).T
    sums[:, :, :, :main_cols] = main_sum.astype(jnp.bfloat16).reshape(
        shards, groups, rows, main_cols
    )
    sums[:, :, :, main_cols:] = side.astype(jnp.bfloat16).reshape(
        shards, groups, rows, pack_cols - main_cols
    )
    sum_scatter = ExpScatter(
        place,
        lambda line, part: sums.at[:, line * 2 + 1 - place.x],
        lambda line, part: sums.at[:, line * 2 + place.x],
        lambda line, part: sums_crossed.at[line],
        lambda line, part: sums_raised.at[raised_slot(line)],
        lambda line, part: sums_lowered.at[lowered_slot(line)],
        1,
        (sum_xs, sum_xr, sum_ls, sum_lr),
    )
    for line in ORDER:
        sum_scatter.begin(line, 0)
    for line in ORDER:
        mix.begin(line, mix_parts - 1)
    normed_scatter.fold(0)
    mix.fold(2)
    mix.hop(0, 2)
    mix.hop(2, 1)
    out_scatter.fold(0)
    out_scatter.hop(0, 0)
    mix.hop(1, 2)
    sum_scatter.fold(0)
    sum_scatter.hop(0, 0)
    out_scatter.hop(1, 0)
    mix.hop(2, 2)
    for copy in early_stores:
        copy.wait()
    stores = []
    for part in range(local_experts):
        for kind, (scatter, held, target) in enumerate(
            ((into, in_mine, in_sum), (downs, down_mine, down_sum))
        ):
            scatter.arrived(part)
            held[place.y, part] = scatter.total(part).astype(jnp.bfloat16)
            copy = pltpu.make_async_copy(
                held.at[place.y, part], target.at[EARLY + part], store_sem.at[kind, part]
            )
            copy.start()
            stores.append(copy)
    sum_scatter.hop(1, 0)
    out_scatter.hop(2, 0)
    mix.fold(3)
    mix.hop(0, 3)
    sum_scatter.hop(2, 0)
    mix.hop(1, 3)
    output_sum[...] = out_scatter.total(0)
    sums_own[...] = sum_scatter.total(0).astype(jnp.bfloat16)
    sums_all[ctx] = sums_own[ctx]
    copies = []
    for lane, to in enumerate((place.core, place.side, place.far)):
        copy = remote(
            sums_own.at[to[0]], sums_all.at[ctx], last_send.at[lane], last_recv.at[lane], to
        )
        copy.start()
        copies.append(copy)
    normed_scatter.arrived(0)
    grad_normed = normed_scatter.total(0)
    own = to_f32(tokens[...])
    scale = rms_scale(own)
    weighted = grad_normed * gain_one_row
    grad_tokens[...] = (
        grad_resid[...]
        + scale * weighted
        - own * (scale * scale * scale) * jnp.mean(weighted * own, -1, keepdims=True)
    )
    mix.hop(2, 3)
    for part in range(mix_parts):
        here = pl.ds(*MIX_CUTS[part])
        mixed_out[here, :] = (resid[here, :] + mix.total(part)).astype(jnp.bfloat16)
    here = pl.ds(mix_rows, COLUMN)
    mixed_out[here, :] = (resid[here, :] + column_sum.total()).astype(jnp.bfloat16)
    for lane, to in enumerate((place.core, place.side, place.far)):
        remote(
            sums_own.at[0], sums_all.at[to[0]], last_send.at[lane], last_recv.at[lane], to
        ).wait_recv()
    side = jnp.zeros((rows, pack_cols - main_cols), jnp.float32)
    for shard in range(shards):
        came = to_f32(sums_all[shard])
        query_sum[:, shard * q_cols : (shard + 1) * q_cols] = came[:, :q_cols]
        key_sum[:, shard * k_cols : (shard + 1) * k_cols] = came[:, q_cols : q_cols + k_cols]
        value_sum[:, shard * k_cols : (shard + 1) * k_cols] = came[:, q_cols + k_cols : main_cols]
        side = side + came[:, main_cols:]
    side_sum[...] = side
    for copy in stores:
        copy.wait()
    for copy in copies:
        copy.wait_send()
    for scatter in (mix, column_sum, into, downs, out_scatter, normed_scatter, sum_scatter):
        scatter.finish()
    for part in range(moe_parts):
        resid_gather.sent(part)


def back(
    moe_in_grads, mixed_part, grad_in, grad_down, in_first, down_first, tokens, cot, resid, side_rows, logit_grads,
    all_moe, all_tokens, weights, out_rows, qkv, heads_out, norm_rows, seg_row,
):
    token_rows, width = tokens.shape
    shards, groups, rows, pack_cols = weights.shape
    seq_len = shards * token_rows
    q_cols, main_cols = heads_out.shape[1], qkv.shape[1]
    k_cols = (main_cols - q_cols) // 2
    experts, _, in_rows, in_cols = grad_in.shape
    down_rows = grad_down.shape[2]
    low, f32 = jnp.bfloat16, jnp.float32

    def shape(dims, dtype):
        return jax.ShapeDtypeStruct(dims, dtype)

    whole, anywhere = pl.BlockSpec(memory_space=VMEM), pl.BlockSpec(memory_space=pl.ANY)
    mix_rows = sum(size for _, size in MIX_CUTS)
    block, steps = (LINES, mix_rows, width), (LINES - 1, mix_rows, width)
    pack = (shards, rows, pack_cols)
    return pl.pallas_call(
        back_kernel,
        name="back",
        out_shape=[
            shape((token_rows, width), low),
            shape((token_rows, width), f32),
            shape((rows, shards * q_cols), f32),
            shape((rows, shards * k_cols), f32),
            shape((rows, shards * k_cols), f32),
            shape((rows, pack_cols - main_cols), f32),
            shape((rows, width), f32),
            shape((EARLY + experts, in_rows, in_cols), low),
            shape((EARLY + experts, down_rows, width), low),
        ],
        in_specs=[whole] + [anywhere] * 5 + [whole] * 5 + [anywhere] * 6 + [whole] * 2,
        out_specs=[whole] * 7 + [anywhere] * 2,
        scratch_shapes=[
            VMEM(block, low),
            VMEM(block, low),
            VMEM(steps, low),
            VMEM(steps, low),
            VMEM((groups, COLUMN, width), low),
            VMEM((2, 2, LINES - 1, COLUMN, width), low),
            VMEM((COLUMN, width), low),
            VMEM((2, experts, in_rows, in_cols), low),
            VMEM((2, experts, in_rows, in_cols), low),
            VMEM((experts, in_rows, in_cols), low),
            VMEM((2, experts, down_rows, width), low),
            VMEM((2, experts, down_rows, width), low),
            VMEM((experts, down_rows, width), low),
            VMEM((token_rows, width), f32),
            VMEM((shards, token_rows, width), low),
            VMEM((seq_len, q_cols), low),
            VMEM((128, seq_len), f32),
            VMEM((2, seq_len, 128), f32),
            VMEM((2, seq_len, 128), f32),
            VMEM((seq_len, main_cols), low),
            VMEM((shards, token_rows, width), low),
            VMEM((2, token_rows, width), low),
            VMEM((token_rows, width), low),
            VMEM((shards, groups, rows, pack_cols), low),
            VMEM((LINES,) + pack, low),
            *[VMEM((LINES - 1,) + pack, low)] * 2,
            VMEM((shards, rows, pack_cols), low),
            VMEM((shards, rows, pack_cols), low),
            VMEM((groups, rows, width), low),
            VMEM((LINES, rows, width), low),
            *[VMEM((LINES - 1, rows, width), low)] * 2,
            VMEM((EARLY, in_rows, in_cols), low),
            VMEM((EARLY, down_rows, width), low),
            DMA((2, experts)),
            VMEM(all_moe.shape, low),
            VMEM(all_tokens.shape, low),
            VMEM(weights.shape, low),
            VMEM(out_rows.shape, low),
            VMEM(qkv.shape, low),
            VMEM(heads_out.shape, f32),
            DMA((6,)),
            DMA((2,)),
            DMA((9,)),
            *scatter_sems(len(MIX_CUTS)),
            *column_sum_sems(),
            *scatter_sems(1),
            *scatter_sems(1),
            *square_sems(experts),
            *square_sems(experts),
            *square_sems(1),
            *square_sems(4),
            DMA((3,)),
            DMA((3,)),
        ],
        compiler_params=pltpu.CompilerParams(
            collective_id=1, has_side_effects=True, vmem_limit_bytes=62 * 2**20
        ),
    )(
        moe_in_grads, mixed_part, grad_in, grad_down, in_first, down_first, tokens, cot, resid, side_rows, logit_grads,
        all_moe, all_tokens, weights, out_rows, qkv, heads_out, norm_rows, seg_row,
    )


def two_parts(values):
    high = values.astype(jnp.bfloat16)
    return high, (values - high.astype(jnp.float32)).astype(jnp.bfloat16)


def finish_kernel(pieces, *refs):
    count = len(pieces)
    kinds = max(kind for kind, _ in pieces) + 1
    sources, targets = refs[:kinds], refs[kinds : 2 * kinds]
    held, ready = refs[2 * kinds : 2 * kinds + count], refs[2 * kinds + count : -2]
    load_sem, store_sem = refs[-2:]
    loads, stores = [], []
    for index, (kind, at) in enumerate(pieces):
        source = sources[kind] if at is None else sources[kind].at[at]
        loads.append(pltpu.make_async_copy(source, held[index], load_sem.at[index]))
        loads[-1].start()
    wide = 0
    for index, (kind, at) in enumerate(pieces):
        loads[index].wait()
        target = targets[kind] if at is None else targets[kind].at[at]
        value = held[index]
        if sources[kind].dtype != targets[kind].dtype:
            ready[wide][...] = to_f32(value[...])
            value = ready[wide]
            wide += 1
        stores.append(pltpu.make_async_copy(value, target, store_sem.at[index]))
        stores[-1].start()
    for copy in stores:
        copy.wait()


def finish(*arrays):
    wide = [array.ndim == 3 for array in arrays]
    pieces, held, ready = [], [], []
    for kind, array in enumerate(arrays):
        places = range(array.shape[0]) if wide[kind] else [None]
        for at in places:
            pieces.append((kind, at))
            dims = array.shape[1:] if wide[kind] else array.shape
            held.append(VMEM(dims, array.dtype))
            if wide[kind]:
                ready.append(VMEM(dims, jnp.float32))
    anywhere = pl.BlockSpec(memory_space=pl.ANY)
    return pl.pallas_call(
        functools.partial(finish_kernel, tuple(pieces)),
        name="finish",
        out_shape=[
            jax.ShapeDtypeStruct(array.shape, jnp.float32 if wide[kind] else array.dtype)
            for kind, array in enumerate(arrays)
        ],
        in_specs=[anywhere] * len(arrays),
        out_specs=[anywhere] * len(arrays),
        scratch_shapes=held + ready + [DMA((len(pieces),)), DMA((len(pieces),))],
        compiler_params=pltpu.CompilerParams(vmem_limit_bytes=GRANT),
    )(*arrays)


def by_heads(
    tokens,
    segments,
    routes,
    gain_attn,
    gain_moe,
    query_weight,
    key_weight,
    value_weight,
    w_output,
    w_router,
    w_expert_in,
    w_expert_out,
    cotangent,
):
    shards = lax.axis_size("ctx")
    groups = lax.axis_size("exp")
    width = tokens.shape[2]
    rows = query_weight.shape[0]
    q_cols = query_weight.shape[1] // shards
    k_cols = key_weight.shape[1] // shards
    main_cols = q_cols + 2 * k_cols
    side = 128

    (
        grad_moe_in,
        mixed_part,
        logit_grads,
        in_first,
        down_first,
        in_rest,
        down_rest,
        all_moe,
        all_tokens,
        all_weights,
        out_rows,
        qkv,
        heads_out,
        norm_rows,
        resid,
        side_rows,
    ) = ahead(
        tokens[0],
        gain_attn[None],
        gain_moe[None],
        w_router,
        query_weight,
        key_weight,
        value_weight,
        w_output,
        routes[0].T,
        segments,
        cotangent[0],
        w_expert_in,
        w_expert_out,
    )
    rest = in_rest.shape[0]
    (
        mixed_out,
        grad_tokens,
        query_sum,
        key_sum,
        value_sum,
        side_sum,
        output_sum,
        in_sum,
        down_sum,
    ) = back(
        grad_moe_in,
        mixed_part,
        in_rest.reshape((rest, shards, -1, width)),
        down_rest.reshape((rest, shards, -1, width)),
        in_first,
        down_first,
        tokens[0],
        cotangent[0],
        resid,
        side_rows,
        logit_grads,
        all_moe,
        all_tokens,
        all_weights.reshape(shards, groups, rows, main_cols + side),
        out_rows.reshape(groups, rows, width),
        qkv.reshape(-1, main_cols),
        heads_out,
        norm_rows,
        segments,
    )
    in_sum, down_sum, grad_tokens, mixed_out, query_sum, output_sum, key_sum, value_sum = finish(
        in_sum, down_sum, grad_tokens, mixed_out, query_sum, output_sum, key_sum, value_sum
    )
    return (
        mixed_out[None],
        grad_tokens[None],
        side_sum[:, EXPERTS],
        side_sum[:, EXPERTS + 1],
        query_sum,
        key_sum,
        value_sum,
        output_sum,
        side_sum[:, :EXPERTS],
        in_sum,
        down_sum,
    )


def solution(mesh):
    sizes = (mesh.shape["ctx"], mesh.shape["exp"])
    return jax.shard_map(
        by_heads if sizes == (4, 8) else local,
        mesh=mesh,
        in_specs=(
            P("exp", "ctx", None),
            P("exp", None),
            P("exp", "ctx", None),
            P(("ctx", "exp")),
            P(("ctx", "exp")),
            P(("ctx", "exp"), None),
            P(("ctx", "exp"), None),
            P(("ctx", "exp"), None),
            P(("ctx", "exp"), None),
            P(("ctx", "exp"), None),
            P("exp", "ctx", None),
            P("exp", "ctx", None),
            P("exp", "ctx", None),
        ),
        out_specs=(
            P("exp", "ctx", None),
            P("exp", "ctx", None),
            P(("ctx", "exp")),
            P(("ctx", "exp")),
            P(("ctx", "exp"), None),
            P(("ctx", "exp"), None),
            P(("ctx", "exp"), None),
            P(("ctx", "exp"), None),
            P(("ctx", "exp"), None),
            P("exp", "ctx", None),
            P("exp", "ctx", None),
        ),
        check_vma=False,
    )
```

```python
import functools
import math

import jax
import jax.numpy as jnp
from jax import lax
from jax.experimental import pallas as pl
from jax.experimental.pallas import tpu as pltpu
from jax.sharding import PartitionSpec as P

QUERY_HEADS = 16
KEY_VALUE_HEADS = 8
HEAD_SIZE = 64
EXPERTS = 32
TOPK = 8
FF = 512
CAP = 72


EPSILON = 1e-06
MASK_FILLER = -1e30


def rms_scale(values):
    return lax.rsqrt(jnp.mean(values * values, -1, keepdims=True) + EPSILON)


def inner_rows(left, right):
    return lax.dot_general(
        left, right, (((0,), (0,)), ((), ())), preferred_element_type=jnp.float32
    )


def outer_cols(left, right):
    return lax.dot_general(
        left, right, (((1,), (1,)), ((), ())), preferred_element_type=jnp.float32
    )


def allowed_block(query_pos, query_seg, seg_all, offset, key_total_count):
    key_pos = offset + jnp.arange(key_total_count, dtype=jnp.int32)
    key_seg = lax.dynamic_slice_in_dim(seg_all, offset, key_total_count)
    return (key_pos[None, :] <= query_pos[:, None]) & (key_seg[None, :] == query_seg[:, None])


def head_scores(heads_of_queries, key_segment_slice, factor):
    key_total_count = key_segment_slice.shape[0]
    heads_of_keys = key_segment_slice.reshape(key_total_count, KEY_VALUE_HEADS, -1)
    return (
        jnp.einsum(
            "ihgd,jhd->hgij", heads_of_queries, heads_of_keys, preferred_element_type=jnp.float32
        )
        * factor
    )


def slot_tables(pair_ids):
    pair_count = pair_ids.shape[0]
    member = (pair_ids[:, None] == jnp.arange(EXPERTS, dtype=jnp.int32)[None, :]).astype(jnp.int32)
    earlier = jnp.cumsum(member, 0) - member
    slot_place = jnp.sum(earlier * member, 1, dtype=jnp.int32)
    is_kept = slot_place < CAP
    slot_index = jnp.where(is_kept, pair_ids * CAP + slot_place, EXPERTS * CAP)
    slot_filler = (
        jnp.full((EXPERTS * CAP,), -1, jnp.int32)
        .at[slot_index]
        .set(jnp.arange(pair_count, dtype=jnp.int32), mode="drop")
    )
    return (slot_index, is_kept, slot_filler)


def local(
    tokens,
    segments,
    routes,
    gain_attn,
    gain_moe,
    query_weight,
    key_weight,
    value_weight,
    w_output,
    w_router,
    w_expert_in,
    w_expert_out,
    cotangent,
):
    shards = lax.axis_size("ctx")
    groups = lax.axis_size("exp")
    ctx_rank = lax.axis_index("ctx")
    gain_one, gain_two, full_query, full_key, full_value, full_output, full_router = (
        lax.all_gather(gain_attn, ("ctx", "exp"), axis=0, tiled=True),
        lax.all_gather(gain_moe, ("ctx", "exp"), axis=0, tiled=True),
        lax.all_gather(query_weight, ("ctx", "exp"), axis=0, tiled=True),
        lax.all_gather(key_weight, ("ctx", "exp"), axis=0, tiled=True),
        lax.all_gather(value_weight, ("ctx", "exp"), axis=0, tiled=True),
        lax.all_gather(w_output, ("ctx", "exp"), axis=0, tiled=True),
        lax.all_gather(w_router, ("ctx", "exp"), axis=0, tiled=True),
    )
    expert_in, expert_out = (
        lax.all_gather(w_expert_in, "ctx", axis=1, tiled=True),
        lax.all_gather(w_expert_out, "ctx", axis=1, tiled=True),
    )
    inputs = tokens[0].astype(jnp.float32)
    token_rows = inputs.shape[0]
    seq_len = token_rows * shards
    head_cluster = QUERY_HEADS // KEY_VALUE_HEADS
    factor = 1.0 / math.sqrt(HEAD_SIZE)
    kv_width = key_weight.shape[1]
    seg_all = segments[0]
    query_pos = ctx_rank * token_rows + jnp.arange(token_rows, dtype=jnp.int32)
    query_seg = lax.dynamic_slice_in_dim(seg_all, ctx_rank * token_rows, token_rows)
    scale_one = rms_scale(inputs)
    gain_one_f = gain_one.astype(jnp.float32)
    normalized_input = (inputs * scale_one * gain_one_f).astype(jnp.bfloat16)
    query_matrix = jnp.dot(normalized_input, full_query, preferred_element_type=jnp.float32).astype(
        jnp.bfloat16
    )
    key_rows = jnp.dot(normalized_input, full_key, preferred_element_type=jnp.float32).astype(
        jnp.bfloat16
    )
    value_rows = jnp.dot(normalized_input, full_value, preferred_element_type=jnp.float32).astype(
        jnp.bfloat16
    )
    heads_of_queries = query_matrix.reshape(token_rows, KEY_VALUE_HEADS, head_cluster, HEAD_SIZE)
    group_size = math.gcd(shards, max(1, 1024 // token_rows))
    key_range_width = group_size * token_rows
    turns_needed = ctx_rank // group_size + 1
    running_maximum = jnp.full(
        (KEY_VALUE_HEADS, head_cluster, token_rows), MASK_FILLER, jnp.float32
    )
    key_segment_slice = lax.all_gather(key_rows, "ctx", axis=0, tiled=True)
    value_segment_slice = lax.all_gather(value_rows, "ctx", axis=0, tiled=True)
    key_total_count = key_segment_slice.shape[0]
    scores = head_scores(heads_of_queries, key_segment_slice, factor)
    allowed = allowed_block(query_pos, query_seg, seg_all, jnp.int32(0), key_total_count)
    scores = jnp.where(allowed, scores, MASK_FILLER)
    new_max = jnp.maximum(running_maximum, jnp.max(scores, -1))
    weights = jnp.where(allowed, jnp.exp(scores - new_max[..., None]), 0.0)
    run_sum = jnp.sum(weights, -1)
    heads_of_values = value_segment_slice.reshape(key_total_count, KEY_VALUE_HEADS, HEAD_SIZE)
    run_acc = jnp.einsum(
        "hgij,jhd->ihgd",
        weights.astype(jnp.bfloat16),
        heads_of_values,
        preferred_element_type=jnp.float32,
    )
    running_maximum, run_sum, run_acc = (new_max, run_sum, run_acc)
    log_norm = running_maximum + jnp.log(run_sum)
    heads_out = run_acc / jnp.transpose(run_sum, (2, 0, 1))[..., None]
    attn_low = heads_out.reshape(token_rows, -1).astype(jnp.bfloat16)
    resid = inputs + jnp.dot(attn_low, full_output, preferred_element_type=jnp.float32)
    scale_two = rms_scale(resid)
    gain_two_f = gain_two.astype(jnp.float32)
    moe_in = (resid * scale_two * gain_two_f).astype(jnp.bfloat16)
    logits = jnp.dot(moe_in, full_router, preferred_element_type=jnp.float32)
    route_ids = routes[0]
    one_hot = (route_ids[:, :, None] == jnp.arange(EXPERTS, dtype=jnp.int32)[None, None, :]).astype(
        jnp.float32
    )
    chosen = jnp.sum(one_hot * logits[:, None, :], -1)
    gates = jax.nn.softmax(chosen, axis=-1)
    slot_index, is_kept, slot_filler = slot_tables(route_ids.reshape(-1))
    filled = slot_filler >= 0
    token_of = jnp.maximum(slot_filler, 0) // TOPK
    local_experts = EXPERTS // groups
    send_rows = jnp.where(
        filled[:, None], jnp.take(moe_in, token_of, axis=0), jnp.zeros((), jnp.bfloat16)
    )
    send_rows = send_rows.reshape(groups, local_experts, CAP, -1)
    received = lax.all_to_all(send_rows, "exp", split_axis=0, concat_axis=0, tiled=True)
    pre = jnp.einsum("sjcd,jdf->sjcf", received, expert_in, preferred_element_type=jnp.float32)
    gate_part = pre[..., :FF]
    up_part = pre[..., FF:]
    hidden = (jax.nn.silu(gate_part) * up_part).astype(jnp.bfloat16)
    expert_rows = jnp.einsum(
        "sjcf,jfd->sjcd", hidden, expert_out, preferred_element_type=jnp.float32
    ).astype(jnp.bfloat16)
    returned = lax.all_to_all(expert_rows, "exp", split_axis=0, concat_axis=0, tiled=True).reshape(
        EXPERTS * CAP, -1
    )
    safe_slot = jnp.minimum(slot_index, EXPERTS * CAP - 1)
    picked = jnp.where(
        is_kept[:, None], jnp.take(returned, safe_slot, axis=0), jnp.zeros((), jnp.bfloat16)
    )
    picked = picked.astype(jnp.float32).reshape(token_rows, TOPK, -1)
    branch = jnp.sum(gates[:, :, None] * picked, 1)
    mixed_out = (resid + branch).astype(jnp.bfloat16)
    grad_out = cotangent[0].astype(jnp.float32)
    grad_picked = jnp.sum(grad_out[:, None, :] * picked, -1)
    grad_chosen = gates * (grad_picked - jnp.sum(gates * grad_picked, -1, keepdims=True))
    grad_logits = jnp.sum(one_hot * grad_chosen[:, :, None], 1)
    slot_gate = jnp.where(filled, jnp.take(gates.reshape(-1), jnp.maximum(slot_filler, 0)), 0.0)
    grad_send = (slot_gate[:, None] * jnp.take(grad_out, token_of, axis=0)).astype(jnp.bfloat16)
    grad_send = grad_send.reshape(groups, local_experts, CAP, -1)
    grad_rows = lax.all_to_all(grad_send, "exp", split_axis=0, concat_axis=0, tiled=True)
    grad_hidden = jnp.einsum(
        "sjcd,jfd->sjcf", grad_rows, expert_out, preferred_element_type=jnp.float32
    )
    sigmoid_gate = jax.nn.sigmoid(gate_part)
    grad_gate = grad_hidden * up_part * sigmoid_gate * (1.0 + gate_part * (1.0 - sigmoid_gate))
    grad_up = grad_hidden * gate_part * sigmoid_gate
    grad_pre = jnp.concatenate([grad_gate, grad_up], -1).astype(jnp.bfloat16)
    grad_expert_out = jnp.einsum(
        "sjcf,sjcd->jfd", hidden, grad_rows, preferred_element_type=jnp.float32
    )
    grad_expert_in = jnp.einsum(
        "sjcd,sjcf->jdf", received, grad_pre, preferred_element_type=jnp.float32
    )
    grad_received = jnp.einsum(
        "sjcf,jdf->sjcd", grad_pre, expert_in, preferred_element_type=jnp.float32
    ).astype(jnp.bfloat16)
    grad_back = lax.all_to_all(
        grad_received, "exp", split_axis=0, concat_axis=0, tiled=True
    ).reshape(EXPERTS * CAP, -1)
    grad_pairs = jnp.where(
        is_kept[:, None], jnp.take(grad_back, safe_slot, axis=0), jnp.zeros((), jnp.bfloat16)
    )
    grad_pairs = grad_pairs.astype(jnp.float32).reshape(token_rows, TOPK, -1)
    grad_moe_in = (
        jnp.sum(grad_pairs, 1)
        + outer_cols(grad_logits.astype(jnp.bfloat16), full_router) * 0.0
        + lax.dot_general(
            grad_logits,
            full_router.astype(jnp.float32),
            (((1,), (1,)), ((), ())),
            precision=lax.Precision.HIGHEST,
            preferred_element_type=jnp.float32,
        )
    )
    grad_router = lax.dot_general(
        moe_in.astype(jnp.float32),
        grad_logits,
        (((0,), (0,)), ((), ())),
        precision=lax.Precision.HIGHEST,
        preferred_element_type=jnp.float32,
    )
    weighted_two = grad_moe_in * gain_two_f
    grad_gain_two = jnp.sum(grad_moe_in * resid * scale_two, 0)
    cube_two = scale_two * scale_two * scale_two
    grad_resid = (
        grad_out
        + scale_two * weighted_two
        - resid * cube_two * jnp.mean(weighted_two * resid, -1, keepdims=True)
    )
    grad_resid_low = grad_resid.astype(jnp.bfloat16)
    grad_output_w = inner_rows(attn_low, grad_resid_low)
    grad_heads = (
        outer_cols(grad_resid_low, full_output)
        .astype(jnp.bfloat16)
        .reshape(token_rows, KEY_VALUE_HEADS, head_cluster, HEAD_SIZE)
    )
    delta = jnp.transpose(jnp.sum(grad_heads.astype(jnp.float32) * heads_out, -1), (1, 2, 0))
    all_keys, all_values = (
        lax.all_gather(key_rows, "ctx", axis=0, tiled=True),
        lax.all_gather(value_rows, "ctx", axis=0, tiled=True),
    )

    def block_grads(offset):
        key_segment_slice = lax.dynamic_slice_in_dim(all_keys, offset, key_range_width)
        value_segment_slice = lax.dynamic_slice_in_dim(all_values, offset, key_range_width)
        scores = head_scores(heads_of_queries, key_segment_slice, factor)
        allowed = allowed_block(query_pos, query_seg, seg_all, offset, key_range_width)
        probs_full = jnp.where(allowed, jnp.exp(scores - log_norm[..., None]), 0.0)
        heads_of_keys = key_segment_slice.reshape(key_range_width, KEY_VALUE_HEADS, HEAD_SIZE)
        heads_of_values = value_segment_slice.reshape(key_range_width, KEY_VALUE_HEADS, HEAD_SIZE)
        grad_probs = jnp.einsum(
            "ihgd,jhd->hgij", grad_heads, heads_of_values, preferred_element_type=jnp.float32
        )
        grad_scores = (probs_full * (grad_probs - delta[..., None])).astype(jnp.bfloat16)
        query_part = jnp.einsum(
            "hgij,jhd->ihgd", grad_scores, heads_of_keys, preferred_element_type=jnp.float32
        )
        return (probs_full, grad_scores, query_part)

    query_begin_index = jnp.zeros(
        (token_rows, KEY_VALUE_HEADS, head_cluster, HEAD_SIZE), jnp.float32
    )

    def back_turn(turn, running):
        grad_query_acc, key_grad_buf = running
        offset = turn * key_range_width
        probs_full, grad_scores, query_part = block_grads(offset)
        grad_key_part = (
            jnp.einsum(
                "hgij,ihgd->jhd", grad_scores, heads_of_queries, preferred_element_type=jnp.float32
            )
            * factor
        )
        grad_value_part = jnp.einsum(
            "hgij,ihgd->jhd",
            probs_full.astype(jnp.bfloat16),
            grad_heads,
            preferred_element_type=jnp.float32,
        )
        joined = jnp.concatenate(
            [
                grad_key_part.reshape(key_range_width, -1),
                grad_value_part.reshape(key_range_width, -1),
            ],
            1,
        )
        key_grad_buf = lax.dynamic_update_slice_in_dim(key_grad_buf, joined, offset, 0)
        return (grad_query_acc + query_part, key_grad_buf)

    back_start = (query_begin_index, jnp.zeros((seq_len, 2 * kv_width), jnp.float32))
    grad_query_acc, key_grad_buf = lax.fori_loop(0, turns_needed, back_turn, back_start)
    own_grads = lax.psum_scatter(
        key_grad_buf.astype(jnp.bfloat16), "ctx", scatter_dimension=0, tiled=True
    ).astype(jnp.float32)
    grad_keys = own_grads[:, :kv_width].astype(jnp.bfloat16)
    grad_values = own_grads[:, kv_width:].astype(jnp.bfloat16)
    grad_query = (grad_query_acc * factor).reshape(token_rows, -1).astype(jnp.bfloat16)
    grad_query_w = inner_rows(normalized_input, grad_query)
    grad_key_w = inner_rows(normalized_input, grad_keys)
    grad_value_w = inner_rows(normalized_input, grad_values)
    grad_normed = (
        outer_cols(grad_query, full_query)
        + outer_cols(grad_keys, full_key)
        + outer_cols(grad_values, full_value)
    )
    weighted_one = grad_normed * gain_one_f
    grad_gain_one = jnp.sum(grad_normed * inputs * scale_one, 0)
    cube_one = scale_one * scale_one * scale_one
    grad_inputs = (
        grad_resid
        + scale_one * weighted_one
        - inputs * cube_one * jnp.mean(weighted_one * inputs, -1, keepdims=True)
    )
    dense_sums = (
        lax.psum_scatter(grad_gain_one, ("ctx", "exp"), scatter_dimension=0, tiled=True),
        lax.psum_scatter(grad_gain_two, ("ctx", "exp"), scatter_dimension=0, tiled=True),
        lax.psum_scatter(grad_query_w, ("ctx", "exp"), scatter_dimension=0, tiled=True),
        lax.psum_scatter(grad_key_w, ("ctx", "exp"), scatter_dimension=0, tiled=True),
        lax.psum_scatter(grad_value_w, ("ctx", "exp"), scatter_dimension=0, tiled=True),
        lax.psum_scatter(grad_output_w, ("ctx", "exp"), scatter_dimension=0, tiled=True),
        lax.psum_scatter(grad_router, ("ctx", "exp"), scatter_dimension=0, tiled=True),
    )
    expert_sums = (
        lax.psum_scatter(
            grad_expert_in.astype(jnp.bfloat16), "ctx", scatter_dimension=1, tiled=True
        ).astype(jnp.float32),
        lax.psum_scatter(
            grad_expert_out.astype(jnp.bfloat16), "ctx", scatter_dimension=1, tiled=True
        ).astype(jnp.float32),
    )
    return (mixed_out[None], grad_inputs[None]) + tuple(dense_sums) + tuple(expert_sums)


MESH = pl.DeviceIdType.MESH
VMEM = pltpu.VMEM
DMA = pltpu.SemaphoreType.DMA
COT_LATE = 32
COLUMN = 32
ORDER = (3, 0, 2, 1)
MIX_CUTS = ((0, 64), (64, 64), (128, 64), (192, 32))
CUTS = ((0, 64), (64, 64), (128, 64), (192, 32))
SUM_CUTS = ((0, 80), (80, 80), (160, 48), (208, 16))
LINES = 4
GRANT = 56 * 2**20


def to_f32(value):
    return value.astype(jnp.float32)


def dot_rows(left, right):
    return jnp.dot(left, right, preferred_element_type=jnp.float32)


def remote(source, target, send, recv, to):
    return pltpu.make_async_remote_copy(
        src_ref=source,
        dst_ref=target,
        send_sem=send,
        recv_sem=recv,
        device_id=to,
        device_id_type=MESH,
    )


class Place:
    def __init__(self):
        ctx, exp = lax.axis_index("ctx"), lax.axis_index("exp")
        self.ctx, self.exp = ctx, exp
        self.y, self.half = ctx // 2, ctx % 2
        self.z, self.x = exp // 2, exp % 2
        other_half = ctx + 1 - 2 * (ctx % 2)
        self.up, self.down = (ctx, exp + 2), (ctx, exp - 2)
        self.across = (ctx, exp + 1 - 2 * (exp % 2))
        self.core = (other_half, exp)
        self.side = (lax.rem(ctx + 2, 4), exp)
        self.far = (lax.rem(other_half + 2, 4), exp)

    def greet(self, lines=True, square=True):
        barrier = pltpu.get_barrier_semaphore()
        count = jnp.int32(0)
        if square:
            for to in (self.core, self.side, self.far):
                pl.semaphore_signal(barrier, inc=1, device_id=to, device_id_type=MESH)
            count = count + 3
        if lines:
            pl.semaphore_signal(barrier, inc=1, device_id=self.across, device_id_type=MESH)

            @pl.when(self.z < LINES - 1)
            def _():
                pl.semaphore_signal(barrier, inc=1, device_id=self.up, device_id_type=MESH)

            @pl.when(self.z > 0)
            def _():
                pl.semaphore_signal(barrier, inc=1, device_id=self.down, device_id_type=MESH)

            count = count + 1 + jnp.where(self.z < LINES - 1, 1, 0) + jnp.where(self.z > 0, 1, 0)
        pl.semaphore_wait(barrier, count)


class ExpGather:
    def __init__(self, place, view, parts, send, recv):
        self.place, self.view, self.parts = place, view, parts
        self.send, self.recv = send, recv

    def copy(self, lane, line, part, to):
        index = line * 2 + self.place.x
        ref = self.view(index, part)
        return remote(ref, ref, self.send.at[lane, line, part], self.recv.at[index, part], to)

    def pass_on(self, line, part, up, down):
        place = self.place
        if up:

            @pl.when(place.z < LINES - 1)
            def _():
                self.copy(1, line, part, place.up).start()

        if down:

            @pl.when(place.z > 0)
            def _():
                self.copy(2, line, part, place.down).start()

        self.copy(0, line, part, place.across).start()

    def begin(self, part):
        self.pass_on(self.place.z, part, True, True)

    def arrived(self, index, part):
        ref = self.view(index, part)
        remote(
            ref, ref, self.send.at[0, 0, part], self.recv.at[index, part], self.place.across
        ).wait_recv()

    def relay(self, step, part):
        place = self.place

        @pl.when(place.z >= step)
        def _():
            line = place.z - step
            self.arrived(line * 2 + place.x, part)
            self.pass_on(line, part, True, False)

        @pl.when(place.z + step < LINES)
        def _():
            line = place.z + step
            self.arrived(line * 2 + place.x, part)
            self.pass_on(line, part, False, True)

    def relays(self):
        for step in range(1, LINES):
            for part in range(self.parts):
                self.relay(step, part)

    def across_arrived(self, line, part):
        self.arrived(line * 2 + 1 - self.place.x, part)

    def finish(self):
        for part in range(self.parts):
            for line in range(LINES):
                self.across_arrived(line, part)
        self.sent()

    def sent(self):
        place = self.place
        for part in range(self.parts):
            for line in range(LINES):
                self.copy(0, line, part, place.across).wait_send()

                @pl.when((place.z >= line) & (place.z < LINES - 1))
                def _():
                    self.copy(1, line, part, place.up).wait_send()

                @pl.when((place.z <= line) & (place.z > 0))
                def _():
                    self.copy(2, line, part, place.down).wait_send()


def gather_sems(parts):
    return [DMA((3, LINES, parts)), DMA((2 * LINES, parts))]


def raised_slot(line):
    return max(line - 1, 0) if isinstance(line, int) else jnp.maximum(line - 1, 0)


def lowered_slot(line):
    return min(line, LINES - 2) if isinstance(line, int) else jnp.minimum(line, LINES - 2)


class ExpScatter:
    def __init__(self, place, outgoing, mine, crossed, raised, lowered, parts, sems, done=0):
        self.place, self.parts = place, parts
        self.done = done
        self.outgoing, self.mine = outgoing, mine
        self.crossed, self.raised, self.lowered = crossed, raised, lowered
        self.cross_send, self.cross_recv, self.line_send, self.line_recv = sems

    def cross(self, line, part):
        place = self.place
        return remote(
            self.outgoing(line, part),
            self.crossed(line, part),
            self.cross_send.at[line, part],
            self.cross_recv.at[line, part],
            place.across,
        )

    def along(self, up, line, part):
        place = self.place
        side = 0 if up else 1
        return remote(
            self.mine(line, part),
            (self.raised if up else self.lowered)(line, part),
            self.line_send.at[side, line, part],
            self.line_recv.at[side, line, part],
            place.up if up else place.down,
        )

    def begin(self, line, part):
        self.cross(line, part).start()

    def fold(self, part, owners=ORDER):
        place = self.place
        for line in owners:

            @pl.when(place.z != line)
            def _():
                self.cross(line, part).wait_recv()
                ref = self.mine(line, part)
                ref[...] = (to_f32(ref[...]) + to_f32(self.crossed(line, part)[...])).astype(
                    ref.dtype
                )

    def hop(self, stage, part, owners=ORDER):
        place = self.place
        for up in (True, False):
            here = stage if up else LINES - 1 - stage
            lines = range(LINES - 1, here, -1) if up else range(here)
            lines = [line for line in lines if line in owners]
            if not lines:
                continue

            @pl.when(place.z == here)
            def _():
                for line in lines:
                    if stage > 0:
                        self.along(up, line, part).wait_recv()
                        ref = self.mine(line, part)
                        came = (self.raised if up else self.lowered)(line, part)
                        ref[...] = (to_f32(ref[...]) + to_f32(came[...])).astype(ref.dtype)
                    self.along(up, line, part).start()

    def total(self, part):
        place = self.place
        line = place.z
        value = to_f32(self.mine(line, part)[...])
        if part >= self.done:
            self.cross(line, part).wait_recv()
            value = value + to_f32(self.crossed(line, part)[...])
        for up in (True, False):
            came = (self.raised if up else self.lowered)(line, part)
            some = line > 0 if up else line < LINES - 1

            @pl.when(some)
            def _():
                self.along(up, line, part).wait_recv()

            value = value + jnp.where(some, to_f32(came[...]), 0.0)
        return value

    def finish(self):
        place = self.place
        for part in range(self.parts):
            for line in range(LINES):
                if part >= self.done:
                    self.cross(line, part).wait_send()
                for up in (True, False):

                    @pl.when(place.z < line if up else place.z > line)
                    def _():
                        self.along(up, line, part).wait_send()


def scatter_sems(parts):
    return [DMA((LINES, parts)), DMA((LINES, parts)), DMA((2, LINES, parts)), DMA((2, LINES, parts))]


class ColumnGather:
    def __init__(self, place, view, send, recv):
        self.place, self.view, self.send, self.recv = place, view, send, recv

    def copy(self, lane, index, to):
        ref = self.view(index)
        return remote(ref, ref, self.send.at[lane, index], self.recv.at[index], to)

    def pass_on(self, index, up, down):
        place = self.place
        if up:

            @pl.when(place.z < LINES - 1)
            def _():
                self.copy(1, index, place.up).start()

        if down:

            @pl.when(place.z > 0)
            def _():
                self.copy(2, index, place.down).start()

    def arrived(self, index):
        ref = self.view(index)
        remote(
            ref, ref, self.send.at[0, index], self.recv.at[index], self.place.across
        ).wait_recv()

    def begin(self):
        self.copy(0, self.place.exp, self.place.across).start()
        self.pass_on(self.place.exp, True, True)

    def turn(self):
        other = self.place.across[1]
        self.arrived(other)
        self.pass_on(other, True, True)

    def relay(self, step):
        place = self.place
        for column in (place.x, 1 - place.x):

            @pl.when(place.z >= step)
            def _():
                index = (place.z - step) * 2 + column
                self.arrived(index)
                self.pass_on(index, True, False)

            @pl.when(place.z + step < LINES)
            def _():
                index = (place.z + step) * 2 + column
                self.arrived(index)
                self.pass_on(index, False, True)

    def sent(self):
        place = self.place
        self.copy(0, place.exp, place.across).wait_send()
        for line in range(LINES):
            for column in range(2):
                index = line * 2 + column

                @pl.when((place.z >= line) & (place.z < LINES - 1))
                def _():
                    self.copy(1, index, place.up).wait_send()

                @pl.when((place.z <= line) & (place.z > 0))
                def _():
                    self.copy(2, index, place.down).wait_send()


def column_sems():
    return [DMA((3, 2 * LINES)), DMA((2 * LINES,))]


class ColumnScatter:
    def __init__(self, place, mine, came, crossed, sems):
        self.place, self.mine, self.came, self.crossed = place, mine, came, crossed
        self.line_send, self.line_recv, self.cross_send, self.cross_recv = sems

    def along(self, up, line, far):
        place = self.place
        side = 0 if up else 1
        slot = raised_slot(line) if up else lowered_slot(line)
        return remote(
            self.mine(line, far),
            self.came(side, far, slot),
            self.line_send.at[side, far, line],
            self.line_recv.at[side, far, line],
            place.up if up else place.down,
        )

    def cross(self):
        return remote(
            self.mine(self.place.z, 1),
            self.crossed,
            self.cross_send.at[0],
            self.cross_recv.at[0],
            self.place.across,
        )

    def hop(self, stage):
        place = self.place
        for up in (True, False):
            here = stage if up else LINES - 1 - stage
            lines = range(LINES - 1, here, -1) if up else range(here)

            @pl.when(place.z == here)
            def _():
                for line in lines:
                    for far in (1, 0):
                        if stage > 0:
                            self.along(up, line, far).wait_recv()
                            ref = self.mine(line, far)
                            slot = raised_slot(line) if up else lowered_slot(line)
                            came = self.came(0 if up else 1, far, slot)
                            ref[...] = (to_f32(ref[...]) + to_f32(came[...])).astype(ref.dtype)
                        self.along(up, line, far).start()

    def line_total(self, far):
        line = self.place.z
        value = to_f32(self.mine(line, far)[...])
        for up in (True, False):
            some = line > 0 if up else line < LINES - 1

            @pl.when(some)
            def _():
                self.along(up, line, far).wait_recv()

            slot = raised_slot(line) if up else lowered_slot(line)
            came = self.came(0 if up else 1, far, slot)
            value = value + jnp.where(some, to_f32(came[...]), 0.0)
        return value

    def turn(self):
        ref = self.mine(self.place.z, 1)
        ref[...] = self.line_total(1).astype(ref.dtype)
        self.cross().start()

    def total(self):
        value = self.line_total(0)
        self.cross().wait_recv()
        return value + to_f32(self.crossed[...])

    def finish(self):
        place = self.place
        self.cross().wait_send()
        for line in range(LINES):
            for far in range(2):
                for up in (True, False):

                    @pl.when(place.z < line if up else place.z > line)
                    def _():
                        self.along(up, line, far).wait_send()


def column_sum_sems():
    return [DMA((2, 2, LINES)), DMA((2, 2, LINES)), DMA((1,)), DMA((1,))]


class CtxGather:
    def __init__(self, place, view, parts, send, recv, own=None):
        self.place, self.view, self.parts = place, view, parts
        self.send, self.recv, self.own = send, recv, own

    def copy(self, lane, part):
        place = self.place
        index = lax.rem(place.ctx + 2, 4) if lane == 2 else place.ctx
        ref = self.view(index, part)
        source = ref if lane == 2 or self.own is None else self.own(part)
        to = place.side if lane == 1 else place.core
        return remote(source, ref, self.send.at[lane, part], self.recv.at[lane, part], to)

    def landed(self, lane, part):
        place = self.place
        index = (place.core, place.side, place.far)[lane][0]
        ref = self.view(index, part)
        return remote(ref, ref, self.send.at[lane, part], self.recv.at[lane, part], place.core)

    def begin(self, part):
        self.copy(1, part).start()
        self.copy(0, part).start()

    def relay(self, part):
        self.landed(1, part).wait_recv()
        self.copy(2, part).start()

    def arrived(self, part):
        self.landed(0, part).wait_recv()
        self.landed(2, part).wait_recv()

    def sent(self, part):
        for lane in range(3):
            self.copy(lane, part).wait_send()


def square_sems(parts):
    return [DMA((3, parts)), DMA((3, parts))]


class CtxScatter:
    def __init__(self, place, outgoing, mine, swapped, crossed, parts, send, recv):
        self.place, self.parts = place, parts
        self.outgoing, self.mine = outgoing, mine
        self.swapped, self.crossed = swapped, crossed
        self.send, self.recv = send, recv

    def swap(self, near, part):
        place = self.place
        y = place.y if near else 1 - place.y
        lane = 0 if near else 1
        return remote(
            self.outgoing(y, part),
            self.swapped(lane, part),
            self.send.at[lane, part],
            self.recv.at[lane, part],
            place.core,
        )

    def over(self, part):
        place = self.place
        return remote(
            self.mine(1 - place.y, part),
            self.crossed(part),
            self.send.at[2, part],
            self.recv.at[2, part],
            place.side,
        )

    def fold(self, part):
        self.swap(False, part).wait_recv()
        ref = self.mine(1 - self.place.y, part)
        ref[...] = (to_f32(ref[...]) + to_f32(self.swapped(1, part)[...])).astype(ref.dtype)
        self.over(part).start()

    def arrived(self, part):
        self.swap(True, part).wait_recv()
        self.over(part).wait_recv()

    def total(self, part, here=slice(None)):
        return (
            to_f32(self.mine(self.place.y, part)[here, :])
            + to_f32(self.swapped(0, part)[here, :])
            + to_f32(self.crossed(part)[here, :])
        )

    def finish(self):
        for part in range(self.parts):
            self.swap(False, part).wait_send()
            self.swap(True, part).wait_send()
            self.over(part).wait_send()


def ahead_kernel(
    tokens,
    gain_attn,
    gain_moe,
    w_router,
    wq,
    wk,
    wv,
    wo,
    routes,
    seg_row,
    cot_hbm,
    in_hbm,
    out_hbm,
    grad_moe_in,
    mixed_part,
    logit_grads,
    in_first,
    down_first,
    in_rest,
    down_rest,
    moe_hbm,
    tokens_hbm,
    weights_hbm,
    out_rows_hbm,
    qkv_hbm,
    heads_hbm,
    norm_rows,
    resid_hbm,
    side_rows,
    moe,
    cot,
    w_in,
    w_out,
    slot_rows,
    slot_cot,
    hidden,
    slopes,
    slot_out,
    pick,
    slot_gate,
    gates,
    all_routes,
    resid_rows,
    moe_crossed,
    moe_raised,
    moe_lowered,
    column_came,
    column_crossed,
    sum_stage,
    load_sem,
    keep_sem,
    store_sem,
    put_sem,
    free_sem,
    tok_send,
    tok_recv,
    swap_send,
    swap_recv,
    w_send,
    w_recv,
    o_send,
    o_recv,
    r_send,
    r_recv,
    c_send,
    c_recv,
    cc_send,
    cc_recv,
    l_send,
    l_recv,
    m_send,
    m_recv,
    mc_send,
    mc_recv,
    i_send,
    i_recv,
    u_send,
    u_recv,
    s_send,
    s_recv,
    moe_xs,
    moe_xr,
    moe_ls,
    moe_lr,
    column_ls,
    column_lr,
    column_xs,
    column_xr,
    cross_sem,
    step_sem,
    mix_send,
    mix_recv,
    in_send,
    in_recv,
    down_send,
    down_recv,
):
    place = Place()
    ctx, exp = place.ctx, place.exp
    groups, token_rows, width = moe.shape
    shards = width // in_hbm.shape[1]
    rows = wq.shape[0]
    q_cols, k_cols = wq.shape[1] // shards, wk.shape[1] // shards
    main_cols = q_cols + 2 * k_cols
    side = side_rows.shape[0]
    pack_cols = main_cols + side
    local_experts = w_in.shape[0]
    in_rows, down_rows = in_hbm.shape[1], out_hbm.shape[1]
    slots = pick.shape[1] // local_experts
    first = exp * local_experts
    factor = 1.0 / math.sqrt(HEAD_SIZE)

    def token_block(index):
        return slot_rows.at[index, pl.ds(0, token_rows)]

    def partial(index, start, size):
        return slot_rows.at[index, pl.ds(token_rows + start, size)]

    def out_part(index):
        return slot_rows.at[
            index // LINES, pl.ds(2 * token_rows + lax.rem(index, LINES) * rows, rows)
        ]

    sources = (ctx, place.core[0], place.side[0], place.far[0])

    def weight_part(index, part):
        return slot_cot.at[sources[part], pl.ds(index * rows, rows), pl.ds(0, pack_cols)]

    def packed(shard):
        return slot_cot.at[shard, pl.ds(2 * token_rows, rows), pl.ds(0, pack_cols)]

    def swap_space(lane, start, size):
        return slot_cot.at[lane, pl.ds(token_rows + start, size)]

    def qkv_cols(low, count):
        return slopes[:, :token_rows, low : low + count].reshape(shards * token_rows, count)

    own_in = pltpu.make_async_copy(
        in_hbm, w_in.at[:, pl.ds(ctx * in_rows, in_rows)], load_sem.at[0]
    )
    own_out = pltpu.make_async_copy(
        out_hbm, w_out.at[:, pl.ds(ctx * down_rows, down_rows)], load_sem.at[1]
    )
    own_cot = pltpu.make_async_copy(cot_hbm, cot.at[exp], load_sem.at[2])
    for copy in (own_cot, own_in, own_out):
        copy.start()
    token_block(ctx)[...] = tokens[...]
    diagonal = lax.broadcasted_iota(jnp.int32, (rows, rows), 0) == lax.broadcasted_iota(
        jnp.int32, (rows, rows), 1
    )
    gain_cols = [
        jnp.sum(jnp.where(diagonal, to_f32(gain[...]), 0.0), 1, keepdims=True)
        for gain in (gain_attn, gain_moe)
    ]
    lane = lax.broadcasted_iota(jnp.int32, (1, side - EXPERTS), 1)
    gain_cols = jnp.where(
        lane == 0, gain_cols[0], jnp.where(lane == 1, gain_cols[1], 0.0)
    ).astype(jnp.bfloat16)
    for shard in range(shards):
        target = packed(shard)
        target[:, :q_cols] = wq[:, shard * q_cols : (shard + 1) * q_cols]
        target[:, q_cols : q_cols + k_cols] = wk[:, shard * k_cols : (shard + 1) * k_cols]
        target[:, q_cols + k_cols : main_cols] = wv[:, shard * k_cols : (shard + 1) * k_cols]
        target[:, main_cols : main_cols + EXPERTS] = w_router[...]
        target[:, main_cols + EXPERTS :] = gain_cols

    def weight_slot(shard):
        return slot_cot.at[shard, pl.ds(exp * rows, rows), pl.ds(0, pack_cols)]

    weight_slot(ctx)[...] = packed(ctx)[...]
    out_part(exp)[...] = wo[...]
    all_routes[exp] = routes[...]
    place.greet()

    mixes = []
    for lane, to in enumerate((place.core, place.side, place.far)):
        copy = remote(
            packed(to[0]),
            weight_slot(ctx),
            swap_send.at[lane],
            swap_recv.at[lane],
            to,
        )
        copy.start()
        mixes.append(copy)
    half_rows = token_rows // 2
    token_gather = CtxGather(
        place,
        lambda index, part: slot_rows.at[index, pl.ds(part * half_rows, half_rows)],
        2,
        tok_send,
        tok_recv,
    )
    for part in range(2):
        token_gather.begin(part)
    cot_parts = c_send.shape[2]
    late_rows = COT_LATE
    cot_rows = (token_rows - late_rows - COLUMN) // cot_parts
    cot_gather = ExpGather(
        place,
        lambda index, part: cot.at[index, pl.ds(part * cot_rows, cot_rows)],
        cot_parts,
        c_send,
        c_recv,
    )
    own_cot.wait()
    cot_gather.begin(0)
    route_gather = ExpGather(place, lambda index, part: all_routes.at[index], 1, r_send, r_recv)
    weight_gather = ExpGather(place, weight_part, shards, w_send, w_recv)
    out_gather = ExpGather(place, lambda index, part: out_part(index), 1, o_send, o_recv)
    weight_gather.begin(0)
    for lane, copy in enumerate(mixes):
        remote(
            packed(0),
            weight_slot(sources[1 + lane]),
            swap_send.at[lane],
            swap_recv.at[lane],
            place.core,
        ).wait_recv()
        weight_gather.begin(1 + lane)
    route_gather.begin(0)
    out_gather.begin(0)
    in_gather = CtxGather(
        place,
        lambda index, part: w_in.at[part, pl.ds(index * in_rows, in_rows)],
        local_experts,
        i_send,
        i_recv,
    )
    down_gather = CtxGather(
        place,
        lambda index, part: w_out.at[part, pl.ds(index * down_rows, down_rows)],
        local_experts,
        u_send,
        u_recv,
    )
    late_gather = ExpGather(
        place,
        lambda index, part: cot.at[index, pl.ds(token_rows - COLUMN - late_rows, late_rows)],
        1,
        l_send,
        l_recv,
    )
    column_rows = pl.ds(token_rows - COLUMN, COLUMN)
    cot_column = ColumnGather(place, lambda index: cot.at[index, column_rows], cc_send, cc_recv)
    own_in.wait()
    own_out.wait()
    half_experts = local_experts // 2
    wanted = [
        (gather, part) for part in range(local_experts) for gather in (in_gather, down_gather)
    ]
    ahead_of_branch = 3
    for gather, part in wanted[:ahead_of_branch]:
        gather.begin(part)
    for step in range(1, LINES):
        for part in range(shards):
            weight_gather.relay(step, part)
        if step < LINES - 1:
            token_gather.relay(step - 1)
    cot_gather.relay(1, 0)
    for step in range(1, LINES):
        out_gather.relay(step, 0)
        route_gather.relay(step, 0)
    cot_column.begin()
    for part in range(1, cot_parts):
        cot_gather.begin(part)
    cot_gather.relay(2, 0)
    for part in range(2):
        token_gather.arrived(part)
    weight_gather.finish()

    same = (
        lax.broadcasted_iota(jnp.int32, (side, side), 0)
        == lax.broadcasted_iota(jnp.int32, (side, side), 1)
    ).astype(jnp.bfloat16)
    full = slot_cot[:, :token_rows, :pack_cols].reshape(width, pack_cols)
    side_t = outer_cols(same, full[:, main_cols:])
    side_rows[...] = side_t.astype(jnp.bfloat16)
    gain_one, gain_two = side_t[EXPERTS : EXPERTS + 1], side_t[EXPERTS + 1 : EXPERTS + 2]
    for block in range(shards):
        values = to_f32(token_block(block)[...])
        normed = (values * rms_scale(values) * gain_one).astype(jnp.bfloat16)
        slopes[block, :token_rows, :main_cols] = dot_rows(normed, full[:, :main_cols]).astype(
            jnp.bfloat16
        )

    low = lax.broadcasted_iota(jnp.int32, (1, 2 * HEAD_SIZE), 1) < HEAD_SIZE

    def spread(start):
        plain = to_f32(qkv_cols(start, k_cols))
        turned = pltpu.roll(plain, HEAD_SIZE, 1)
        zero = jnp.zeros((), jnp.float32)
        return [
            [
                jnp.where(low, plain, zero).astype(jnp.bfloat16),
                jnp.where(low, zero, turned).astype(jnp.bfloat16),
            ],
            [
                jnp.where(low, turned, zero).astype(jnp.bfloat16),
                jnp.where(low, zero, plain).astype(jnp.bfloat16),
            ],
        ]

    keys, values = spread(q_cols), spread(q_cols + k_cols)
    parts = slot_rows.shape[1] - 2 * token_rows
    keep = []
    for block in range(shards - 1, -1, -1):
        count = (block + 1) * token_rows
        at_row = block * token_rows + lax.broadcasted_iota(jnp.int32, (token_rows, 1), 0)
        at_col = lax.broadcasted_iota(jnp.int32, (1, count), 1)
        documents = seg_row[:, block * token_rows : count].astype(jnp.float32)
        own_document = jnp.broadcast_to(documents, (128, token_rows)).T[:, :1]
        bias = jnp.where(
            (at_col <= at_row) & (own_document == seg_row[:, :count].astype(jnp.float32)),
            0.0,
            MASK_FILLER,
        )
        lows = []
        norms = jnp.zeros((token_rows, 128), jnp.float32)
        at_lane = lax.broadcasted_iota(jnp.int32, (1, 128), 1)
        for pair in range(2):
            queries = slopes[block, :token_rows, pair * 128 : pair * 128 + 128]
            heads = jnp.zeros((token_rows, 128), jnp.float32)
            for head in range(2):
                scores = outer_cols(queries, keys[pair][head][:count]) * factor + bias
                top = jnp.max(scores, -1, keepdims=True)
                shares = jnp.exp(scores - top)
                total = jnp.sum(shares, -1, keepdims=True)
                norms = jnp.where(at_lane == 2 * pair + head, top + jnp.log(total), norms)
                heads = heads + dot_rows(
                    shares.astype(jnp.bfloat16), values[pair][head][:count]
                ) / total
            start = block * q_cols + pair * 128
            resid_rows[:, start : start + 128] = heads
            lows.append(heads.astype(jnp.bfloat16))
        norm_rows[:, block * token_rows : count] = norms.T[:8]
        slopes[block, token_rows : 2 * token_rows, :q_cols] = jnp.concatenate(lows, 1)
        keep.append(
            pltpu.make_async_copy(
                resid_rows.at[:, pl.ds(block * q_cols, q_cols)],
                heads_hbm.at[pl.ds(block * token_rows, token_rows)],
                keep_sem.at[len(keep)],
            )
        )
        keep[-1].start()
        if block == 2:
            cot_column.turn()
            for part in range(1, cot_parts):
                cot_gather.relay(1, part)
            cot_gather.relay(3, 0)
        pl.semaphore_signal(step_sem, inc=1)
        pl.semaphore_wait(step_sem, 1)

    out_gather.finish()
    full_out = jnp.concatenate(
        [slot_rows[part, 2 * token_rows :, :] for part in range(q_cols // parts)], 0
    )
    for block in range(shards):
        partial(block, 0, token_rows)[...] = dot_rows(
            slopes[block, token_rows : 2 * token_rows, :q_cols], full_out
        ).astype(
            jnp.bfloat16
        )
    stored = len(keep)
    here = pl.ds(0, token_rows)
    for source, target in (
        (slot_rows.at[:, here], tokens_hbm),
        (slot_cot.at[:, here, pl.ds(0, pack_cols)], weights_hbm),
        (slopes.at[:, here, pl.ds(0, main_cols)], qkv_hbm),
        (slot_rows.at[pl.ds(0, q_cols // parts), pl.ds(2 * token_rows, parts)], out_rows_hbm),
    ):
        keep.append(pltpu.make_async_copy(source, target, keep_sem.at[len(keep)]))
        keep[-1].start()

    branch = CtxScatter(
        place,
        lambda y, part: partial(2 * y + 1 - place.half, part * half_rows, half_rows),
        lambda y, part: partial(2 * y + place.half, part * half_rows, half_rows),
        lambda lane, part: swap_space(lane, part * half_rows, half_rows),
        lambda part: swap_space(2, part * half_rows, half_rows),
        2,
        s_send,
        s_recv,
    )
    for part in range(2):
        branch.swap(False, part).start()
    for part in range(2):
        branch.swap(True, part).start()
    cot_column.relay(1)
    for part in range(1, cot_parts):
        cot_gather.relay(2, part)
    for part in range(2):
        branch.fold(part)
    for gather, part in wanted[ahead_of_branch:]:
        gather.begin(part)
    gather_parts = len(CUTS)
    moe_gather = ExpGather(
        place,
        lambda index, part: moe.at[index, pl.ds(*CUTS[part])],
        gather_parts,
        m_send,
        m_recv,
    )
    moe_column = ColumnGather(place, lambda index: moe.at[index, column_rows], mc_send, mc_recv)
    cot_column.relay(2)
    for copy in keep[:stored]:
        copy.wait()
    for part in range(2):
        here = pl.ds(part * half_rows, half_rows)
        branch.arrived(part)
        resid = to_f32(tokens[here, :]) + branch.total(part)
        resid_rows[here, :] = resid
        moe[exp, here, :] = (resid * rms_scale(resid) * gain_two).astype(jnp.bfloat16)
        if part == 1:
            moe_column.begin()
        for piece, (start, size) in enumerate(CUTS):
            if start // half_rows == part:
                moe_gather.begin(piece)
    keep.append(pltpu.make_async_copy(resid_rows, resid_hbm, keep_sem.at[len(keep)]))
    keep[-1].start()
    cot_column.relay(3)
    for part in range(1, cot_parts):
        cot_gather.relay(3, part)
    moe_column.turn()
    for step in range(1, LINES):
        for part in range(gather_parts):
            moe_gather.relay(step, part)
        moe_column.relay(step)
        if step == 1:
            for gather, part in wanted[:ahead_of_branch]:
                gather.relay(part)
    late_gather.begin(0)
    route_gather.finish()
    branch.finish()
    for part in range(2):
        token_gather.sent(part)
    for copy in mixes:
        copy.wait_send()
    for copy in keep[stored:]:
        copy.wait()

    at_expert = lax.broadcasted_iota(jnp.int32, (EXPERTS, 1), 0)
    at_lane = lax.broadcasted_iota(jnp.int32, (1, 128), 1)
    at_slot = lax.broadcasted_iota(jnp.int32, (slots, 1), 0)
    before = (
        lax.broadcasted_iota(jnp.int32, (token_rows, token_rows), 0)
        < lax.broadcasted_iota(jnp.int32, (token_rows, token_rows), 1)
    ).astype(jnp.bfloat16)
    router = side_rows[:EXPERTS, :]
    all_slots = groups * slots
    def block_of(line, far):
        return line * 2 + (1 - place.x if far else place.x)

    def slot_range(line, far):
        start = (far * LINES + line) * slots
        return pl.ds(start if isinstance(line, int) else pl.multiple_of(start, slots), slots)

    def dispatch(line, far):
        block = block_of(line, far)
        routes = all_routes[block]
        member = routes[0:1, :] == at_expert
        for rank in range(1, TOPK):
            member = member | (routes[rank : rank + 1, :] == at_expert)
        tokens = moe[block]
        logits = outer_cols(router, tokens)
        top = jnp.max(jnp.where(member, logits, MASK_FILLER), 0, keepdims=True)
        weights = jnp.where(member, jnp.exp(logits - top), 0.0)
        shares = weights / jnp.sum(weights, 0, keepdims=True)
        gates[block] = shares
        ranks = dot_rows(jnp.where(member, 1.0, 0.0).astype(jnp.bfloat16), before)
        filled = jnp.where(member & (ranks < CAP), ranks, -1.0)
        columns = jnp.zeros((slots, 128), jnp.float32)
        for expert in range(local_experts):
            mine = at_expert == first + expert
            spot = jnp.sum(jnp.where(mine, filled, 0.0), 0, keepdims=True)
            share = jnp.sum(jnp.where(mine, shares, 0.0), 0, keepdims=True)
            chosen = spot == at_slot.astype(jnp.float32)
            here = pl.ds(expert * slots, slots)
            pick[block, here, :] = jnp.where(chosen, 1.0, 0.0).astype(jnp.bfloat16)
            column = jnp.sum(jnp.where(chosen, share, 0.0), 1, keepdims=True)
            columns = jnp.where(at_lane == expert, column, columns)
        slot_gate[block] = columns
        chosen = pick[block]
        rows = dot_rows(chosen, tokens).astype(jnp.bfloat16)
        here = slot_range(line, far)
        for expert in range(local_experts):
            slot_rows[expert, here, :] = rows[expert * slots : (expert + 1) * slots]

    half_slots = all_slots // 2

    def each(count, body, far):
        def step(index, carry):
            body(index, far)
            return carry

        lax.fori_loop(0, count, step, 0)

    def near_line(step, carry):
        dispatch(place.z ^ step, 0)
        return carry

    def far_line(step, carry):
        line = place.z ^ step
        for part in range(gather_parts):
            moe_gather.across_arrived(line, part)
        dispatch(line, 1)
        return carry

    lax.fori_loop(0, LINES, near_line, 0)
    def forward(expert, far):
        half = pl.ds(far * half_slots, half_slots)
        rows = slot_rows[expert, half, :]
        for first_col in range(0, FF, 256):
            gate_cols, up_cols = pl.ds(first_col, 256), pl.ds(FF + first_col, 256)
            gate_part = dot_rows(rows, w_in[expert, :, gate_cols])
            up_part = dot_rows(rows, w_in[expert, :, up_cols])
            sigmoid_gate = jax.nn.sigmoid(gate_part)
            silu = gate_part * sigmoid_gate
            hidden[expert, half, gate_cols] = (silu * up_part).astype(jnp.bfloat16)
            slopes[expert, half, gate_cols] = (
                up_part * sigmoid_gate * (1.0 + gate_part * (1.0 - sigmoid_gate))
            ).astype(jnp.bfloat16)
            slopes[expert, half, up_cols] = silu.astype(jnp.bfloat16)
        slot_out[expert, half, :] = dot_rows(hidden[expert, half, :], w_out[expert]).astype(
            jnp.bfloat16
        )

    def pass_weights(expert):
        for gather, part in wanted[ahead_of_branch:]:
            if part == expert:
                gather.relay(part)

    def need(expert):
        in_gather.arrived(expert)
        down_gather.arrived(expert)

    last = local_experts - 1
    for expert in range(last):
        if expert + 1 < last:
            pass_weights(expert + 1)
        need(expert)
        forward(expert, 0)
    lax.fori_loop(0, LINES, far_line, 0)
    moe_gather.sent()
    moe_column.sent()
    moe_store = pltpu.make_async_copy(moe, moe_hbm, load_sem.at[0])
    moe_store.start()
    late_gather.relay(1, 0)
    each(half_experts, forward, 1)
    pass_weights(last)
    for expert in range(half_experts, last):
        forward(expert, 1)
    need(last)
    forward(last, 0)
    late_gather.relay(2, 0)
    forward(last, 1)
    moe_store.wait()

    def block_rows(line, far):
        here = slot_range(line, far)
        return jnp.concatenate([slot_out[expert, here, :] for expert in range(local_experts)], 0)

    def combine(line, far):
        block = block_of(line, far)
        shares = gates[block]
        weighted = []
        for expert in range(local_experts):
            mine = at_expert == first + expert
            share = jnp.sum(jnp.where(mine, shares, 0.0), 0, keepdims=True)
            chosen = to_f32(pick[block, pl.ds(expert * slots, slots), :])
            weighted.append((chosen * share).astype(jnp.bfloat16))
        moe[block] = inner_rows(
            jnp.concatenate(weighted, 0), block_rows(line, far)
        ).astype(jnp.bfloat16)

    late_gather.relay(3, 0)
    each(LINES, combine, 1)

    cot_gather.finish()
    cot_column.sent()
    late_gather.finish()

    def dispatch_back(line, far):
        block = block_of(line, far)
        shares = gates[block]
        chosen = pick[block]
        cots = dot_rows(chosen, cot[block])
        dots = jnp.sum(cots * to_f32(block_rows(line, far)), 1, keepdims=True)
        picked_grads = jnp.zeros_like(shares)
        there = slot_range(line, far)
        for expert in range(local_experts):
            here = slice(expert * slots, (expert + 1) * slots)
            row = jnp.sum(to_f32(chosen[here]) * dots[here], 0, keepdims=True)
            picked_grads = jnp.where(at_expert == first + expert, row, picked_grads)
            share = slot_gate[block, :, expert : expert + 1]
            slot_cot[expert, there, :] = (share * cots[here]).astype(jnp.bfloat16)
        grads = shares * (picked_grads - jnp.sum(shares * picked_grads, 0, keepdims=True))
        high, low = two_parts(grads)
        logit_grads[block] = jnp.concatenate([high, low], 0)

    def backward(expert, far):
        half = pl.ds(far * half_slots, half_slots)
        grads = outer_cols(slot_cot[expert, half, :], w_out[expert])
        slopes[expert, half, :FF] = (grads * to_f32(slopes[expert, half, :FF])).astype(jnp.bfloat16)
        slopes[expert, half, FF:] = (grads * to_f32(slopes[expert, half, FF:])).astype(jnp.bfloat16)
        slot_out[expert, half, :] = outer_cols(slopes[expert, half, :], w_in[expert]).astype(
            jnp.bfloat16
        )

    def combine_back(line, far):
        block = block_of(line, far)
        left = jnp.concatenate([pick[block], logit_grads[block]], 0)
        right = jnp.concatenate([block_rows(line, far), router, router], 0)
        cot[block] = inner_rows(left, right).astype(jnp.bfloat16)

    moe_parts = len(SUM_CUTS)

    def piece(ref, part):
        return ref.at[pl.ds(*SUM_CUTS[part])]

    back_sum = ExpScatter(
        place,
        lambda line, part: piece(cot.at[line * 2 + 1 - place.x], part),
        lambda line, part: piece(cot.at[line * 2 + place.x], part),
        lambda line, part: piece(moe_crossed.at[line], part),
        lambda line, part: piece(moe_raised.at[raised_slot(line)], part),
        lambda line, part: piece(moe_lowered.at[lowered_slot(line)], part),
        moe_parts,
        (moe_xs, moe_xr, moe_ls, moe_lr),
    )
    column_sum = ColumnScatter(
        place,
        lambda line, far: cot.at[block_of(line, far), column_rows],
        lambda side, far, slot: column_came.at[side, far, slot],
        column_crossed,
        (column_ls, column_lr, column_xs, column_xr),
    )
    each(LINES, dispatch_back, 1)
    each(local_experts, backward, 1)
    each(LINES, combine_back, 1)
    units = [(part, owners) for owners in (ORDER[:2], ORDER[2:]) for part in range(moe_parts)]
    for part, owners in units:
        for line in owners:
            back_sum.begin(line, part)
    each(LINES, combine, 0)
    mix_rows = pl.ds(*MIX_CUTS[0])
    later_rows = pl.ds(MIX_CUTS[0][1], token_rows - MIX_CUTS[0][1])
    part_store = pltpu.make_async_copy(
        moe.at[:, later_rows], mixed_part.at[:, later_rows], load_sem.at[0]
    )
    part_store.start()
    each(LINES, dispatch_back, 0)
    each(local_experts, backward, 0)
    each(LINES, combine_back, 0)

    for to in (place.core, place.side):
        pl.semaphore_signal(free_sem, inc=1, device_id=to, device_id_type=MESH)

    early = in_first.shape[0]
    for part in range(local_experts):
        in_gather.sent(part)
        down_gather.sent(part)
    into = CtxScatter(
        place,
        lambda y, part: w_in.at[part, pl.ds((2 * y + 1 - place.half) * in_rows, in_rows)],
        lambda y, part: w_in.at[part, pl.ds((2 * y + place.half) * in_rows, in_rows)],
        lambda lane, part: slot_out.at[part, pl.ds(lane * in_rows, in_rows)],
        lambda part: slot_out.at[early + part, pl.ds(2 * down_rows, in_rows)],
        early,
        in_send,
        in_recv,
    )
    downs = CtxScatter(
        place,
        lambda y, part: w_out.at[part, pl.ds((2 * y + 1 - place.half) * down_rows, down_rows)],
        lambda y, part: w_out.at[part, pl.ds((2 * y + place.half) * down_rows, down_rows)],
        lambda lane, part: slot_out.at[early + part, pl.ds(lane * down_rows, down_rows)],
        lambda part: slot_out.at[early + part, pl.ds(2 * down_rows + in_rows, down_rows)],
        early,
        down_send,
        down_recv,
    )
    part_store.wait()
    pl.semaphore_wait(free_sem, 2)
    stores = []

    def store(source, target, sem):
        copy = pltpu.make_async_copy(source, target, sem)
        copy.start()
        stores.append(copy)

    column_sum.hop(0)
    for expert in range(local_experts):
        w_out[expert] = inner_rows(hidden[expert], slot_cot[expert]).astype(jnp.bfloat16)
        if expert < early:
            downs.swap(False, expert).start()
            downs.swap(True, expert).start()
        else:
            store(w_out.at[expert], down_rest.at[expert - early], store_sem.at[0, expert])
        w_in[expert] = inner_rows(slot_rows[expert], slopes[expert]).astype(jnp.bfloat16)
        if expert < early:
            into.swap(False, expert).start()
            into.swap(True, expert).start()
        else:
            store(w_in.at[expert], in_rest.at[expert - early], store_sem.at[1, expert])
        if expert > 0 and expert <= early:
            downs.fold(expert - 1)
            into.fold(expert - 1)
        if expert == 1:
            back_sum.fold(*units[0])
            back_sum.hop(0, *units[0])
            column_sum.hop(1)
    pl.semaphore_signal(cross_sem, inc=1, device_id=place.across, device_id_type=MESH)

    def mix_cross(line):
        return remote(
            moe.at[line * 2 + 1 - place.x, mix_rows],
            slot_rows.at[line, mix_rows],
            mix_send.at[line],
            mix_recv.at[line],
            place.across,
        )

    for unit in range(1, len(units) + 2):
        if unit == 2:
            column_sum.hop(2)
        if unit == 3:
            column_sum.turn()
        if unit == len(units) - 1:
            pl.semaphore_wait(cross_sem, 1)
            for line in ORDER:
                mix_cross(line).start()
        if unit >= 2:
            back_sum.hop(2, *units[unit - 2])
        if unit <= len(units):
            back_sum.hop(1, *units[unit - 1])
        if unit < len(units):
            back_sum.fold(*units[unit])
            back_sum.hop(0, *units[unit])

    staged = [None, None]
    stage_rows = sum_stage.shape[1]

    def put(slot, value, target, sem):
        if staged[slot] is not None:
            staged[slot].wait()
        stage = sum_stage.at[slot, pl.ds(0, value.shape[0])]
        stage[...] = value
        staged[slot] = pltpu.make_async_copy(stage, target, sem)
        staged[slot].start()

    def finish_expert(part):
        for kind, (scatter, target) in enumerate(((downs, down_first), (into, in_first))):
            scatter.arrived(part)
            held = scatter.mine(place.y, part)
            held[...] = scatter.total(part).astype(jnp.bfloat16)
            store(held, target.at[part], store_sem.at[kind, part])

    for part in range(early - 1):
        finish_expert(part)
    mix_stores = []
    for part in range(moe_parts):
        here = pl.ds(*SUM_CUTS[part])
        put(part % 2, back_sum.total(part), grad_moe_in.at[here], put_sem.at[part % 2])
    put(moe_parts % 2, column_sum.total(), grad_moe_in.at[column_rows], put_sem.at[moe_parts % 2])
    finish_expert(early - 1)
    for line in ORDER:
        mix_cross(line).wait_recv()
        block = line * 2 + place.x
        moe[block, mix_rows, :] = (
            to_f32(moe[block, mix_rows, :]) + to_f32(slot_rows[line, mix_rows, :])
        ).astype(jnp.bfloat16)
        mix_stores.append(
            pltpu.make_async_copy(
                moe.at[block, mix_rows], mixed_part.at[block, mix_rows], load_sem.at[1 + line]
            )
        )
        mix_stores[-1].start()
    for line in ORDER:
        mix_cross(line).wait_send()
    for copy in mix_stores:
        copy.wait()
    for copy in staged:
        copy.wait()
    for copy in stores:
        copy.wait()
    for scatter in (back_sum, column_sum, into, downs):
        scatter.finish()


EARLY = 2


def ahead(
    tokens, gain_attn, gain_moe, w_router, wq, wk, wv, wo, routes, seg_row, cot, exp_in, exp_out
):
    shards, groups = lax.axis_size("ctx"), lax.axis_size("exp")
    token_rows, width = tokens.shape
    rows = wq.shape[0]
    q_cols, k_cols = wq.shape[1] // shards, wk.shape[1] // shards
    main_cols = q_cols + 2 * k_cols
    side = 128
    pack_cols = main_cols + side
    seq_len = token_rows * shards
    low, f32 = jnp.bfloat16, jnp.float32
    local_experts, in_rows, in_cols = exp_in.shape
    down_rows = exp_out.shape[1]
    slots = -(-CAP // 16) * 16
    arena = (local_experts, groups * slots)

    def shape(dims, dtype):
        return jax.ShapeDtypeStruct(dims, dtype)

    whole, anywhere = pl.BlockSpec(memory_space=VMEM), pl.BlockSpec(memory_space=pl.ANY)
    rest = local_experts - EARLY
    block, steps = (LINES, token_rows, width), (LINES - 1, token_rows, width)
    out_parts = groups * slots - 2 * token_rows
    return pl.pallas_call(
        ahead_kernel,
        name="ahead",
        out_shape=[
            shape((token_rows, width), f32),
            shape((groups, token_rows, width), low),
            shape((groups, 2 * EXPERTS, token_rows), low),
            shape((EARLY, in_rows, in_cols), low),
            shape((EARLY, down_rows, width), low),
            shape((rest, width, in_cols), low),
            shape((rest, FF, width), low),
            shape((groups, token_rows, width), low),
            shape((shards, token_rows, width), low),
            shape((shards, groups * rows, pack_cols), low),
            shape((q_cols // out_parts, out_parts, width), low),
            shape((shards, token_rows, main_cols), low),
            shape((seq_len, q_cols), f32),
            shape((8, seq_len), f32),
            shape((token_rows, width), f32),
            shape((side, width), low),
        ],
        in_specs=[whole] * 10 + [anywhere] * 3,
        out_specs=[anywhere, anywhere, whole]
        + [anywhere] * 10
        + [whole, anywhere, whole],
        scratch_shapes=[
            VMEM((groups, token_rows, width), low),
            VMEM((groups, token_rows, width), low),
            VMEM((local_experts, width, in_cols), low),
            VMEM((local_experts, FF, width), low),
            VMEM(arena + (width,), low),
            VMEM(arena + (width,), low),
            VMEM(arena + (FF,), low),
            VMEM(arena + (2 * FF,), low),
            VMEM(arena + (width,), low),
            VMEM((groups, local_experts * slots, token_rows), low),
            VMEM((groups, slots, 128), f32),
            VMEM((groups, EXPERTS, token_rows), f32),
            VMEM((groups,) + routes.shape, jnp.int32),
            VMEM((token_rows, width), f32),
            VMEM(block, low),
            VMEM(steps, low),
            VMEM(steps, low),
            VMEM((2, 2, LINES - 1, COLUMN, width), low),
            VMEM((COLUMN, width), low),
            VMEM((2, max(size for _, size in SUM_CUTS), width), f32),
            DMA((1 + LINES,)),
            DMA((shards + 5,)),
            DMA((2, local_experts)),
            DMA((2,)),
            pltpu.SemaphoreType.REGULAR,
            *square_sems(2),
            DMA((3,)),
            DMA((3,)),
            *gather_sems(shards),
            *gather_sems(1),
            *gather_sems(1),
            *gather_sems(2),
            *column_sems(),
            *gather_sems(1),
            *gather_sems(len(CUTS)),
            *column_sems(),
            *square_sems(local_experts),
            *square_sems(local_experts),
            *square_sems(2),
            *scatter_sems(len(SUM_CUTS)),
            *column_sum_sems(),
            pltpu.SemaphoreType.REGULAR,
            pltpu.SemaphoreType.REGULAR,
            DMA((LINES,)),
            DMA((LINES,)),
            *square_sems(EARLY),
            *square_sems(EARLY),
        ],
        compiler_params=pltpu.CompilerParams(
            collective_id=0, has_side_effects=True, vmem_limit_bytes=63 * 2**20
        ),
    )(tokens, gain_attn, gain_moe, w_router, wq, wk, wv, wo, routes, seg_row, cot, exp_in, exp_out)


def back_kernel(
    moe_in_grads,
    mixed_part,
    grad_in,
    grad_down,
    in_first,
    down_first,
    tokens,
    cot,
    resid,
    side_rows,
    logit_grads,
    all_moe_hbm,
    all_tokens_hbm,
    weights_hbm,
    out_rows_hbm,
    qkv_hbm,
    heads_out_hbm,
    norm_rows,
    seg_row,
    mixed_out,
    grad_tokens,
    query_sum,
    key_sum,
    value_sum,
    router_out,
    gain_one_out,
    gain_two_out,
    output_sum,
    in_sum,
    down_sum,
    mix_mine,
    mix_crossed,
    mix_raised,
    mix_lowered,
    column_mine,
    column_came,
    column_crossed,
    in_mine,
    in_swapped,
    in_crossed,
    down_mine,
    down_swapped,
    down_crossed,
    grad_resid,
    all_resid,
    head_grads,
    turned,
    key_grads,
    value_grads,
    qkv_grads,
    normed_part,
    normed_swapped,
    normed_crossed,
    sums,
    sums_crossed,
    sums_raised,
    sums_lowered,
    sums_own,
    sums_all,
    out_grads,
    out_crossed,
    out_raised,
    out_lowered,
    in_stage,
    down_stage,
    store_sem,
    all_moe,
    all_tokens,
    weights,
    out_rows,
    qkv,
    heads_out,
    late_sem,
    early_sem,
    local_sem,
    mix_xs,
    mix_xr,
    mix_ls,
    mix_lr,
    column_ls,
    column_lr,
    column_xs,
    column_xr,
    sum_xs,
    sum_xr,
    sum_ls,
    sum_lr,
    out_xs,
    out_xr,
    out_ls,
    out_lr,
    in_send,
    in_recv,
    down_send,
    down_recv,
    normed_send,
    normed_recv,
    resid_send,
    resid_recv,
    last_send,
    last_recv,
):
    place = Place()
    ctx, exp = place.ctx, place.exp
    token_rows, width = tokens.shape
    shards, groups, rows, pack_cols = weights.shape
    local_experts = grad_in.shape[0]
    q_cols = heads_out.shape[1]
    main_cols = qkv.shape[1]
    k_cols = (main_cols - q_cols) // 2
    factor = 1.0 / math.sqrt(HEAD_SIZE)

    loads = []

    def load(source, target):
        copy = pltpu.make_async_copy(source, target, local_sem.at[len(loads)])
        copy.start()
        loads.append(copy)

    for y in range(2):
        load(grad_in.at[:, 2 * y + place.half], in_mine.at[y])
        load(grad_down.at[:, 2 * y + place.half], down_mine.at[y])
    mix_rows = sum(size for _, size in MIX_CUTS)
    for line in ORDER:
        load(mixed_part.at[line * 2 + place.x, pl.ds(0, mix_rows)], mix_mine.at[line])
    load(mixed_part.at[:, pl.ds(mix_rows, COLUMN)], column_mine)
    place.greet()

    def piece(ref, count, part):
        size = ref.shape[0] // count
        return ref.at[pl.ds(part * size, size)]

    moe_parts, mix_parts = 4, len(MIX_CUTS)

    def cut(ref, part):
        return ref.at[pl.ds(*MIX_CUTS[part])]

    mix = ExpScatter(
        place,
        lambda line, part: cut(mixed_part.at[line * 2 + 1 - place.x], part),
        lambda line, part: cut(mix_mine.at[line], part),
        lambda line, part: cut(mix_crossed.at[line], part),
        lambda line, part: cut(mix_raised.at[raised_slot(line)], part),
        lambda line, part: cut(mix_lowered.at[lowered_slot(line)], part),
        mix_parts,
        (mix_xs, mix_xr, mix_ls, mix_lr),
        1,
    )
    column_sum = ColumnScatter(
        place,
        lambda line, far: column_mine.at[line * 2 + (1 - place.x if far else place.x)],
        lambda side, far, slot: column_came.at[side, far, slot],
        column_crossed,
        (column_ls, column_lr, column_xs, column_xr),
    )
    into = CtxScatter(
        place,
        lambda y, part: grad_in.at[part, 2 * y + 1 - place.half],
        lambda y, part: in_mine.at[y, part],
        lambda lane, part: in_swapped.at[lane, part],
        lambda part: in_crossed.at[part],
        local_experts,
        in_send,
        in_recv,
    )
    downs = CtxScatter(
        place,
        lambda y, part: grad_down.at[part, 2 * y + 1 - place.half],
        lambda y, part: down_mine.at[y, part],
        lambda lane, part: down_swapped.at[lane, part],
        lambda part: down_crossed.at[part],
        local_experts,
        down_send,
        down_recv,
    )
    for near in (False, True):
        for part in range(local_experts):
            into.swap(near, part).start()
        for part in range(local_experts):
            downs.swap(near, part).start()
    early_loads = [
        pltpu.make_async_copy(source, target, early_sem.at[index])
        for index, (source, target) in enumerate(((in_first, in_stage), (down_first, down_stage)))
    ]
    for copy in early_loads:
        copy.start()
    gain_one_row = to_f32(side_rows[EXPERTS : EXPERTS + 1, :])
    gain_two_row = to_f32(side_rows[EXPERTS + 1 : EXPERTS + 2, :])
    moe_rows = token_rows // moe_parts
    gain_two_sum = jnp.zeros((1, width), jnp.float32)
    resid_gather = CtxGather(
        place,
        lambda index, part: all_resid.at[index, pl.ds(part * moe_rows, moe_rows)],
        moe_parts,
        resid_send,
        resid_recv,
    )
    for part in range(moe_parts):
        here = pl.ds(part * moe_rows, moe_rows)
        grad_moe_in = moe_in_grads[here, :]
        values = resid[here, :]
        scale = rms_scale(values)
        weighted = grad_moe_in * gain_two_row
        gain_two_sum = gain_two_sum + jnp.sum(grad_moe_in * values * scale, 0, keepdims=True)
        grads = (
            to_f32(cot[here, :])
            + scale * weighted
            - values * (scale * scale * scale) * jnp.mean(weighted * values, -1, keepdims=True)
        )
        grad_resid[here, :] = grads
        all_resid[ctx, here, :] = grads.astype(jnp.bfloat16)
        resid_gather.begin(part)
    for part in range(1, mix_parts - 1):
        for line in ORDER:
            mix.begin(line, part)
    for copy in loads:
        copy.wait()
    column_sum.hop(0)
    late = []
    for index, (source, target) in enumerate(
        (
            (all_moe_hbm, all_moe),
            (qkv_hbm, qkv),
            (out_rows_hbm, out_rows),
            (heads_out_hbm, heads_out),
            (weights_hbm, weights),
            (all_tokens_hbm, all_tokens),
        )
    ):
        late.append(pltpu.make_async_copy(source, target, late_sem.at[index]))
        late[-1].start()

    low = lax.broadcasted_iota(jnp.int32, (1, 2 * HEAD_SIZE), 1) < HEAD_SIZE

    def spread(first):
        plain = to_f32(qkv[:, first : first + k_cols])
        other = pltpu.roll(plain, HEAD_SIZE, 1)
        zero = jnp.zeros((), jnp.float32)
        return [
            [
                jnp.where(low, plain, zero).astype(jnp.bfloat16),
                jnp.where(low, zero, other).astype(jnp.bfloat16),
            ],
            [
                jnp.where(low, other, zero).astype(jnp.bfloat16),
                jnp.where(low, zero, plain).astype(jnp.bfloat16),
            ],
        ]

    for copy in early_loads:
        copy.wait()
    early_stores = [
        pltpu.make_async_copy(source, target, early_sem.at[index])
        for index, (source, target) in enumerate(
            (
                (in_stage, in_sum.at[pl.ds(0, EARLY)]),
                (down_stage, down_sum.at[pl.ds(0, EARLY)]),
            )
        )
    ]
    for copy in early_stores:
        copy.start()

    def add_router(block, total):
        return total + dot_rows(logit_grads[block], all_moe[block])

    for part in range(moe_parts // 2):
        resid_gather.relay(part)
    for copy in late:
        copy.wait()
    full = weights[...].reshape(width, pack_cols)
    full_out = out_rows[...].reshape(q_cols, width)
    keys, values = spread(q_cols), spread(q_cols + k_cols)
    documents = seg_row[...].astype(jnp.float32)
    columns = jnp.broadcast_to(documents, (128, documents.shape[1])).T[:, :1]
    router_grads = lax.fori_loop(
        0, groups, add_router, jnp.zeros((2 * EXPERTS, width), jnp.float32)
    )
    router_sum = router_grads[:EXPERTS] + router_grads[EXPERTS:]
    for part in range(moe_parts // 2, moe_parts):
        resid_gather.relay(part)
    column_sum.hop(1)
    mix.hop(0, 0)
    for part in range(moe_parts):
        resid_gather.arrived(part)
    for part in range(local_experts):
        into.fold(part)
        downs.fold(part)
    at_lane = lax.broadcasted_iota(jnp.int32, (1, 128), 1)
    for block in range(shards):
        here = pl.ds(block * token_rows, token_rows)
        grads = outer_cols(all_resid[block], full_out).astype(jnp.bfloat16)
        head_grads[here, :] = grads
        products = to_f32(grads) * heads_out[here, :]
        deltas = jnp.zeros((token_rows, 128), jnp.float32)
        for pair in range(2):
            both = products[:, pair * 128 : pair * 128 + 128]
            first = jnp.sum(jnp.where(low, both, 0.0), -1, keepdims=True)
            second = jnp.sum(jnp.where(low, 0.0, both), -1, keepdims=True)
            deltas = jnp.where(at_lane == 2 * pair, first, deltas)
            deltas = jnp.where(at_lane == 2 * pair + 1, second, deltas)
        turned[:, here] = deltas.T
    attn_low = heads_out[...].astype(jnp.bfloat16)
    flat_resid = all_resid[...].reshape(shards * token_rows, width)
    out_grads[...] = (
        inner_rows(attn_low, flat_resid).astype(jnp.bfloat16).reshape(groups, rows, width)
    )
    out_scatter = ExpScatter(
        place,
        lambda line, part: out_grads.at[line * 2 + 1 - place.x],
        lambda line, part: out_grads.at[line * 2 + place.x],
        lambda line, part: out_crossed.at[line],
        lambda line, part: out_raised.at[raised_slot(line)],
        lambda line, part: out_lowered.at[lowered_slot(line)],
        1,
        (out_xs, out_xr, out_ls, out_lr),
    )
    for line in ORDER:
        out_scatter.begin(line, 0)
    column_sum.hop(2)
    mix.hop(1, 0)
    key_grads[...] = jnp.zeros_like(key_grads)
    value_grads[...] = jnp.zeros_like(value_grads)
    for block in range(shards):
        here = pl.ds(block * token_rows, token_rows)
        count = (block + 1) * token_rows
        at_col = block * token_rows + lax.broadcasted_iota(jnp.int32, (1, token_rows), 1)
        at_row = lax.broadcasted_iota(jnp.int32, (count, 1), 0)
        bias = jnp.where(
            (at_row <= at_col)
            & (columns[:count] == documents[:, block * token_rows : count]),
            0.0,
            MASK_FILLER,
        )
        for pair in range(2):
            lanes = slice(pair * 128, pair * 128 + 128)
            queries = qkv[here, lanes]
            grads = head_grads[here, lanes]
            query_grad = jnp.zeros((token_rows, 128), jnp.float32)
            for head in range(2):
                row = 2 * pair + head
                mine = low if head == 0 else jnp.logical_not(low)
                own_queries = jnp.where(mine, queries, jnp.zeros((), jnp.bfloat16))
                own_grads = jnp.where(mine, grads, jnp.zeros((), jnp.bfloat16))
                key, value = keys[pair][head][:count], values[pair][head][:count]
                scores = outer_cols(key, queries) * factor + bias
                probs = jnp.exp(scores - norm_rows[row : row + 1, block * token_rows : count])
                grad_probs = outer_cols(value, grads)
                grad_scores = (probs * (grad_probs - turned[row : row + 1, here])).astype(
                    jnp.bfloat16
                )
                value_grads[pair, :count, :] += dot_rows(probs.astype(jnp.bfloat16), own_grads)
                key_grads[pair, :count, :] += dot_rows(grad_scores, own_queries)
                query_grad = query_grad + inner_rows(grad_scores, key)
            qkv_grads[here, lanes] = (query_grad * factor).astype(jnp.bfloat16)
        if block == 1:
            mix.fold(1)
            mix.hop(0, 1)
            column_sum.turn()
        if block == 3:
            mix.hop(2, 0)
            mix.hop(1, 1)

    def fold_heads(first, second):
        return jnp.where(
            low,
            first + pltpu.roll(first, HEAD_SIZE, 1),
            second + pltpu.roll(second, HEAD_SIZE, 1),
        )

    qkv_grads[:, q_cols : q_cols + k_cols] = (
        fold_heads(key_grads[0], key_grads[1]) * factor
    ).astype(jnp.bfloat16)
    qkv_grads[:, q_cols + k_cols :] = fold_heads(value_grads[0], value_grads[1]).astype(
        jnp.bfloat16
    )

    normed_scatter = CtxScatter(
        place,
        lambda y, part: normed_part.at[2 * y + 1 - place.half],
        lambda y, part: normed_part.at[2 * y + place.half],
        lambda lane, part: normed_swapped.at[lane],
        lambda part: normed_crossed,
        1,
        normed_send,
        normed_recv,
    )
    gain_one_sum = jnp.zeros((1, width), jnp.float32)
    main_sum = jnp.zeros((width, main_cols), jnp.float32)
    for block in range(shards):
        here = pl.ds(block * token_rows, token_rows)
        grads = outer_cols(qkv_grads[here, :], full[:, :main_cols])
        normed_part[block] = grads.astype(jnp.bfloat16)
        own = to_f32(all_tokens[block])
        scaled = own * rms_scale(own)
        gain_one_sum = gain_one_sum + jnp.sum(grads * scaled, 0, keepdims=True)
        normed = (scaled * gain_one_row).astype(jnp.bfloat16)
        main_sum = main_sum + inner_rows(normed, qkv_grads[here, :])
    normed_scatter.swap(False, 0).start()
    normed_scatter.swap(True, 0).start()
    at_sub = lax.broadcasted_iota(jnp.int32, (128, 1), 0)
    gain_rows = jnp.where(
        at_sub == EXPERTS, gain_one_sum, jnp.where(at_sub == EXPERTS + 1, gain_two_sum, 0.0)
    )
    side = jnp.concatenate([router_sum, gain_rows[EXPERTS:, :]], 0).T
    sums[:, :, :, :main_cols] = main_sum.astype(jnp.bfloat16).reshape(
        shards, groups, rows, main_cols
    )
    sums[:, :, :, main_cols:] = side.astype(jnp.bfloat16).reshape(
        shards, groups, rows, pack_cols - main_cols
    )
    sum_scatter = ExpScatter(
        place,
        lambda line, part: sums.at[:, line * 2 + 1 - place.x],
        lambda line, part: sums.at[:, line * 2 + place.x],
        lambda line, part: sums_crossed.at[line],
        lambda line, part: sums_raised.at[raised_slot(line)],
        lambda line, part: sums_lowered.at[lowered_slot(line)],
        1,
        (sum_xs, sum_xr, sum_ls, sum_lr),
    )
    for line in ORDER:
        sum_scatter.begin(line, 0)
    for line in ORDER:
        mix.begin(line, mix_parts - 1)
    normed_scatter.fold(0)
    mix.fold(2)
    mix.hop(0, 2)
    mix.hop(2, 1)
    out_scatter.fold(0)
    out_scatter.hop(0, 0)
    mix.hop(1, 2)
    sum_scatter.fold(0)
    sum_scatter.hop(0, 0)
    out_scatter.hop(1, 0)
    mix.hop(2, 2)
    for copy in early_stores:
        copy.wait()
    stores = []
    for part in range(local_experts):
        for kind, (scatter, held, target) in enumerate(
            ((into, in_mine, in_sum), (downs, down_mine, down_sum))
        ):
            scatter.arrived(part)
            held[place.y, part] = scatter.total(part).astype(jnp.bfloat16)
            copy = pltpu.make_async_copy(
                held.at[place.y, part], target.at[EARLY + part], store_sem.at[kind, part]
            )
            copy.start()
            stores.append(copy)
    sum_scatter.hop(1, 0)
    out_scatter.hop(2, 0)
    mix.fold(3)
    mix.hop(0, 3)
    sum_scatter.hop(2, 0)
    mix.hop(1, 3)
    output_sum[...] = out_scatter.total(0)
    sums_own[...] = sum_scatter.total(0).astype(jnp.bfloat16)
    sums_all[ctx] = sums_own[ctx]
    copies = []
    for lane, to in enumerate((place.core, place.side, place.far)):
        copy = remote(
            sums_own.at[to[0]], sums_all.at[ctx], last_send.at[lane], last_recv.at[lane], to
        )
        copy.start()
        copies.append(copy)
    normed_scatter.arrived(0)
    grad_normed = normed_scatter.total(0)
    own = to_f32(tokens[...])
    scale = rms_scale(own)
    weighted = grad_normed * gain_one_row
    grad_tokens[...] = (
        grad_resid[...]
        + scale * weighted
        - own * (scale * scale * scale) * jnp.mean(weighted * own, -1, keepdims=True)
    )
    mix.hop(2, 3)
    for part in range(mix_parts):
        here = pl.ds(*MIX_CUTS[part])
        mixed_out[here, :] = (resid[here, :] + mix.total(part)).astype(jnp.bfloat16)
    here = pl.ds(mix_rows, COLUMN)
    mixed_out[here, :] = (resid[here, :] + column_sum.total()).astype(jnp.bfloat16)
    for lane, to in enumerate((place.core, place.side, place.far)):
        remote(
            sums_own.at[0], sums_all.at[to[0]], last_send.at[lane], last_recv.at[lane], to
        ).wait_recv()
    side = jnp.zeros((rows, pack_cols - main_cols), jnp.float32)
    for shard in range(shards):
        came = to_f32(sums_all[shard])
        query_sum[:, shard * q_cols : (shard + 1) * q_cols] = came[:, :q_cols]
        key_sum[:, shard * k_cols : (shard + 1) * k_cols] = came[:, q_cols : q_cols + k_cols]
        value_sum[:, shard * k_cols : (shard + 1) * k_cols] = came[:, q_cols + k_cols : main_cols]
        side = side + came[:, main_cols:]
    router_out[...] = side[:, :EXPERTS]
    diagonal = lax.broadcasted_iota(jnp.int32, (rows, rows), 0) == lax.broadcasted_iota(
        jnp.int32, (rows, rows), 1
    )
    for target, column in ((gain_one_out, EXPERTS), (gain_two_out, EXPERTS + 1)):
        target[...] = jnp.sum(
            jnp.where(diagonal, side[:, column : column + 1], 0.0), 0, keepdims=True
        )
    for copy in stores:
        copy.wait()
    for copy in copies:
        copy.wait_send()
    for scatter in (mix, column_sum, into, downs, out_scatter, normed_scatter, sum_scatter):
        scatter.finish()
    for part in range(moe_parts):
        resid_gather.sent(part)


def back(
    moe_in_grads, mixed_part, grad_in, grad_down, in_first, down_first, tokens, cot, resid, side_rows, logit_grads,
    all_moe, all_tokens, weights, out_rows, qkv, heads_out, norm_rows, seg_row,
):
    token_rows, width = tokens.shape
    shards, groups, rows, pack_cols = weights.shape
    seq_len = shards * token_rows
    q_cols, main_cols = heads_out.shape[1], qkv.shape[1]
    k_cols = (main_cols - q_cols) // 2
    experts, _, in_rows, in_cols = grad_in.shape
    down_rows = grad_down.shape[2]
    low, f32 = jnp.bfloat16, jnp.float32

    def shape(dims, dtype):
        return jax.ShapeDtypeStruct(dims, dtype)

    whole, anywhere = pl.BlockSpec(memory_space=VMEM), pl.BlockSpec(memory_space=pl.ANY)
    mix_rows = sum(size for _, size in MIX_CUTS)
    block, steps = (LINES, mix_rows, width), (LINES - 1, mix_rows, width)
    pack = (shards, rows, pack_cols)
    return pl.pallas_call(
        back_kernel,
        name="back",
        out_shape=[
            shape((token_rows, width), low),
            shape((token_rows, width), f32),
            shape((rows, shards * q_cols), f32),
            shape((rows, shards * k_cols), f32),
            shape((rows, shards * k_cols), f32),
            shape((rows, EXPERTS), f32),
            shape((1, rows), f32),
            shape((1, rows), f32),
            shape((rows, width), f32),
            shape((EARLY + experts, in_rows, in_cols), low),
            shape((EARLY + experts, down_rows, width), low),
        ],
        in_specs=[whole] + [anywhere] * 5 + [whole] * 5 + [anywhere] * 6 + [whole] * 2,
        out_specs=[whole] * 9 + [anywhere] * 2,
        scratch_shapes=[
            VMEM(block, low),
            VMEM(block, low),
            VMEM(steps, low),
            VMEM(steps, low),
            VMEM((groups, COLUMN, width), low),
            VMEM((2, 2, LINES - 1, COLUMN, width), low),
            VMEM((COLUMN, width), low),
            VMEM((2, experts, in_rows, in_cols), low),
            VMEM((2, experts, in_rows, in_cols), low),
            VMEM((experts, in_rows, in_cols), low),
            VMEM((2, experts, down_rows, width), low),
            VMEM((2, experts, down_rows, width), low),
            VMEM((experts, down_rows, width), low),
            VMEM((token_rows, width), f32),
            VMEM((shards, token_rows, width), low),
            VMEM((seq_len, q_cols), low),
            VMEM((128, seq_len), f32),
            VMEM((2, seq_len, 128), f32),
            VMEM((2, seq_len, 128), f32),
            VMEM((seq_len, main_cols), low),
            VMEM((shards, token_rows, width), low),
            VMEM((2, token_rows, width), low),
            VMEM((token_rows, width), low),
            VMEM((shards, groups, rows, pack_cols), low),
            VMEM((LINES,) + pack, low),
            *[VMEM((LINES - 1,) + pack, low)] * 2,
            VMEM((shards, rows, pack_cols), low),
            VMEM((shards, rows, pack_cols), low),
            VMEM((groups, rows, width), low),
            VMEM((LINES, rows, width), low),
            *[VMEM((LINES - 1, rows, width), low)] * 2,
            VMEM((EARLY, in_rows, in_cols), low),
            VMEM((EARLY, down_rows, width), low),
            DMA((2, experts)),
            VMEM(all_moe.shape, low),
            VMEM(all_tokens.shape, low),
            VMEM(weights.shape, low),
            VMEM(out_rows.shape, low),
            VMEM(qkv.shape, low),
            VMEM(heads_out.shape, f32),
            DMA((6,)),
            DMA((2,)),
            DMA((9,)),
            *scatter_sems(len(MIX_CUTS)),
            *column_sum_sems(),
            *scatter_sems(1),
            *scatter_sems(1),
            *square_sems(experts),
            *square_sems(experts),
            *square_sems(1),
            *square_sems(4),
            DMA((3,)),
            DMA((3,)),
        ],
        compiler_params=pltpu.CompilerParams(
            collective_id=1, has_side_effects=True, vmem_limit_bytes=62 * 2**20
        ),
    )(
        moe_in_grads, mixed_part, grad_in, grad_down, in_first, down_first, tokens, cot, resid, side_rows, logit_grads,
        all_moe, all_tokens, weights, out_rows, qkv, heads_out, norm_rows, seg_row,
    )


def two_parts(values):
    high = values.astype(jnp.bfloat16)
    return high, (values - high.astype(jnp.float32)).astype(jnp.bfloat16)


def finish_kernel(pieces, *refs):
    count = len(pieces)
    kinds = max(kind for kind, _ in pieces) + 1
    sources, targets = refs[:kinds], refs[kinds : 2 * kinds]
    held, ready = refs[2 * kinds : 2 * kinds + count], refs[2 * kinds + count : -2]
    load_sem, store_sem = refs[-2:]
    loads, stores = [], []
    for index, (kind, at) in enumerate(pieces):
        source = sources[kind] if at is None else sources[kind].at[at]
        loads.append(pltpu.make_async_copy(source, held[index], load_sem.at[index]))
        loads[-1].start()
    wide = 0
    for index, (kind, at) in enumerate(pieces):
        loads[index].wait()
        target = targets[kind] if at is None else targets[kind].at[at]
        value = held[index]
        if sources[kind].dtype != targets[kind].dtype:
            ready[wide][...] = to_f32(value[...])
            value = ready[wide]
            wide += 1
        stores.append(pltpu.make_async_copy(value, target, store_sem.at[index]))
        stores[-1].start()
    for copy in stores:
        copy.wait()


def finish(*arrays):
    wide = [array.ndim == 3 for array in arrays]
    pieces, held, ready = [], [], []
    for kind, array in enumerate(arrays):
        places = range(array.shape[0]) if wide[kind] else [None]
        for at in places:
            pieces.append((kind, at))
            dims = array.shape[1:] if wide[kind] else array.shape
            held.append(VMEM(dims, array.dtype))
            if wide[kind]:
                ready.append(VMEM(dims, jnp.float32))
    anywhere = pl.BlockSpec(memory_space=pl.ANY)
    return pl.pallas_call(
        functools.partial(finish_kernel, tuple(pieces)),
        name="finish",
        out_shape=[
            jax.ShapeDtypeStruct(array.shape, jnp.float32 if wide[kind] else array.dtype)
            for kind, array in enumerate(arrays)
        ],
        in_specs=[anywhere] * len(arrays),
        out_specs=[anywhere] * len(arrays),
        scratch_shapes=held + ready + [DMA((len(pieces),)), DMA((len(pieces),))],
        compiler_params=pltpu.CompilerParams(vmem_limit_bytes=GRANT),
    )(*arrays)


def by_heads(
    tokens,
    segments,
    routes,
    gain_attn,
    gain_moe,
    query_weight,
    key_weight,
    value_weight,
    w_output,
    w_router,
    w_expert_in,
    w_expert_out,
    cotangent,
):
    shards = lax.axis_size("ctx")
    groups = lax.axis_size("exp")
    width = tokens.shape[2]
    rows = query_weight.shape[0]
    q_cols = query_weight.shape[1] // shards
    k_cols = key_weight.shape[1] // shards
    main_cols = q_cols + 2 * k_cols
    side = 128

    (
        grad_moe_in,
        mixed_part,
        logit_grads,
        in_first,
        down_first,
        in_rest,
        down_rest,
        all_moe,
        all_tokens,
        all_weights,
        out_rows,
        qkv,
        heads_out,
        norm_rows,
        resid,
        side_rows,
    ) = ahead(
        tokens[0],
        gain_attn[None],
        gain_moe[None],
        w_router,
        query_weight,
        key_weight,
        value_weight,
        w_output,
        routes[0].T,
        segments,
        cotangent[0],
        w_expert_in,
        w_expert_out,
    )
    rest = in_rest.shape[0]
    (
        mixed_out,
        grad_tokens,
        query_sum,
        key_sum,
        value_sum,
        router_out,
        gain_one_out,
        gain_two_out,
        output_sum,
        in_sum,
        down_sum,
    ) = back(
        grad_moe_in,
        mixed_part,
        in_rest.reshape((rest, shards, -1, width)),
        down_rest.reshape((rest, shards, -1, width)),
        in_first,
        down_first,
        tokens[0],
        cotangent[0],
        resid,
        side_rows,
        logit_grads,
        all_moe,
        all_tokens,
        all_weights.reshape(shards, groups, rows, main_cols + side),
        out_rows.reshape(groups, rows, width),
        qkv.reshape(-1, main_cols),
        heads_out,
        norm_rows,
        segments,
    )
    (
        in_sum,
        down_sum,
        grad_tokens,
        mixed_out,
        query_sum,
        output_sum,
        key_sum,
        value_sum,
        router_out,
        gain_one_out,
        gain_two_out,
    ) = finish(
        in_sum,
        down_sum,
        grad_tokens,
        mixed_out,
        query_sum,
        output_sum,
        key_sum,
        value_sum,
        router_out,
        gain_one_out,
        gain_two_out,
    )
    return (
        mixed_out[None],
        grad_tokens[None],
        gain_one_out[0],
        gain_two_out[0],
        query_sum,
        key_sum,
        value_sum,
        output_sum,
        router_out,
        in_sum,
        down_sum,
    )


def solution(mesh):
    sizes = (mesh.shape["ctx"], mesh.shape["exp"])
    return jax.shard_map(
        by_heads if sizes == (4, 8) else local,
        mesh=mesh,
        in_specs=(
            P("exp", "ctx", None),
            P("exp", None),
            P("exp", "ctx", None),
            P(("ctx", "exp")),
            P(("ctx", "exp")),
            P(("ctx", "exp"), None),
            P(("ctx", "exp"), None),
            P(("ctx", "exp"), None),
            P(("ctx", "exp"), None),
            P(("ctx", "exp"), None),
            P("exp", "ctx", None),
            P("exp", "ctx", None),
            P("exp", "ctx", None),
        ),
        out_specs=(
            P("exp", "ctx", None),
            P("exp", "ctx", None),
            P(("ctx", "exp")),
            P(("ctx", "exp")),
            P(("ctx", "exp"), None),
            P(("ctx", "exp"), None),
            P(("ctx", "exp"), None),
            P(("ctx", "exp"), None),
            P(("ctx", "exp"), None),
            P("exp", "ctx", None),
            P("exp", "ctx", None),
        ),
        check_vma=False,
    )
```
